32 devices in a mesh: dp: 16 (over z, x, core), tensor: 2 (over y).
Axes of the slice: x: 2, y: 2, z: 4, core: 2. Of those that a mesh axis runs over, the one named last changes fastest.
Arguments:
- hidden: bfloat16 [64, 128, 768], P('dp'), may hold values from -6 to 6
- image: bfloat16 [64, 257, 1408], P('dp'), may hold values from -6 to 6
- segment_ids: int32 [64, 128], P('dp'), may hold values from 0 to 3, never falling along the last dimension, each value on 1 to 64 neighbouring positions
- cotangent: bfloat16 [64, 128, 768], P('dp'), may hold values from -6 to 6
- slot_block: int32 [2, 464], P('tensor'), may hold values from 0 to 463, as said below
- weight_master: float32 [2, 464, 128, 128], P('tensor', 'dp')
- moment_one: float32 [2, 464, 128, 128], P('tensor', 'dp')
- moment_two: float32 [2, 464, 128, 128], P('tensor', 'dp'), as said below
- left_stat: float32 [2, 464, 128, 128], P('tensor', 'dp'), as said below
- right_stat: float32 [2, 464, 128, 128], P('tensor', 'dp'), as said below
- left_basis: float32 [2, 464, 128, 128], P('tensor', 'dp'), as said below
- right_basis: float32 [2, 464, 128, 128], P('tensor', 'dp'), as said below
- norm_params: float32 [4, 2, 768], replicated, as said below
- norm_moment_one: float32 [4, 2, 768], replicated
- norm_moment_two: float32 [4, 2, 768], replicated, as said below
Outputs:
- output: bfloat16 [64, 128, 768], P('dp')
- input_grad: float32 [64, 128, 768], P('dp')
- weight_new: float32 [2, 464, 128, 128], P('tensor', 'dp')
- weight_copy: bfloat16 [2, 464, 128, 128], P('tensor', 'dp')
- moment_one_new: float32 [2, 464, 128, 128], P('tensor', 'dp')
- moment_two_new: float32 [2, 464, 128, 128], P('tensor', 'dp')
- left_stat_new: float32 [2, 464, 128, 128], P('tensor', 'dp')
- right_stat_new: float32 [2, 464, 128, 128], P('tensor', 'dp')
- left_basis_new: float32 [2, 464, 128, 128], P('tensor', 'dp')
- right_basis_new: float32 [2, 464, 128, 128], P('tensor', 'dp')
- norm_moment_one_new: float32 [4, 2, 768], replicated
- norm_moment_two_new: float32 [4, 2, 768], replicated
- norm_new: float32 [4, 2, 768], replicated
The draws below stay inside these ranges and needn't reach their ends.
Inputs may be any that keep to these rules, and one draw needn't show every extreme that they name: `slot_block`: each row is a permutation of 0 to 463; numbers below 462 name blocks, the others spare slots. `left_basis`: every block is orthogonal. `right_basis`: every block is orthogonal. `left_stat`: every block is symmetric positive definite. `right_stat`: every block is symmetric positive definite. `moment_two`: every entry is positive. `norm_moment_two`: every entry is positive. `norm_params`: gains are positive.
All inputs are finite; a program needn't handle non-finite values.
Results may differ from the reference program's by a relative error of at most 0.034.
Values may be sent and summed in bfloat16 or wider, within the bound.
No kernel may reach another device: no remote copies, remote signals or barrier semaphores. Data moves between devices by JAX's collectives and lax.ppermute only.
A program may use at most 256 MiB of HBM per device.

```python
import math
import jax
import jax.numpy as jnp
import numpy as np
from jax import lax

D = 768
HEADS = 12
FF = 3072
DI = 1408
NQ = 32
NPATCH = 257
NT = 96
BLOCK_EDGE = 128
STEP = 10
SEQ = 128
ROWS = 64
BLOCKS_PER_INDEX = 462
SLOTS_PER_INDEX = 464
N_TENSOR = 2


def slot_order(key):
    row_listing = [jax.random.permutation(jax.random.fold_in(key, 100 + owner_index), SLOTS_PER_INDEX) for owner_index in range(N_TENSOR)]
    return jnp.stack(row_listing).astype(jnp.int32)


def block_tables():
    half_width = D // N_TENSOR
    half_hidden = FF // N_TENSOR
    every = math.sqrt(ROWS * SEQ)
    learned = math.sqrt(ROWS * NQ)
    texts = math.sqrt(ROWS * NT)
    patches = math.sqrt(ROWS * NPATCH)
    entries = [(D, half_width, D ** (-0.5), 0.05 * every), (D, half_width, D ** (-0.5), 0.05 * every), (D, half_width, D ** (-0.5), 0.15 * every), (half_width, D, 4.0 * D ** (-0.5), 0.2 * every), (D, half_width, D ** (-0.5), 0.05 * learned), (DI, half_width, DI ** (-0.5), 0.02 * patches), (DI, half_width, DI ** (-0.5), 0.05 * patches), (half_width, D, 8.0 * D ** (-0.5), 0.2 * learned), (D, half_hidden, D ** (-0.5), 0.3 * learned), (half_hidden, D, FF ** (-0.5), 0.4 * learned), (D, half_hidden, D ** (-0.5), 0.3 * texts), (half_hidden, D, FF ** (-0.5), 0.4 * texts)]
    spread_values = []
    sizes_list = []
    for rows_count, cols_count, spread, typical in entries:
        number = rows_count // BLOCK_EDGE * (cols_count // BLOCK_EDGE)
        spread_values = spread_values + [spread] * number
        sizes_list = sizes_list + [typical] * number
    leftover_slots = SLOTS_PER_INDEX - len(spread_values)
    spread_values = spread_values + [D ** (-0.5)] * leftover_slots
    sizes_list = sizes_list + [0.1 * every] * leftover_slots
    return (np.array(spread_values, np.float32), np.array(sizes_list, np.float32))


def slot_scales(key, column):
    tables = block_tables()
    return jnp.asarray(tables[column])[slot_order(key)][:, :, None, None]


def block_shape():
    return (N_TENSOR, SLOTS_PER_INDEX, BLOCK_EDGE, BLOCK_EDGE)


def draw_slot_block(key, part):
    return slot_order(key)


def draw_weight_master(key, part):
    spread = slot_scales(key, 0)
    key = jax.random.fold_in(key, 1)
    values = jax.random.normal(key, block_shape(), jnp.float32)
    return values * spread


def draw_moment_one(key, part):
    typical = slot_scales(key, 1)
    key = jax.random.fold_in(key, 2)
    values = jax.random.normal(key, block_shape(), jnp.float32)
    return values * typical * (1.0 / 9.0)


def draw_moment_two(key, part):
    typical = slot_scales(key, 1)
    key = jax.random.fold_in(key, 3)
    factor = jax.random.uniform(key, block_shape(), jnp.float32, 1.0, 4.0)
    return factor * typical * typical * 0.001


def stats_blocks(key, typical):
    diagonal_seed, side_key = jax.random.split(key)
    diagonal_entries = jax.random.uniform(diagonal_seed, (N_TENSOR, SLOTS_PER_INDEX, BLOCK_EDGE), jnp.float32, 1.5, 6.0)
    raw = jax.random.normal(side_key, block_shape(), jnp.float32)
    symmetric = (raw + jnp.swapaxes(raw, -1, -2)) * (0.05 / math.sqrt(2.0))
    eye = jnp.eye(BLOCK_EDGE, dtype=jnp.float32)
    return (diagonal_entries[..., None] * eye + symmetric) * typical * typical * (0.05 / 0.95) * BLOCK_EDGE


def draw_left_stat(key, part):
    typical = slot_scales(key, 1)
    key = jax.random.fold_in(key, 4)
    return stats_blocks(key, typical)


def draw_right_stat(key, part):
    typical = slot_scales(key, 1)
    key = jax.random.fold_in(key, 5)
    return stats_blocks(key, typical)


def basis_blocks(key):
    block_matrix = jnp.broadcast_to(jnp.eye(BLOCK_EDGE, dtype=jnp.float32), block_shape())
    levels = BLOCK_EDGE.bit_length() - 1
    for depth_level in range(levels):
        step_stride = 1 << depth_level
        group_total = BLOCK_EDGE // (2 * step_stride)
        turn_angle = jax.random.uniform(jax.random.fold_in(key, depth_level), (N_TENSOR, SLOTS_PER_INDEX, group_total, 1, step_stride, 1), jnp.float32, -math.pi, math.pi)
        cosine = jnp.cos(turn_angle)
        sine = jnp.sin(turn_angle)
        grouped_rows = block_matrix.reshape(N_TENSOR, SLOTS_PER_INDEX, group_total, 2, step_stride, BLOCK_EDGE)
        lower = grouped_rows[:, :, :, 0:1]
        upper = grouped_rows[:, :, :, 1:2]
        turned = jnp.concatenate([cosine * lower - sine * upper, sine * lower + cosine * upper], axis=3)
        block_matrix = turned.reshape(block_shape())
    return block_matrix


def draw_left_basis(key, part):
    key = jax.random.fold_in(key, 6)
    return basis_blocks(key)


def draw_right_basis(key, part):
    key = jax.random.fold_in(key, 7)
    return basis_blocks(key)


def draw_norm_params(key, part):
    key = jax.random.fold_in(key, 8)
    gain_key, shift_key = jax.random.split(key)
    gains = jax.random.uniform(gain_key, (4, 1, D), jnp.float32, 0.6, 1.4)
    shifts = 0.2 * jax.random.normal(shift_key, (4, 1, D), jnp.float32)
    return jnp.concatenate([gains, shifts], axis=1)


def norm_scales():
    every = math.sqrt(ROWS * SEQ)
    learned = math.sqrt(ROWS * NQ)
    texts = math.sqrt(ROWS * NT)
    return jnp.array([0.7 * every, 0.7 * learned, learned, texts], jnp.float32)[:, None, None]


def draw_norm_moment_one(key, part):
    key = jax.random.fold_in(key, 9)
    values = jax.random.normal(key, (4, 2, D), jnp.float32)
    return values * norm_scales() * (1.0 / 9.0)


def draw_norm_moment_two(key, part):
    key = jax.random.fold_in(key, 10)
    factor = jax.random.uniform(key, (4, 2, D), jnp.float32, 1.0, 4.0)
    typical = norm_scales()
    return factor * typical * typical * 0.001


def steps_of(stream_key, shape, cuts, least, high):
    loudness, own = 1.0, jax.random.fold_in(stream_key, 6)
    for dim, parts in cuts:
        steps = jnp.exp(jax.random.uniform(jax.random.fold_in(own, dim), (parts,), jnp.float32, least / len(cuts), high / len(cuts)))
        loudness = loudness * jnp.repeat(steps, shape[dim] // parts).reshape([-1 if axis == dim else 1 for axis in range(len(shape))])
    return loudness


def length_profile(number_of, total, most, lean):
    portions = [(1 << 20) // math.isqrt(grade ** lean) + 1 for grade in range(2, number_of + 1)]
    spare, counts = total - most - (number_of - 1), [1] * (number_of - 1)
    while spare > 0:
        free = [i for i in range(number_of - 1) if counts[i] < most]
        mass, left = sum([portions[i] for i in free]), spare
        for i in free:
            addition = min(most - counts[i], max(1, left * portions[i] // mass), spare)
            counts[i] = counts[i] + addition
            spare = spare - addition
    return np.array([most] + counts)


def uneven_parts(stream_key, count, total, reach, skew):
    if count == 2:
        one = jax.random.randint(stream_key, (), max(1, total - reach), min(reach, total - 1) + 1)
        return jnp.stack([one, total - one])
    tallies = jnp.asarray(length_profile(count, total, reach, skew), jnp.int32)
    twos = (count - 1) // 2
    donor, receiver = tallies[1:1 + 2 * twos:2], tallies[2:2 + 2 * twos:2]
    room = jnp.minimum(donor - 1, reach - receiver)
    shifted = jax.random.randint(jax.random.fold_in(stream_key, 1), (twos,), 0, 1 << 20) % (room + 1)
    tallies = tallies.at[1:1 + 2 * twos:2].set(donor - shifted).at[2:2 + 2 * twos:2].set(receiver + shifted)
    return tallies[jax.random.permutation(jax.random.fold_in(stream_key, 2), count)]


def centred(rng, shape, scale, limit, cuts=(), kind=jnp.bfloat16):
    values = jax.random.normal(rng, shape, jnp.float32) * scale
    if len(cuts) > 0:
        values = steps_of(rng, shape, cuts, -0.22, 0.18) * values
    return jnp.clip(values, min=-limit, max=limit).astype(kind)


def setup_inputs(seed: int = 0) -> dict:
    streams_of = jax.random.split(jax.random.key(seed), 16)
    return {
        "hidden": centred(streams_of[0], (ROWS, SEQ, D), 1.0, 6.0, ((0, 16),)),
        "image": centred(streams_of[1], (ROWS, NPATCH, DI), 1.0, 6.0, ((0, 16),)),
        "segment_ids": jax.vmap(lambda own: jnp.searchsorted(jnp.cumsum(uneven_parts(own, 4, SEQ, SEQ // 2, 1)), jnp.arange(SEQ), side="right"))(jax.random.split(streams_of[2], ROWS)).reshape((ROWS, SEQ)).astype(jnp.int32),
        "cotangent": centred(streams_of[3], (ROWS, SEQ, D), 1.0, 6.0, ((0, 16),)),
        "slot_block": draw_slot_block(jax.random.fold_in(streams_of[15], 71), 0),
        "weight_master": draw_weight_master(jax.random.fold_in(streams_of[15], 71), 0),
        "moment_one": draw_moment_one(jax.random.fold_in(streams_of[15], 71), 0),
        "moment_two": draw_moment_two(jax.random.fold_in(streams_of[15], 71), 0),
        "left_stat": draw_left_stat(jax.random.fold_in(streams_of[15], 71), 0),
        "right_stat": draw_right_stat(jax.random.fold_in(streams_of[15], 71), 0),
        "left_basis": draw_left_basis(jax.random.fold_in(streams_of[15], 71), 0),
        "right_basis": draw_right_basis(jax.random.fold_in(streams_of[15], 71), 0),
        "norm_params": draw_norm_params(jax.random.fold_in(streams_of[15], 71), 0),
        "norm_moment_one": draw_norm_moment_one(jax.random.fold_in(streams_of[15], 71), 0),
        "norm_moment_two": draw_norm_moment_two(jax.random.fold_in(streams_of[15], 71), 0),
    }


@jax.custom_vjp
def low(v):
    return lax.optimization_barrier(v.astype(jnp.bfloat16)).astype(jnp.float32)

@jax.custom_vjp
def low_back(v):
    return v

def low_keep(v):
    return (low(v), None)

def low_pass(kept, grad):
    return (grad,)

def back_keep(v):
    return (v, None)

def back_low(kept, grad):
    return (low(grad),)
low.defvjp(low_keep, low_pass)
low_back.defvjp(back_keep, back_low)
beta_first = 0.9
beta_second = 0.999
beta_stats = 0.95
adam_epsilon = 1e-08
norm_epsilon = 1e-06
matrix_rate = 0.03
matrix_decay = 0.05
norm_rate = 0.6
masked_score = -1000000000.0
highest = lax.Precision.HIGHEST
column_split = (True, True, True, False, True, True, True, False, True, False, True, False)

def matrix_shapes(width, image_width, hidden_units, tensor_count):
    half_width = width // tensor_count
    half_hidden = hidden_units // tensor_count
    return [(width, half_width), (width, half_width), (width, half_width), (half_width, width), (width, half_width), (image_width, half_width), (image_width, half_width), (half_width, width), (width, half_hidden), (half_hidden, width), (width, half_hidden), (half_hidden, width)]

def unpack_blocks(blocks, shapes, block_side):
    matrices = []
    offset = 0
    for rows_count, cols_count in shapes:
        row_tiles = rows_count // block_side
        col_tiles = cols_count // block_side
        number = row_tiles * col_tiles
        portion = blocks[offset:offset + number].reshape(row_tiles, col_tiles, block_side, block_side)
        matrices.append(portion.transpose(0, 2, 1, 3).reshape(rows_count, cols_count))
        offset = offset + number
    return matrices

def pack_blocks(matrices, block_side):
    pieces = []
    for block_matrix in matrices:
        rows_count, cols_count = block_matrix.shape
        portion = block_matrix.reshape(rows_count // block_side, block_side, cols_count // block_side, block_side)
        pieces.append(portion.transpose(0, 2, 1, 3).reshape(-1, block_side, block_side))
    return jnp.concatenate(pieces, axis=0)

def layer_norm(resid_rows, gain, shift):
    center = resid_rows - lax.optimization_barrier(jnp.mean(resid_rows, axis=-1, keepdims=True))
    variance = lax.optimization_barrier(jnp.mean(center * center, axis=-1, keepdims=True))
    return center * lax.rsqrt(variance + norm_epsilon) * gain + shift

def project(inputs, weight):
    return jnp.einsum('rsd,de->rse', inputs, weight, precision=highest)

def attention(queries, key_rows, value_rows, allowed, heads):
    head_size = queries.shape[-1] // heads
    scale = head_size ** (-0.5)
    query_heads = queries.reshape(queries.shape[0], queries.shape[1], heads, head_size)
    key_heads = key_rows.reshape(key_rows.shape[0], key_rows.shape[1], heads, head_size)
    value_heads = value_rows.reshape(value_rows.shape[0], value_rows.shape[1], heads, head_size)
    scores = low_back(jnp.einsum('rqhd,rkhd->rhqk', query_heads, key_heads, precision=highest))
    scaled = scores * scale
    if allowed is not None:
        scaled = jnp.where(allowed, scaled, masked_score)
    probs = jax.nn.softmax(scaled, axis=-1)
    mixed = jnp.einsum('rhqk,rkhd->rqhd', low(probs), value_heads, precision=highest)
    return low_back(low(mixed.reshape(queries.shape)))

def feed_forward(states, weight_up, weight_down, norm_pair):
    before = low_back(project(low(states), weight_up))
    after = low_back(project(low(jax.nn.gelu(before, approximate=False)), weight_down))
    return layer_norm(states + after, norm_pair[0], norm_pair[1])

def layer(matrix_list, norm_values, layer_inputs, image_rows, allowed):
    rounded = [low(block_matrix) for block_matrix in matrix_list]
    self_query, self_key, self_value, self_out, cross_query, cross_key, cross_value, cross_out, query_up, query_down, text_up, text_down = rounded
    queries = low_back(low(project(layer_inputs, self_query)))
    key_rows = low_back(low(project(layer_inputs, self_key)))
    value_rows = low_back(low(project(layer_inputs, self_value)))
    mixed = attention(queries, key_rows, value_rows, allowed, HEADS)
    branch = low_back(project(mixed, self_out))
    first = layer_norm(layer_inputs + branch, norm_values[0, 0], norm_values[0, 1])
    learned = first[:, :NQ]
    cross_queries = low_back(low(project(low(learned), cross_query)))
    image_keys = low_back(low(project(image_rows, cross_key)))
    image_values = low_back(low(project(image_rows, cross_value)))
    looked = attention(cross_queries, image_keys, image_values, None, HEADS)
    cross_branch = low_back(project(looked, cross_out))
    second = layer_norm(learned + cross_branch, norm_values[1, 0], norm_values[1, 1])
    query_rows = feed_forward(second, query_up, query_down, norm_values[2])
    text_rows = feed_forward(first[:, NQ:], text_up, text_down, norm_values[3])
    return jnp.concatenate([query_rows, text_rows], axis=1)

def times(left_matrix, right_matrix):
    return jnp.einsum('...ij,...jk->...ik', left_matrix, right_matrix, precision=highest)

def flipped(block_matrix):
    return jnp.swapaxes(block_matrix, -1, -2)

def orthonormal(columns):
    gram = times(flipped(columns), columns)
    factor = jnp.linalg.cholesky(gram)
    return lax.linalg.triangular_solve(factor, columns, left_side=False, lower=True, transpose_a=True)

def rotated_update(gradient, master, first_moment, second_moment, left_stats, right_stats, left_bases, right_bases):
    rotated = times(times(flipped(left_bases), gradient), right_bases)
    first_new = beta_first * first_moment + (1 - beta_first) * rotated
    second_new = beta_second * second_moment + (1 - beta_second) * rotated * rotated
    step_rotated = first_new / (1 - beta_first ** STEP) / (jnp.sqrt(second_new / (1 - beta_second ** STEP)) + adam_epsilon)
    step_full = times(times(left_bases, step_rotated), flipped(right_bases))
    master_new = master - matrix_rate * (step_full + matrix_decay * master)
    left_new = beta_stats * left_stats + (1 - beta_stats) * times(gradient, flipped(gradient))
    right_new = beta_stats * right_stats + (1 - beta_stats) * times(flipped(gradient), gradient)
    return (master_new, first_new, second_new, left_new, right_new, orthonormal(times(left_new, left_bases)), orthonormal(times(right_new, right_bases)))

def reference(hidden, image, segment_ids, cotangent, slot_block, weight_master, moment_one, moment_two, left_stat, right_stat, left_basis, right_basis, norm_params, norm_moment_one, norm_moment_two):
    tensors = N_TENSOR
    shapes = matrix_shapes(D, DI, FF, tensors)
    shard_matrices = []
    for owner_index in range(tensors):
        natural = jnp.zeros_like(weight_master[owner_index]).at[slot_block[owner_index]].set(weight_master[owner_index])
        shard_matrices.append(unpack_blocks(natural[:BLOCKS_PER_INDEX], shapes, BLOCK_EDGE))
    matrices = []
    for position in range(12):
        join_axis = 1 if column_split[position] else 0
        matrices.append(jnp.concatenate([shard_matrices[owner_index][position] for owner_index in range(tensors)], axis=join_axis))
    group = math.gcd(ROWS, 32)
    group_total = ROWS // group

    def regroup(array):
        return array.reshape((group_total, group) + array.shape[1:])

    def one_group(carry, pieces):
        matrix_sums, norm_sum = carry
        group_inputs, group_image, group_segments, group_back = pieces
        layer_inputs = group_inputs.astype(jnp.float32)
        image_rows = group_image.astype(jnp.float32)
        allowed = (group_segments[:, :, None] == group_segments[:, None, :])[:, None]
        result, pullback = jax.vjp(lambda matrix_list, norm_values, acts: layer(matrix_list, norm_values, acts, image_rows, allowed), matrices, norm_params, layer_inputs)
        grad_matrices, grad_norms, grad_inputs = pullback(group_back.astype(jnp.float32))
        summed = [total + update for total, update in zip(matrix_sums, grad_matrices)]
        return ((summed, norm_sum + grad_norms), (result.astype(jnp.bfloat16), grad_inputs))
    start = ([jnp.zeros_like(block_matrix) for block_matrix in matrices], jnp.zeros_like(norm_params))
    (grad_matrices, grad_norms), (outputs, input_grads) = lax.scan(one_group, start, (regroup(hidden), regroup(image), regroup(segment_ids), regroup(cotangent)))
    output = outputs.reshape(ROWS, SEQ, D)
    input_grad = input_grads.reshape(ROWS, SEQ, D)
    slot_grads = []
    for owner_index in range(tensors):
        shard_parts = []
        for position, (rows_count, cols_count) in enumerate(shapes):
            full_grad = grad_matrices[position]
            if column_split[position]:
                shard_parts.append(full_grad[:, owner_index * cols_count:(owner_index + 1) * cols_count])
            else:
                shard_parts.append(full_grad[owner_index * rows_count:(owner_index + 1) * rows_count, :])
        packed_blocks = pack_blocks(shard_parts, BLOCK_EDGE)
        padded_matrix = jnp.concatenate([packed_blocks, jnp.zeros((SLOTS_PER_INDEX - BLOCKS_PER_INDEX, BLOCK_EDGE, BLOCK_EDGE), jnp.float32)], axis=0)
        slot_grads.append(padded_matrix[slot_block[owner_index]])
    gradient = jnp.stack(slot_grads)
    weight_new, moment_one_new, moment_two_new, left_stat_new, right_stat_new, left_basis_new, right_basis_new = rotated_update(gradient, weight_master, moment_one, moment_two, left_stat, right_stat, left_basis, right_basis)
    norm_first = beta_first * norm_moment_one + (1 - beta_first) * grad_norms
    norm_second = beta_second * norm_moment_two + (1 - beta_second) * grad_norms * grad_norms
    norm_new = norm_params - norm_rate * (norm_first / (1 - beta_first ** STEP)) / (jnp.sqrt(norm_second / (1 - beta_second ** STEP)) + adam_epsilon)
    return (output, input_grad, weight_new, weight_new.astype(jnp.bfloat16), moment_one_new, moment_two_new, left_stat_new, right_stat_new, left_basis_new, right_basis_new, norm_first, norm_second, norm_new)
```

```python
import functools

import jax
import jax.numpy as jnp
from jax import lax
from jax.experimental import pallas as pl
from jax.experimental.pallas import tpu as pltpu
from jax.sharding import PartitionSpec as P

HEADS = 12
FF = 3072
NQ = 32
STEP = 10


beta_first = 0.9
beta_second = 0.999
beta_stats = 0.95
adam_epsilon = 1e-08
norm_epsilon = 1e-06
matrix_rate = 0.03
matrix_decay = 0.05
norm_rate = 0.6
masked_score = -1000000000.0
highest = lax.Precision.HIGHEST


def matrix_shapes(width, image_width, hidden_units, tensor_count):
    half_width = width // tensor_count
    half_hidden = hidden_units // tensor_count
    return [
        (width, half_width),
        (width, half_width),
        (width, half_width),
        (half_width, width),
        (width, half_width),
        (image_width, half_width),
        (image_width, half_width),
        (half_width, width),
        (width, half_hidden),
        (half_hidden, width),
        (width, half_hidden),
        (half_hidden, width),
    ]


def unpack_blocks(blocks, shapes, block_side):
    matrices = []
    offset = 0
    for rows_count, cols_count in shapes:
        row_tiles = rows_count // block_side
        col_tiles = cols_count // block_side
        number = row_tiles * col_tiles
        portion = blocks[offset : offset + number].reshape(
            row_tiles, col_tiles, block_side, block_side
        )
        matrices.append(portion.transpose(0, 2, 1, 3).reshape(rows_count, cols_count))
        offset = offset + number
    return matrices


def layer_norm(resid_rows, gain, shift):
    center = resid_rows - jnp.mean(resid_rows, axis=-1, keepdims=True)
    variance = jnp.mean(center * center, axis=-1, keepdims=True)
    return center * lax.rsqrt(variance + norm_epsilon) * gain + shift


def first_norm(resid_rows, params):
    return layer_norm(resid_rows, params[0, 0], params[0, 1])


def second_norm(resid_rows, params):
    return layer_norm(resid_rows, params[1, 0], params[1, 1])


def last_norm(resid_rows, params):
    return jnp.concatenate(
        [
            layer_norm(resid_rows[:, :NQ], params[2, 0], params[2, 1]),
            layer_norm(resid_rows[:, NQ:], params[3, 0], params[3, 1]),
        ],
        axis=1,
    )


def gelu_exact(values):
    return jax.nn.gelu(values, approximate=False)


def dense(inputs, weight):
    return jnp.einsum("rsd,de->rse", inputs, weight, preferred_element_type=jnp.float32)


def dense_back(grads, weight):
    return jnp.einsum("rse,de->rsd", grads, weight, preferred_element_type=jnp.float32)


def block_grad(inputs, grads, block_side):
    row_count, seq_count, in_width = inputs.shape
    out_width = grads.shape[2]
    left_tiles = inputs.reshape(row_count, seq_count, in_width // block_side, block_side)
    right_tiles = grads.reshape(row_count, seq_count, out_width // block_side, block_side)
    tiles = jnp.einsum(
        "rsia,rsjb->ijab", left_tiles, right_tiles, preferred_element_type=jnp.float32
    )
    return tiles.reshape(-1, block_side, block_side)


def split_heads(array, heads):
    return array.reshape(array.shape[0], array.shape[1], heads, array.shape[2] // heads)


def masked_scores(queries, key_rows, allowed, heads, scale):
    scores = (
        jnp.einsum(
            "rqhd,rkhd->rhqk",
            split_heads(queries, heads),
            split_heads(key_rows, heads),
            preferred_element_type=jnp.float32,
        )
        * scale
    )
    if allowed is not None:
        scores = jnp.where(allowed, scores, masked_score)
    return scores


def attend(queries, key_rows, value_rows, allowed, heads, scale):
    scores = masked_scores(queries, key_rows, allowed, heads, scale)
    totals = jax.nn.logsumexp(scores, axis=-1)
    probs = jnp.exp(scores - totals[..., None]).astype(jnp.bfloat16)
    mixed = jnp.einsum(
        "rhqk,rkhd->rqhd", probs, split_heads(value_rows, heads), preferred_element_type=jnp.float32
    )
    return (mixed.reshape(queries.shape).astype(jnp.bfloat16), totals)


def attend_back(queries, key_rows, value_rows, allowed, heads, scale, totals, mixed_grad):
    scores = masked_scores(queries, key_rows, allowed, heads, scale)
    probs = jnp.exp(scores - totals[..., None])
    grad_heads = split_heads(mixed_grad, heads)
    value_grad = jnp.einsum(
        "rhqk,rqhd->rkhd",
        probs.astype(jnp.bfloat16),
        grad_heads,
        preferred_element_type=jnp.float32,
    )
    prob_grad = jnp.einsum(
        "rqhd,rkhd->rhqk",
        grad_heads,
        split_heads(value_rows, heads),
        preferred_element_type=jnp.float32,
    )
    score_grad = (
        probs * (prob_grad - jnp.sum(probs * prob_grad, axis=-1, keepdims=True)) * scale
    ).astype(jnp.bfloat16)
    query_grad = jnp.einsum(
        "rhqk,rkhd->rqhd",
        score_grad,
        split_heads(key_rows, heads),
        preferred_element_type=jnp.float32,
    )
    key_grad = jnp.einsum(
        "rhqk,rqhd->rkhd",
        score_grad,
        split_heads(queries, heads),
        preferred_element_type=jnp.float32,
    )
    return (
        query_grad.reshape(queries.shape).astype(jnp.bfloat16),
        key_grad.reshape(key_rows.shape).astype(jnp.bfloat16),
        value_grad.reshape(value_rows.shape).astype(jnp.bfloat16),
    )


def tensor_sum(partial_sum):
    mine = partial_sum.astype(jnp.bfloat16)
    if lax.axis_size("tensor") != 2:
        return lax.psum(mine, "tensor").astype(jnp.float32)
    other = lax.ppermute(mine, "tensor", [(0, 1), (1, 0)])
    return mine.astype(jnp.float32) + other.astype(jnp.float32)


def finish_branch(partial_sum, residual, normalize):
    total = tensor_sum(partial_sum)
    summed = residual + total
    return (summed, normalize(summed))


def back_sum(partial_sum):
    return tensor_sum(partial_sum)


def layer_rows(
    hidden, image, segment_ids, cotangent, weights, norm_params, heads_local, scale, block_side
):
    (
        self_query,
        self_key,
        self_value,
        self_out,
        cross_query,
        cross_key,
        cross_value,
        cross_out,
        query_up,
        query_down,
        text_up,
        text_down,
    ) = weights
    resid_input = hidden.astype(jnp.float32)
    allowed = (segment_ids[:, :, None] == segment_ids[:, None, :])[:, None]
    queries = dense(hidden, self_query).astype(jnp.bfloat16)
    key_rows = dense(hidden, self_key).astype(jnp.bfloat16)
    value_rows = dense(hidden, self_value).astype(jnp.bfloat16)
    mixed, self_totals = attend(queries, key_rows, value_rows, allowed, heads_local, scale)
    first_sum, first = finish_branch(
        dense(mixed, self_out), resid_input, lambda resid_rows: first_norm(resid_rows, norm_params)
    )
    learned = first[:, :NQ]
    learned_low = learned.astype(jnp.bfloat16)
    cross_queries = dense(learned_low, cross_query).astype(jnp.bfloat16)
    image_keys = dense(image, cross_key).astype(jnp.bfloat16)
    image_values = dense(image, cross_value).astype(jnp.bfloat16)
    looked, cross_totals = attend(cross_queries, image_keys, image_values, None, heads_local, scale)
    second_sum, second = finish_branch(
        dense(looked, cross_out), learned, lambda resid_rows: second_norm(resid_rows, norm_params)
    )
    middle_states = jnp.concatenate([second, first[:, NQ:]], axis=1)
    middle_low = middle_states.astype(jnp.bfloat16)
    query_before = dense(middle_low[:, :NQ], query_up)
    text_before = dense(middle_low[:, NQ:], text_up)
    query_hidden = gelu_exact(query_before).astype(jnp.bfloat16)
    text_hidden = gelu_exact(text_before).astype(jnp.bfloat16)
    forward_partial = jnp.concatenate(
        [dense(query_hidden, query_down), dense(text_hidden, text_down)], axis=1
    )
    third_sum, output_rows = finish_branch(
        forward_partial, middle_states, lambda resid_rows: last_norm(resid_rows, norm_params)
    )
    upstream = cotangent.astype(jnp.float32)
    _, third_pull = jax.vjp(last_norm, third_sum, norm_params)
    third_grad, norm_grad_three = third_pull(upstream)
    down_low = third_grad.astype(jnp.bfloat16)
    grad_query_down = block_grad(query_hidden, down_low[:, :NQ], block_side)
    grad_text_down = block_grad(text_hidden, down_low[:, NQ:], block_side)
    _, query_gelu_pull = jax.vjp(gelu_exact, query_before)
    _, text_gelu_pull = jax.vjp(gelu_exact, text_before)
    query_pre_grad = query_gelu_pull(dense_back(down_low[:, :NQ], query_down))[0].astype(
        jnp.bfloat16
    )
    text_pre_grad = text_gelu_pull(dense_back(down_low[:, NQ:], text_down))[0].astype(jnp.bfloat16)
    grad_query_up = block_grad(middle_low[:, :NQ], query_pre_grad, block_side)
    grad_text_up = block_grad(middle_low[:, NQ:], text_pre_grad, block_side)
    middle_partial = jnp.concatenate(
        [dense_back(query_pre_grad, query_up), dense_back(text_pre_grad, text_up)], axis=1
    )
    middle_grad = third_grad + back_sum(middle_partial)
    _, second_pull = jax.vjp(second_norm, second_sum, norm_params)
    second_grad, norm_grad_two = second_pull(middle_grad[:, :NQ])
    cross_out_low = second_grad.astype(jnp.bfloat16)
    grad_cross_out = block_grad(looked, cross_out_low, block_side)
    looked_grad = dense_back(cross_out_low, cross_out).astype(jnp.bfloat16)
    cross_query_back, image_key_back, image_value_back = attend_back(
        cross_queries, image_keys, image_values, None, heads_local, scale, cross_totals, looked_grad
    )
    grad_cross_query = block_grad(learned_low, cross_query_back, block_side)
    grad_cross_key = block_grad(image, image_key_back, block_side)
    grad_cross_value = block_grad(image, image_value_back, block_side)
    learned_grad = second_grad + back_sum(dense_back(cross_query_back, cross_query))
    first_grad_rows = jnp.concatenate([learned_grad, middle_grad[:, NQ:]], axis=1)
    _, first_pull = jax.vjp(first_norm, first_sum, norm_params)
    first_grad, norm_grad_one = first_pull(first_grad_rows)
    self_out_low = first_grad.astype(jnp.bfloat16)
    grad_self_out = block_grad(mixed, self_out_low, block_side)
    mixed_grad = dense_back(self_out_low, self_out).astype(jnp.bfloat16)
    self_query_back, self_key_back, self_value_back = attend_back(
        queries, key_rows, value_rows, allowed, heads_local, scale, self_totals, mixed_grad
    )
    grad_self_query = block_grad(hidden, self_query_back, block_side)
    grad_self_key = block_grad(hidden, self_key_back, block_side)
    grad_self_value = block_grad(hidden, self_value_back, block_side)
    input_partial = (
        dense_back(self_query_back, self_query)
        + dense_back(self_key_back, self_key)
        + dense_back(self_value_back, self_value)
    )
    input_grad = first_grad + back_sum(input_partial)
    packed = jnp.concatenate(
        [
            grad_self_query,
            grad_self_key,
            grad_self_value,
            grad_self_out,
            grad_cross_query,
            grad_cross_key,
            grad_cross_value,
            grad_cross_out,
            grad_query_up,
            grad_query_down,
            grad_text_up,
            grad_text_down,
        ],
        axis=0,
    )
    return (
        output_rows.astype(jnp.bfloat16),
        input_grad,
        packed,
        norm_grad_one + norm_grad_two + norm_grad_three,
    )


def times(left_matrix, right_matrix):
    return jnp.einsum("...ij,...jk->...ik", left_matrix, right_matrix, precision=highest)


def flipped(block_matrix):
    return jnp.swapaxes(block_matrix, -1, -2)


f32=jnp.float32; bf16=jnp.bfloat16

def split3(a):
    h=a.astype(bf16); r=a-h.astype(f32); m=r.astype(bf16); l=(r-m.astype(f32)).astype(bf16)
    return h,m,l
def split2(a):
    h=a.astype(bf16); return h,(a-h.astype(f32)).astype(bf16)
def mm(a,b,dims):
    return lax.dot_general(a,b,(dims,((),())),preferred_element_type=f32)
NN=((1,),(0,)); NT=((1,),(1,)); TN=((0,),(0,))
def dot3(a,b,dims):
    ah,al=split2(a); bh,bl=split2(b)
    return mm(ah,bh,dims)+(mm(ah,bl,dims)+mm(al,bh,dims))
def gram6(p):
    h,m,l=split3(p)
    hh=mm(h,h,TN); mmm=mm(m,m,TN); hm=mm(h,m,TN)+mm(h,l,TN)
    return hh+(mmm+(hm+hm.T))

PB=16
def panel_steps(x, kb, g):
    base=kb*PB
    lane=lax.broadcasted_iota(jnp.int32,(1,8,128),2)
    sub=lax.broadcasted_iota(jnp.int32,(1,8,128),1)
    halves=[x[:,:8],x[:,8:]]
    rinvs=[]
    for s in range(PB):
        k=base+s
        hs=s//8; r=s%8
        cur=halves[hs]
        row=cur[:,r:r+1,:]
        piv=cur[:,r:r+1,k:k+1]
        rinv=1.0/piv
        rinvs.append(rinv)
        scaled=jnp.where(lane[:,:1]==k,1.0,row)*rinv
        for h in range(hs,2):
            y=halves[h]
            col=jnp.broadcast_to(y[:,:,k:k+1],y.shape)
            if h==hs:
                low=(sub>r)
                col=jnp.where(low,col,0.0)
                y=jnp.where((lane==k)&(sub>r),0.0,y)
                y=jnp.where((lane==k)&(sub==r),1.0,y)
            else:
                y=jnp.where(lane==k,0.0,y)
            halves[h]=y-col*scaled
    return jnp.concatenate(halves,axis=1), jnp.concatenate(rinvs,axis=1)

def ortho_body(n_pad, n, g, s_ref,b_ref,q_ref,a_ref,p_ref,d_ref):
    def first(i,c):
        p=dot3(s_ref[i],b_ref[i],NN)
        p_ref[i]=p
        a_ref[i]=gram6(p)
        return c
    lax.fori_loop(0,n,first,0)
    eye=(lax.broadcasted_iota(jnp.int32,(128,128),0)==lax.broadcasted_iota(jnp.int32,(128,128),1)).astype(f32)
    for i in range(n,n_pad):
        a_ref[i]=eye
    lane=lax.broadcasted_iota(jnp.int32,(1,PB,128),2)
    sub=lax.broadcasted_iota(jnp.int32,(1,PB,128),1)
    for kb in range(128//PB):
        base=kb*PB; end=base+PB
        def group(gi,c):
            i0=gi*g
            x=a_ref[pl.ds(i0,g),base:end,:]
            x,rinv=panel_steps(x,kb,g)
            w=jnp.where((lane>=base)&(lane<end)&(lane-base>sub),0.0,x)
            d_ref[pl.ds(i0,g),base:end,:]=jnp.broadcast_to(rinv,x.shape)
            a_ref[pl.ds(i0,g),base:end,:]=w
            if end<128:
                u=jnp.where(lane>=end,x*rinv,0.0)
                wh,wm,wl=split3(w); uh,um,ul=split3(u)
                lhs=jnp.concatenate([uh,uh,um,uh,ul,um],axis=1)
                rhs=jnp.concatenate([wh,wm,wh,wl,wh,wm],axis=1)
                lane2=lax.broadcasted_iota(jnp.int32,(128-end,128),1)
                inside=(lane2>=base)&(lane2<end)
                for j in range(g):
                    upd=mm(lhs[j],rhs[j],TN)
                    old=a_ref[i0+j,end:,:]
                    a_ref[i0+j,end:,:]=jnp.where(inside,0.0,old)-upd[end:,:]
            return c
        lax.fori_loop(0,n_pad//g,group,0)
    ii=lax.broadcasted_iota(jnp.int32,(128,128),0); jj=lax.broadcasted_iota(jnp.int32,(128,128),1)
    def last(i,c):
        inv=jnp.where(ii>=jj,a_ref[i],0.0)*jnp.sqrt(d_ref[i])
        q_ref[i]=dot3(p_ref[i],inv,NT)
        return c
    lax.fori_loop(0,n,last,0)

def ortho(s,b,g=29):
    n=s.shape[0]; n_pad=-(-n//g)*g
    return pl.pallas_call(
        functools.partial(ortho_body,n_pad,n,g),
        out_shape=jax.ShapeDtypeStruct(s.shape,f32),
        in_specs=[pl.BlockSpec(memory_space=pltpu.VMEM)]*2,
        out_specs=pl.BlockSpec(memory_space=pltpu.VMEM),
        scratch_shapes=[pltpu.VMEM((n_pad,128,128),f32),pltpu.VMEM((n,128,128),f32),pltpu.VMEM((n_pad,128,128),f32)],
        compiler_params=pltpu.CompilerParams(vmem_limit_bytes=50*1024*1024),
    )(s,b)


def orthonormal_pair(left_new, left_bases, right_new, right_bases):
    count = left_new.shape[0]
    both = ortho(
        jnp.concatenate([left_new, right_new]), jnp.concatenate([left_bases, right_bases]), count
    )
    return both[:count], both[count:]


def rotated_update(
    gradient, master, first_moment, second_moment, left_stats, right_stats, left_bases, right_bases
):
    rotated = times(times(flipped(left_bases), gradient), right_bases)
    first_new = beta_first * first_moment + (1 - beta_first) * rotated
    second_new = beta_second * second_moment + (1 - beta_second) * rotated * rotated
    step_rotated = (
        first_new
        / (1 - beta_first**STEP)
        / (jnp.sqrt(second_new / (1 - beta_second**STEP)) + adam_epsilon)
    )
    step_full = times(times(left_bases, step_rotated), flipped(right_bases))
    master_new = master - matrix_rate * (step_full + matrix_decay * master)
    left_new = beta_stats * left_stats + (1 - beta_stats) * times(gradient, flipped(gradient))
    right_new = beta_stats * right_stats + (1 - beta_stats) * times(flipped(gradient), gradient)
    return (
        master_new,
        first_new,
        second_new,
        left_new,
        right_new,
        *orthonormal_pair(left_new, left_bases, right_new, right_bases),
    )


def per_device(
    hidden,
    image,
    segment_ids,
    cotangent,
    slot_block,
    weight_master,
    moment_one,
    moment_two,
    left_stat,
    right_stat,
    left_basis,
    right_basis,
    norm_params,
    norm_moment_one,
    norm_moment_two,
):
    tensors = lax.axis_size("tensor")
    width = hidden.shape[2]
    image_width = image.shape[2]
    block_side = weight_master.shape[2]
    heads_local = HEADS // tensors
    scale = (width // HEADS) ** (-0.5)
    shapes = matrix_shapes(width, image_width, FF, tensors)
    block_count = sum(
        (rows_count // block_side * (cols_count // block_side) for rows_count, cols_count in shapes)
    )
    order = slot_block[0]
    slot_count = order.shape[0]
    gathered = lax.all_gather(weight_master[0].astype(jnp.bfloat16), "dp", axis=0, tiled=True)
    inverse = jnp.zeros_like(order).at[order].set(jnp.arange(slot_count, dtype=jnp.int32))
    natural = gathered[inverse[:block_count]]
    weights = unpack_blocks(natural, shapes, block_side)
    used_slot = (order < block_count)[:, None, None]
    safe_order = jnp.minimum(order, block_count - 1)
    owned = None
    out_rows, in_grad, packed, norm_part = layer_rows(
        hidden, image, segment_ids, cotangent, weights, norm_params, heads_local, scale, block_side
    )
    owned = lax.psum_scatter(
        jnp.where(used_slot, packed.astype(jnp.bfloat16)[safe_order], 0.0),
        "dp",
        scatter_dimension=0,
        tiled=True,
    ).astype(jnp.float32)
    norm_total = lax.psum(norm_part, "dp")
    updated = rotated_update(
        owned,
        weight_master[0],
        moment_one[0],
        moment_two[0],
        left_stat[0],
        right_stat[0],
        left_basis[0],
        right_basis[0],
    )
    (
        weight_new,
        moment_one_new,
        moment_two_new,
        left_stat_new,
        right_stat_new,
        left_basis_new,
        right_basis_new,
    ) = [array[None] for array in updated]
    norm_first = beta_first * norm_moment_one + (1 - beta_first) * norm_total
    norm_second = beta_second * norm_moment_two + (1 - beta_second) * norm_total * norm_total
    norm_new = norm_params - norm_rate * (norm_first / (1 - beta_first**STEP)) / (
        jnp.sqrt(norm_second / (1 - beta_second**STEP)) + adam_epsilon
    )
    return (
        out_rows,
        in_grad,
        weight_new,
        weight_new.astype(jnp.bfloat16),
        moment_one_new,
        moment_two_new,
        left_stat_new,
        right_stat_new,
        left_basis_new,
        right_basis_new,
        norm_first,
        norm_second,
        norm_new,
    )


def solution(mesh):
    in_specs = (
        P("dp", None, None),
        P("dp", None, None),
        P("dp", None),
        P("dp", None, None),
        P("tensor", None),
        P("tensor", "dp", None, None),
        P("tensor", "dp", None, None),
        P("tensor", "dp", None, None),
        P("tensor", "dp", None, None),
        P("tensor", "dp", None, None),
        P("tensor", "dp", None, None),
        P("tensor", "dp", None, None),
        P(),
        P(),
        P(),
    )
    out_specs = (
        P("dp", None, None),
        P("dp", None, None),
        P("tensor", "dp", None, None),
        P("tensor", "dp", None, None),
        P("tensor", "dp", None, None),
        P("tensor", "dp", None, None),
        P("tensor", "dp", None, None),
        P("tensor", "dp", None, None),
        P("tensor", "dp", None, None),
        P("tensor", "dp", None, None),
        P(),
        P(),
        P(),
    )
    return jax.shard_map(
        per_device, mesh=mesh, in_specs=in_specs, out_specs=out_specs, check_vma=False
    )
```

```python
import functools

import jax
import jax.numpy as jnp
from jax import lax
from jax.experimental import pallas as pl
from jax.experimental.pallas import tpu as pltpu
from jax.sharding import PartitionSpec as P

HEADS = 12
FF = 3072
NQ = 32
STEP = 10


beta_first = 0.9
beta_second = 0.999
beta_stats = 0.95
adam_epsilon = 1e-08
norm_epsilon = 1e-06
matrix_rate = 0.03
matrix_decay = 0.05
norm_rate = 0.6
masked_score = -1000000000.0
highest = lax.Precision.HIGHEST


TILE = 128
PATCHES_PAD = 16
f32 = jnp.float32
bf16 = jnp.bfloat16
NN = ((1,), (0,))
NT = ((1,), (1,))
TN = ((0,), (0,))
VMEM_BYTES = 56 * 1024 * 1024


def mm(left, right, dims):
    return lax.dot_general(left, right, (dims, ((), ())), preferred_element_type=f32)


def vmem_specs(count):
    return [pl.BlockSpec(memory_space=pltpu.VMEM)] * count


def any_specs(count):
    return [pl.BlockSpec(memory_space=pl.ANY)] * count


def vmem_params():
    return pltpu.CompilerParams(vmem_limit_bytes=VMEM_BYTES)


def cost(flops, bytes_accessed, transcendentals=0):
    return pl.CostEstimate(
        flops=int(flops), bytes_accessed=int(bytes_accessed), transcendentals=int(transcendentals)
    )


def matrix_of(blocks_ref, row_first, row_count, col_first, col_count, col_total, base=0):
    rows = []
    for row in range(row_count):
        first = base + (row_first + row) * col_total + col_first
        rows.append(
            jnp.concatenate([blocks_ref[first + col] for col in range(col_count)], axis=1)
        )
    return jnp.concatenate(rows, axis=0)


def norm_forward(resid):
    center = resid - jnp.mean(resid, axis=-1, keepdims=True)
    inverse = lax.rsqrt(jnp.mean(center * center, axis=-1, keepdims=True) + norm_epsilon)
    return center * inverse, inverse


def norm_backward(resid, upstream, gain):
    unit, inverse = norm_forward(resid)
    scaled = upstream * gain
    mean_scaled = jnp.mean(scaled, axis=-1, keepdims=True)
    mean_product = jnp.mean(scaled * unit, axis=-1, keepdims=True)
    grad = inverse * (scaled - mean_scaled - unit * mean_product)
    gain_grad = jnp.sum(upstream * unit, axis=0, keepdims=True)
    shift_grad = jnp.sum(upstream, axis=0, keepdims=True)
    return grad, gain_grad, shift_grad


def head_pair(tile):
    low_half = lax.broadcasted_iota(jnp.int32, tile.shape, 1) < TILE // 2
    zero = jnp.zeros_like(tile)
    return jnp.concatenate(
        [jnp.where(low_half, tile, zero), jnp.where(low_half, zero, tile)], axis=0
    )


def side_by_side(stacked):
    half = stacked.shape[0] // 2
    return jnp.concatenate([stacked[:half], stacked[half:]], axis=1)


def pair_probs(queries, keys, allowed, scale):
    scores = mm(head_pair(queries), keys, NT) * scale
    scores = jnp.where(allowed, scores, masked_score)
    weights = jnp.exp(scores - jnp.max(scores, axis=-1, keepdims=True))
    return weights / jnp.sum(weights, axis=-1, keepdims=True)


def pair_mix(probs, values):
    count = probs.shape[0] // 2
    low_half = lax.broadcasted_iota(jnp.int32, (count, TILE), 1) < TILE // 2
    mixed = mm(probs.astype(bf16), values, NN)
    return jnp.where(low_half, mixed[:count], mixed[count:]).astype(bf16)


def pair_backward(queries, keys, values, probs, mixed_grad, scale):
    grad_pair = head_pair(mixed_grad)
    value_grad = mm(probs.astype(bf16), grad_pair, TN).astype(bf16)
    prob_grad = mm(grad_pair, values, NT)
    inner = jnp.sum(probs * prob_grad, axis=-1, keepdims=True)
    score_grad = (probs * (prob_grad - inner) * scale).astype(bf16)
    count = queries.shape[0]
    low_half = lax.broadcasted_iota(jnp.int32, (count, TILE), 1) < TILE // 2
    both = mm(score_grad, keys, NN)
    query_grad = jnp.where(low_half, both[:count], both[count:]).astype(bf16)
    key_grad = mm(score_grad, head_pair(queries), TN).astype(bf16)
    return query_grad, key_grad, value_grad


def load_blocks(source, first, count, target, semaphore):
    copy = pltpu.make_async_copy(source.at[pl.ds(first, count)], target, semaphore)
    copy.start()
    return copy


class Plan:
    def __init__(self, rows, seq, width, image_width, patches, heads, hidden_units):
        self.rows, self.seq, self.width = rows, seq, width
        self.image_width, self.heads, self.hidden = image_width, heads, hidden_units
        self.half = heads * (TILE // 2)
        self.patches = patches
        self.keys = -(-patches // PATCHES_PAD) * PATCHES_PAD
        self.wt, self.ht = width // TILE, self.half // TILE
        self.it, self.ft = image_width // TILE, hidden_units // TILE
        square, cross, feed = self.wt * self.ht, self.it * self.ht, self.wt * self.ft
        self.square, self.cross, self.feed = square, cross, feed
        self.self_first, self.self_count = 0, 4 * square
        self.cross_first, self.cross_count = 4 * square, 2 * square + 2 * cross
        self.query_first = self.cross_first + self.cross_count
        self.text_first = self.query_first + 2 * feed
        self.block_count = self.text_first + 2 * feed
        self.tokens = rows * seq
        self.learned = rows * NQ
        self.texts = rows * (seq - NQ)


def self_forward_body(plan, scale, nat, hidden, seg_row, seg_col, qkv, probs, mixed, part, w, sem):
    copy = load_blocks(nat, plan.self_first, plan.self_count, w, sem)
    copy.wait()
    for piece in range(3):
        matrix = matrix_of(w, 0, plan.wt, 0, plan.ht, plan.ht, piece * plan.square)
        qkv[piece] = mm(hidden[...], matrix, NN).astype(bf16)

    def one(row, carry):
        place = pl.ds(pl.multiple_of(row * plan.seq, plan.seq), plan.seq)
        allowed = seg_col[row] == seg_row[row]
        allowed = jnp.concatenate([allowed, allowed], axis=0)
        for tile in range(plan.ht):
            cols = slice(tile * TILE, (tile + 1) * TILE)
            found = pair_probs(qkv[0, place, cols], qkv[1, place, cols], allowed, scale)
            probs[row, tile] = found
            mixed[place, cols] = pair_mix(found, qkv[2, place, cols])
        return carry

    lax.fori_loop(0, plan.rows, one, 0)
    matrix = matrix_of(w, 0, plan.ht, 0, plan.wt, plan.wt, 3 * plan.square)
    part[...] = mm(mixed[...], matrix, NN).astype(bf16)


def self_forward(plan, scale, nat, hidden, seg_row, seg_col):
    tokens, half, width = plan.tokens, plan.half, plan.width
    return pl.pallas_call(
        functools.partial(self_forward_body, plan, scale),
        out_shape=(
            jax.ShapeDtypeStruct((3, tokens, half), bf16),
            jax.ShapeDtypeStruct((plan.rows, plan.ht, 2 * plan.seq, plan.seq), f32),
            jax.ShapeDtypeStruct((tokens, half), bf16),
            jax.ShapeDtypeStruct((tokens, width), bf16),
        ),
        in_specs=any_specs(1) + vmem_specs(3),
        out_specs=tuple(vmem_specs(4)),
        scratch_shapes=[
            pltpu.VMEM((plan.self_count, TILE, TILE), bf16),
            pltpu.SemaphoreType.DMA,
        ],
        compiler_params=vmem_params(),
        cost_estimate=cost(2 * tokens * width * half * 4, 8e6),
        name="self_forward",
    )(nat, hidden, seg_row, seg_col)


def image_body(plan, nat, image, keys, values, w, sem):
    copy = load_blocks(nat, plan.cross_first + plan.square, 2 * plan.cross, w, sem)
    copy.wait()
    for piece, target in ((0, keys), (1, values)):
        matrix = matrix_of(w, 0, plan.it, 0, plan.ht, plan.ht, piece * plan.cross)

        def one(row, carry):
            place = pl.ds(pl.multiple_of(row * plan.keys, plan.keys), plan.keys)
            target[place, :] = mm(image[place, :], matrix, NN).astype(bf16)
            return carry

        lax.fori_loop(0, plan.rows, one, 0)


def image_forward(plan, nat, image):
    total = plan.rows * plan.keys
    return pl.pallas_call(
        functools.partial(image_body, plan),
        out_shape=(jax.ShapeDtypeStruct((total, plan.half), bf16),) * 2,
        in_specs=any_specs(1) + vmem_specs(1),
        out_specs=tuple(vmem_specs(2)),
        scratch_shapes=[
            pltpu.VMEM((2 * plan.cross, TILE, TILE), bf16),
            pltpu.SemaphoreType.DMA,
        ],
        compiler_params=vmem_params(),
        cost_estimate=cost(4 * total * plan.image_width * plan.half, 8e6),
        name="image_forward",
    )(nat, image)


def cross_forward_body(
    plan, scale, nat, hidden, mine, other, params, image_keys, image_values,
    resid, first_query, first_text, low_query, low_text, queries, probs, mixed, part, w, sem,
):
    copy = load_blocks(nat, plan.cross_first, plan.cross_count, w, sem)
    gain, shift = params[0, 0:1], params[0, 1:2]
    text = plan.seq - NQ

    def one_norm(row, carry):
        place = pl.ds(pl.multiple_of(row * plan.seq, plan.seq), plan.seq)
        summed = hidden[place, :].astype(f32) + (
            mine[place, :].astype(f32) + other[place, :].astype(f32)
        )
        resid[place, :] = summed
        first = norm_forward(summed)[0] * gain + shift
        query_place = pl.ds(pl.multiple_of(row * NQ, NQ), NQ)
        text_place = pl.ds(pl.multiple_of(row * text, text), text)
        first_query[query_place, :] = first[:NQ]
        first_text[text_place, :] = first[NQ:]
        low_query[query_place, :] = first[:NQ].astype(bf16)
        low_text[text_place, :] = first[NQ:].astype(bf16)
        return carry

    lax.fori_loop(0, plan.rows, one_norm, 0)
    copy.wait()
    matrix = matrix_of(w, 0, plan.wt, 0, plan.ht, plan.ht)
    queries[...] = mm(low_query[...], matrix, NN).astype(bf16)
    allowed = lax.broadcasted_iota(jnp.int32, (2 * NQ, plan.keys), 1) < plan.patches

    def one(row, carry):
        query_place = pl.ds(pl.multiple_of(row * NQ, NQ), NQ)
        place = pl.ds(pl.multiple_of(row * plan.keys, plan.keys), plan.keys)
        for tile in range(plan.ht):
            cols = slice(tile * TILE, (tile + 1) * TILE)
            found = pair_probs(queries[query_place, cols], image_keys[place, cols], allowed, scale)
            probs[row, tile] = found
            mixed[query_place, cols] = pair_mix(found, image_values[place, cols])
        return carry

    lax.fori_loop(0, plan.rows, one, 0)
    matrix = matrix_of(w, 0, plan.ht, 0, plan.wt, plan.wt, plan.square + 2 * plan.cross)
    part[...] = mm(mixed[...], matrix, NN).astype(bf16)


def cross_forward(plan, scale, nat, hidden, mine, other, params, image_keys, image_values):
    learned, texts, width, half = plan.learned, plan.texts, plan.width, plan.half
    return pl.pallas_call(
        functools.partial(cross_forward_body, plan, scale),
        out_shape=(
            jax.ShapeDtypeStruct((plan.tokens, width), f32),
            jax.ShapeDtypeStruct((learned, width), f32),
            jax.ShapeDtypeStruct((texts, width), f32),
            jax.ShapeDtypeStruct((learned, width), bf16),
            jax.ShapeDtypeStruct((texts, width), bf16),
            jax.ShapeDtypeStruct((learned, half), bf16),
            jax.ShapeDtypeStruct((plan.rows, plan.ht, 2 * NQ, plan.keys), f32),
            jax.ShapeDtypeStruct((learned, half), bf16),
            jax.ShapeDtypeStruct((learned, width), bf16),
        ),
        in_specs=any_specs(1) + vmem_specs(6),
        out_specs=tuple(vmem_specs(9)),
        scratch_shapes=[
            pltpu.VMEM((plan.cross_count, TILE, TILE), bf16),
            pltpu.SemaphoreType.DMA,
        ],
        compiler_params=vmem_params(),
        cost_estimate=cost(4 * learned * width * half, 1.2e7),
        name="cross_forward",
    )(nat, hidden, mine, other, params, image_keys, image_values)


def gelu_parts(values):
    normal = 0.5 * (1.0 + lax.erf(values * 0.7071067811865476))
    density = 0.3989422804014327 * jnp.exp(-0.5 * values * values)
    return values * normal, normal + values * density


def feed_forward_tail(plan, states_low, w, gated, slope, part):
    def one_up(chunk, carry):
        matrix = matrix_of(w, 0, plan.wt, chunk * 2, 2, plan.ft)
        active, derivative = gelu_parts(mm(states_low[...], matrix, NN))
        cols = pl.ds(pl.multiple_of(chunk * 2 * TILE, 2 * TILE), 2 * TILE)
        gated[:, cols] = active.astype(bf16)
        slope[:, cols] = derivative
        return carry

    lax.fori_loop(0, plan.ft // 2, one_up, 0)

    def one_down(chunk, carry):
        matrix = matrix_of(w, 0, plan.ft, chunk * 2, 2, plan.wt, plan.feed)
        cols = pl.ds(pl.multiple_of(chunk * 2 * TILE, 2 * TILE), 2 * TILE)
        part[:, cols] = mm(gated[...], matrix, NN).astype(bf16)
        return carry

    lax.fori_loop(0, plan.wt // 2, one_down, 0)


def text_forward_body(plan, nat, low_text, gated, slope, part, w, sem):
    copy = load_blocks(nat, plan.text_first, 2 * plan.feed, w, sem)
    copy.wait()
    feed_forward_tail(plan, low_text, w, gated, slope, part)


def query_forward_body(
    plan, nat, first_query, mine, other, params, resid, second, low, gated, slope, part, w, sem
):
    copy = load_blocks(nat, plan.query_first, 2 * plan.feed, w, sem)
    summed = first_query[...] + (mine[...].astype(f32) + other[...].astype(f32))
    resid[...] = summed
    normed = norm_forward(summed)[0] * params[1, 0:1] + params[1, 1:2]
    second[...] = normed
    low[...] = normed.astype(bf16)
    copy.wait()
    feed_forward_tail(plan, low, w, gated, slope, part)


def feed_shapes(plan, count):
    return (
        jax.ShapeDtypeStruct((count, plan.hidden), bf16),
        jax.ShapeDtypeStruct((count, plan.hidden), f32),
        jax.ShapeDtypeStruct((count, plan.width), bf16),
    )


def feed_scratch(plan):
    return [pltpu.VMEM((2 * plan.feed, TILE, TILE), bf16), pltpu.SemaphoreType.DMA]


def text_forward(plan, nat, low_text):
    return pl.pallas_call(
        functools.partial(text_forward_body, plan),
        out_shape=feed_shapes(plan, plan.texts),
        in_specs=any_specs(1) + vmem_specs(1),
        out_specs=tuple(vmem_specs(3)),
        scratch_shapes=feed_scratch(plan),
        compiler_params=vmem_params(),
        cost_estimate=cost(4 * plan.texts * plan.width * plan.hidden, 1e7),
        name="text_forward",
    )(nat, low_text)


def query_forward(plan, nat, first_query, mine, other, params):
    count, width = plan.learned, plan.width
    return pl.pallas_call(
        functools.partial(query_forward_body, plan),
        out_shape=(
            jax.ShapeDtypeStruct((count, width), f32),
            jax.ShapeDtypeStruct((count, width), f32),
            jax.ShapeDtypeStruct((count, width), bf16),
        )
        + feed_shapes(plan, count),
        in_specs=any_specs(1) + vmem_specs(4),
        out_specs=tuple(vmem_specs(6)),
        scratch_shapes=feed_scratch(plan),
        compiler_params=vmem_params(),
        cost_estimate=cost(4 * count * width * plan.hidden, 8e6),
        name="query_forward",
    )(nat, first_query, mine, other, params)


def feed_backward_body(
    plan, first_block, which, nat, states, mine, other, upstream, params, slope,
    out, grad, grad_low, before_low, part, norm_grad, w, sem,
):
    copy = load_blocks(nat, first_block, 2 * plan.feed, w, sem)
    gain, shift = params[which, 0:1], params[which, 1:2]
    count = states.shape[0] // plan.rows
    norm_grad[...] = jnp.zeros_like(norm_grad)

    def one_norm(row, carry):
        place = pl.ds(pl.multiple_of(row * count, count), count)
        summed = states[place, :] + (mine[place, :].astype(f32) + other[place, :].astype(f32))
        out[place, :] = (norm_forward(summed)[0] * gain + shift).astype(bf16)
        found, gain_grad, shift_grad = norm_backward(
            summed, upstream[place, :].astype(f32), gain
        )
        grad[place, :] = found
        grad_low[place, :] = found.astype(bf16)
        norm_grad[0:1] += gain_grad
        norm_grad[1:2] += shift_grad
        return carry

    lax.fori_loop(0, plan.rows, one_norm, 0)
    copy.wait()

    def one_down(chunk, carry):
        matrix = matrix_of(w, chunk * 2, 2, 0, plan.wt, plan.wt, plan.feed)
        cols = pl.ds(pl.multiple_of(chunk * 2 * TILE, 2 * TILE), 2 * TILE)
        before_low[:, cols] = (mm(grad_low[...], matrix, NT) * slope[:, cols]).astype(bf16)
        return carry

    lax.fori_loop(0, plan.ft // 2, one_down, 0)

    def one_up(chunk, carry):
        matrix = matrix_of(w, chunk * 2, 2, 0, plan.ft, plan.ft)
        cols = pl.ds(pl.multiple_of(chunk * 2 * TILE, 2 * TILE), 2 * TILE)
        part[:, cols] = mm(before_low[...], matrix, NT).astype(bf16)
        return carry

    lax.fori_loop(0, plan.wt // 2, one_up, 0)


def feed_backward(plan, first_block, which, nat, states, mine, other, upstream, params, slope):
    count, width = states.shape
    return pl.pallas_call(
        functools.partial(feed_backward_body, plan, first_block, which),
        out_shape=(
            jax.ShapeDtypeStruct((count, width), bf16),
            jax.ShapeDtypeStruct((count, width), f32),
            jax.ShapeDtypeStruct((count, width), bf16),
            jax.ShapeDtypeStruct((count, plan.hidden), bf16),
            jax.ShapeDtypeStruct((count, width), bf16),
            jax.ShapeDtypeStruct((2, width), f32),
        ),
        in_specs=any_specs(1) + vmem_specs(6),
        out_specs=tuple(vmem_specs(6)),
        scratch_shapes=feed_scratch(plan),
        compiler_params=vmem_params(),
        cost_estimate=cost(4 * count * width * plan.hidden, 1e7),
        name="feed_backward",
    )(nat, states, mine, other, upstream, params, slope)


def cross_backward_body(
    plan, scale, nat, resid, third_grad, mine, other, params, queries, keys, values, probs,
    grad, grad_low, query_back, key_back, value_back, part, norm_grad, looked, w, sem,
):
    copy = load_blocks(nat, plan.cross_first, plan.cross_count, w, sem)
    upstream = third_grad[...] + (mine[...].astype(f32) + other[...].astype(f32))
    found, gain_grad, shift_grad = norm_backward(resid[...], upstream, params[1, 0:1])
    grad[...] = found
    grad_low[...] = found.astype(bf16)
    norm_grad[0:1] = gain_grad
    norm_grad[1:2] = shift_grad
    copy.wait()
    matrix = matrix_of(w, 0, plan.ht, 0, plan.wt, plan.wt, plan.square + 2 * plan.cross)
    looked[...] = mm(grad_low[...], matrix, NT).astype(bf16)

    def one(row, carry):
        query_place = pl.ds(pl.multiple_of(row * NQ, NQ), NQ)
        place = pl.ds(pl.multiple_of(row * plan.keys, plan.keys), plan.keys)
        for tile in range(plan.ht):
            cols = slice(tile * TILE, (tile + 1) * TILE)
            query_grad, key_grad, value_grad = pair_backward(
                queries[query_place, cols], keys[place, cols], values[place, cols],
                probs[row, tile], looked[query_place, cols], scale,
            )
            query_back[query_place, cols] = query_grad
            key_back[place, cols] = key_grad
            value_back[place, cols] = value_grad
        return carry

    lax.fori_loop(0, plan.rows, one, 0)
    matrix = matrix_of(w, 0, plan.wt, 0, plan.ht, plan.ht)
    part[...] = mm(query_back[...], matrix, NT).astype(bf16)


def cross_backward(
    plan, scale, nat, resid, third_grad, mine, other, params, queries, keys, values, probs
):
    learned, width, half = plan.learned, plan.width, plan.half
    return pl.pallas_call(
        functools.partial(cross_backward_body, plan, scale),
        out_shape=(
            jax.ShapeDtypeStruct((learned, width), f32),
            jax.ShapeDtypeStruct((learned, width), bf16),
            jax.ShapeDtypeStruct((learned, half), bf16),
            jax.ShapeDtypeStruct(keys.shape, bf16),
            jax.ShapeDtypeStruct(keys.shape, bf16),
            jax.ShapeDtypeStruct((learned, width), bf16),
            jax.ShapeDtypeStruct((2, width), f32),
        ),
        in_specs=any_specs(1) + vmem_specs(9),
        out_specs=tuple(vmem_specs(7)),
        scratch_shapes=[
            pltpu.VMEM((learned, half), bf16),
            pltpu.VMEM((plan.cross_count, TILE, TILE), bf16),
            pltpu.SemaphoreType.DMA,
        ],
        compiler_params=vmem_params(),
        cost_estimate=cost(8 * learned * width * half, 1e7),
        name="cross_backward",
    )(nat, resid, third_grad, mine, other, params, queries, keys, values, probs)


def self_backward_body(
    plan, scale, nat, resid, query_grad, query_mine, query_other, text_grad, text_mine,
    text_other, params, qkv, probs,
    grad, grad_low, back, part, norm_grad, mixed, w, sem,
):
    copy = load_blocks(nat, plan.self_first, plan.self_count, w, sem)
    text = plan.seq - NQ
    gain = params[0, 0:1]
    norm_grad[...] = jnp.zeros_like(norm_grad)

    def one_norm(row, carry):
        place = pl.ds(pl.multiple_of(row * plan.seq, plan.seq), plan.seq)
        query_place = pl.ds(pl.multiple_of(row * NQ, NQ), NQ)
        text_place = pl.ds(pl.multiple_of(row * text, text), text)
        upstream = jnp.concatenate(
            [
                query_grad[query_place, :]
                + (query_mine[query_place, :].astype(f32) + query_other[query_place, :].astype(f32)),
                text_grad[text_place, :]
                + (text_mine[text_place, :].astype(f32) + text_other[text_place, :].astype(f32)),
            ],
            axis=0,
        )
        found, gain_grad, shift_grad = norm_backward(resid[place, :], upstream, gain)
        grad[place, :] = found
        grad_low[place, :] = found.astype(bf16)
        norm_grad[0:1] += gain_grad
        norm_grad[1:2] += shift_grad
        return carry

    lax.fori_loop(0, plan.rows, one_norm, 0)
    copy.wait()
    matrix = matrix_of(w, 0, plan.ht, 0, plan.wt, plan.wt, 3 * plan.square)
    mixed[...] = mm(grad_low[...], matrix, NT).astype(bf16)

    def one(row, carry):
        place = pl.ds(pl.multiple_of(row * plan.seq, plan.seq), plan.seq)
        for tile in range(plan.ht):
            cols = slice(tile * TILE, (tile + 1) * TILE)
            found = pair_backward(
                qkv[0, place, cols], qkv[1, place, cols], qkv[2, place, cols],
                probs[row, tile], mixed[place, cols], scale,
            )
            for piece in range(3):
                first = piece * plan.half + tile * TILE
                back[place, first : first + TILE] = found[piece]
        return carry

    lax.fori_loop(0, plan.rows, one, 0)
    matrix = jnp.concatenate(
        [matrix_of(w, 0, plan.wt, 0, plan.ht, plan.ht, p * plan.square) for p in range(3)], axis=1
    )
    part[...] = mm(back[...], matrix, NT).astype(bf16)


def self_backward(
    plan, scale, nat, resid, query_grad, query_mine, query_other, text_grad, text_mine,
    text_other, params, qkv, probs,
):
    tokens, width, half = plan.tokens, plan.width, plan.half
    return pl.pallas_call(
        functools.partial(self_backward_body, plan, scale),
        out_shape=(
            jax.ShapeDtypeStruct((tokens, width), f32),
            jax.ShapeDtypeStruct((tokens, width), bf16),
            jax.ShapeDtypeStruct((tokens, 3 * half), bf16),
            jax.ShapeDtypeStruct((tokens, width), bf16),
            jax.ShapeDtypeStruct((2, width), f32),
        ),
        in_specs=any_specs(1) + vmem_specs(10),
        out_specs=tuple(vmem_specs(5)),
        scratch_shapes=[
            pltpu.VMEM((tokens, half), bf16),
            pltpu.VMEM((plan.self_count, TILE, TILE), bf16),
            pltpu.SemaphoreType.DMA,
        ],
        compiler_params=vmem_params(),
        cost_estimate=cost(8 * tokens * width * half, 1.2e7),
        name="self_backward",
    )(
        nat, resid, query_grad, query_mine, query_other, text_grad, text_mine, text_other,
        params, qkv, probs,
    )


def store_blocks(target, first, product, col_total):
    for row in range(product.shape[0] // TILE):
        for col in range(col_total):
            target[first + row * col_total + col] = product[
                row * TILE : (row + 1) * TILE, col * TILE : (col + 1) * TILE
            ].astype(bf16)


def grad_blocks_body(first_block, pairs, total, *refs):
    sources, target, staged, sems = refs[: len(refs) - 4], refs[-3], refs[-2], refs[-1]
    copies = []
    base = 0
    for number, (left_at, right_at, right_first, right_width, step) in enumerate(pairs):
        left, right = sources[left_at], sources[right_at]
        left_tiles, col_total = left.shape[1] // TILE, right_width // TILE

        def one(chunk, carry, base=base, left=left, right=right, step=step, col_total=col_total,
                right_first=right_first, right_width=right_width):
            cols = pl.ds(pl.multiple_of(chunk * step * TILE, step * TILE), step * TILE)
            product = mm(left[:, cols], right[:, right_first : right_first + right_width], TN)
            store_blocks(staged, base + chunk * step * col_total, product, col_total)
            return carry

        lax.fori_loop(0, left_tiles // step, one, 0)
        count = left_tiles * col_total
        copy = pltpu.make_async_copy(
            staged.at[pl.ds(base, count)],
            target.at[pl.ds(first_block + base, count)],
            sems.at[number],
        )
        copy.start()
        copies.append(copy)
        base += count
    for copy in copies:
        copy.wait()


def grad_blocks(buffer, first_block, sources, pairs, flops):
    total = sum(sources[a].shape[1] // TILE * (width // TILE) for a, _, _, width, _ in pairs)
    return pl.pallas_call(
        functools.partial(grad_blocks_body, first_block, pairs, total),
        out_shape=jax.ShapeDtypeStruct(buffer.shape, buffer.dtype),
        in_specs=vmem_specs(len(sources)) + any_specs(1),
        out_specs=any_specs(1)[0],
        scratch_shapes=[
            pltpu.VMEM((total, TILE, TILE), bf16),
            pltpu.SemaphoreType.DMA((len(pairs),)),
        ],
        input_output_aliases={len(sources): 0},
        compiler_params=vmem_params(),
        cost_estimate=cost(flops, 1e7),
        name="grad_blocks",
    )(*sources, buffer)


def swap_tensor(part):
    if lax.axis_size("tensor") != 2:
        total = lax.psum(part.astype(f32), "tensor")
        return (total - part.astype(f32)).astype(bf16)
    return lax.ppermute(part, "tensor", [(0, 1), (1, 0)])


def layer_rows(
    hidden, image, segment_ids, cotangent, nat, norm_params, heads_local, scale, slot_count
):
    rows, seq, width = hidden.shape
    plan = Plan(
        rows, seq, width, image.shape[2], image.shape[1], heads_local, FF // lax.axis_size("tensor")
    )
    tokens, learned, texts, half = plan.tokens, plan.learned, plan.texts, plan.half
    flat_hidden = hidden.reshape(tokens, width)
    flat_image = jnp.pad(image, ((0, 0), (0, plan.keys - plan.patches), (0, 0))).reshape(
        rows * plan.keys, plan.image_width
    )
    up_query = cotangent[:, :NQ].reshape(learned, width)
    up_text = cotangent[:, NQ:].reshape(texts, width)
    buffer = jnp.zeros((slot_count, TILE, TILE), bf16)

    qkv, self_probs, mixed, part_one = self_forward(
        plan, scale, nat, flat_hidden, segment_ids[:, None, :], segment_ids[:, :, None]
    )
    other_one = swap_tensor(part_one)
    image_keys, image_values = image_forward(plan, nat, flat_image)
    (
        first_sum, first_query, first_text, low_query, low_text, cross_queries, cross_probs,
        looked, part_two,
    ) = cross_forward(
        plan, scale, nat, flat_hidden, part_one, other_one, norm_params, image_keys, image_values
    )
    other_two = swap_tensor(part_two)
    text_gated, text_slope, part_text = text_forward(plan, nat, low_text)
    other_text = swap_tensor(part_text)
    second_sum, second, low_second, query_gated, query_slope, part_query = query_forward(
        plan, nat, first_query, part_two, other_two, norm_params
    )
    other_query = swap_tensor(part_query)
    out_text, third_text, third_text_low, before_text, part_four_text, norm_text = feed_backward(
        plan, plan.text_first, 3, nat, first_text, part_text, other_text, up_text, norm_params,
        text_slope,
    )
    other_four_text = swap_tensor(part_four_text)
    out_query, third_query, third_query_low, before_query, part_four_query, norm_query = (
        feed_backward(
            plan, plan.query_first, 2, nat, second, part_query, other_query, up_query, norm_params,
            query_slope,
        )
    )
    other_four_query = swap_tensor(part_four_query)
    feed_pairs = [(0, 1, 0, plan.hidden, 2), (2, 3, 0, width, 2)]
    buffer = grad_blocks(
        buffer, plan.text_first, [low_text, before_text, text_gated, third_text_low], feed_pairs,
        4 * texts * width * plan.hidden,
    )
    second_grad, cross_low, query_back, key_back, value_back, part_five, norm_second = (
        cross_backward(
            plan, scale, nat, second_sum, third_query, part_four_query, other_four_query,
            norm_params, cross_queries, image_keys, image_values, cross_probs,
        )
    )
    other_five = swap_tensor(part_five)
    buffer = grad_blocks(
        buffer, plan.query_first, [low_second, before_query, query_gated, third_query_low],
        feed_pairs, 4 * learned * width * plan.hidden,
    )
    buffer = grad_blocks(
        buffer, plan.cross_first,
        [low_query, query_back, flat_image, key_back, value_back, looked, cross_low],
        [(0, 1, 0, half, 2), (2, 3, 0, half, 1), (2, 4, 0, half, 1), (5, 6, 0, width, 1)],
        4 * rows * plan.keys * plan.image_width * half,
    )
    first_grad, self_low, self_back, part_six, norm_first = self_backward(
        plan, scale, nat, first_sum, second_grad, part_five, other_five, third_text,
        part_four_text, other_four_text, norm_params, qkv, self_probs,
    )
    other_six = swap_tensor(part_six)
    buffer = grad_blocks(
        buffer, plan.self_first, [flat_hidden, self_back, mixed, self_low],
        [(0, 1, 0, half, 2), (0, 1, half, half, 2), (0, 1, 2 * half, half, 2), (2, 3, 0, width, 1)],
        8 * tokens * width * half,
    )
    input_grad = first_grad + (part_six.astype(f32) + other_six.astype(f32))
    output_rows = jnp.concatenate(
        [out_query.reshape(rows, NQ, width), out_text.reshape(rows, seq - NQ, width)], axis=1
    )
    norm_part = jnp.stack([norm_first, norm_second, norm_query, norm_text])
    return (output_rows, input_grad.reshape(rows, seq, width), buffer, norm_part)


def times(left_matrix, right_matrix):
    return jnp.einsum("...ij,...jk->...ik", left_matrix, right_matrix, precision=highest)


def flipped(block_matrix):
    return jnp.swapaxes(block_matrix, -1, -2)


def split3(a):
    h=a.astype(bf16); r=a-h.astype(f32); m=r.astype(bf16); l=(r-m.astype(f32)).astype(bf16)
    return h,m,l
def split2(a):
    h=a.astype(bf16); return h,(a-h.astype(f32)).astype(bf16)
def dot3(a,b,dims):
    ah,al=split2(a); bh,bl=split2(b)
    return mm(ah,bh,dims)+(mm(ah,bl,dims)+mm(al,bh,dims))
def gram6(p):
    h,m,l=split3(p)
    hh=mm(h,h,TN); mmm=mm(m,m,TN); hm=mm(h,m,TN)+mm(h,l,TN)
    return hh+(mmm+(hm+hm.T))

PB=16
def panel_steps(x, kb, g):
    base=kb*PB
    lane=lax.broadcasted_iota(jnp.int32,(1,8,128),2)
    sub=lax.broadcasted_iota(jnp.int32,(1,8,128),1)
    halves=[x[:,:8],x[:,8:]]
    rinvs=[]
    for s in range(PB):
        k=base+s
        hs=s//8; r=s%8
        cur=halves[hs]
        row=cur[:,r:r+1,:]
        piv=cur[:,r:r+1,k:k+1]
        rinv=1.0/piv
        rinvs.append(rinv)
        scaled=jnp.where(lane[:,:1]==k,1.0,row)*rinv
        for h in range(hs,2):
            y=halves[h]
            col=jnp.broadcast_to(y[:,:,k:k+1],y.shape)
            if h==hs:
                low=(sub>r)
                col=jnp.where(low,col,0.0)
                y=jnp.where((lane==k)&(sub>r),0.0,y)
                y=jnp.where((lane==k)&(sub==r),1.0,y)
            else:
                y=jnp.where(lane==k,0.0,y)
            halves[h]=y-col*scaled
    return jnp.concatenate(halves,axis=1), jnp.concatenate(rinvs,axis=1)

def ortho_body(n_pad, n, g, s_ref,b_ref,q_ref,a_ref,p_ref,d_ref):
    def first(i,c):
        p=dot3(s_ref[i],b_ref[i],NN)
        p_ref[i]=p
        a_ref[i]=gram6(p)
        return c
    lax.fori_loop(0,n,first,0)
    eye=(lax.broadcasted_iota(jnp.int32,(128,128),0)==lax.broadcasted_iota(jnp.int32,(128,128),1)).astype(f32)
    for i in range(n,n_pad):
        a_ref[i]=eye
    lane=lax.broadcasted_iota(jnp.int32,(1,PB,128),2)
    sub=lax.broadcasted_iota(jnp.int32,(1,PB,128),1)
    for kb in range(128//PB):
        base=kb*PB; end=base+PB
        def group(gi,c):
            i0=gi*g
            x=a_ref[pl.ds(i0,g),base:end,:]
            x,rinv=panel_steps(x,kb,g)
            w=jnp.where((lane>=base)&(lane<end)&(lane-base>sub),0.0,x)
            d_ref[pl.ds(i0,g),base:end,:]=jnp.broadcast_to(rinv,x.shape)
            a_ref[pl.ds(i0,g),base:end,:]=w
            if end<128:
                u=jnp.where(lane>=end,x*rinv,0.0)
                wh,wm,wl=split3(w); uh,um,ul=split3(u)
                lhs=jnp.concatenate([uh,uh,um,uh,ul,um],axis=1)
                rhs=jnp.concatenate([wh,wm,wh,wl,wh,wm],axis=1)
                lane2=lax.broadcasted_iota(jnp.int32,(128-end,128),1)
                inside=(lane2>=base)&(lane2<end)
                for j in range(g):
                    upd=mm(lhs[j],rhs[j],TN)
                    old=a_ref[i0+j,end:,:]
                    a_ref[i0+j,end:,:]=jnp.where(inside,0.0,old)-upd[end:,:]
            return c
        lax.fori_loop(0,n_pad//g,group,0)
    ii=lax.broadcasted_iota(jnp.int32,(128,128),0); jj=lax.broadcasted_iota(jnp.int32,(128,128),1)
    def last(i,c):
        inv=jnp.where(ii>=jj,a_ref[i],0.0)*jnp.sqrt(d_ref[i])
        q_ref[i]=dot3(p_ref[i],inv,NT)
        return c
    lax.fori_loop(0,n,last,0)

def ortho(s,b,g=29):
    n=s.shape[0]; n_pad=-(-n//g)*g
    return pl.pallas_call(
        functools.partial(ortho_body,n_pad,n,g),
        out_shape=jax.ShapeDtypeStruct(s.shape,f32),
        in_specs=[pl.BlockSpec(memory_space=pltpu.VMEM)]*2,
        out_specs=pl.BlockSpec(memory_space=pltpu.VMEM),
        scratch_shapes=[pltpu.VMEM((n_pad,128,128),f32),pltpu.VMEM((n,128,128),f32),pltpu.VMEM((n_pad,128,128),f32)],
        compiler_params=pltpu.CompilerParams(vmem_limit_bytes=50*1024*1024),
    )(s,b)


def orthonormal_pair(left_new, left_bases, right_new, right_bases):
    count = left_new.shape[0]
    both = ortho(
        jnp.concatenate([left_new, right_new]), jnp.concatenate([left_bases, right_bases]), count
    )
    return both[:count], both[count:]


def rotated_update(
    gradient, master, first_moment, second_moment, left_stats, right_stats, left_bases, right_bases
):
    rotated = times(times(flipped(left_bases), gradient), right_bases)
    first_new = beta_first * first_moment + (1 - beta_first) * rotated
    second_new = beta_second * second_moment + (1 - beta_second) * rotated * rotated
    step_rotated = (
        first_new
        / (1 - beta_first**STEP)
        / (jnp.sqrt(second_new / (1 - beta_second**STEP)) + adam_epsilon)
    )
    step_full = times(times(left_bases, step_rotated), flipped(right_bases))
    master_new = master - matrix_rate * (step_full + matrix_decay * master)
    left_new = beta_stats * left_stats + (1 - beta_stats) * times(gradient, flipped(gradient))
    right_new = beta_stats * right_stats + (1 - beta_stats) * times(flipped(gradient), gradient)
    return (
        master_new,
        first_new,
        second_new,
        left_new,
        right_new,
        *orthonormal_pair(left_new, left_bases, right_new, right_bases),
    )


def per_device(
    hidden,
    image,
    segment_ids,
    cotangent,
    slot_block,
    weight_master,
    moment_one,
    moment_two,
    left_stat,
    right_stat,
    left_basis,
    right_basis,
    norm_params,
    norm_moment_one,
    norm_moment_two,
):
    tensors = lax.axis_size("tensor")
    width = hidden.shape[2]
    heads_local = HEADS // tensors
    scale = (width // HEADS) ** (-0.5)
    order = slot_block[0]
    slot_count = order.shape[0]
    gathered = lax.all_gather(weight_master[0].astype(jnp.bfloat16), "dp", axis=0, tiled=True)
    inverse = jnp.zeros_like(order).at[order].set(jnp.arange(slot_count, dtype=jnp.int32))
    natural = gathered[inverse]
    out_rows, in_grad, packed, norm_part = layer_rows(
        hidden, image, segment_ids, cotangent, natural, norm_params, heads_local, scale, slot_count
    )
    owned = lax.psum_scatter(
        packed[order], "dp", scatter_dimension=0, tiled=True
    ).astype(jnp.float32)
    norm_total = lax.psum(norm_part, "dp")
    updated = rotated_update(
        owned,
        weight_master[0],
        moment_one[0],
        moment_two[0],
        left_stat[0],
        right_stat[0],
        left_basis[0],
        right_basis[0],
    )
    (
        weight_new,
        moment_one_new,
        moment_two_new,
        left_stat_new,
        right_stat_new,
        left_basis_new,
        right_basis_new,
    ) = [array[None] for array in updated]
    norm_first = beta_first * norm_moment_one + (1 - beta_first) * norm_total
    norm_second = beta_second * norm_moment_two + (1 - beta_second) * norm_total * norm_total
    norm_new = norm_params - norm_rate * (norm_first / (1 - beta_first**STEP)) / (
        jnp.sqrt(norm_second / (1 - beta_second**STEP)) + adam_epsilon
    )
    return (
        out_rows,
        in_grad,
        weight_new,
        weight_new.astype(jnp.bfloat16),
        moment_one_new,
        moment_two_new,
        left_stat_new,
        right_stat_new,
        left_basis_new,
        right_basis_new,
        norm_first,
        norm_second,
        norm_new,
    )


def solution(mesh):
    in_specs = (
        P("dp", None, None),
        P("dp", None, None),
        P("dp", None),
        P("dp", None, None),
        P("tensor", None),
        P("tensor", "dp", None, None),
        P("tensor", "dp", None, None),
        P("tensor", "dp", None, None),
        P("tensor", "dp", None, None),
        P("tensor", "dp", None, None),
        P("tensor", "dp", None, None),
        P("tensor", "dp", None, None),
        P(),
        P(),
        P(),
    )
    out_specs = (
        P("dp", None, None),
        P("dp", None, None),
        P("tensor", "dp", None, None),
        P("tensor", "dp", None, None),
        P("tensor", "dp", None, None),
        P("tensor", "dp", None, None),
        P("tensor", "dp", None, None),
        P("tensor", "dp", None, None),
        P("tensor", "dp", None, None),
        P("tensor", "dp", None, None),
        P(),
        P(),
        P(),
    )
    return jax.shard_map(
        per_device, mesh=mesh, in_specs=in_specs, out_specs=out_specs, check_vma=False
    )
```

```python
import functools

import jax
import jax.numpy as jnp
import numpy as np
from jax import lax
from jax.experimental import pallas as pl
from jax.experimental.pallas import tpu as pltpu
from jax.sharding import PartitionSpec as P

HEADS = 12
FF = 3072
NQ = 32
STEP = 10


beta_first = 0.9
beta_second = 0.999
beta_stats = 0.95
adam_epsilon = 1e-08
norm_epsilon = 1e-06
matrix_rate = 0.03
matrix_decay = 0.05
norm_rate = 0.6
masked_score = -1000000000.0
highest = lax.Precision.HIGHEST


TILE = 128
PATCHES_PAD = 16
f32 = jnp.float32
bf16 = jnp.bfloat16
NN = ((1,), (0,))
NT = ((1,), (1,))
TN = ((0,), (0,))
VMEM_BYTES = 56 * 1024 * 1024


def mm(left, right, dims):
    return lax.dot_general(left, right, (dims, ((), ())), preferred_element_type=f32)


def vmem_specs(count):
    return [pl.BlockSpec(memory_space=pltpu.VMEM)] * count


def any_specs(count):
    return [pl.BlockSpec(memory_space=pl.ANY)] * count


def vmem_params():
    return pltpu.CompilerParams(vmem_limit_bytes=VMEM_BYTES)


def cost(flops, bytes_accessed, transcendentals=0):
    return pl.CostEstimate(
        flops=int(flops), bytes_accessed=int(bytes_accessed), transcendentals=int(transcendentals)
    )


def matrix_of(blocks_ref, row_first, row_count, col_first, col_count, col_total, base=0):
    rows = []
    for row in range(row_count):
        first = base + (row_first + row) * col_total + col_first
        rows.append(
            jnp.concatenate([blocks_ref[first + col] for col in range(col_count)], axis=1)
        )
    return jnp.concatenate(rows, axis=0)


def norm_forward(resid):
    center = resid - jnp.mean(resid, axis=-1, keepdims=True)
    inverse = lax.rsqrt(jnp.mean(center * center, axis=-1, keepdims=True) + norm_epsilon)
    return center * inverse, inverse


def norm_backward(resid, upstream, gain):
    unit, inverse = norm_forward(resid)
    scaled = upstream * gain
    mean_scaled = jnp.mean(scaled, axis=-1, keepdims=True)
    mean_product = jnp.mean(scaled * unit, axis=-1, keepdims=True)
    grad = inverse * (scaled - mean_scaled - unit * mean_product)
    gain_grad = jnp.sum(upstream * unit, axis=0, keepdims=True)
    shift_grad = jnp.sum(upstream, axis=0, keepdims=True)
    return grad, gain_grad, shift_grad


def head_pair(tile):
    low_half = lax.broadcasted_iota(jnp.int32, tile.shape, 1) < TILE // 2
    zero = jnp.zeros_like(tile)
    return jnp.concatenate(
        [jnp.where(low_half, tile, zero), jnp.where(low_half, zero, tile)], axis=0
    )


def side_by_side(stacked):
    half = stacked.shape[0] // 2
    return jnp.concatenate([stacked[:half], stacked[half:]], axis=1)


def pair_probs(queries, keys, allowed, scale):
    scores = mm(head_pair(queries), keys, NT) * scale
    scores = jnp.where(allowed, scores, masked_score)
    weights = jnp.exp(scores - jnp.max(scores, axis=-1, keepdims=True))
    return weights / jnp.sum(weights, axis=-1, keepdims=True)


def pair_mix(probs, values):
    count = probs.shape[0] // 2
    low_half = lax.broadcasted_iota(jnp.int32, (count, TILE), 1) < TILE // 2
    mixed = mm(probs.astype(bf16), values, NN)
    return jnp.where(low_half, mixed[:count], mixed[count:]).astype(bf16)


def pair_backward(queries, keys, values, probs, mixed_grad, scale):
    grad_pair = head_pair(mixed_grad)
    value_grad = mm(probs.astype(bf16), grad_pair, TN).astype(bf16)
    prob_grad = mm(grad_pair, values, NT)
    inner = jnp.sum(probs * prob_grad, axis=-1, keepdims=True)
    score_grad = (probs * (prob_grad - inner) * scale).astype(bf16)
    count = queries.shape[0]
    low_half = lax.broadcasted_iota(jnp.int32, (count, TILE), 1) < TILE // 2
    both = mm(score_grad, keys, NN)
    query_grad = jnp.where(low_half, both[:count], both[count:]).astype(bf16)
    key_grad = mm(score_grad, head_pair(queries), TN).astype(bf16)
    return query_grad, key_grad, value_grad


def load_blocks(source, first, count, target, semaphore):
    copy = pltpu.make_async_copy(source.at[pl.ds(first, count)], target, semaphore)
    copy.start()
    return copy


class Plan:
    def __init__(self, rows, seq, width, image_width, patches, heads, hidden_units):
        self.rows, self.seq, self.width = rows, seq, width
        self.image_width, self.heads, self.hidden = image_width, heads, hidden_units
        self.half = heads * (TILE // 2)
        self.patches = patches
        self.keys = -(-patches // PATCHES_PAD) * PATCHES_PAD
        self.wt, self.ht = width // TILE, self.half // TILE
        self.it, self.ft = image_width // TILE, hidden_units // TILE
        square, cross, feed = self.wt * self.ht, self.it * self.ht, self.wt * self.ft
        self.square, self.cross, self.feed = square, cross, feed
        self.self_first, self.self_count = 0, 4 * square
        self.cross_first, self.cross_count = 4 * square, 2 * square + 2 * cross
        self.query_first = self.cross_first + self.cross_count
        self.text_first = self.query_first + 2 * feed
        self.block_count = self.text_first + 2 * feed
        self.tokens = rows * seq
        self.learned = rows * NQ
        self.texts = rows * (seq - NQ)


def self_forward_body(plan, scale, nat, hidden, seg_row, seg_col, qkv, probs, mixed, part, w, sem):
    copy = load_blocks(nat, plan.self_first, plan.self_count, w, sem)
    copy.wait()
    for piece in range(3):
        matrix = matrix_of(w, 0, plan.wt, 0, plan.ht, plan.ht, piece * plan.square)
        qkv[piece] = mm(hidden[...], matrix, NN).astype(bf16)

    def one(row, carry):
        place = pl.ds(pl.multiple_of(row * plan.seq, plan.seq), plan.seq)
        allowed = seg_col[row] == seg_row[row]
        allowed = jnp.concatenate([allowed, allowed], axis=0)
        for tile in range(plan.ht):
            cols = slice(tile * TILE, (tile + 1) * TILE)
            found = pair_probs(qkv[0, place, cols], qkv[1, place, cols], allowed, scale)
            probs[row, tile] = found
            mixed[place, cols] = pair_mix(found, qkv[2, place, cols])
        return carry

    lax.fori_loop(0, plan.rows, one, 0)
    matrix = matrix_of(w, 0, plan.ht, 0, plan.wt, plan.wt, 3 * plan.square)
    part[...] = mm(mixed[...], matrix, NN).astype(bf16)


def self_forward(plan, scale, nat, hidden, seg_row, seg_col):
    tokens, half, width = plan.tokens, plan.half, plan.width
    return pl.pallas_call(
        functools.partial(self_forward_body, plan, scale),
        out_shape=(
            jax.ShapeDtypeStruct((3, tokens, half), bf16),
            jax.ShapeDtypeStruct((plan.rows, plan.ht, 2 * plan.seq, plan.seq), f32),
            jax.ShapeDtypeStruct((tokens, half), bf16),
            jax.ShapeDtypeStruct((tokens, width), bf16),
        ),
        in_specs=any_specs(1) + vmem_specs(3),
        out_specs=tuple(vmem_specs(4)),
        scratch_shapes=[
            pltpu.VMEM((plan.self_count, TILE, TILE), bf16),
            pltpu.SemaphoreType.DMA,
        ],
        compiler_params=vmem_params(),
        cost_estimate=cost(2 * tokens * width * half * 4, 8e6),
        name="self_forward",
    )(nat, hidden, seg_row, seg_col)


def image_body(plan, nat, image, keys, values, w, sem):
    copy = load_blocks(nat, plan.cross_first + plan.square, 2 * plan.cross, w, sem)
    copy.wait()
    for piece, target in ((0, keys), (1, values)):
        matrix = matrix_of(w, 0, plan.it, 0, plan.ht, plan.ht, piece * plan.cross)

        def one(row, carry):
            place = pl.ds(pl.multiple_of(row * plan.keys, plan.keys), plan.keys)
            target[place, :] = mm(image[place, :], matrix, NN).astype(bf16)
            return carry

        lax.fori_loop(0, plan.rows, one, 0)


def image_forward(plan, nat, image):
    total = plan.rows * plan.keys
    return pl.pallas_call(
        functools.partial(image_body, plan),
        out_shape=(jax.ShapeDtypeStruct((total, plan.half), bf16),) * 2,
        in_specs=any_specs(1) + vmem_specs(1),
        out_specs=tuple(vmem_specs(2)),
        scratch_shapes=[
            pltpu.VMEM((2 * plan.cross, TILE, TILE), bf16),
            pltpu.SemaphoreType.DMA,
        ],
        compiler_params=vmem_params(),
        cost_estimate=cost(4 * total * plan.image_width * plan.half, 8e6),
        name="image_forward",
    )(nat, image)


def cross_forward_body(
    plan, scale, nat, hidden, mine, other, params, image_keys, image_values,
    resid, first_query, first_text, low_query, low_text, queries, probs, mixed, part, w, sem,
):
    copy = load_blocks(nat, plan.cross_first, plan.cross_count, w, sem)
    gain, shift = params[0, 0:1], params[0, 1:2]
    text = plan.seq - NQ

    def one_norm(row, carry):
        place = pl.ds(pl.multiple_of(row * plan.seq, plan.seq), plan.seq)
        summed = hidden[place, :].astype(f32) + (
            mine[place, :].astype(f32) + other[place, :].astype(f32)
        )
        resid[place, :] = summed
        first = norm_forward(summed)[0] * gain + shift
        query_place = pl.ds(pl.multiple_of(row * NQ, NQ), NQ)
        text_place = pl.ds(pl.multiple_of(row * text, text), text)
        first_query[query_place, :] = first[:NQ]
        first_text[text_place, :] = first[NQ:]
        low_query[query_place, :] = first[:NQ].astype(bf16)
        low_text[text_place, :] = first[NQ:].astype(bf16)
        return carry

    lax.fori_loop(0, plan.rows, one_norm, 0)
    copy.wait()
    matrix = matrix_of(w, 0, plan.wt, 0, plan.ht, plan.ht)
    queries[...] = mm(low_query[...], matrix, NN).astype(bf16)
    allowed = lax.broadcasted_iota(jnp.int32, (2 * NQ, plan.keys), 1) < plan.patches

    def one(row, carry):
        query_place = pl.ds(pl.multiple_of(row * NQ, NQ), NQ)
        place = pl.ds(pl.multiple_of(row * plan.keys, plan.keys), plan.keys)
        for tile in range(plan.ht):
            cols = slice(tile * TILE, (tile + 1) * TILE)
            found = pair_probs(queries[query_place, cols], image_keys[place, cols], allowed, scale)
            probs[row, tile] = found
            mixed[query_place, cols] = pair_mix(found, image_values[place, cols])
        return carry

    lax.fori_loop(0, plan.rows, one, 0)
    matrix = matrix_of(w, 0, plan.ht, 0, plan.wt, plan.wt, plan.square + 2 * plan.cross)
    part[...] = mm(mixed[...], matrix, NN).astype(bf16)


def cross_forward(plan, scale, nat, hidden, mine, other, params, image_keys, image_values):
    learned, texts, width, half = plan.learned, plan.texts, plan.width, plan.half
    return pl.pallas_call(
        functools.partial(cross_forward_body, plan, scale),
        out_shape=(
            jax.ShapeDtypeStruct((plan.tokens, width), f32),
            jax.ShapeDtypeStruct((learned, width), f32),
            jax.ShapeDtypeStruct((texts, width), f32),
            jax.ShapeDtypeStruct((learned, width), bf16),
            jax.ShapeDtypeStruct((texts, width), bf16),
            jax.ShapeDtypeStruct((learned, half), bf16),
            jax.ShapeDtypeStruct((plan.rows, plan.ht, 2 * NQ, plan.keys), f32),
            jax.ShapeDtypeStruct((learned, half), bf16),
            jax.ShapeDtypeStruct((learned, width), bf16),
        ),
        in_specs=any_specs(1) + vmem_specs(6),
        out_specs=tuple(vmem_specs(9)),
        scratch_shapes=[
            pltpu.VMEM((plan.cross_count, TILE, TILE), bf16),
            pltpu.SemaphoreType.DMA,
        ],
        compiler_params=vmem_params(),
        cost_estimate=cost(4 * learned * width * half, 1.2e7),
        name="cross_forward",
    )(nat, hidden, mine, other, params, image_keys, image_values)


def gelu_parts(values):
    normal = 0.5 * (1.0 + lax.erf(values * 0.7071067811865476))
    density = 0.3989422804014327 * jnp.exp(-0.5 * values * values)
    return values * normal, normal + values * density


def feed_forward_tail(plan, states_low, w, gated, slope, part):
    def one_up(chunk, carry):
        matrix = matrix_of(w, 0, plan.wt, chunk * 2, 2, plan.ft)
        active, derivative = gelu_parts(mm(states_low[...], matrix, NN))
        cols = pl.ds(pl.multiple_of(chunk * 2 * TILE, 2 * TILE), 2 * TILE)
        gated[:, cols] = active.astype(bf16)
        slope[:, cols] = derivative
        return carry

    lax.fori_loop(0, plan.ft // 2, one_up, 0)

    def one_down(chunk, carry):
        matrix = matrix_of(w, 0, plan.ft, chunk * 2, 2, plan.wt, plan.feed)
        cols = pl.ds(pl.multiple_of(chunk * 2 * TILE, 2 * TILE), 2 * TILE)
        part[:, cols] = mm(gated[...], matrix, NN).astype(bf16)
        return carry

    lax.fori_loop(0, plan.wt // 2, one_down, 0)


def text_forward_body(plan, nat, low_text, gated, slope, part, w, sem):
    copy = load_blocks(nat, plan.text_first, 2 * plan.feed, w, sem)
    copy.wait()
    feed_forward_tail(plan, low_text, w, gated, slope, part)


def query_forward_body(
    plan, nat, first_query, mine, other, params, resid, second, low, gated, slope, part, w, sem
):
    copy = load_blocks(nat, plan.query_first, 2 * plan.feed, w, sem)
    summed = first_query[...] + (mine[...].astype(f32) + other[...].astype(f32))
    resid[...] = summed
    normed = norm_forward(summed)[0] * params[1, 0:1] + params[1, 1:2]
    second[...] = normed
    low[...] = normed.astype(bf16)
    copy.wait()
    feed_forward_tail(plan, low, w, gated, slope, part)


def feed_shapes(plan, count):
    return (
        jax.ShapeDtypeStruct((count, plan.hidden), bf16),
        jax.ShapeDtypeStruct((count, plan.hidden), f32),
        jax.ShapeDtypeStruct((count, plan.width), bf16),
    )


def feed_scratch(plan):
    return [pltpu.VMEM((2 * plan.feed, TILE, TILE), bf16), pltpu.SemaphoreType.DMA]


def text_forward(plan, nat, low_text):
    return pl.pallas_call(
        functools.partial(text_forward_body, plan),
        out_shape=feed_shapes(plan, plan.texts),
        in_specs=any_specs(1) + vmem_specs(1),
        out_specs=tuple(vmem_specs(3)),
        scratch_shapes=feed_scratch(plan),
        compiler_params=vmem_params(),
        cost_estimate=cost(4 * plan.texts * plan.width * plan.hidden, 1e7),
        name="text_forward",
    )(nat, low_text)


def query_forward(plan, nat, first_query, mine, other, params):
    count, width = plan.learned, plan.width
    return pl.pallas_call(
        functools.partial(query_forward_body, plan),
        out_shape=(
            jax.ShapeDtypeStruct((count, width), f32),
            jax.ShapeDtypeStruct((count, width), f32),
            jax.ShapeDtypeStruct((count, width), bf16),
        )
        + feed_shapes(plan, count),
        in_specs=any_specs(1) + vmem_specs(4),
        out_specs=tuple(vmem_specs(6)),
        scratch_shapes=feed_scratch(plan),
        compiler_params=vmem_params(),
        cost_estimate=cost(4 * count * width * plan.hidden, 8e6),
        name="query_forward",
    )(nat, first_query, mine, other, params)


def feed_backward_body(
    plan, first_block, which, nat, states, mine, other, upstream, params, slope,
    out, grad, grad_low, before_low, part, norm_grad, w, sem,
):
    copy = load_blocks(nat, first_block, 2 * plan.feed, w, sem)
    gain, shift = params[which, 0:1], params[which, 1:2]
    count = states.shape[0] // plan.rows
    norm_grad[...] = jnp.zeros_like(norm_grad)

    def one_norm(row, carry):
        place = pl.ds(pl.multiple_of(row * count, count), count)
        summed = states[place, :] + (mine[place, :].astype(f32) + other[place, :].astype(f32))
        out[place, :] = (norm_forward(summed)[0] * gain + shift).astype(bf16)
        found, gain_grad, shift_grad = norm_backward(
            summed, upstream[place, :].astype(f32), gain
        )
        grad[place, :] = found
        grad_low[place, :] = found.astype(bf16)
        norm_grad[0:1] += gain_grad
        norm_grad[1:2] += shift_grad
        return carry

    lax.fori_loop(0, plan.rows, one_norm, 0)
    copy.wait()

    def one_down(chunk, carry):
        matrix = matrix_of(w, chunk * 2, 2, 0, plan.wt, plan.wt, plan.feed)
        cols = pl.ds(pl.multiple_of(chunk * 2 * TILE, 2 * TILE), 2 * TILE)
        before_low[:, cols] = (mm(grad_low[...], matrix, NT) * slope[:, cols]).astype(bf16)
        return carry

    lax.fori_loop(0, plan.ft // 2, one_down, 0)

    def one_up(chunk, carry):
        matrix = matrix_of(w, chunk * 2, 2, 0, plan.ft, plan.ft)
        cols = pl.ds(pl.multiple_of(chunk * 2 * TILE, 2 * TILE), 2 * TILE)
        part[:, cols] = mm(before_low[...], matrix, NT).astype(bf16)
        return carry

    lax.fori_loop(0, plan.wt // 2, one_up, 0)


def feed_backward(plan, first_block, which, nat, states, mine, other, upstream, params, slope):
    count, width = states.shape
    return pl.pallas_call(
        functools.partial(feed_backward_body, plan, first_block, which),
        out_shape=(
            jax.ShapeDtypeStruct((count, width), bf16),
            jax.ShapeDtypeStruct((count, width), f32),
            jax.ShapeDtypeStruct((count, width), bf16),
            jax.ShapeDtypeStruct((count, plan.hidden), bf16),
            jax.ShapeDtypeStruct((count, width), bf16),
            jax.ShapeDtypeStruct((2, width), f32),
        ),
        in_specs=any_specs(1) + vmem_specs(6),
        out_specs=tuple(vmem_specs(6)),
        scratch_shapes=feed_scratch(plan),
        compiler_params=vmem_params(),
        cost_estimate=cost(4 * count * width * plan.hidden, 1e7),
        name="feed_backward",
    )(nat, states, mine, other, upstream, params, slope)


def cross_backward_body(
    plan, scale, nat, resid, third_grad, mine, other, params, queries, keys, values, probs,
    grad, grad_low, query_back, key_back, value_back, part, norm_grad, looked, w, sem,
):
    copy = load_blocks(nat, plan.cross_first, plan.cross_count, w, sem)
    upstream = third_grad[...] + (mine[...].astype(f32) + other[...].astype(f32))
    found, gain_grad, shift_grad = norm_backward(resid[...], upstream, params[1, 0:1])
    grad[...] = found
    grad_low[...] = found.astype(bf16)
    norm_grad[0:1] = gain_grad
    norm_grad[1:2] = shift_grad
    copy.wait()
    matrix = matrix_of(w, 0, plan.ht, 0, plan.wt, plan.wt, plan.square + 2 * plan.cross)
    looked[...] = mm(grad_low[...], matrix, NT).astype(bf16)

    def one(row, carry):
        query_place = pl.ds(pl.multiple_of(row * NQ, NQ), NQ)
        place = pl.ds(pl.multiple_of(row * plan.keys, plan.keys), plan.keys)
        for tile in range(plan.ht):
            cols = slice(tile * TILE, (tile + 1) * TILE)
            query_grad, key_grad, value_grad = pair_backward(
                queries[query_place, cols], keys[place, cols], values[place, cols],
                probs[row, tile], looked[query_place, cols], scale,
            )
            query_back[query_place, cols] = query_grad
            key_back[place, cols] = key_grad
            value_back[place, cols] = value_grad
        return carry

    lax.fori_loop(0, plan.rows, one, 0)
    matrix = matrix_of(w, 0, plan.wt, 0, plan.ht, plan.ht)
    part[...] = mm(query_back[...], matrix, NT).astype(bf16)


def cross_backward(
    plan, scale, nat, resid, third_grad, mine, other, params, queries, keys, values, probs
):
    learned, width, half = plan.learned, plan.width, plan.half
    return pl.pallas_call(
        functools.partial(cross_backward_body, plan, scale),
        out_shape=(
            jax.ShapeDtypeStruct((learned, width), f32),
            jax.ShapeDtypeStruct((learned, width), bf16),
            jax.ShapeDtypeStruct((learned, half), bf16),
            jax.ShapeDtypeStruct(keys.shape, bf16),
            jax.ShapeDtypeStruct(keys.shape, bf16),
            jax.ShapeDtypeStruct((learned, width), bf16),
            jax.ShapeDtypeStruct((2, width), f32),
        ),
        in_specs=any_specs(1) + vmem_specs(9),
        out_specs=tuple(vmem_specs(7)),
        scratch_shapes=[
            pltpu.VMEM((learned, half), bf16),
            pltpu.VMEM((plan.cross_count, TILE, TILE), bf16),
            pltpu.SemaphoreType.DMA,
        ],
        compiler_params=vmem_params(),
        cost_estimate=cost(8 * learned * width * half, 1e7),
        name="cross_backward",
    )(nat, resid, third_grad, mine, other, params, queries, keys, values, probs)


def self_backward_body(
    plan, scale, nat, resid, query_grad, query_mine, query_other, text_grad, text_mine,
    text_other, params, qkv, probs,
    grad, grad_low, back, part, norm_grad, mixed, w, sem,
):
    copy = load_blocks(nat, plan.self_first, plan.self_count, w, sem)
    text = plan.seq - NQ
    gain = params[0, 0:1]
    norm_grad[...] = jnp.zeros_like(norm_grad)

    def one_norm(row, carry):
        place = pl.ds(pl.multiple_of(row * plan.seq, plan.seq), plan.seq)
        query_place = pl.ds(pl.multiple_of(row * NQ, NQ), NQ)
        text_place = pl.ds(pl.multiple_of(row * text, text), text)
        upstream = jnp.concatenate(
            [
                query_grad[query_place, :]
                + (query_mine[query_place, :].astype(f32) + query_other[query_place, :].astype(f32)),
                text_grad[text_place, :]
                + (text_mine[text_place, :].astype(f32) + text_other[text_place, :].astype(f32)),
            ],
            axis=0,
        )
        found, gain_grad, shift_grad = norm_backward(resid[place, :], upstream, gain)
        grad[place, :] = found
        grad_low[place, :] = found.astype(bf16)
        norm_grad[0:1] += gain_grad
        norm_grad[1:2] += shift_grad
        return carry

    lax.fori_loop(0, plan.rows, one_norm, 0)
    copy.wait()
    matrix = matrix_of(w, 0, plan.ht, 0, plan.wt, plan.wt, 3 * plan.square)
    mixed[...] = mm(grad_low[...], matrix, NT).astype(bf16)

    def one(row, carry):
        place = pl.ds(pl.multiple_of(row * plan.seq, plan.seq), plan.seq)
        for tile in range(plan.ht):
            cols = slice(tile * TILE, (tile + 1) * TILE)
            found = pair_backward(
                qkv[0, place, cols], qkv[1, place, cols], qkv[2, place, cols],
                probs[row, tile], mixed[place, cols], scale,
            )
            for piece in range(3):
                first = piece * plan.half + tile * TILE
                back[place, first : first + TILE] = found[piece]
        return carry

    lax.fori_loop(0, plan.rows, one, 0)
    matrix = jnp.concatenate(
        [matrix_of(w, 0, plan.wt, 0, plan.ht, plan.ht, p * plan.square) for p in range(3)], axis=1
    )
    part[...] = mm(back[...], matrix, NT).astype(bf16)


def self_backward(
    plan, scale, nat, resid, query_grad, query_mine, query_other, text_grad, text_mine,
    text_other, params, qkv, probs,
):
    tokens, width, half = plan.tokens, plan.width, plan.half
    return pl.pallas_call(
        functools.partial(self_backward_body, plan, scale),
        out_shape=(
            jax.ShapeDtypeStruct((tokens, width), f32),
            jax.ShapeDtypeStruct((tokens, width), bf16),
            jax.ShapeDtypeStruct((tokens, 3 * half), bf16),
            jax.ShapeDtypeStruct((tokens, width), bf16),
            jax.ShapeDtypeStruct((2, width), f32),
        ),
        in_specs=any_specs(1) + vmem_specs(10),
        out_specs=tuple(vmem_specs(5)),
        scratch_shapes=[
            pltpu.VMEM((tokens, half), bf16),
            pltpu.VMEM((plan.self_count, TILE, TILE), bf16),
            pltpu.SemaphoreType.DMA,
        ],
        compiler_params=vmem_params(),
        cost_estimate=cost(8 * tokens * width * half, 1.2e7),
        name="self_backward",
    )(
        nat, resid, query_grad, query_mine, query_other, text_grad, text_mine, text_other,
        params, qkv, probs,
    )


def store_blocks(target, first, product, col_total):
    for row in range(product.shape[0] // TILE):
        for col in range(col_total):
            target[first + row * col_total + col] = product[
                row * TILE : (row + 1) * TILE, col * TILE : (col + 1) * TILE
            ].astype(bf16)


def send_block(source, position, targets, sem):
    base = 0
    for target in targets:
        count = target.shape[0]

        @pl.when((position >= base) & (position < base + count))
        def _(base=base, target=target):
            pltpu.make_async_copy(source, target.at[position - base], sem).start()

        base += count


def grad_blocks_body(first_block, pairs, source_count, target_count, spare, place, *refs):
    sources, targets = refs[:source_count], refs[-3 - target_count : -3]
    staged, blank, sem = refs[-3:]
    base = 0
    sent = 0
    if spare is not None:
        blank[...] = jnp.zeros_like(blank)

        def one_spare(number, carry):
            send_block(blank, place[spare[0] + number], targets, sem)
            return carry

        lax.fori_loop(0, spare[1], one_spare, 0)
        sent += spare[1]
    for left_at, right_at, right_first, right_width, step in pairs:
        left, right = sources[left_at], sources[right_at]
        left_tiles, col_total = left.shape[1] // TILE, right_width // TILE

        def one(chunk, carry, base=base, left=left, right=right, step=step, col_total=col_total,
                right_first=right_first, right_width=right_width):
            cols = pl.ds(pl.multiple_of(chunk * step * TILE, step * TILE), step * TILE)
            product = mm(left[:, cols], right[:, right_first : right_first + right_width], TN)
            first = base + chunk * step * col_total
            store_blocks(staged, first, product, col_total)

            def send(number, carry):
                block = first + number
                send_block(staged.at[block], place[first_block + block], targets, sem)
                return carry

            lax.fori_loop(0, step * col_total, send, 0)
            return carry

        lax.fori_loop(0, left_tiles // step, one, 0)
        base += left_tiles * col_total
    sent += base
    whole = staged.at[pl.ds(0, base)]
    pltpu.make_async_copy(whole, whole, sem).wait()
    for _ in range(sent - base):
        pltpu.make_async_copy(blank, blank, sem).wait()


def grad_blocks(buffers, place, first_block, sources, pairs, flops, spare=None):
    total = sum(sources[a].shape[1] // TILE * (width // TILE) for a, _, _, width, _ in pairs)
    fresh = isinstance(buffers[0], jax.ShapeDtypeStruct)
    given = [] if fresh else list(buffers)
    aliases = {1 + len(sources) + number: number for number in range(len(given))}
    return pl.pallas_call(
        functools.partial(
            grad_blocks_body, first_block, pairs, len(sources), len(buffers), spare
        ),
        out_shape=tuple(jax.ShapeDtypeStruct(b.shape, b.dtype) for b in buffers),
        in_specs=[pl.BlockSpec(memory_space=pltpu.SMEM)]
        + vmem_specs(len(sources))
        + any_specs(len(given)),
        out_specs=tuple(any_specs(len(buffers))),
        scratch_shapes=[
            pltpu.VMEM((total, TILE, TILE), bf16),
            pltpu.VMEM((TILE, TILE), bf16),
            pltpu.SemaphoreType.DMA,
        ],
        input_output_aliases=aliases,
        compiler_params=vmem_params(),
        cost_estimate=cost(flops, 1e7),
        name="grad_blocks",
    )(place, *sources, *given)


def swap_tensor(part):
    if lax.axis_size("tensor") != 2:
        total = lax.psum(part.astype(f32), "tensor")
        return (total - part.astype(f32)).astype(bf16)
    return lax.ppermute(part, "tensor", [(0, 1), (1, 0)])


def layer_rows(
    hidden, image, segment_ids, cotangent, nat, norm_params, heads_local, scale, place, regions
):
    rows, seq, width = hidden.shape
    plan = Plan(
        rows, seq, width, image.shape[2], image.shape[1], heads_local, FF // lax.axis_size("tensor")
    )
    tokens, learned, texts, half = plan.tokens, plan.learned, plan.texts, plan.half
    flat_hidden = hidden.reshape(tokens, width)
    flat_image = jnp.pad(image, ((0, 0), (0, plan.keys - plan.patches), (0, 0))).reshape(
        rows * plan.keys, plan.image_width
    )
    up_query = cotangent[:, :NQ].reshape(learned, width)
    up_text = cotangent[:, NQ:].reshape(texts, width)
    buffers = [jax.ShapeDtypeStruct((count, TILE, TILE), bf16) for count in regions]

    qkv, self_probs, mixed, part_one = self_forward(
        plan, scale, nat, flat_hidden, segment_ids[:, None, :], segment_ids[:, :, None]
    )
    other_one = swap_tensor(part_one)
    image_keys, image_values = image_forward(plan, nat, flat_image)
    (
        first_sum, first_query, first_text, low_query, low_text, cross_queries, cross_probs,
        looked, part_two,
    ) = cross_forward(
        plan, scale, nat, flat_hidden, part_one, other_one, norm_params, image_keys, image_values
    )
    other_two = swap_tensor(part_two)
    text_gated, text_slope, part_text = text_forward(plan, nat, low_text)
    other_text = swap_tensor(part_text)
    second_sum, second, low_second, query_gated, query_slope, part_query = query_forward(
        plan, nat, first_query, part_two, other_two, norm_params
    )
    other_query = swap_tensor(part_query)
    out_text, third_text, third_text_low, before_text, part_four_text, norm_text = feed_backward(
        plan, plan.text_first, 3, nat, first_text, part_text, other_text, up_text, norm_params,
        text_slope,
    )
    other_four_text = swap_tensor(part_four_text)
    out_query, third_query, third_query_low, before_query, part_four_query, norm_query = (
        feed_backward(
            plan, plan.query_first, 2, nat, second, part_query, other_query, up_query, norm_params,
            query_slope,
        )
    )
    other_four_query = swap_tensor(part_four_query)
    feed_pairs = [(0, 1, 0, plan.hidden, 2), (2, 3, 0, width, 2)]
    buffers = grad_blocks(
        buffers, place, plan.text_first, [low_text, before_text, text_gated, third_text_low], feed_pairs,
        4 * texts * width * plan.hidden,
        spare=(plan.block_count, place.shape[0] - plan.block_count),
    )
    second_grad, cross_low, query_back, key_back, value_back, part_five, norm_second = (
        cross_backward(
            plan, scale, nat, second_sum, third_query, part_four_query, other_four_query,
            norm_params, cross_queries, image_keys, image_values, cross_probs,
        )
    )
    other_five = swap_tensor(part_five)
    buffers = grad_blocks(
        buffers, place, plan.query_first, [low_second, before_query, query_gated, third_query_low],
        feed_pairs, 4 * learned * width * plan.hidden,
    )
    buffers = grad_blocks(
        buffers, place, plan.cross_first,
        [low_query, query_back, flat_image, key_back, value_back, looked, cross_low],
        [(0, 1, 0, half, 2), (2, 3, 0, half, 1), (2, 4, 0, half, 1), (5, 6, 0, width, 1)],
        4 * rows * plan.keys * plan.image_width * half,
    )
    first_grad, self_low, self_back, part_six, norm_first = self_backward(
        plan, scale, nat, first_sum, second_grad, part_five, other_five, third_text,
        part_four_text, other_four_text, norm_params, qkv, self_probs,
    )
    other_six = swap_tensor(part_six)
    buffers = grad_blocks(
        buffers, place, plan.self_first, [flat_hidden, self_back, mixed, self_low],
        [(0, 1, 0, half, 2), (0, 1, half, half, 2), (0, 1, 2 * half, half, 2), (2, 3, 0, width, 1)],
        8 * tokens * width * half,
    )
    input_grad = first_grad + (part_six.astype(f32) + other_six.astype(f32))
    output_rows = jnp.concatenate(
        [out_query.reshape(rows, NQ, width), out_text.reshape(rows, seq - NQ, width)], axis=1
    )
    norm_part = jnp.stack([norm_first, norm_second, norm_query, norm_text])
    return (output_rows, input_grad.reshape(rows, seq, width), buffers, norm_part)


CHIP_RING = ((0, 0), (1, 0), (2, 0), (3, 0), (3, 1), (2, 1), (1, 1), (0, 1))
RING = len(CHIP_RING)
RING_DEVICES = 2 * RING


def ring_index(position, core):
    z, x = CHIP_RING[position % RING]
    return (z * 2 + x) * 2 + core


def direction_of(core):
    return 1 - 2 * core


RING_PAIRS = [
    (ring_index(position, core), ring_index(position + direction_of(core), core))
    for position in range(RING)
    for core in range(2)
]


def ring_place(index):
    return CHIP_RING.index((index // 4, index // 2 % 2)), index % 2


CORE_PAIRS = [(index, index ^ 1) for index in range(RING_DEVICES)]


def chain_parts(slots, chains):
    cuts = [slots * number // chains for number in range(chains + 1)]
    return [(first, last - first) for first, last in zip(cuts, cuts[1:])]


def place_blocks_body(counts, first, ids, *refs):
    sources, target, sem = refs[: len(counts)], refs[-2], refs[-1]
    base = first
    for source, count in zip(sources, counts):

        def one(number, carry, base=base, source=source):
            pltpu.make_async_copy(
                source.at[number], target.at[ids[base + number]], sem
            ).start()
            return carry

        lax.fori_loop(0, count, one, 0)
        base += count
    total = sum(counts)
    pltpu.make_async_copy(
        target.at[pl.ds(0, total)], target.at[pl.ds(0, total)], sem
    ).wait()


def place_blocks(ids, first, sources, target, shape):
    counts = [source.shape[0] for source in sources]
    operands = [ids, *sources]
    specs = [pl.BlockSpec(memory_space=pltpu.SMEM)] + vmem_specs(len(sources))
    aliases = {}
    if target is not None:
        operands.append(target)
        specs += any_specs(1)
        aliases = {len(operands) - 1: 0}
    return pl.pallas_call(
        functools.partial(place_blocks_body, counts, first),
        out_shape=jax.ShapeDtypeStruct(shape, bf16),
        in_specs=specs,
        out_specs=any_specs(1)[0],
        scratch_shapes=[pltpu.SemaphoreType.DMA],
        input_output_aliases=aliases,
        cost_estimate=cost(0, 4 * sum(counts) * TILE * TILE),
        name="place_blocks",
    )(*operands)


def gather_ring(shard, order, chains=2):
    slots = shard.shape[0]
    parts = chain_parts(slots, chains)
    table = np.zeros((RING_DEVICES, RING_DEVICES * slots), np.int32)
    for index in range(RING_DEVICES):
        position, core = ring_place(index)
        found = []
        for step in range(RING):
            for side in (core, 1 - core):
                owner = ring_index(position - direction_of(side) * step, side)
                found += [owner * slots + slot for slot in range(slots)]
        table[index] = found
    ids = order[jnp.asarray(table)[lax.axis_index("dp")]]
    shape = (order.shape[0], TILE, TILE)
    other = lax.ppermute(shard, "dp", CORE_PAIRS)
    held = [shard[first : first + count] for first, count in parts]
    natural = None
    waiting, first = [shard, other], 0
    for step in range(1, RING):
        held = [lax.ppermute(piece, "dp", RING_PAIRS) for piece in held]
        if step > 1:
            natural = place_blocks(ids, first, waiting, natural, shape)
            held[0], natural = lax.optimization_barrier((held[0], natural))
            waiting, first = [], step * 2 * slots
        waiting = waiting + held + [lax.ppermute(piece, "dp", CORE_PAIRS) for piece in held]
    return place_blocks(ids, first, waiting, natural, shape)


def scatter_positions(slots):
    table = np.zeros((RING_DEVICES, RING_DEVICES * slots), np.int32)
    for index in range(RING_DEVICES):
        position, core = ring_place(index)
        for step in range(1, RING + 1):
            for number, side in enumerate((1 - core, core)):
                owner = ring_index(position - direction_of(side) * step, side)
                base = (number * RING + step - 1) * slots
                table[index, owner * slots : (owner + 1) * slots] = base + np.arange(slots)
    return table


def scatter_ring(early, late, own, slots, chains=2):
    others = [lax.ppermute(early, "dp", CORE_PAIRS), lax.ppermute(late, "dp", CORE_PAIRS)]
    early_steps = early.shape[0] // slots
    parts = chain_parts(slots, chains)
    held = [None] * chains
    for step in range(1, RING + 1):
        base = (step - 1) * slots
        other, other_base = others[0], base
        if step > early_steps:
            other, other_base = others[1], base - early_steps * slots
        for number, (first, count) in enumerate(parts):
            summed = own[base + first : base + first + count].astype(f32) + other[
                other_base + first : other_base + first + count
            ].astype(f32)
            if held[number] is not None:
                summed = summed + held[number].astype(f32)
            if step < RING:
                summed = lax.ppermute(summed.astype(bf16), "dp", RING_PAIRS)
            held[number] = summed
    return jnp.concatenate(held, axis=0)


def sum_small(values):
    for bit in (1, 2, 4, 8):
        pairs = [(index, index ^ bit) for index in range(RING_DEVICES)]
        values = values + lax.ppermute(values, "dp", pairs)
    return values


def times(left_matrix, right_matrix):
    return jnp.einsum("...ij,...jk->...ik", left_matrix, right_matrix, precision=highest)


def flipped(block_matrix):
    return jnp.swapaxes(block_matrix, -1, -2)


def split3(a):
    h=a.astype(bf16); r=a-h.astype(f32); m=r.astype(bf16); l=(r-m.astype(f32)).astype(bf16)
    return h,m,l
def split2(a):
    h=a.astype(bf16); return h,(a-h.astype(f32)).astype(bf16)
def dot3(a,b,dims):
    ah,al=split2(a); bh,bl=split2(b)
    return mm(ah,bh,dims)+(mm(ah,bl,dims)+mm(al,bh,dims))
def gram6(p):
    h,m,l=split3(p)
    hh=mm(h,h,TN); mmm=mm(m,m,TN); hm=mm(h,m,TN)+mm(h,l,TN)
    return hh+(mmm+(hm+hm.T))

PB=16
def panel_steps(x, kb, g):
    base=kb*PB
    lane=lax.broadcasted_iota(jnp.int32,(1,8,128),2)
    sub=lax.broadcasted_iota(jnp.int32,(1,8,128),1)
    halves=[x[:,:8],x[:,8:]]
    rinvs=[]
    for s in range(PB):
        k=base+s
        hs=s//8; r=s%8
        cur=halves[hs]
        row=cur[:,r:r+1,:]
        piv=cur[:,r:r+1,k:k+1]
        rinv=1.0/piv
        rinvs.append(rinv)
        scaled=jnp.where(lane[:,:1]==k,1.0,row)*rinv
        for h in range(hs,2):
            y=halves[h]
            col=jnp.broadcast_to(y[:,:,k:k+1],y.shape)
            if h==hs:
                low=(sub>r)
                col=jnp.where(low,col,0.0)
                y=jnp.where((lane==k)&(sub>r),0.0,y)
                y=jnp.where((lane==k)&(sub==r),1.0,y)
            else:
                y=jnp.where(lane==k,0.0,y)
            halves[h]=y-col*scaled
    return jnp.concatenate(halves,axis=1), jnp.concatenate(rinvs,axis=1)

def ortho_body(n_pad, n, g, s_ref,b_ref,q_ref,a_ref,p_ref,d_ref):
    def first(i,c):
        p=dot3(s_ref[i],b_ref[i],NN)
        p_ref[i]=p
        a_ref[i]=gram6(p)
        return c
    lax.fori_loop(0,n,first,0)
    eye=(lax.broadcasted_iota(jnp.int32,(128,128),0)==lax.broadcasted_iota(jnp.int32,(128,128),1)).astype(f32)
    for i in range(n,n_pad):
        a_ref[i]=eye
    lane=lax.broadcasted_iota(jnp.int32,(1,PB,128),2)
    sub=lax.broadcasted_iota(jnp.int32,(1,PB,128),1)
    for kb in range(128//PB):
        base=kb*PB; end=base+PB
        def group(gi,c):
            i0=gi*g
            x=a_ref[pl.ds(i0,g),base:end,:]
            x,rinv=panel_steps(x,kb,g)
            w=jnp.where((lane>=base)&(lane<end)&(lane-base>sub),0.0,x)
            d_ref[pl.ds(i0,g),base:end,:]=jnp.broadcast_to(rinv,x.shape)
            a_ref[pl.ds(i0,g),base:end,:]=w
            if end<128:
                u=jnp.where(lane>=end,x*rinv,0.0)
                wh,wm,wl=split3(w); uh,um,ul=split3(u)
                lhs=jnp.concatenate([uh,uh,um,uh,ul,um],axis=1)
                rhs=jnp.concatenate([wh,wm,wh,wl,wh,wm],axis=1)
                lane2=lax.broadcasted_iota(jnp.int32,(128-end,128),1)
                inside=(lane2>=base)&(lane2<end)
                for j in range(g):
                    upd=mm(lhs[j],rhs[j],TN)
                    old=a_ref[i0+j,end:,:]
                    a_ref[i0+j,end:,:]=jnp.where(inside,0.0,old)-upd[end:,:]
            return c
        lax.fori_loop(0,n_pad//g,group,0)
    ii=lax.broadcasted_iota(jnp.int32,(128,128),0); jj=lax.broadcasted_iota(jnp.int32,(128,128),1)
    def last(i,c):
        inv=jnp.where(ii>=jj,a_ref[i],0.0)*jnp.sqrt(d_ref[i])
        q_ref[i]=dot3(p_ref[i],inv,NT)
        return c
    lax.fori_loop(0,n,last,0)

def ortho(s,b,g=29):
    n=s.shape[0]; n_pad=-(-n//g)*g
    return pl.pallas_call(
        functools.partial(ortho_body,n_pad,n,g),
        out_shape=jax.ShapeDtypeStruct(s.shape,f32),
        in_specs=[pl.BlockSpec(memory_space=pltpu.VMEM)]*2,
        out_specs=pl.BlockSpec(memory_space=pltpu.VMEM),
        scratch_shapes=[pltpu.VMEM((n_pad,128,128),f32),pltpu.VMEM((n,128,128),f32),pltpu.VMEM((n_pad,128,128),f32)],
        compiler_params=pltpu.CompilerParams(vmem_limit_bytes=50*1024*1024),
    )(s,b)


def orthonormal_pair(left_new, left_bases, right_new, right_bases):
    count = left_new.shape[0]
    both = ortho(
        jnp.concatenate([left_new, right_new]), jnp.concatenate([left_bases, right_bases]), count
    )
    return both[:count], both[count:]


def rotated_update(
    gradient, master, first_moment, second_moment, left_stats, right_stats, left_bases, right_bases
):
    rotated = times(times(flipped(left_bases), gradient), right_bases)
    first_new = beta_first * first_moment + (1 - beta_first) * rotated
    second_new = beta_second * second_moment + (1 - beta_second) * rotated * rotated
    step_rotated = (
        first_new
        / (1 - beta_first**STEP)
        / (jnp.sqrt(second_new / (1 - beta_second**STEP)) + adam_epsilon)
    )
    step_full = times(times(left_bases, step_rotated), flipped(right_bases))
    master_new = master - matrix_rate * (step_full + matrix_decay * master)
    left_new = beta_stats * left_stats + (1 - beta_stats) * times(gradient, flipped(gradient))
    right_new = beta_stats * right_stats + (1 - beta_stats) * times(flipped(gradient), gradient)
    return (
        master_new,
        first_new,
        second_new,
        left_new,
        right_new,
        *orthonormal_pair(left_new, left_bases, right_new, right_bases),
    )


def per_device(
    hidden,
    image,
    segment_ids,
    cotangent,
    slot_block,
    weight_master,
    moment_one,
    moment_two,
    left_stat,
    right_stat,
    left_basis,
    right_basis,
    norm_params,
    norm_moment_one,
    norm_moment_two,
):
    tensors = lax.axis_size("tensor")
    width = hidden.shape[2]
    heads_local = HEADS // tensors
    scale = (width // HEADS) ** (-0.5)
    order = slot_block[0]
    slot_count = order.shape[0]
    slots = weight_master.shape[1]
    shard = weight_master[0].astype(bf16)
    ring = lax.axis_size("dp") == RING_DEVICES
    if ring:
        natural = gather_ring(shard, order)
        positions = jnp.asarray(scatter_positions(slots))[lax.axis_index("dp")]
        regions = (2 * slots, (RING - 2) * slots, RING * slots)
    else:
        positions = jnp.arange(slot_count, dtype=jnp.int32)
        gathered = lax.all_gather(shard, "dp", axis=0, tiled=True)
        natural = gathered[jnp.zeros_like(order).at[order].set(positions)]
        regions = (slot_count,)
    place = jnp.zeros_like(order).at[order].set(positions)
    out_rows, in_grad, packed, norm_part = layer_rows(
        hidden, image, segment_ids, cotangent, natural, norm_params, heads_local, scale, place,
        regions,
    )
    if ring:
        owned = scatter_ring(*packed, slots)
        norm_total = sum_small(norm_part)
    else:
        owned = lax.psum_scatter(packed[0], "dp", scatter_dimension=0, tiled=True).astype(f32)
        norm_total = lax.psum(norm_part, "dp")
    updated = rotated_update(
        owned,
        weight_master[0],
        moment_one[0],
        moment_two[0],
        left_stat[0],
        right_stat[0],
        left_basis[0],
        right_basis[0],
    )
    (
        weight_new,
        moment_one_new,
        moment_two_new,
        left_stat_new,
        right_stat_new,
        left_basis_new,
        right_basis_new,
    ) = [array[None] for array in updated]
    norm_first = beta_first * norm_moment_one + (1 - beta_first) * norm_total
    norm_second = beta_second * norm_moment_two + (1 - beta_second) * norm_total * norm_total
    norm_new = norm_params - norm_rate * (norm_first / (1 - beta_first**STEP)) / (
        jnp.sqrt(norm_second / (1 - beta_second**STEP)) + adam_epsilon
    )
    return (
        out_rows,
        in_grad,
        weight_new,
        weight_new.astype(jnp.bfloat16),
        moment_one_new,
        moment_two_new,
        left_stat_new,
        right_stat_new,
        left_basis_new,
        right_basis_new,
        norm_first,
        norm_second,
        norm_new,
    )


def solution(mesh):
    in_specs = (
        P("dp", None, None),
        P("dp", None, None),
        P("dp", None),
        P("dp", None, None),
        P("tensor", None),
        P("tensor", "dp", None, None),
        P("tensor", "dp", None, None),
        P("tensor", "dp", None, None),
        P("tensor", "dp", None, None),
        P("tensor", "dp", None, None),
        P("tensor", "dp", None, None),
        P("tensor", "dp", None, None),
        P(),
        P(),
        P(),
    )
    out_specs = (
        P("dp", None, None),
        P("dp", None, None),
        P("tensor", "dp", None, None),
        P("tensor", "dp", None, None),
        P("tensor", "dp", None, None),
        P("tensor", "dp", None, None),
        P("tensor", "dp", None, None),
        P("tensor", "dp", None, None),
        P("tensor", "dp", None, None),
        P("tensor", "dp", None, None),
        P(),
        P(),
        P(),
    )
    return jax.shard_map(
        per_device, mesh=mesh, in_specs=in_specs, out_specs=out_specs, check_vma=False
    )
```

```python
import functools

import jax
import jax.numpy as jnp
import numpy as np
from jax import lax
from jax.experimental import pallas as pl
from jax.experimental.pallas import tpu as pltpu
from jax.sharding import PartitionSpec as P

HEADS = 12
FF = 3072
NQ = 32
STEP = 10


beta_first = 0.9
beta_second = 0.999
beta_stats = 0.95
adam_epsilon = 1e-08
norm_epsilon = 1e-06
matrix_rate = 0.03
matrix_decay = 0.05
norm_rate = 0.6
masked_score = -1000000000.0


TILE = 128
PATCHES_PAD = 16
f32 = jnp.float32
bf16 = jnp.bfloat16
NN = ((1,), (0,))
NT = ((1,), (1,))
TN = ((0,), (0,))
VMEM_BYTES = 56 * 1024 * 1024


def mm(left, right, dims):
    return lax.dot_general(left, right, (dims, ((), ())), preferred_element_type=f32)


def vmem_specs(count):
    return [pl.BlockSpec(memory_space=pltpu.VMEM)] * count


def any_specs(count):
    return [pl.BlockSpec(memory_space=pl.ANY)] * count


def vmem_params():
    return pltpu.CompilerParams(vmem_limit_bytes=VMEM_BYTES)


def cost(flops, bytes_accessed, transcendentals=0):
    return pl.CostEstimate(
        flops=int(flops), bytes_accessed=int(bytes_accessed), transcendentals=int(transcendentals)
    )


def matrix_of(blocks_ref, row_first, row_count, col_first, col_count, col_total, base=0):
    rows = []
    for row in range(row_count):
        first = base + (row_first + row) * col_total + col_first
        rows.append(
            jnp.concatenate([blocks_ref[first + col] for col in range(col_count)], axis=1)
        )
    return jnp.concatenate(rows, axis=0)


def norm_forward(resid):
    center = resid - jnp.mean(resid, axis=-1, keepdims=True)
    inverse = lax.rsqrt(jnp.mean(center * center, axis=-1, keepdims=True) + norm_epsilon)
    return center * inverse, inverse


def norm_backward(resid, upstream, gain):
    unit, inverse = norm_forward(resid)
    scaled = upstream * gain
    mean_scaled = jnp.mean(scaled, axis=-1, keepdims=True)
    mean_product = jnp.mean(scaled * unit, axis=-1, keepdims=True)
    grad = inverse * (scaled - mean_scaled - unit * mean_product)
    gain_grad = jnp.sum(upstream * unit, axis=0, keepdims=True)
    shift_grad = jnp.sum(upstream, axis=0, keepdims=True)
    return grad, gain_grad, shift_grad


def head_pair(tile):
    low_half = lax.broadcasted_iota(jnp.int32, tile.shape, 1) < TILE // 2
    zero = jnp.zeros_like(tile)
    return jnp.concatenate(
        [jnp.where(low_half, tile, zero), jnp.where(low_half, zero, tile)], axis=0
    )


def side_by_side(stacked):
    half = stacked.shape[0] // 2
    return jnp.concatenate([stacked[:half], stacked[half:]], axis=1)


def pair_probs(queries, keys, allowed, scale):
    scores = mm(head_pair(queries), keys, NT) * scale
    scores = jnp.where(allowed, scores, masked_score)
    weights = jnp.exp(scores - jnp.max(scores, axis=-1, keepdims=True))
    return weights / jnp.sum(weights, axis=-1, keepdims=True)


def pair_mix(probs, values):
    count = probs.shape[0] // 2
    low_half = lax.broadcasted_iota(jnp.int32, (count, TILE), 1) < TILE // 2
    mixed = mm(probs.astype(bf16), values, NN)
    return jnp.where(low_half, mixed[:count], mixed[count:]).astype(bf16)


def pair_backward(queries, keys, values, probs, mixed_grad, scale):
    grad_pair = head_pair(mixed_grad)
    value_grad = mm(probs.astype(bf16), grad_pair, TN).astype(bf16)
    prob_grad = mm(grad_pair, values, NT)
    inner = jnp.sum(probs * prob_grad, axis=-1, keepdims=True)
    score_grad = (probs * (prob_grad - inner) * scale).astype(bf16)
    count = queries.shape[0]
    low_half = lax.broadcasted_iota(jnp.int32, (count, TILE), 1) < TILE // 2
    both = mm(score_grad, keys, NN)
    query_grad = jnp.where(low_half, both[:count], both[count:]).astype(bf16)
    key_grad = mm(score_grad, head_pair(queries), TN).astype(bf16)
    return query_grad, key_grad, value_grad


def load_blocks(source, first, count, target, semaphore):
    copy = pltpu.make_async_copy(source.at[pl.ds(first, count)], target, semaphore)
    copy.start()
    return copy


class Plan:
    def __init__(self, rows, seq, width, image_width, patches, heads, hidden_units):
        self.rows, self.seq, self.width = rows, seq, width
        self.image_width, self.heads, self.hidden = image_width, heads, hidden_units
        self.half = heads * (TILE // 2)
        self.patches = patches
        self.keys = -(-patches // PATCHES_PAD) * PATCHES_PAD
        self.wt, self.ht = width // TILE, self.half // TILE
        self.it, self.ft = image_width // TILE, hidden_units // TILE
        square, cross, feed = self.wt * self.ht, self.it * self.ht, self.wt * self.ft
        self.square, self.cross, self.feed = square, cross, feed
        self.self_first, self.self_count = 0, 4 * square
        self.cross_first, self.cross_count = 4 * square, 2 * square + 2 * cross
        self.query_first = self.cross_first + self.cross_count
        self.text_first = self.query_first + 2 * feed
        self.block_count = self.text_first + 2 * feed
        self.tokens = rows * seq
        self.learned = rows * NQ
        self.texts = rows * (seq - NQ)


def self_forward_body(plan, scale, nat, hidden, seg_row, seg_col, qkv, probs, mixed, part, w, sem):
    copy = load_blocks(nat, plan.self_first, plan.self_count, w, sem)
    copy.wait()
    for piece in range(3):
        matrix = matrix_of(w, 0, plan.wt, 0, plan.ht, plan.ht, piece * plan.square)
        qkv[piece] = mm(hidden[...], matrix, NN).astype(bf16)

    def one(row, carry):
        place = pl.ds(pl.multiple_of(row * plan.seq, plan.seq), plan.seq)
        allowed = seg_col[row] == seg_row[row]
        allowed = jnp.concatenate([allowed, allowed], axis=0)
        for tile in range(plan.ht):
            cols = slice(tile * TILE, (tile + 1) * TILE)
            found = pair_probs(qkv[0, place, cols], qkv[1, place, cols], allowed, scale)
            probs[row, tile] = found
            mixed[place, cols] = pair_mix(found, qkv[2, place, cols])
        return carry

    lax.fori_loop(0, plan.rows, one, 0)
    matrix = matrix_of(w, 0, plan.ht, 0, plan.wt, plan.wt, 3 * plan.square)
    part[...] = mm(mixed[...], matrix, NN).astype(bf16)


def self_forward(plan, scale, nat, hidden, seg_row, seg_col):
    tokens, half, width = plan.tokens, plan.half, plan.width
    return pl.pallas_call(
        functools.partial(self_forward_body, plan, scale),
        out_shape=(
            jax.ShapeDtypeStruct((3, tokens, half), bf16),
            jax.ShapeDtypeStruct((plan.rows, plan.ht, 2 * plan.seq, plan.seq), f32),
            jax.ShapeDtypeStruct((tokens, half), bf16),
            jax.ShapeDtypeStruct((tokens, width), bf16),
        ),
        in_specs=any_specs(1) + vmem_specs(3),
        out_specs=tuple(vmem_specs(4)),
        scratch_shapes=[
            pltpu.VMEM((plan.self_count, TILE, TILE), bf16),
            pltpu.SemaphoreType.DMA,
        ],
        compiler_params=vmem_params(),
        cost_estimate=cost(2 * tokens * width * half * 4, 8e6),
        name="self_forward",
    )(nat, hidden, seg_row, seg_col)


def image_body(plan, nat, image, keys, values, w, sem):
    copy = load_blocks(nat, plan.cross_first + plan.square, 2 * plan.cross, w, sem)
    copy.wait()
    for piece, target in ((0, keys), (1, values)):
        matrix = matrix_of(w, 0, plan.it, 0, plan.ht, plan.ht, piece * plan.cross)

        def one(row, carry):
            place = pl.ds(pl.multiple_of(row * plan.keys, plan.keys), plan.keys)
            target[place, :] = mm(image[place, :], matrix, NN).astype(bf16)
            return carry

        lax.fori_loop(0, plan.rows, one, 0)


def image_forward(plan, nat, image):
    total = plan.rows * plan.keys
    return pl.pallas_call(
        functools.partial(image_body, plan),
        out_shape=(jax.ShapeDtypeStruct((total, plan.half), bf16),) * 2,
        in_specs=any_specs(1) + vmem_specs(1),
        out_specs=tuple(vmem_specs(2)),
        scratch_shapes=[
            pltpu.VMEM((2 * plan.cross, TILE, TILE), bf16),
            pltpu.SemaphoreType.DMA,
        ],
        compiler_params=vmem_params(),
        cost_estimate=cost(4 * total * plan.image_width * plan.half, 8e6),
        name="image_forward",
    )(nat, image)


def cross_forward_body(
    plan, scale, nat, hidden, mine, other, params, image_keys, image_values,
    resid, first_query, first_text, low_query, low_text, queries, probs, mixed, part, w, sem,
):
    copy = load_blocks(nat, plan.cross_first, plan.cross_count, w, sem)
    gain, shift = params[0, 0:1], params[0, 1:2]
    text = plan.seq - NQ

    def one_norm(row, carry):
        place = pl.ds(pl.multiple_of(row * plan.seq, plan.seq), plan.seq)
        summed = hidden[place, :].astype(f32) + (
            mine[place, :].astype(f32) + other[place, :].astype(f32)
        )
        resid[place, :] = summed
        first = norm_forward(summed)[0] * gain + shift
        query_place = pl.ds(pl.multiple_of(row * NQ, NQ), NQ)
        text_place = pl.ds(pl.multiple_of(row * text, text), text)
        first_query[query_place, :] = first[:NQ]
        first_text[text_place, :] = first[NQ:]
        low_query[query_place, :] = first[:NQ].astype(bf16)
        low_text[text_place, :] = first[NQ:].astype(bf16)
        return carry

    lax.fori_loop(0, plan.rows, one_norm, 0)
    copy.wait()
    matrix = matrix_of(w, 0, plan.wt, 0, plan.ht, plan.ht)
    queries[...] = mm(low_query[...], matrix, NN).astype(bf16)
    allowed = lax.broadcasted_iota(jnp.int32, (2 * NQ, plan.keys), 1) < plan.patches

    def one(row, carry):
        query_place = pl.ds(pl.multiple_of(row * NQ, NQ), NQ)
        place = pl.ds(pl.multiple_of(row * plan.keys, plan.keys), plan.keys)
        for tile in range(plan.ht):
            cols = slice(tile * TILE, (tile + 1) * TILE)
            found = pair_probs(queries[query_place, cols], image_keys[place, cols], allowed, scale)
            probs[row, tile] = found
            mixed[query_place, cols] = pair_mix(found, image_values[place, cols])
        return carry

    lax.fori_loop(0, plan.rows, one, 0)
    matrix = matrix_of(w, 0, plan.ht, 0, plan.wt, plan.wt, plan.square + 2 * plan.cross)
    part[...] = mm(mixed[...], matrix, NN).astype(bf16)


def cross_forward(plan, scale, nat, hidden, mine, other, params, image_keys, image_values):
    learned, texts, width, half = plan.learned, plan.texts, plan.width, plan.half
    return pl.pallas_call(
        functools.partial(cross_forward_body, plan, scale),
        out_shape=(
            jax.ShapeDtypeStruct((plan.tokens, width), f32),
            jax.ShapeDtypeStruct((learned, width), f32),
            jax.ShapeDtypeStruct((texts, width), f32),
            jax.ShapeDtypeStruct((learned, width), bf16),
            jax.ShapeDtypeStruct((texts, width), bf16),
            jax.ShapeDtypeStruct((learned, half), bf16),
            jax.ShapeDtypeStruct((plan.rows, plan.ht, 2 * NQ, plan.keys), f32),
            jax.ShapeDtypeStruct((learned, half), bf16),
            jax.ShapeDtypeStruct((learned, width), bf16),
        ),
        in_specs=any_specs(1) + vmem_specs(6),
        out_specs=tuple(vmem_specs(9)),
        scratch_shapes=[
            pltpu.VMEM((plan.cross_count, TILE, TILE), bf16),
            pltpu.SemaphoreType.DMA,
        ],
        compiler_params=vmem_params(),
        cost_estimate=cost(4 * learned * width * half, 1.2e7),
        name="cross_forward",
    )(nat, hidden, mine, other, params, image_keys, image_values)


def gelu_parts(values):
    normal = 0.5 * (1.0 + lax.erf(values * 0.7071067811865476))
    density = 0.3989422804014327 * jnp.exp(-0.5 * values * values)
    return values * normal, normal + values * density


def feed_forward_tail(plan, states_low, w, gated, slope, part):
    def one_up(chunk, carry):
        matrix = matrix_of(w, 0, plan.wt, chunk * 2, 2, plan.ft)
        active, derivative = gelu_parts(mm(states_low[...], matrix, NN))
        cols = pl.ds(pl.multiple_of(chunk * 2 * TILE, 2 * TILE), 2 * TILE)
        gated[:, cols] = active.astype(bf16)
        slope[:, cols] = derivative
        return carry

    lax.fori_loop(0, plan.ft // 2, one_up, 0)

    def one_down(chunk, carry):
        matrix = matrix_of(w, 0, plan.ft, chunk * 2, 2, plan.wt, plan.feed)
        cols = pl.ds(pl.multiple_of(chunk * 2 * TILE, 2 * TILE), 2 * TILE)
        part[:, cols] = mm(gated[...], matrix, NN).astype(bf16)
        return carry

    lax.fori_loop(0, plan.wt // 2, one_down, 0)


def text_forward_body(plan, nat, low_text, gated, slope, part, w, sem):
    copy = load_blocks(nat, plan.text_first, 2 * plan.feed, w, sem)
    copy.wait()
    feed_forward_tail(plan, low_text, w, gated, slope, part)


def query_forward_body(
    plan, nat, first_query, mine, other, params, resid, second, low, gated, slope, part, w, sem
):
    copy = load_blocks(nat, plan.query_first, 2 * plan.feed, w, sem)
    summed = first_query[...] + (mine[...].astype(f32) + other[...].astype(f32))
    resid[...] = summed
    normed = norm_forward(summed)[0] * params[1, 0:1] + params[1, 1:2]
    second[...] = normed
    low[...] = normed.astype(bf16)
    copy.wait()
    feed_forward_tail(plan, low, w, gated, slope, part)


def feed_shapes(plan, count):
    return (
        jax.ShapeDtypeStruct((count, plan.hidden), bf16),
        jax.ShapeDtypeStruct((count, plan.hidden), f32),
        jax.ShapeDtypeStruct((count, plan.width), bf16),
    )


def feed_scratch(plan):
    return [pltpu.VMEM((2 * plan.feed, TILE, TILE), bf16), pltpu.SemaphoreType.DMA]


def text_forward(plan, nat, low_text):
    return pl.pallas_call(
        functools.partial(text_forward_body, plan),
        out_shape=feed_shapes(plan, plan.texts),
        in_specs=any_specs(1) + vmem_specs(1),
        out_specs=tuple(vmem_specs(3)),
        scratch_shapes=feed_scratch(plan),
        compiler_params=vmem_params(),
        cost_estimate=cost(4 * plan.texts * plan.width * plan.hidden, 1e7),
        name="text_forward",
    )(nat, low_text)


def query_forward(plan, nat, first_query, mine, other, params):
    count, width = plan.learned, plan.width
    return pl.pallas_call(
        functools.partial(query_forward_body, plan),
        out_shape=(
            jax.ShapeDtypeStruct((count, width), f32),
            jax.ShapeDtypeStruct((count, width), f32),
            jax.ShapeDtypeStruct((count, width), bf16),
        )
        + feed_shapes(plan, count),
        in_specs=any_specs(1) + vmem_specs(4),
        out_specs=tuple(vmem_specs(6)),
        scratch_shapes=feed_scratch(plan),
        compiler_params=vmem_params(),
        cost_estimate=cost(4 * count * width * plan.hidden, 8e6),
        name="query_forward",
    )(nat, first_query, mine, other, params)


def feed_backward_body(
    plan, first_block, which, nat, states, mine, other, upstream, params, slope,
    out, grad, grad_low, before_low, part, norm_grad, w, sem,
):
    copy = load_blocks(nat, first_block, 2 * plan.feed, w, sem)
    gain, shift = params[which, 0:1], params[which, 1:2]
    count = states.shape[0] // plan.rows
    norm_grad[...] = jnp.zeros_like(norm_grad)

    def one_norm(row, carry):
        place = pl.ds(pl.multiple_of(row * count, count), count)
        summed = states[place, :] + (mine[place, :].astype(f32) + other[place, :].astype(f32))
        out[place, :] = (norm_forward(summed)[0] * gain + shift).astype(bf16)
        found, gain_grad, shift_grad = norm_backward(
            summed, upstream[place, :].astype(f32), gain
        )
        grad[place, :] = found
        grad_low[place, :] = found.astype(bf16)
        norm_grad[0:1] += gain_grad
        norm_grad[1:2] += shift_grad
        return carry

    lax.fori_loop(0, plan.rows, one_norm, 0)
    copy.wait()

    def one_down(chunk, carry):
        matrix = matrix_of(w, chunk * 2, 2, 0, plan.wt, plan.wt, plan.feed)
        cols = pl.ds(pl.multiple_of(chunk * 2 * TILE, 2 * TILE), 2 * TILE)
        before_low[:, cols] = (mm(grad_low[...], matrix, NT) * slope[:, cols]).astype(bf16)
        return carry

    lax.fori_loop(0, plan.ft // 2, one_down, 0)

    def one_up(chunk, carry):
        matrix = matrix_of(w, chunk * 2, 2, 0, plan.ft, plan.ft)
        cols = pl.ds(pl.multiple_of(chunk * 2 * TILE, 2 * TILE), 2 * TILE)
        part[:, cols] = mm(before_low[...], matrix, NT).astype(bf16)
        return carry

    lax.fori_loop(0, plan.wt // 2, one_up, 0)


def feed_backward(plan, first_block, which, nat, states, mine, other, upstream, params, slope):
    count, width = states.shape
    return pl.pallas_call(
        functools.partial(feed_backward_body, plan, first_block, which),
        out_shape=(
            jax.ShapeDtypeStruct((count, width), bf16),
            jax.ShapeDtypeStruct((count, width), f32),
            jax.ShapeDtypeStruct((count, width), bf16),
            jax.ShapeDtypeStruct((count, plan.hidden), bf16),
            jax.ShapeDtypeStruct((count, width), bf16),
            jax.ShapeDtypeStruct((2, width), f32),
        ),
        in_specs=any_specs(1) + vmem_specs(6),
        out_specs=tuple(vmem_specs(6)),
        scratch_shapes=feed_scratch(plan),
        compiler_params=vmem_params(),
        cost_estimate=cost(4 * count * width * plan.hidden, 1e7),
        name="feed_backward",
    )(nat, states, mine, other, upstream, params, slope)


def cross_backward_body(
    plan, scale, nat, resid, third_grad, mine, other, params, queries, keys, values, probs,
    grad, grad_low, query_back, key_back, value_back, part, norm_grad, looked, w, sem,
):
    copy = load_blocks(nat, plan.cross_first, plan.cross_count, w, sem)
    upstream = third_grad[...] + (mine[...].astype(f32) + other[...].astype(f32))
    found, gain_grad, shift_grad = norm_backward(resid[...], upstream, params[1, 0:1])
    grad[...] = found
    grad_low[...] = found.astype(bf16)
    norm_grad[0:1] = gain_grad
    norm_grad[1:2] = shift_grad
    copy.wait()
    matrix = matrix_of(w, 0, plan.ht, 0, plan.wt, plan.wt, plan.square + 2 * plan.cross)
    looked[...] = mm(grad_low[...], matrix, NT).astype(bf16)

    def one(row, carry):
        query_place = pl.ds(pl.multiple_of(row * NQ, NQ), NQ)
        place = pl.ds(pl.multiple_of(row * plan.keys, plan.keys), plan.keys)
        for tile in range(plan.ht):
            cols = slice(tile * TILE, (tile + 1) * TILE)
            query_grad, key_grad, value_grad = pair_backward(
                queries[query_place, cols], keys[place, cols], values[place, cols],
                probs[row, tile], looked[query_place, cols], scale,
            )
            query_back[query_place, cols] = query_grad
            key_back[place, cols] = key_grad
            value_back[place, cols] = value_grad
        return carry

    lax.fori_loop(0, plan.rows, one, 0)
    matrix = matrix_of(w, 0, plan.wt, 0, plan.ht, plan.ht)
    part[...] = mm(query_back[...], matrix, NT).astype(bf16)


def cross_backward(
    plan, scale, nat, resid, third_grad, mine, other, params, queries, keys, values, probs
):
    learned, width, half = plan.learned, plan.width, plan.half
    return pl.pallas_call(
        functools.partial(cross_backward_body, plan, scale),
        out_shape=(
            jax.ShapeDtypeStruct((learned, width), f32),
            jax.ShapeDtypeStruct((learned, width), bf16),
            jax.ShapeDtypeStruct((learned, half), bf16),
            jax.ShapeDtypeStruct(keys.shape, bf16),
            jax.ShapeDtypeStruct(keys.shape, bf16),
            jax.ShapeDtypeStruct((learned, width), bf16),
            jax.ShapeDtypeStruct((2, width), f32),
        ),
        in_specs=any_specs(1) + vmem_specs(9),
        out_specs=tuple(vmem_specs(7)),
        scratch_shapes=[
            pltpu.VMEM((learned, half), bf16),
            pltpu.VMEM((plan.cross_count, TILE, TILE), bf16),
            pltpu.SemaphoreType.DMA,
        ],
        compiler_params=vmem_params(),
        cost_estimate=cost(8 * learned * width * half, 1e7),
        name="cross_backward",
    )(nat, resid, third_grad, mine, other, params, queries, keys, values, probs)


def self_backward_body(
    plan, scale, nat, resid, query_grad, query_mine, query_other, text_grad, text_mine,
    text_other, params, qkv, probs,
    grad, grad_low, back, part, norm_grad, mixed, w, sem,
):
    copy = load_blocks(nat, plan.self_first, plan.self_count, w, sem)
    text = plan.seq - NQ
    gain = params[0, 0:1]
    norm_grad[...] = jnp.zeros_like(norm_grad)

    def one_norm(row, carry):
        place = pl.ds(pl.multiple_of(row * plan.seq, plan.seq), plan.seq)
        query_place = pl.ds(pl.multiple_of(row * NQ, NQ), NQ)
        text_place = pl.ds(pl.multiple_of(row * text, text), text)
        upstream = jnp.concatenate(
            [
                query_grad[query_place, :]
                + (query_mine[query_place, :].astype(f32) + query_other[query_place, :].astype(f32)),
                text_grad[text_place, :]
                + (text_mine[text_place, :].astype(f32) + text_other[text_place, :].astype(f32)),
            ],
            axis=0,
        )
        found, gain_grad, shift_grad = norm_backward(resid[place, :], upstream, gain)
        grad[place, :] = found
        grad_low[place, :] = found.astype(bf16)
        norm_grad[0:1] += gain_grad
        norm_grad[1:2] += shift_grad
        return carry

    lax.fori_loop(0, plan.rows, one_norm, 0)
    copy.wait()
    matrix = matrix_of(w, 0, plan.ht, 0, plan.wt, plan.wt, 3 * plan.square)
    mixed[...] = mm(grad_low[...], matrix, NT).astype(bf16)

    def one(row, carry):
        place = pl.ds(pl.multiple_of(row * plan.seq, plan.seq), plan.seq)
        for tile in range(plan.ht):
            cols = slice(tile * TILE, (tile + 1) * TILE)
            found = pair_backward(
                qkv[0, place, cols], qkv[1, place, cols], qkv[2, place, cols],
                probs[row, tile], mixed[place, cols], scale,
            )
            for piece in range(3):
                first = piece * plan.half + tile * TILE
                back[place, first : first + TILE] = found[piece]
        return carry

    lax.fori_loop(0, plan.rows, one, 0)
    matrix = jnp.concatenate(
        [matrix_of(w, 0, plan.wt, 0, plan.ht, plan.ht, p * plan.square) for p in range(3)], axis=1
    )
    part[...] = mm(back[...], matrix, NT).astype(bf16)


def self_backward(
    plan, scale, nat, resid, query_grad, query_mine, query_other, text_grad, text_mine,
    text_other, params, qkv, probs,
):
    tokens, width, half = plan.tokens, plan.width, plan.half
    return pl.pallas_call(
        functools.partial(self_backward_body, plan, scale),
        out_shape=(
            jax.ShapeDtypeStruct((tokens, width), f32),
            jax.ShapeDtypeStruct((tokens, width), bf16),
            jax.ShapeDtypeStruct((tokens, 3 * half), bf16),
            jax.ShapeDtypeStruct((tokens, width), bf16),
            jax.ShapeDtypeStruct((2, width), f32),
        ),
        in_specs=any_specs(1) + vmem_specs(10),
        out_specs=tuple(vmem_specs(5)),
        scratch_shapes=[
            pltpu.VMEM((tokens, half), bf16),
            pltpu.VMEM((plan.self_count, TILE, TILE), bf16),
            pltpu.SemaphoreType.DMA,
        ],
        compiler_params=vmem_params(),
        cost_estimate=cost(8 * tokens * width * half, 1.2e7),
        name="self_backward",
    )(
        nat, resid, query_grad, query_mine, query_other, text_grad, text_mine, text_other,
        params, qkv, probs,
    )


def store_blocks(target, first, product, col_total):
    for row in range(product.shape[0] // TILE):
        for col in range(col_total):
            target[first + row * col_total + col] = product[
                row * TILE : (row + 1) * TILE, col * TILE : (col + 1) * TILE
            ].astype(bf16)


def send_block(source, position, targets, sem):
    base = 0
    for target in targets:
        count = target.shape[0]

        @pl.when((position >= base) & (position < base + count))
        def _(base=base, target=target):
            pltpu.make_async_copy(source, target.at[position - base], sem).start()

        base += count


def grad_blocks_body(first_block, pairs, source_count, target_count, spare, place, *refs):
    sources, targets = refs[:source_count], refs[-3 - target_count : -3]
    staged, blank, sem = refs[-3:]
    base = 0
    sent = 0
    if spare is not None:
        blank[...] = jnp.zeros_like(blank)

        def one_spare(number, carry):
            send_block(blank, place[spare[0] + number], targets, sem)
            return carry

        lax.fori_loop(0, spare[1], one_spare, 0)
        sent += spare[1]
    for left_at, right_at, right_first, right_width, step in pairs:
        left, right = sources[left_at], sources[right_at]
        left_tiles, col_total = left.shape[1] // TILE, right_width // TILE

        def one(chunk, carry, base=base, left=left, right=right, step=step, col_total=col_total,
                right_first=right_first, right_width=right_width):
            cols = pl.ds(pl.multiple_of(chunk * step * TILE, step * TILE), step * TILE)
            product = mm(left[:, cols], right[:, right_first : right_first + right_width], TN)
            first = base + chunk * step * col_total
            store_blocks(staged, first, product, col_total)

            def send(number, carry):
                block = first + number
                send_block(staged.at[block], place[first_block + block], targets, sem)
                return carry

            lax.fori_loop(0, step * col_total, send, 0)
            return carry

        lax.fori_loop(0, left_tiles // step, one, 0)
        base += left_tiles * col_total
    sent += base
    whole = staged.at[pl.ds(0, base)]
    pltpu.make_async_copy(whole, whole, sem).wait()
    for _ in range(sent - base):
        pltpu.make_async_copy(blank, blank, sem).wait()


def grad_blocks(buffers, place, first_block, sources, pairs, flops, spare=None):
    total = sum(sources[a].shape[1] // TILE * (width // TILE) for a, _, _, width, _ in pairs)
    fresh = isinstance(buffers[0], jax.ShapeDtypeStruct)
    given = [] if fresh else list(buffers)
    aliases = {1 + len(sources) + number: number for number in range(len(given))}
    return pl.pallas_call(
        functools.partial(
            grad_blocks_body, first_block, pairs, len(sources), len(buffers), spare
        ),
        out_shape=tuple(jax.ShapeDtypeStruct(b.shape, b.dtype) for b in buffers),
        in_specs=[pl.BlockSpec(memory_space=pltpu.SMEM)]
        + vmem_specs(len(sources))
        + any_specs(len(given)),
        out_specs=tuple(any_specs(len(buffers))),
        scratch_shapes=[
            pltpu.VMEM((total, TILE, TILE), bf16),
            pltpu.VMEM((TILE, TILE), bf16),
            pltpu.SemaphoreType.DMA,
        ],
        input_output_aliases=aliases,
        compiler_params=vmem_params(),
        cost_estimate=cost(flops, 1e7),
        name="grad_blocks",
    )(place, *sources, *given)


def swap_tensor(part):
    if lax.axis_size("tensor") != 2:
        total = lax.psum(part.astype(f32), "tensor")
        return (total - part.astype(f32)).astype(bf16)
    return lax.ppermute(part, "tensor", [(0, 1), (1, 0)])


def layer_rows(
    hidden, image, segment_ids, cotangent, nat, norm_params, heads_local, scale, place, regions
):
    rows, seq, width = hidden.shape
    plan = Plan(
        rows, seq, width, image.shape[2], image.shape[1], heads_local, FF // lax.axis_size("tensor")
    )
    tokens, learned, texts, half = plan.tokens, plan.learned, plan.texts, plan.half
    flat_hidden = hidden.reshape(tokens, width)
    flat_image = jnp.pad(image, ((0, 0), (0, plan.keys - plan.patches), (0, 0))).reshape(
        rows * plan.keys, plan.image_width
    )
    up_query = cotangent[:, :NQ].reshape(learned, width)
    up_text = cotangent[:, NQ:].reshape(texts, width)
    buffers = [jax.ShapeDtypeStruct((count, TILE, TILE), bf16) for count in regions]

    qkv, self_probs, mixed, part_one = self_forward(
        plan, scale, nat, flat_hidden, segment_ids[:, None, :], segment_ids[:, :, None]
    )
    other_one = swap_tensor(part_one)
    image_keys, image_values = image_forward(plan, nat, flat_image)
    (
        first_sum, first_query, first_text, low_query, low_text, cross_queries, cross_probs,
        looked, part_two,
    ) = cross_forward(
        plan, scale, nat, flat_hidden, part_one, other_one, norm_params, image_keys, image_values
    )
    other_two = swap_tensor(part_two)
    text_gated, text_slope, part_text = text_forward(plan, nat, low_text)
    other_text = swap_tensor(part_text)
    second_sum, second, low_second, query_gated, query_slope, part_query = query_forward(
        plan, nat, first_query, part_two, other_two, norm_params
    )
    other_query = swap_tensor(part_query)
    out_text, third_text, third_text_low, before_text, part_four_text, norm_text = feed_backward(
        plan, plan.text_first, 3, nat, first_text, part_text, other_text, up_text, norm_params,
        text_slope,
    )
    other_four_text = swap_tensor(part_four_text)
    out_query, third_query, third_query_low, before_query, part_four_query, norm_query = (
        feed_backward(
            plan, plan.query_first, 2, nat, second, part_query, other_query, up_query, norm_params,
            query_slope,
        )
    )
    other_four_query = swap_tensor(part_four_query)
    feed_pairs = [(0, 1, 0, plan.hidden, 2), (2, 3, 0, width, 2)]
    buffers = grad_blocks(
        buffers, place, plan.text_first, [low_text, before_text, text_gated, third_text_low], feed_pairs,
        4 * texts * width * plan.hidden,
        spare=(plan.block_count, place.shape[0] - plan.block_count),
    )
    second_grad, cross_low, query_back, key_back, value_back, part_five, norm_second = (
        cross_backward(
            plan, scale, nat, second_sum, third_query, part_four_query, other_four_query,
            norm_params, cross_queries, image_keys, image_values, cross_probs,
        )
    )
    other_five = swap_tensor(part_five)
    buffers = grad_blocks(
        buffers, place, plan.query_first, [low_second, before_query, query_gated, third_query_low],
        feed_pairs, 4 * learned * width * plan.hidden,
    )
    buffers = grad_blocks(
        buffers, place, plan.cross_first,
        [low_query, query_back, flat_image, key_back, value_back, looked, cross_low],
        [(0, 1, 0, half, 2), (2, 3, 0, half, 1), (2, 4, 0, half, 1), (5, 6, 0, width, 1)],
        4 * rows * plan.keys * plan.image_width * half,
    )
    first_grad, self_low, self_back, part_six, norm_first = self_backward(
        plan, scale, nat, first_sum, second_grad, part_five, other_five, third_text,
        part_four_text, other_four_text, norm_params, qkv, self_probs,
    )
    other_six = swap_tensor(part_six)
    buffers = grad_blocks(
        buffers, place, plan.self_first, [flat_hidden, self_back, mixed, self_low],
        [(0, 1, 0, half, 2), (0, 1, half, half, 2), (0, 1, 2 * half, half, 2), (2, 3, 0, width, 1)],
        8 * tokens * width * half,
    )
    input_grad = first_grad + (part_six.astype(f32) + other_six.astype(f32))
    output_rows = jnp.concatenate(
        [out_query.reshape(rows, NQ, width), out_text.reshape(rows, seq - NQ, width)], axis=1
    )
    norm_part = jnp.stack([norm_first, norm_second, norm_query, norm_text])
    return (output_rows, input_grad.reshape(rows, seq, width), buffers, norm_part)


CHIP_RING = ((0, 0), (1, 0), (2, 0), (3, 0), (3, 1), (2, 1), (1, 1), (0, 1))
RING = len(CHIP_RING)
RING_DEVICES = 2 * RING


def ring_index(position, core):
    z, x = CHIP_RING[position % RING]
    return (z * 2 + x) * 2 + core


def direction_of(core):
    return 1 - 2 * core


RING_PAIRS = [
    (ring_index(position, core), ring_index(position + direction_of(core), core))
    for position in range(RING)
    for core in range(2)
]


def ring_place(index):
    return CHIP_RING.index((index // 4, index // 2 % 2)), index % 2


CORE_PAIRS = [(index, index ^ 1) for index in range(RING_DEVICES)]


def chain_parts(slots, chains):
    cuts = [slots * number // chains for number in range(chains + 1)]
    return [(first, last - first) for first, last in zip(cuts, cuts[1:])]


def place_blocks_body(counts, first, ids, *refs):
    sources, target, sem = refs[: len(counts)], refs[-2], refs[-1]
    base = first
    for source, count in zip(sources, counts):

        def one(number, carry, base=base, source=source):
            pltpu.make_async_copy(
                source.at[number], target.at[ids[base + number]], sem
            ).start()
            return carry

        lax.fori_loop(0, count, one, 0)
        base += count
    total = sum(counts)
    pltpu.make_async_copy(
        target.at[pl.ds(0, total)], target.at[pl.ds(0, total)], sem
    ).wait()


def place_blocks(ids, first, sources, target, shape):
    counts = [source.shape[0] for source in sources]
    operands = [ids, *sources]
    specs = [pl.BlockSpec(memory_space=pltpu.SMEM)] + vmem_specs(len(sources))
    aliases = {}
    if target is not None:
        operands.append(target)
        specs += any_specs(1)
        aliases = {len(operands) - 1: 0}
    return pl.pallas_call(
        functools.partial(place_blocks_body, counts, first),
        out_shape=jax.ShapeDtypeStruct(shape, bf16),
        in_specs=specs,
        out_specs=any_specs(1)[0],
        scratch_shapes=[pltpu.SemaphoreType.DMA],
        input_output_aliases=aliases,
        cost_estimate=cost(0, 4 * sum(counts) * TILE * TILE),
        name="place_blocks",
    )(*operands)


def gather_ring(shard, order, chains=2):
    slots = shard.shape[0]
    parts = chain_parts(slots, chains)
    table = np.zeros((RING_DEVICES, RING_DEVICES * slots), np.int32)
    for index in range(RING_DEVICES):
        position, core = ring_place(index)
        found = []
        for step in range(RING):
            for side in (core, 1 - core):
                owner = ring_index(position - direction_of(side) * step, side)
                found += [owner * slots + slot for slot in range(slots)]
        table[index] = found
    ids = order[jnp.asarray(table)[lax.axis_index("dp")]]
    shape = (order.shape[0], TILE, TILE)
    other = lax.ppermute(shard, "dp", CORE_PAIRS)
    held = [shard[first : first + count] for first, count in parts]
    natural = None
    waiting, first = [shard, other], 0
    for step in range(1, RING):
        held = [lax.ppermute(piece, "dp", RING_PAIRS) for piece in held]
        if step > 1:
            natural = place_blocks(ids, first, waiting, natural, shape)
            held[0], natural = lax.optimization_barrier((held[0], natural))
            waiting, first = [], step * 2 * slots
        waiting = waiting + held + [lax.ppermute(piece, "dp", CORE_PAIRS) for piece in held]
    return place_blocks(ids, first, waiting, natural, shape)


def scatter_positions(slots):
    table = np.zeros((RING_DEVICES, RING_DEVICES * slots), np.int32)
    for index in range(RING_DEVICES):
        position, core = ring_place(index)
        for step in range(1, RING + 1):
            for number, side in enumerate((1 - core, core)):
                owner = ring_index(position - direction_of(side) * step, side)
                base = (number * RING + step - 1) * slots
                table[index, owner * slots : (owner + 1) * slots] = base + np.arange(slots)
    return table


def scatter_ring(early, late, own, slots, chains=2):
    others = [lax.ppermute(early, "dp", CORE_PAIRS), lax.ppermute(late, "dp", CORE_PAIRS)]
    early_steps = early.shape[0] // slots
    parts = chain_parts(slots, chains)
    held = [None] * chains
    for step in range(1, RING + 1):
        base = (step - 1) * slots
        other, other_base = others[0], base
        if step > early_steps:
            other, other_base = others[1], base - early_steps * slots
        for number, (first, count) in enumerate(parts):
            summed = own[base + first : base + first + count].astype(f32) + other[
                other_base + first : other_base + first + count
            ].astype(f32)
            if held[number] is not None:
                summed = summed + held[number].astype(f32)
            if step < RING:
                summed = lax.ppermute(summed.astype(bf16), "dp", RING_PAIRS)
            held[number] = summed
    return jnp.concatenate(held, axis=0)


def sum_small(values):
    for bit in (1, 2, 4, 8):
        pairs = [(index, index ^ bit) for index in range(RING_DEVICES)]
        values = values + lax.ppermute(values, "dp", pairs)
    return values


PANEL = 16
PACK = TILE // PANEL


def split_two(values):
    high = values.astype(bf16)
    return high, (values - high.astype(f32)).astype(bf16)


def split_three(values):
    high = values.astype(bf16)
    rest = values - high.astype(f32)
    middle = rest.astype(bf16)
    return high, middle, (rest - middle.astype(f32)).astype(bf16)


def join(axis, *pieces):
    return jnp.concatenate(pieces, axis=axis)


def fold(product):
    return product[:, :TILE] + product[:, TILE:]


def times_nn(left, right):
    high, low = split_two(right)
    row = join(1, high, low)
    return fold(mm(join(1, *split_two(left)), join(0, row, row), NN))


def times_precise(left, right):
    lh, lm, ll = split_three(left)
    rh, rm, rl = split_three(right)
    both = mm(join(1, lh, lm), join(0, join(1, rh, rm), join(1, rm, rh)), NN)
    return fold(both) + mm(join(1, lh, ll), join(0, rl, rh), NN)


def diagonal_blocks(rows, base):
    lane = lax.broadcasted_iota(jnp.int32, (PANEL, TILE), 1) // PANEL
    packed = jnp.zeros((PANEL, TILE), f32)
    for number in range(PACK):
        piece = rows[number * PANEL : (number + 1) * PANEL]
        shift = (number * PANEL - base) % TILE
        if shift:
            piece = pltpu.roll(piece, shift, 1)
        packed = jnp.where(lane == number, piece, packed)
    return packed


def factor_inverses(packed):
    groups = packed.shape[0] // PANEL
    shape = packed.shape
    lane = lax.broadcasted_iota(jnp.int32, shape, 1)
    row = lax.broadcasted_iota(jnp.int32, shape, 0) % PANEL
    col = lane % PANEL
    first = lane - col

    def spread(values, step):
        picked = values.reshape(groups, PANEL, TILE)[:, step : step + 1]
        return jnp.broadcast_to(picked, (groups, PANEL, TILE)).reshape(shape)

    scale = jnp.zeros(shape, f32)
    column = jnp.take_along_axis(packed, first, axis=1)
    for step in range(PANEL):
        pivot = spread(column, step)
        inverse = reciprocal(pivot)
        if step + 1 < PANEL:
            following = jnp.take_along_axis(packed, first + (step + 1), axis=1)
            following = following - column * (spread(column, step + 1) * inverse)
        scaled = jnp.where(col == step, 1.0, spread(packed, step)) * inverse
        kept = jnp.where(col == step, jnp.where(row > step, 0.0, 1.0), packed)
        packed = jnp.where(
            row > step, kept - column * scaled, jnp.where(row == step, kept, packed)
        )
        scale = jnp.where(row == step, lax.rsqrt(pivot), scale)
        if step + 1 < PANEL:
            column = following
    return jnp.where(col <= row, packed * scale, 0.0)


def reciprocal(values):
    rough = pl.reciprocal(values, approx=True)
    rough = rough * (2.0 - values * rough)
    return rough * (2.0 - values * rough)


def panel_products(solved, masked):
    lh, lm, ll = split_three(masked)
    rh, rm, rl = split_three(solved)
    found = []
    for number in range(PACK):
        rows = slice(number * PANEL, (number + 1) * PANEL)
        left = join(0, lh[rows], lh[rows], lm[rows], lh[rows], ll[rows], lm[rows])
        right = join(0, rh[rows], rm[rows], rh[rows], rl[rows], rh[rows], rm[rows])
        found.append(mm(left, right, TN))
    return found


def invert_factors(grams, inverses, count):
    groups = count // PACK
    lane = lax.broadcasted_iota(jnp.int32, (TILE, TILE), 1)
    sub = lax.broadcasted_iota(jnp.int32, (TILE, TILE), 0)
    same_block = lane // PANEL == sub // PANEL
    for panel in range(TILE // PANEL):
        base, end = panel * PANEL, (panel + 1) * PANEL
        inside = (lane >= base) & (lane < end)
        unit = (lane - base == sub % PANEL).astype(f32)
        packed = []
        for group in range(groups):
            rows = grams[group * PACK : (group + 1) * PACK, base:end, :].reshape(TILE, TILE)
            packed.append(diagonal_blocks(rows, base))
        inverses[...] = factor_inverses(jnp.concatenate(packed, axis=0))

        def one(first, width, base=base, end=end, inside=inside, unit=unit):
            solved = []
            for offset in range(width):
                group = first + offset
                place = pl.ds(pl.multiple_of(group * PANEL, PANEL), PANEL)
                spread = jnp.where(
                    same_block, jnp.concatenate([inverses[place, :]] * PACK, axis=0), 0.0
                )
                rows = grams[pl.ds(group * PACK, PACK), base:end, :].reshape(TILE, TILE)
                solved.append(times_precise(spread, jnp.where(inside, unit, rows)))
            for offset in range(width):
                grams[pl.ds((first + offset) * PACK, PACK), base:end, :] = solved[offset].reshape(
                    PACK, PANEL, TILE
                )
            if end == TILE:
                return
            for offset in range(width):
                matrices = pl.ds((first + offset) * PACK, PACK)
                old = grams[matrices, end:, :]
                products = panel_products(
                    solved[offset], jnp.where(lane >= end, solved[offset], 0.0)
                )
                products = jnp.stack([product[end:] for product in products])
                grams[matrices, end:, :] = jnp.where(inside[None, end:], 0.0, old) - products

        loop_groups(groups, GROUPS_AT_ONCE, one)


GROUPS_AT_ONCE = 4


def optimizer_slots(first, count, inputs, outputs, grams, products):
    slots = products.shape[0] // 2
    loaded = [[ref[first + offset] for ref in inputs] for offset in range(count)]
    grad, weight, moment, square, left, right, left_base, right_base = map(list, zip(*loaded))
    every = range(count)
    turned_base = [left_base[n].T for n in every]
    turned_grad = [grad[n].T for n in every]
    turned_right = [right_base[n].T for n in every]
    half = [times_nn(turned_base[n], grad[n]) for n in every]
    left = [
        beta_stats * left[n] + (1 - beta_stats) * times_nn(grad[n], turned_grad[n]) for n in every
    ]
    right = [
        beta_stats * right[n] + (1 - beta_stats) * times_nn(turned_grad[n], grad[n])
        for n in every
    ]
    rotated = [times_nn(half[n], right_base[n]) for n in every]
    left_product = [times_nn(left[n], left_base[n]) for n in every]
    right_product = [times_nn(right[n], right_base[n]) for n in every]
    moment = [beta_first * moment[n] + (1 - beta_first) * rotated[n] for n in every]
    square = [
        beta_second * square[n] + (1 - beta_second) * rotated[n] * rotated[n] for n in every
    ]
    step = [
        (moment[n] / (1 - beta_first**STEP))
        / (jnp.sqrt(square[n] / (1 - beta_second**STEP)) + adam_epsilon)
        for n in every
    ]
    half = [times_nn(left_base[n], step[n]) for n in every]
    left_gram = [times_precise(left_product[n].T, left_product[n]) for n in every]
    right_gram = [times_precise(right_product[n].T, right_product[n]) for n in every]
    full = [times_nn(half[n], turned_right[n]) for n in every]
    weight = [weight[n] - matrix_rate * (full[n] + matrix_decay * weight[n]) for n in every]
    for n in every:
        slot = first + n
        values = (weight[n], weight[n].astype(bf16), moment[n], square[n], left[n], right[n])
        for ref, value in zip(outputs, values):
            ref[slot] = value
        products[slot] = left_product[n]
        products[slots + slot] = right_product[n]
        grams[slot] = left_gram[n]
        grams[slots + slot] = right_gram[n]


def loop_groups(total, width, body):
    def one(number, carry):
        body(number * width, width)
        return carry

    lax.fori_loop(0, total // width, one, 0)
    if total % width:
        body(total - total % width, total % width)


def optimizer_body(padded, *refs):
    sources, targets = refs[:8], refs[8:16]
    inputs, outputs = refs[16:24], refs[24:32]
    grams, products, inverses, in_sems, out_sems = refs[32:]
    slots = sources[0].shape[0]
    lane = lax.broadcasted_iota(jnp.int32, (TILE, TILE), 1)
    sub = lax.broadcasted_iota(jnp.int32, (TILE, TILE), 0)
    cuts = [cut for cut in (0, SLOTS_AT_ONCE, 3 * SLOTS_AT_ONCE) if cut < slots] + [slots]
    parts = [(first, last - first) for first, last in zip(cuts, cuts[1:])]
    loads = [
        [
            pltpu.make_async_copy(
                source.at[pl.ds(*part)], target.at[pl.ds(*part)], in_sems.at[number, index]
            )
            for index, (source, target) in enumerate(zip(sources, inputs))
        ]
        for number, part in enumerate(parts)
    ]
    for load in loads:
        for copy in load:
            copy.start()
    for number in range(2 * slots, padded):
        grams[number] = (lane == sub).astype(f32)
    for load, (start, count) in zip(loads, parts):
        for copy in load:
            copy.wait()
        loop_groups(
            count,
            min(SLOTS_AT_ONCE, count),
            lambda first, width: optimizer_slots(
                start + first, width, inputs, outputs, grams, products
            ),
        )
    stores = [
        pltpu.make_async_copy(staged, target, out_sems.at[index])
        for index, (staged, target) in enumerate(zip(outputs, targets))
    ]
    for copy in stores[:6]:
        copy.start()
    invert_factors(grams, inverses, padded)

    def finish(first, count):
        found = []
        for offset in range(count):
            for side in range(2):
                number = side * slots + first + offset
                turned = jnp.where(sub >= lane, grams[number], 0.0).T
                found.append(times_nn(products[number], turned))
        for offset in range(count):
            outputs[6][first + offset] = found[2 * offset]
            outputs[7][first + offset] = found[2 * offset + 1]

    loop_groups(slots, 4, finish)
    for copy in stores[6:]:
        copy.start()
    for copy in stores:
        copy.wait()


SLOTS_AT_ONCE = 6


def optimizer(*arrays):
    shape = arrays[0].shape
    slots = shape[0]
    padded = -(-2 * slots // PACK) * PACK
    kinds = [f32, bf16] + [f32] * 6
    return pl.pallas_call(
        functools.partial(optimizer_body, padded),
        out_shape=tuple(jax.ShapeDtypeStruct(shape, kind) for kind in kinds),
        in_specs=any_specs(8),
        out_specs=tuple(any_specs(8)),
        scratch_shapes=[pltpu.VMEM(shape, f32)] * 8
        + [pltpu.VMEM(shape, kind) for kind in kinds]
        + [
            pltpu.VMEM((padded, TILE, TILE), f32),
            pltpu.VMEM((2 * slots, TILE, TILE), f32),
            pltpu.VMEM((padded // PACK * PANEL, TILE), f32),
            pltpu.SemaphoreType.DMA((3, 8)),
            pltpu.SemaphoreType.DMA((8,)),
        ],
        compiler_params=pltpu.CompilerParams(vmem_limit_bytes=60 * 1024 * 1024),
        name="optimizer",
    )(*arrays)


def per_device(
    hidden,
    image,
    segment_ids,
    cotangent,
    slot_block,
    weight_master,
    moment_one,
    moment_two,
    left_stat,
    right_stat,
    left_basis,
    right_basis,
    norm_params,
    norm_moment_one,
    norm_moment_two,
):
    tensors = lax.axis_size("tensor")
    width = hidden.shape[2]
    heads_local = HEADS // tensors
    scale = (width // HEADS) ** (-0.5)
    order = slot_block[0]
    slot_count = order.shape[0]
    slots = weight_master.shape[1]
    shard = weight_master[0].astype(bf16)
    ring = lax.axis_size("dp") == RING_DEVICES
    if ring:
        natural = gather_ring(shard, order)
        positions = jnp.asarray(scatter_positions(slots))[lax.axis_index("dp")]
        regions = (2 * slots, (RING - 2) * slots, RING * slots)
    else:
        positions = jnp.arange(slot_count, dtype=jnp.int32)
        gathered = lax.all_gather(shard, "dp", axis=0, tiled=True)
        natural = gathered[jnp.zeros_like(order).at[order].set(positions)]
        regions = (slot_count,)
    place = jnp.zeros_like(order).at[order].set(positions)
    out_rows, in_grad, packed, norm_part = layer_rows(
        hidden, image, segment_ids, cotangent, natural, norm_params, heads_local, scale, place,
        regions,
    )
    if ring:
        owned = scatter_ring(*packed, slots)
        norm_total = sum_small(norm_part)
    else:
        owned = lax.psum_scatter(packed[0], "dp", scatter_dimension=0, tiled=True).astype(f32)
        norm_total = lax.psum(norm_part, "dp")
    updated = optimizer(
        owned,
        weight_master[0],
        moment_one[0],
        moment_two[0],
        left_stat[0],
        right_stat[0],
        left_basis[0],
        right_basis[0],
    )
    (
        weight_new,
        weight_copy,
        moment_one_new,
        moment_two_new,
        left_stat_new,
        right_stat_new,
        left_basis_new,
        right_basis_new,
    ) = [array[None] for array in updated]
    norm_first = beta_first * norm_moment_one + (1 - beta_first) * norm_total
    norm_second = beta_second * norm_moment_two + (1 - beta_second) * norm_total * norm_total
    norm_new = norm_params - norm_rate * (norm_first / (1 - beta_first**STEP)) / (
        jnp.sqrt(norm_second / (1 - beta_second**STEP)) + adam_epsilon
    )
    return (
        out_rows,
        in_grad,
        weight_new,
        weight_copy,
        moment_one_new,
        moment_two_new,
        left_stat_new,
        right_stat_new,
        left_basis_new,
        right_basis_new,
        norm_first,
        norm_second,
        norm_new,
    )


def solution(mesh):
    in_specs = (
        P("dp", None, None),
        P("dp", None, None),
        P("dp", None),
        P("dp", None, None),
        P("tensor", None),
        P("tensor", "dp", None, None),
        P("tensor", "dp", None, None),
        P("tensor", "dp", None, None),
        P("tensor", "dp", None, None),
        P("tensor", "dp", None, None),
        P("tensor", "dp", None, None),
        P("tensor", "dp", None, None),
        P(),
        P(),
        P(),
    )
    out_specs = (
        P("dp", None, None),
        P("dp", None, None),
        P("tensor", "dp", None, None),
        P("tensor", "dp", None, None),
        P("tensor", "dp", None, None),
        P("tensor", "dp", None, None),
        P("tensor", "dp", None, None),
        P("tensor", "dp", None, None),
        P("tensor", "dp", None, None),
        P("tensor", "dp", None, None),
        P(),
        P(),
        P(),
    )
    return jax.shard_map(
        per_device, mesh=mesh, in_specs=in_specs, out_specs=out_specs, check_vma=False
    )
```

```python
import functools

import jax
import jax.numpy as jnp
import numpy as np
from jax import lax
from jax.experimental import pallas as pl
from jax.experimental.pallas import tpu as pltpu
from jax.sharding import PartitionSpec as P

HEADS = 12
FF = 3072
NQ = 32
STEP = 10


beta_first = 0.9
beta_second = 0.999
beta_stats = 0.95
adam_epsilon = 1e-08
norm_epsilon = 1e-06
matrix_rate = 0.03
matrix_decay = 0.05
norm_rate = 0.6
masked_score = -1000000000.0


TILE = 128
PATCHES_PAD = 16
f32 = jnp.float32
bf16 = jnp.bfloat16
NN = ((1,), (0,))
NT = ((1,), (1,))
TN = ((0,), (0,))
VMEM_BYTES = 10 * 1024 * 1024


def mm(left, right, dims):
    return lax.dot_general(left, right, (dims, ((), ())), preferred_element_type=f32)


def vmem_specs(count):
    return [pl.BlockSpec(memory_space=pltpu.VMEM)] * count


def any_specs(count):
    return [pl.BlockSpec(memory_space=pl.ANY)] * count


def vmem_params():
    return pltpu.CompilerParams(vmem_limit_bytes=VMEM_BYTES)


def held(shape, kind):
    return pltpu.VMEM(shape, kind)


def pin(*arrays):
    return [pltpu.with_memory_space_constraint(array, pltpu.VMEM) for array in arrays]


def cost(flops, bytes_accessed, transcendentals=0):
    return pl.CostEstimate(
        flops=int(flops), bytes_accessed=int(bytes_accessed), transcendentals=int(transcendentals)
    )


def join(axis, *pieces):
    return jnp.concatenate(pieces, axis=axis)


def matrix_of(blocks_ref, row_first, row_count, col_first, col_count, col_total, base=0):
    rows = []
    for row in range(row_count):
        first = base + (row_first + row) * col_total + col_first
        rows.append(
            jnp.concatenate([blocks_ref[first + col] for col in range(col_count)], axis=1)
        )
    return jnp.concatenate(rows, axis=0)


def norm_forward(resid):
    center = resid - jnp.mean(resid, axis=-1, keepdims=True)
    inverse = lax.rsqrt(jnp.mean(center * center, axis=-1, keepdims=True) + norm_epsilon)
    return center * inverse, inverse


def norm_backward(resid, upstream, gain):
    unit, inverse = norm_forward(resid)
    scaled = upstream * gain
    mean_scaled = jnp.mean(scaled, axis=-1, keepdims=True)
    mean_product = jnp.mean(scaled * unit, axis=-1, keepdims=True)
    grad = inverse * (scaled - mean_scaled - unit * mean_product)
    gain_grad = jnp.sum(upstream * unit, axis=0, keepdims=True)
    shift_grad = jnp.sum(upstream, axis=0, keepdims=True)
    return grad, gain_grad, shift_grad


def head_pair(tile):
    low_half = lax.broadcasted_iota(jnp.int32, tile.shape, 1) < TILE // 2
    zero = jnp.zeros_like(tile)
    return jnp.concatenate(
        [jnp.where(low_half, tile, zero), jnp.where(low_half, zero, tile)], axis=0
    )


def side_by_side(stacked):
    half = stacked.shape[0] // 2
    return jnp.concatenate([stacked[:half], stacked[half:]], axis=1)


def pair_probs(queries, keys, allowed, scale):
    scores = mm(head_pair(queries), keys, NT) * scale
    scores = jnp.where(allowed, scores, masked_score)
    weights = jnp.exp(scores - jnp.max(scores, axis=-1, keepdims=True))
    return weights / jnp.sum(weights, axis=-1, keepdims=True)


def pair_mix(probs, values):
    count = probs.shape[0] // 2
    low_half = lax.broadcasted_iota(jnp.int32, (count, TILE), 1) < TILE // 2
    mixed = mm(probs.astype(bf16), values, NN)
    return jnp.where(low_half, mixed[:count], mixed[count:]).astype(bf16)


def pair_backward(queries, keys, values, probs, mixed_grad, scale):
    grad_pair = head_pair(mixed_grad)
    value_grad = mm(probs.astype(bf16), grad_pair, TN).astype(bf16)
    prob_grad = mm(grad_pair, values, NT)
    inner = jnp.sum(probs * prob_grad, axis=-1, keepdims=True)
    score_grad = (probs * (prob_grad - inner) * scale).astype(bf16)
    count = queries.shape[0]
    low_half = lax.broadcasted_iota(jnp.int32, (count, TILE), 1) < TILE // 2
    both = mm(score_grad, keys, NN)
    query_grad = jnp.where(low_half, both[:count], both[count:]).astype(bf16)
    key_grad = mm(score_grad, head_pair(queries), TN).astype(bf16)
    return query_grad, key_grad, value_grad


class Plan:
    def __init__(self, rows, seq, width, image_width, patches, heads, hidden_units):
        self.rows, self.seq, self.width = rows, seq, width
        self.image_width, self.heads, self.hidden = image_width, heads, hidden_units
        self.half = heads * (TILE // 2)
        self.patches = patches
        self.keys = -(-patches // PATCHES_PAD) * PATCHES_PAD
        self.wt, self.ht = width // TILE, self.half // TILE
        self.it, self.ft = image_width // TILE, hidden_units // TILE
        square, cross, feed = self.wt * self.ht, self.it * self.ht, self.wt * self.ft
        self.square, self.cross, self.feed = square, cross, feed
        self.self_first, self.self_count = 0, 4 * square
        self.cross_first, self.cross_count = 4 * square, 2 * square + 2 * cross
        self.query_first = self.cross_first + self.cross_count
        self.text_first = self.query_first + 2 * feed
        self.block_count = self.text_first + 2 * feed
        self.self_out = 3 * square
        self.image_first = self.cross_first + square
        self.cross_out = self.image_first + 2 * cross
        self.tokens = rows * seq
        self.learned = rows * NQ
        self.texts = rows * (seq - NQ)


def self_forward_body(plan, scale, nat, hidden, segments, qkv, probs, mixed, part):
    for piece in range(3):
        matrix = matrix_of(nat, 0, plan.wt, 0, plan.ht, plan.ht, piece * plan.square)
        qkv[piece] = mm(hidden[...], matrix, NN).astype(bf16)

    def one(row, carry):
        place = pl.ds(pl.multiple_of(row * plan.seq, plan.seq), plan.seq)
        along = jnp.broadcast_to(segments[row].astype(f32), (plan.seq, plan.seq))
        allowed = jnp.concatenate([along.T, along.T], axis=0) == join(0, along, along)
        for tile in range(plan.ht):
            cols = slice(tile * TILE, (tile + 1) * TILE)
            found = pair_probs(qkv[0, place, cols], qkv[1, place, cols], allowed, scale)
            probs[row, tile] = found
            mixed[place, cols] = pair_mix(found, qkv[2, place, cols])
        return carry

    lax.fori_loop(0, plan.rows, one, 0)
    matrix = matrix_of(nat, 0, plan.ht, 0, plan.wt, plan.wt, plan.self_out)
    part[...] = mm(mixed[...], matrix, NN).astype(bf16)


def self_forward(plan, scale, nat, hidden, segments):
    tokens, half, width = plan.tokens, plan.half, plan.width
    return pl.pallas_call(
        functools.partial(self_forward_body, plan, scale),
        out_shape=(
            held((3, tokens, half), bf16),
            held((plan.rows, plan.ht, 2 * plan.seq, plan.seq), f32),
            held((tokens, half), bf16),
            jax.ShapeDtypeStruct((tokens, width), bf16),
        ),
        in_specs=vmem_specs(3),
        out_specs=tuple(vmem_specs(4)),
        compiler_params=vmem_params(),
        cost_estimate=cost(2 * tokens * width * half * 4, 8e6),
        name="self_forward",
    )(*pin(nat, hidden), segments)


def image_body(plan, nat, image, keys, values):
    for piece, target in ((0, keys), (1, values)):
        matrix = matrix_of(nat, 0, plan.it, 0, plan.ht, plan.ht, plan.image_first + piece * plan.cross)

        def one(row, carry):
            place = pl.ds(pl.multiple_of(row * plan.keys, plan.keys), plan.keys)
            target[place, :] = mm(image[place, :], matrix, NN).astype(bf16)
            return carry

        lax.fori_loop(0, plan.rows, one, 0)


def image_forward(plan, nat, image):
    total = plan.rows * plan.keys
    return pl.pallas_call(
        functools.partial(image_body, plan),
        out_shape=(held((total, plan.half), bf16),) * 2,
        in_specs=vmem_specs(2),
        out_specs=tuple(vmem_specs(2)),
        compiler_params=vmem_params(),
        cost_estimate=cost(4 * total * plan.image_width * plan.half, 8e6),
        name="image_forward",
    )(*pin(nat, image))


def cross_forward_body(
    plan, scale, nat, hidden, mine, other, params, image_keys, image_values,
    resid, first_query, first_text, low_query, low_text, queries, probs, mixed, part,
):
    gain, shift = params[0, 0:1], params[0, 1:2]
    text = plan.seq - NQ

    def one_norm(row, carry):
        place = pl.ds(pl.multiple_of(row * plan.seq, plan.seq), plan.seq)
        summed = hidden[place, :].astype(f32) + (
            mine[place, :].astype(f32) + other[place, :].astype(f32)
        )
        resid[place, :] = summed
        first = norm_forward(summed)[0] * gain + shift
        query_place = pl.ds(pl.multiple_of(row * NQ, NQ), NQ)
        text_place = pl.ds(pl.multiple_of(row * text, text), text)
        first_query[query_place, :] = first[:NQ]
        first_text[text_place, :] = first[NQ:]
        low_query[query_place, :] = first[:NQ].astype(bf16)
        low_text[text_place, :] = first[NQ:].astype(bf16)
        return carry

    lax.fori_loop(0, plan.rows, one_norm, 0)
    matrix = matrix_of(nat, 0, plan.wt, 0, plan.ht, plan.ht, plan.cross_first)
    queries[...] = mm(low_query[...], matrix, NN).astype(bf16)
    allowed = lax.broadcasted_iota(jnp.int32, (2 * NQ, plan.keys), 1) < plan.patches

    def one(row, carry):
        query_place = pl.ds(pl.multiple_of(row * NQ, NQ), NQ)
        place = pl.ds(pl.multiple_of(row * plan.keys, plan.keys), plan.keys)
        for tile in range(plan.ht):
            cols = slice(tile * TILE, (tile + 1) * TILE)
            found = pair_probs(queries[query_place, cols], image_keys[place, cols], allowed, scale)
            probs[row, tile] = found
            mixed[query_place, cols] = pair_mix(found, image_values[place, cols])
        return carry

    lax.fori_loop(0, plan.rows, one, 0)
    matrix = matrix_of(nat, 0, plan.ht, 0, plan.wt, plan.wt, plan.cross_out)
    part[...] = mm(mixed[...], matrix, NN).astype(bf16)


def cross_forward(plan, scale, nat, hidden, mine, other, params, image_keys, image_values):
    learned, texts, width, half = plan.learned, plan.texts, plan.width, plan.half
    return pl.pallas_call(
        functools.partial(cross_forward_body, plan, scale),
        out_shape=(
            held((plan.tokens, width), f32),
            held((learned, width), f32),
            held((texts, width), f32),
            held((learned, width), bf16),
            held((texts, width), bf16),
            held((learned, half), bf16),
            held((plan.rows, plan.ht, 2 * NQ, plan.keys), f32),
            held((learned, half), bf16),
            jax.ShapeDtypeStruct((learned, width), bf16),
        ),
        in_specs=vmem_specs(7),
        out_specs=tuple(vmem_specs(9)),
        compiler_params=vmem_params(),
        cost_estimate=cost(4 * learned * width * half, 1.2e7),
        name="cross_forward",
    )(*pin(nat, hidden), mine, other, params, *pin(image_keys, image_values))


def gelu_parts(values):
    normal = 0.5 * (1.0 + lax.erf(values * 0.7071067811865476))
    density = 0.3989422804014327 * jnp.exp(-0.5 * values * values)
    return values * normal, normal + values * density


def feed_forward_tail(plan, first_block, nat, states_low, gated, slope, part):
    def one_up(chunk, carry):
        matrix = matrix_of(nat, 0, plan.wt, chunk * 2, 2, plan.ft, first_block)
        active, derivative = gelu_parts(mm(states_low[...], matrix, NN))
        cols = pl.ds(pl.multiple_of(chunk * 2 * TILE, 2 * TILE), 2 * TILE)
        gated[:, cols] = active.astype(bf16)
        slope[:, cols] = derivative
        return carry

    lax.fori_loop(0, plan.ft // 2, one_up, 0)

    def one_down(chunk, carry):
        matrix = matrix_of(nat, 0, plan.ft, chunk * 2, 2, plan.wt, first_block + plan.feed)
        cols = pl.ds(pl.multiple_of(chunk * 2 * TILE, 2 * TILE), 2 * TILE)
        part[:, cols] = mm(gated[...], matrix, NN).astype(bf16)
        return carry

    lax.fori_loop(0, plan.wt // 2, one_down, 0)


def text_forward_body(plan, nat, low_text, gated, slope, part):
    feed_forward_tail(plan, plan.text_first, nat, low_text, gated, slope, part)


def query_forward_body(
    plan, nat, first_query, mine, other, params, resid, second, low, gated, slope, part,
):
    summed = first_query[...] + (mine[...].astype(f32) + other[...].astype(f32))
    resid[...] = summed
    normed = norm_forward(summed)[0] * params[1, 0:1] + params[1, 1:2]
    second[...] = normed
    low[...] = normed.astype(bf16)
    feed_forward_tail(plan, plan.query_first, nat, low, gated, slope, part)


def feed_shapes(plan, count):
    return (
        held((count, plan.hidden), bf16),
        held((count, plan.hidden), f32),
        jax.ShapeDtypeStruct((count, plan.width), bf16),
    )


def text_forward(plan, nat, low_text):
    return pl.pallas_call(
        functools.partial(text_forward_body, plan),
        out_shape=feed_shapes(plan, plan.texts),
        in_specs=vmem_specs(2),
        out_specs=tuple(vmem_specs(3)),
        compiler_params=vmem_params(),
        cost_estimate=cost(4 * plan.texts * plan.width * plan.hidden, 1e7),
        name="text_forward",
    )(*pin(nat, low_text))


def query_forward(plan, nat, first_query, mine, other, params):
    count, width = plan.learned, plan.width
    return pl.pallas_call(
        functools.partial(query_forward_body, plan),
        out_shape=(
            held((count, width), f32),
            held((count, width), f32),
            held((count, width), bf16),
        )
        + feed_shapes(plan, count),
        in_specs=vmem_specs(5),
        out_specs=tuple(vmem_specs(6)),
        compiler_params=vmem_params(),
        cost_estimate=cost(4 * count * width * plan.hidden, 8e6),
        name="query_forward",
    )(*pin(nat, first_query), mine, other, params)


def feed_backward_body(
    plan, first_block, first_token, which, nat, states, mine, other, upstream, params, slope,
    out, grad, grad_low, before_low, part, norm_grad,
):
    gain, shift = params[which, 0:1], params[which, 1:2]
    count = states.shape[0] // plan.rows
    norm_grad[...] = jnp.zeros_like(norm_grad)

    def one_norm(row, carry):
        place = pl.ds(pl.multiple_of(row * count, count), count)
        summed = states[place, :] + (mine[place, :].astype(f32) + other[place, :].astype(f32))
        out[place, :] = (norm_forward(summed)[0] * gain + shift).astype(bf16)
        found, gain_grad, shift_grad = norm_backward(
            summed, upstream[pl.ds(row * plan.seq + first_token, count), :].astype(f32), gain
        )
        grad[place, :] = found
        grad_low[place, :] = found.astype(bf16)
        norm_grad[0:1] += gain_grad
        norm_grad[1:2] += shift_grad
        return carry

    lax.fori_loop(0, plan.rows, one_norm, 0)

    def one_down(chunk, carry):
        matrix = matrix_of(nat, chunk * 2, 2, 0, plan.wt, plan.wt, first_block + plan.feed)
        cols = pl.ds(pl.multiple_of(chunk * 2 * TILE, 2 * TILE), 2 * TILE)
        before_low[:, cols] = (mm(grad_low[...], matrix, NT) * slope[:, cols]).astype(bf16)
        return carry

    lax.fori_loop(0, plan.ft // 2, one_down, 0)

    def one_up(chunk, carry):
        matrix = matrix_of(nat, chunk * 2, 2, 0, plan.ft, plan.ft, first_block)
        cols = pl.ds(pl.multiple_of(chunk * 2 * TILE, 2 * TILE), 2 * TILE)
        part[:, cols] = mm(before_low[...], matrix, NT).astype(bf16)
        return carry

    lax.fori_loop(0, plan.wt // 2, one_up, 0)


def feed_backward(plan, first_block, first_token, which, nat, states, mine, other, upstream, params, slope):
    count, width = states.shape
    return pl.pallas_call(
        functools.partial(feed_backward_body, plan, first_block, first_token, which),
        out_shape=(
            jax.ShapeDtypeStruct((count, width), bf16),
            held((count, width), f32),
            held((count, width), bf16),
            held((count, plan.hidden), bf16),
            jax.ShapeDtypeStruct((count, width), bf16),
            jax.ShapeDtypeStruct((2, width), f32),
        ),
        in_specs=vmem_specs(7),
        out_specs=tuple(vmem_specs(6)),
        compiler_params=vmem_params(),
        cost_estimate=cost(4 * count * width * plan.hidden, 1e7),
        name="feed_backward",
    )(*pin(nat, states), mine, other, *pin(upstream), params, *pin(slope))


def cross_backward_body(
    plan, scale, nat, resid, third_grad, mine, other, params, queries, keys, values, probs,
    grad, grad_low, query_back, key_back, value_back, part, norm_grad, looked,
):
    upstream = third_grad[...] + (mine[...].astype(f32) + other[...].astype(f32))
    found, gain_grad, shift_grad = norm_backward(resid[...], upstream, params[1, 0:1])
    grad[...] = found
    grad_low[...] = found.astype(bf16)
    norm_grad[0:1] = gain_grad
    norm_grad[1:2] = shift_grad
    matrix = matrix_of(nat, 0, plan.ht, 0, plan.wt, plan.wt, plan.cross_out)
    looked[...] = mm(grad_low[...], matrix, NT).astype(bf16)

    def one(row, carry):
        query_place = pl.ds(pl.multiple_of(row * NQ, NQ), NQ)
        place = pl.ds(pl.multiple_of(row * plan.keys, plan.keys), plan.keys)
        for tile in range(plan.ht):
            cols = slice(tile * TILE, (tile + 1) * TILE)
            query_grad, key_grad, value_grad = pair_backward(
                queries[query_place, cols], keys[place, cols], values[place, cols],
                probs[row, tile], looked[query_place, cols], scale,
            )
            query_back[query_place, cols] = query_grad
            key_back[place, cols] = key_grad
            value_back[place, cols] = value_grad
        return carry

    lax.fori_loop(0, plan.rows, one, 0)
    matrix = matrix_of(nat, 0, plan.wt, 0, plan.ht, plan.ht, plan.cross_first)
    part[...] = mm(query_back[...], matrix, NT).astype(bf16)


def cross_backward(
    plan, scale, nat, resid, third_grad, mine, other, params, queries, keys, values, probs
):
    learned, width, half = plan.learned, plan.width, plan.half
    return pl.pallas_call(
        functools.partial(cross_backward_body, plan, scale),
        out_shape=(
            held((learned, width), f32),
            held((learned, width), bf16),
            held((learned, half), bf16),
            held(keys.shape, bf16),
            held(keys.shape, bf16),
            jax.ShapeDtypeStruct((learned, width), bf16),
            jax.ShapeDtypeStruct((2, width), f32),
        ),
        in_specs=vmem_specs(10),
        out_specs=tuple(vmem_specs(7)),
        scratch_shapes=[
            pltpu.VMEM((learned, half), bf16),
        ],
        compiler_params=vmem_params(),
        cost_estimate=cost(8 * learned * width * half, 1e7),
        name="cross_backward",
    )(*pin(nat, resid, third_grad), mine, other, params, *pin(queries, keys, values, probs))


def self_backward_body(
    plan, scale, nat, resid, query_grad, query_mine, query_other, text_grad, text_mine,
    text_other, params, qkv, probs,
    grad, grad_low, back, part, norm_grad, mixed,
):
    text = plan.seq - NQ
    gain = params[0, 0:1]
    norm_grad[...] = jnp.zeros_like(norm_grad)

    def one_norm(row, carry):
        place = pl.ds(pl.multiple_of(row * plan.seq, plan.seq), plan.seq)
        query_place = pl.ds(pl.multiple_of(row * NQ, NQ), NQ)
        text_place = pl.ds(pl.multiple_of(row * text, text), text)
        upstream = jnp.concatenate(
            [
                query_grad[query_place, :]
                + (query_mine[query_place, :].astype(f32) + query_other[query_place, :].astype(f32)),
                text_grad[text_place, :]
                + (text_mine[text_place, :].astype(f32) + text_other[text_place, :].astype(f32)),
            ],
            axis=0,
        )
        found, gain_grad, shift_grad = norm_backward(resid[place, :], upstream, gain)
        grad[place, :] = found
        grad_low[place, :] = found.astype(bf16)
        norm_grad[0:1] += gain_grad
        norm_grad[1:2] += shift_grad
        return carry

    lax.fori_loop(0, plan.rows, one_norm, 0)
    matrix = matrix_of(nat, 0, plan.ht, 0, plan.wt, plan.wt, plan.self_out)
    mixed[...] = mm(grad_low[...], matrix, NT).astype(bf16)

    def one(row, carry):
        place = pl.ds(pl.multiple_of(row * plan.seq, plan.seq), plan.seq)
        for tile in range(plan.ht):
            cols = slice(tile * TILE, (tile + 1) * TILE)
            found = pair_backward(
                qkv[0, place, cols], qkv[1, place, cols], qkv[2, place, cols],
                probs[row, tile], mixed[place, cols], scale,
            )
            for piece in range(3):
                first = piece * plan.half + tile * TILE
                back[place, first : first + TILE] = found[piece]
        return carry

    lax.fori_loop(0, plan.rows, one, 0)
    matrix = jnp.concatenate(
        [matrix_of(nat, 0, plan.wt, 0, plan.ht, plan.ht, p * plan.square) for p in range(3)],
        axis=1,
    )
    part[...] = mm(back[...], matrix, NT).astype(bf16)


def self_backward(
    plan, scale, nat, resid, query_grad, query_mine, query_other, text_grad, text_mine,
    text_other, params, qkv, probs,
):
    tokens, width, half = plan.tokens, plan.width, plan.half
    return pl.pallas_call(
        functools.partial(self_backward_body, plan, scale),
        out_shape=(
            jax.ShapeDtypeStruct((tokens, width), f32),
            held((tokens, width), bf16),
            held((tokens, 3 * half), bf16),
            jax.ShapeDtypeStruct((tokens, width), bf16),
            jax.ShapeDtypeStruct((2, width), f32),
        ),
        in_specs=vmem_specs(11),
        out_specs=tuple(vmem_specs(5)),
        scratch_shapes=[
            pltpu.VMEM((tokens, half), bf16),
        ],
        compiler_params=vmem_params(),
        cost_estimate=cost(8 * tokens * width * half, 1.2e7),
        name="self_backward",
    )(
        *pin(nat, resid, query_grad), query_mine, query_other, *pin(text_grad), text_mine,
        text_other, params, *pin(qkv, probs),
    )


def store_blocks(target, first, product, col_total):
    for row in range(product.shape[0] // TILE):
        for col in range(col_total):
            target[first + row * col_total + col] = product[
                row * TILE : (row + 1) * TILE, col * TILE : (col + 1) * TILE
            ].astype(bf16)


def send_block(source, position, targets, sem):
    base = 0
    for target in targets:
        count = target.shape[0]

        @pl.when((position >= base) & (position < base + count))
        def _(base=base, target=target):
            pltpu.make_async_copy(source, target.at[position - base], sem).start()

        base += count


def grad_blocks_body(first_block, pairs, source_count, target_count, spare, place, *refs):
    sources, targets = refs[:source_count], refs[-3 - target_count : -3]
    staged, blank, sem = refs[-3:]
    base = 0
    sent = 0
    if spare is not None:
        blank[...] = jnp.zeros_like(blank)

        def one_spare(number, carry):
            send_block(blank, place[spare[0] + number], targets, sem)
            return carry

        lax.fori_loop(0, spare[1], one_spare, 0)
        sent += spare[1]
    for left_at, right_at, right_first, right_width, step in pairs:
        left, right = sources[left_at], sources[right_at]
        left_tiles, col_total = left.shape[1] // TILE, right_width // TILE

        def one(chunk, carry, base=base, left=left, right=right, step=step, col_total=col_total,
                right_first=right_first, right_width=right_width):
            cols = pl.ds(pl.multiple_of(chunk * step * TILE, step * TILE), step * TILE)
            product = mm(left[:, cols], right[:, right_first : right_first + right_width], TN)
            first = base + chunk * step * col_total
            store_blocks(staged, first, product, col_total)

            def send(number, carry):
                block = first + number
                send_block(staged.at[block], place[first_block + block], targets, sem)
                return carry

            lax.fori_loop(0, step * col_total, send, 0)
            return carry

        lax.fori_loop(0, left_tiles // step, one, 0)
        base += left_tiles * col_total
    sent += base
    whole = staged.at[pl.ds(0, base)]
    pltpu.make_async_copy(whole, whole, sem).wait()
    for _ in range(sent - base):
        pltpu.make_async_copy(blank, blank, sem).wait()


def grad_blocks(buffers, place, first_block, sources, pairs, flops, spare=None):
    total = sum(sources[a].shape[1] // TILE * (width // TILE) for a, _, _, width, _ in pairs)
    fresh = isinstance(buffers[0], jax.ShapeDtypeStruct)
    given = [] if fresh else list(buffers)
    aliases = {1 + len(sources) + number: number for number in range(len(given))}
    return pl.pallas_call(
        functools.partial(
            grad_blocks_body, first_block, pairs, len(sources), len(buffers), spare
        ),
        out_shape=tuple(pltpu.HBM(b.shape, b.dtype) for b in buffers),
        in_specs=[pl.BlockSpec(memory_space=pltpu.SMEM)]
        + vmem_specs(len(sources))
        + [pl.BlockSpec(memory_space=pltpu.HBM)] * len(given),
        out_specs=tuple([pl.BlockSpec(memory_space=pltpu.HBM)] * len(buffers)),
        scratch_shapes=[
            pltpu.VMEM((total, TILE, TILE), bf16),
            pltpu.VMEM((TILE, TILE), bf16),
            pltpu.SemaphoreType.DMA,
        ],
        input_output_aliases=aliases,
        compiler_params=vmem_params(),
        cost_estimate=cost(flops, 1e7),
        name="grad_blocks",
    )(place, *pin(*sources), *given)


def swap_tensor(part):
    if lax.axis_size("tensor") != 2:
        total = lax.psum(part.astype(f32), "tensor")
        return (total - part.astype(f32)).astype(bf16)
    return lax.ppermute(part, "tensor", [(0, 1), (1, 0)])


def layer_rows(
    hidden, image, patches, segment_ids, cotangent, nat, norm_params, heads_local, scale, place, regions
):
    rows, seq, width = hidden.shape
    plan = Plan(
        rows, seq, width, image.shape[2], patches, heads_local, FF // lax.axis_size("tensor")
    )
    tokens, learned, texts, half = plan.tokens, plan.learned, plan.texts, plan.half
    flat_hidden = hidden.reshape(tokens, width)
    flat_image = image.reshape(rows * plan.keys, plan.image_width)
    flat_back = cotangent.reshape(tokens, width)
    buffers = [jax.ShapeDtypeStruct((count, TILE, TILE), bf16) for count in regions]

    qkv, self_probs, mixed, part_one = self_forward(
        plan, scale, nat, flat_hidden, segment_ids[:, None, :]
    )
    other_one = swap_tensor(part_one)
    image_keys, image_values = image_forward(plan, nat, flat_image)
    (
        first_sum, first_query, first_text, low_query, low_text, cross_queries, cross_probs,
        looked, part_two,
    ) = cross_forward(
        plan, scale, nat, flat_hidden, part_one, other_one, norm_params, image_keys, image_values
    )
    other_two = swap_tensor(part_two)
    text_gated, text_slope, part_text = text_forward(plan, nat, low_text)
    other_text = swap_tensor(part_text)
    second_sum, second, low_second, query_gated, query_slope, part_query = query_forward(
        plan, nat, first_query, part_two, other_two, norm_params
    )
    other_query = swap_tensor(part_query)
    out_text, third_text, third_text_low, before_text, part_four_text, norm_text = feed_backward(
        plan, plan.text_first, NQ, 3, nat, first_text, part_text, other_text, flat_back, norm_params,
        text_slope,
    )
    other_four_text = swap_tensor(part_four_text)
    out_query, third_query, third_query_low, before_query, part_four_query, norm_query = (
        feed_backward(
            plan, plan.query_first, 0, 2, nat, second, part_query, other_query, flat_back, norm_params,
            query_slope,
        )
    )
    other_four_query = swap_tensor(part_four_query)
    feed_pairs = [(0, 1, 0, plan.hidden, 2), (2, 3, 0, width, 2)]
    buffers = grad_blocks(
        buffers, place, plan.text_first, [low_text, before_text, text_gated, third_text_low], feed_pairs,
        4 * texts * width * plan.hidden,
        spare=(plan.block_count, place.shape[0] - plan.block_count),
    )
    second_grad, cross_low, query_back, key_back, value_back, part_five, norm_second = (
        cross_backward(
            plan, scale, nat, second_sum, third_query, part_four_query, other_four_query,
            norm_params, cross_queries, image_keys, image_values, cross_probs,
        )
    )
    other_five = swap_tensor(part_five)
    buffers = grad_blocks(
        buffers, place, plan.query_first, [low_second, before_query, query_gated, third_query_low],
        feed_pairs, 4 * learned * width * plan.hidden,
    )
    buffers = grad_blocks(
        buffers, place, plan.cross_first,
        [low_query, query_back, flat_image, key_back, value_back, looked, cross_low],
        [(0, 1, 0, half, 2), (2, 3, 0, half, 1), (2, 4, 0, half, 1), (5, 6, 0, width, 1)],
        4 * rows * plan.keys * plan.image_width * half,
    )
    first_grad, self_low, self_back, part_six, norm_first = self_backward(
        plan, scale, nat, first_sum, second_grad, part_five, other_five, third_text,
        part_four_text, other_four_text, norm_params, qkv, self_probs,
    )
    other_six = swap_tensor(part_six)
    buffers = grad_blocks(
        buffers, place, plan.self_first, [flat_hidden, self_back, mixed, self_low],
        [(0, 1, 0, half, 2), (0, 1, half, half, 2), (0, 1, 2 * half, half, 2), (2, 3, 0, width, 1)],
        8 * tokens * width * half,
    )
    input_grad = first_grad + (part_six.astype(f32) + other_six.astype(f32))
    output_rows = jnp.concatenate(
        [out_query.reshape(rows, NQ, width), out_text.reshape(rows, seq - NQ, width)], axis=1
    )
    norm_part = jnp.stack([norm_first, norm_second, norm_query, norm_text])
    return (output_rows, input_grad.reshape(rows, seq, width), buffers, norm_part)


CHIP_RING = ((0, 0), (1, 0), (2, 0), (3, 0), (3, 1), (2, 1), (1, 1), (0, 1))
RING = len(CHIP_RING)
RING_DEVICES = 2 * RING


def ring_index(position, core):
    z, x = CHIP_RING[position % RING]
    return (z * 2 + x) * 2 + core


def direction_of(core):
    return 1 - 2 * core


RING_PAIRS = [
    (ring_index(position, core), ring_index(position + direction_of(core), core))
    for position in range(RING)
    for core in range(2)
]


def ring_place(index):
    return CHIP_RING.index((index // 4, index // 2 % 2)), index % 2


CORE_PAIRS = [(index, index ^ 1) for index in range(RING_DEVICES)]


def chain_parts(slots, chains):
    cuts = [slots * number // chains for number in range(chains + 1)]
    return [(first, last - first) for first, last in zip(cuts, cuts[1:])]


def place_blocks_body(counts, first, ids, *refs):
    sources, target, sem = refs[: len(counts)], refs[-2], refs[-1]
    base = first
    for source, count in zip(sources, counts):

        def one(number, carry, base=base, source=source):
            pltpu.make_async_copy(
                source.at[number], target.at[ids[base + number]], sem
            ).start()
            return carry

        lax.fori_loop(0, count, one, 0)
        base += count
    total = sum(counts)
    pltpu.make_async_copy(
        target.at[pl.ds(0, total)], target.at[pl.ds(0, total)], sem
    ).wait()


def place_blocks(ids, first, sources, target, shape):
    counts = [source.shape[0] for source in sources]
    operands = [ids, *sources]
    specs = [pl.BlockSpec(memory_space=pltpu.SMEM)] + any_specs(len(sources))
    aliases = {}
    if target is not None:
        operands += pin(target)
        specs += vmem_specs(1)
        aliases = {len(operands) - 1: 0}
    return pl.pallas_call(
        functools.partial(place_blocks_body, counts, first),
        out_shape=held(shape, bf16),
        in_specs=specs,
        out_specs=vmem_specs(1)[0],
        scratch_shapes=[pltpu.SemaphoreType.DMA],
        input_output_aliases=aliases,
        compiler_params=pltpu.CompilerParams(vmem_limit_bytes=1024 * 1024),
        cost_estimate=cost(0, 4 * sum(counts) * TILE * TILE),
        name="place_blocks",
    )(*operands)


def gather_positions(slots):
    table = np.zeros((RING_DEVICES, RING_DEVICES * slots), np.int32)
    for index in range(RING_DEVICES):
        position, core = ring_place(index)
        found = []
        for step in range(RING):
            for side in (core, 1 - core):
                owner = ring_index(position - direction_of(side) * step, side)
                found += [owner * slots + slot for slot in range(slots)]
        table[index] = found
    return table


def index_body(count, device, order, arrival, departure, ids, place):
    me = device[0]

    def one(number, carry):
        ids[number] = order[arrival[me, number]]
        place[order[number]] = departure[me, number]
        return carry

    lax.fori_loop(0, count, one, 0)


def block_indices(order, slots):
    count = order.shape[0]
    smem = pl.BlockSpec(memory_space=pltpu.SMEM)
    return pl.pallas_call(
        functools.partial(index_body, count),
        out_shape=(jax.ShapeDtypeStruct((count,), jnp.int32),) * 2,
        in_specs=[smem] * 4,
        out_specs=(smem, smem),
        compiler_params=vmem_params(),
        name="block_indices",
    )(
        lax.axis_index("dp").reshape(1),
        order,
        jnp.asarray(gather_positions(slots)),
        jnp.asarray(scatter_positions(slots)),
    )


def gather_ring(shard, ids, chains=2):
    slots = shard.shape[0]
    parts = chain_parts(slots, chains)
    shape = (ids.shape[0], TILE, TILE)
    other = lax.ppermute(shard, "dp", CORE_PAIRS)
    held = [shard[first : first + count] for first, count in parts]
    natural = None
    waiting, first = [shard, other], 0
    for step in range(1, RING):
        held = [lax.ppermute(piece, "dp", RING_PAIRS) for piece in held]
        if step > 1:
            natural = place_blocks(ids, first, waiting, natural, shape)
            held[0], natural = lax.optimization_barrier((held[0], natural))
            waiting, first = [], step * 2 * slots
        waiting = waiting + held + [lax.ppermute(piece, "dp", CORE_PAIRS) for piece in held]
    return place_blocks(ids, first, waiting, natural, shape)


def scatter_positions(slots):
    table = np.zeros((RING_DEVICES, RING_DEVICES * slots), np.int32)
    for index in range(RING_DEVICES):
        position, core = ring_place(index)
        for step in range(1, RING + 1):
            for number, side in enumerate((1 - core, core)):
                owner = ring_index(position - direction_of(side) * step, side)
                base = (number * RING + step - 1) * slots
                table[index, owner * slots : (owner + 1) * slots] = base + np.arange(slots)
    return table


def scatter_ring(early, late, own, slots, chains=2):
    others = [lax.ppermute(early, "dp", CORE_PAIRS), lax.ppermute(late, "dp", CORE_PAIRS)]
    early_steps = early.shape[0] // slots
    parts = chain_parts(slots, chains)
    held = [None] * chains
    for step in range(1, RING + 1):
        base = (step - 1) * slots
        other, other_base = others[0], base
        if step > early_steps:
            other, other_base = others[1], base - early_steps * slots
        for number, (first, count) in enumerate(parts):
            summed = own[base + first : base + first + count].astype(f32) + other[
                other_base + first : other_base + first + count
            ].astype(f32)
            if held[number] is not None:
                summed = summed + held[number].astype(f32)
            if step < RING:
                summed = lax.ppermute(summed.astype(bf16), "dp", RING_PAIRS)
            held[number] = summed
    return jnp.concatenate(held, axis=0)


def sum_small(values):
    for bit in (1, 2, 4, 8):
        pairs = [(index, index ^ bit) for index in range(RING_DEVICES)]
        values = values + lax.ppermute(values, "dp", pairs)
    return values


PANEL = 16
PACK = TILE // PANEL


def split_two(values):
    high = values.astype(bf16)
    return high, (values - high.astype(f32)).astype(bf16)


def split_three(values):
    high = values.astype(bf16)
    rest = values - high.astype(f32)
    middle = rest.astype(bf16)
    return high, middle, (rest - middle.astype(f32)).astype(bf16)


def fold(product):
    return product[:, :TILE] + product[:, TILE:]


def times_nn(left, right):
    high, low = split_two(right)
    row = join(1, high, low)
    return fold(mm(join(1, *split_two(left)), join(0, row, row), NN))


def times_precise(left, right):
    lh, lm, ll = split_three(left)
    rh, rm, rl = split_three(right)
    both = mm(join(1, lh, lm), join(0, join(1, rh, rm), join(1, rm, rh)), NN)
    return fold(both) + mm(join(1, lh, ll), join(0, rl, rh), NN)


def diagonal_blocks(rows, base):
    lane = lax.broadcasted_iota(jnp.int32, (PANEL, TILE), 1) // PANEL
    packed = jnp.zeros((PANEL, TILE), f32)
    for number in range(PACK):
        piece = rows[number * PANEL : (number + 1) * PANEL]
        shift = (number * PANEL - base) % TILE
        if shift:
            piece = pltpu.roll(piece, shift, 1)
        packed = jnp.where(lane == number, piece, packed)
    return packed


def factor_inverses(packed):
    groups = packed.shape[0] // PANEL
    shape = packed.shape
    lane = lax.broadcasted_iota(jnp.int32, shape, 1)
    row = lax.broadcasted_iota(jnp.int32, shape, 0) % PANEL
    col = lane % PANEL
    first = lane - col

    def spread(values, step):
        picked = values.reshape(groups, PANEL, TILE)[:, step : step + 1]
        return jnp.broadcast_to(picked, (groups, PANEL, TILE)).reshape(shape)

    scale = jnp.zeros(shape, f32)
    column = jnp.take_along_axis(packed, first, axis=1)
    for step in range(PANEL):
        pivot = spread(column, step)
        inverse = reciprocal(pivot)
        if step + 1 < PANEL:
            following = jnp.take_along_axis(packed, first + (step + 1), axis=1)
            following = following - column * (spread(column, step + 1) * inverse)
        scaled = jnp.where(col == step, 1.0, spread(packed, step)) * inverse
        kept = jnp.where(col == step, jnp.where(row > step, 0.0, 1.0), packed)
        packed = jnp.where(
            row > step, kept - column * scaled, jnp.where(row == step, kept, packed)
        )
        scale = jnp.where(row == step, lax.rsqrt(pivot), scale)
        if step + 1 < PANEL:
            column = following
    return jnp.where(col <= row, packed * scale, 0.0)


def reciprocal(values):
    rough = pl.reciprocal(values, approx=True)
    rough = rough * (2.0 - values * rough)
    return rough * (2.0 - values * rough)


def panel_products(solved, masked):
    lh, lm, ll = split_three(masked)
    rh, rm, rl = split_three(solved)
    found = []
    for number in range(PACK):
        rows = slice(number * PANEL, (number + 1) * PANEL)
        left = join(0, lh[rows], lh[rows], lm[rows], lh[rows], ll[rows], lm[rows])
        right = join(0, rh[rows], rm[rows], rh[rows], rl[rows], rh[rows], rm[rows])
        found.append(mm(left, right, TN))
    return found


def invert_factors(grams, inverses, count):
    groups = count // PACK
    lane = lax.broadcasted_iota(jnp.int32, (TILE, TILE), 1)
    sub = lax.broadcasted_iota(jnp.int32, (TILE, TILE), 0)
    same_block = lane // PANEL == sub // PANEL
    for panel in range(TILE // PANEL):
        base, end = panel * PANEL, (panel + 1) * PANEL
        inside = (lane >= base) & (lane < end)
        unit = (lane - base == sub % PANEL).astype(f32)
        packed = []
        for group in range(groups):
            rows = grams[group * PACK : (group + 1) * PACK, base:end, :].reshape(TILE, TILE)
            packed.append(diagonal_blocks(rows, base))
        inverses[...] = factor_inverses(jnp.concatenate(packed, axis=0))

        def one(first, width, base=base, end=end, inside=inside, unit=unit):
            solved = []
            for offset in range(width):
                group = first + offset
                place = pl.ds(pl.multiple_of(group * PANEL, PANEL), PANEL)
                spread = jnp.where(
                    same_block, jnp.concatenate([inverses[place, :]] * PACK, axis=0), 0.0
                )
                rows = grams[pl.ds(group * PACK, PACK), base:end, :].reshape(TILE, TILE)
                solved.append(times_precise(spread, jnp.where(inside, unit, rows)))
            for offset in range(width):
                grams[pl.ds((first + offset) * PACK, PACK), base:end, :] = solved[offset].reshape(
                    PACK, PANEL, TILE
                )
            if end == TILE:
                return
            for offset in range(width):
                matrices = pl.ds((first + offset) * PACK, PACK)
                old = grams[matrices, end:, :]
                products = panel_products(
                    solved[offset], jnp.where(lane >= end, solved[offset], 0.0)
                )
                products = jnp.stack([product[end:] for product in products])
                grams[matrices, end:, :] = jnp.where(inside[None, end:], 0.0, old) - products

        loop_groups(groups, GROUPS_AT_ONCE, one)


GROUPS_AT_ONCE = 4


def optimizer_slots(first, count, inputs, outputs, grams, products):
    slots = products.shape[0] // 2
    loaded = [[ref[first + offset] for ref in inputs] for offset in range(count)]
    grad, weight, moment, square, left, right, left_base, right_base = map(list, zip(*loaded))
    every = range(count)
    turned_base = [left_base[n].T for n in every]
    turned_grad = [grad[n].T for n in every]
    turned_right = [right_base[n].T for n in every]
    half = [times_nn(turned_base[n], grad[n]) for n in every]
    left = [
        beta_stats * left[n] + (1 - beta_stats) * times_nn(grad[n], turned_grad[n]) for n in every
    ]
    right = [
        beta_stats * right[n] + (1 - beta_stats) * times_nn(turned_grad[n], grad[n])
        for n in every
    ]
    rotated = [times_nn(half[n], right_base[n]) for n in every]
    left_product = [times_nn(left[n], left_base[n]) for n in every]
    right_product = [times_nn(right[n], right_base[n]) for n in every]
    moment = [beta_first * moment[n] + (1 - beta_first) * rotated[n] for n in every]
    square = [
        beta_second * square[n] + (1 - beta_second) * rotated[n] * rotated[n] for n in every
    ]
    step = [
        (moment[n] / (1 - beta_first**STEP))
        / (jnp.sqrt(square[n] / (1 - beta_second**STEP)) + adam_epsilon)
        for n in every
    ]
    half = [times_nn(left_base[n], step[n]) for n in every]
    left_gram = [times_precise(left_product[n].T, left_product[n]) for n in every]
    right_gram = [times_precise(right_product[n].T, right_product[n]) for n in every]
    full = [times_nn(half[n], turned_right[n]) for n in every]
    weight = [weight[n] - matrix_rate * (full[n] + matrix_decay * weight[n]) for n in every]
    for n in every:
        slot = first + n
        values = (weight[n], weight[n].astype(bf16), moment[n], square[n], left[n], right[n])
        for ref, value in zip(outputs, values):
            ref[slot] = value
        products[slot] = left_product[n]
        products[slots + slot] = right_product[n]
        grams[slot] = left_gram[n]
        grams[slots + slot] = right_gram[n]


def loop_groups(total, width, body):
    def one(number, carry):
        body(number * width, width)
        return carry

    lax.fori_loop(0, total // width, one, 0)
    if total % width:
        body(total - total % width, total % width)


def optimizer_body(padded, *refs):
    sources, targets = refs[:8], refs[8:16]
    inputs, outputs = refs[16:24], refs[24:32]
    grams, products, inverses, in_sems, out_sems = refs[32:]
    slots = sources[0].shape[0]
    lane = lax.broadcasted_iota(jnp.int32, (TILE, TILE), 1)
    sub = lax.broadcasted_iota(jnp.int32, (TILE, TILE), 0)
    cuts = [cut for cut in (0, SLOTS_AT_ONCE, 3 * SLOTS_AT_ONCE) if cut < slots] + [slots]
    parts = [(first, last - first) for first, last in zip(cuts, cuts[1:])]
    loads = [
        [
            pltpu.make_async_copy(
                source.at[pl.ds(*part)], target.at[pl.ds(*part)], in_sems.at[number, index]
            )
            for index, (source, target) in enumerate(zip(sources, inputs))
        ]
        for number, part in enumerate(parts)
    ]
    for load in loads:
        for copy in load:
            copy.start()
    for number in range(2 * slots, padded):
        grams[number] = (lane == sub).astype(f32)
    for load, (start, count) in zip(loads, parts):
        for copy in load:
            copy.wait()
        loop_groups(
            count,
            min(SLOTS_AT_ONCE, count),
            lambda first, width: optimizer_slots(
                start + first, width, inputs, outputs, grams, products
            ),
        )
    stores = [
        pltpu.make_async_copy(staged, target, out_sems.at[index])
        for index, (staged, target) in enumerate(zip(outputs, targets))
    ]
    for copy in stores[:6]:
        copy.start()
    invert_factors(grams, inverses, padded)

    def finish(first, count):
        found = []
        for offset in range(count):
            for side in range(2):
                number = side * slots + first + offset
                turned = jnp.where(sub >= lane, grams[number], 0.0).T
                found.append(times_nn(products[number], turned))
        for offset in range(count):
            outputs[6][first + offset] = found[2 * offset]
            outputs[7][first + offset] = found[2 * offset + 1]

    loop_groups(slots, 4, finish)
    for copy in stores[6:]:
        copy.start()
    for copy in stores:
        copy.wait()


SLOTS_AT_ONCE = 6


def optimizer(*arrays):
    shape = arrays[0].shape
    slots = shape[0]
    padded = -(-2 * slots // PACK) * PACK
    kinds = [f32, bf16] + [f32] * 6
    return pl.pallas_call(
        functools.partial(optimizer_body, padded),
        out_shape=tuple(jax.ShapeDtypeStruct(shape, kind) for kind in kinds),
        in_specs=any_specs(8),
        out_specs=tuple(any_specs(8)),
        scratch_shapes=[pltpu.VMEM(shape, f32)] * 8
        + [pltpu.VMEM(shape, kind) for kind in kinds]
        + [
            pltpu.VMEM((padded, TILE, TILE), f32),
            pltpu.VMEM((2 * slots, TILE, TILE), f32),
            pltpu.VMEM((padded // PACK * PANEL, TILE), f32),
            pltpu.SemaphoreType.DMA((3, 8)),
            pltpu.SemaphoreType.DMA((8,)),
        ],
        compiler_params=pltpu.CompilerParams(vmem_limit_bytes=60 * 1024 * 1024),
        name="optimizer",
    )(*arrays)


def per_device(
    hidden,
    image,
    segment_ids,
    cotangent,
    slot_block,
    weight_master,
    moment_one,
    moment_two,
    left_stat,
    right_stat,
    left_basis,
    right_basis,
    norm_params,
    norm_moment_one,
    norm_moment_two,
):
    tensors = lax.axis_size("tensor")
    width = hidden.shape[2]
    heads_local = HEADS // tensors
    scale = (width // HEADS) ** (-0.5)
    order = slot_block[0]
    slot_count = order.shape[0]
    slots = weight_master.shape[1]
    shard = weight_master[0].astype(bf16)
    ring = lax.axis_size("dp") == RING_DEVICES
    patches = image.shape[1]
    image = jnp.pad(image, ((0, 0), (0, -patches % PATCHES_PAD), (0, 0)))
    if ring:
        ids, place = block_indices(order, slots)
        ids, image = lax.optimization_barrier((ids, image))
        natural = gather_ring(shard, ids)
        regions = (2 * slots, (RING - 2) * slots, RING * slots)
    else:
        positions = jnp.arange(slot_count, dtype=jnp.int32)
        place = jnp.zeros_like(order).at[order].set(positions)
        gathered = lax.all_gather(shard, "dp", axis=0, tiled=True)
        natural = gathered[place]
        regions = (slot_count,)
    out_rows, in_grad, packed, norm_part = layer_rows(
        hidden, image, patches, segment_ids, cotangent, natural, norm_params, heads_local, scale,
        place, regions,
    )
    if ring:
        owned = scatter_ring(*packed, slots)
        norm_total = sum_small(norm_part)
    else:
        owned = lax.psum_scatter(packed[0], "dp", scatter_dimension=0, tiled=True).astype(f32)
        norm_total = lax.psum(norm_part, "dp")
    updated = optimizer(
        owned,
        weight_master[0],
        moment_one[0],
        moment_two[0],
        left_stat[0],
        right_stat[0],
        left_basis[0],
        right_basis[0],
    )
    (
        weight_new,
        weight_copy,
        moment_one_new,
        moment_two_new,
        left_stat_new,
        right_stat_new,
        left_basis_new,
        right_basis_new,
    ) = [array[None] for array in updated]
    norm_first = beta_first * norm_moment_one + (1 - beta_first) * norm_total
    norm_second = beta_second * norm_moment_two + (1 - beta_second) * norm_total * norm_total
    norm_new = norm_params - norm_rate * (norm_first / (1 - beta_first**STEP)) / (
        jnp.sqrt(norm_second / (1 - beta_second**STEP)) + adam_epsilon
    )
    return (
        out_rows,
        in_grad,
        weight_new,
        weight_copy,
        moment_one_new,
        moment_two_new,
        left_stat_new,
        right_stat_new,
        left_basis_new,
        right_basis_new,
        norm_first,
        norm_second,
        norm_new,
    )


def solution(mesh):
    in_specs = (
        P("dp", None, None),
        P("dp", None, None),
        P("dp", None),
        P("dp", None, None),
        P("tensor", None),
        P("tensor", "dp", None, None),
        P("tensor", "dp", None, None),
        P("tensor", "dp", None, None),
        P("tensor", "dp", None, None),
        P("tensor", "dp", None, None),
        P("tensor", "dp", None, None),
        P("tensor", "dp", None, None),
        P(),
        P(),
        P(),
    )
    out_specs = (
        P("dp", None, None),
        P("dp", None, None),
        P("tensor", "dp", None, None),
        P("tensor", "dp", None, None),
        P("tensor", "dp", None, None),
        P("tensor", "dp", None, None),
        P("tensor", "dp", None, None),
        P("tensor", "dp", None, None),
        P("tensor", "dp", None, None),
        P("tensor", "dp", None, None),
        P(),
        P(),
        P(),
    )
    return jax.shard_map(
        per_device, mesh=mesh, in_specs=in_specs, out_specs=out_specs, check_vma=False
    )
```

```python
import functools

import jax
import jax.numpy as jnp
import numpy as np
from jax import lax
from jax.experimental import pallas as pl
from jax.experimental.pallas import tpu as pltpu
from jax.sharding import PartitionSpec as P

HEADS = 12
FF = 3072
NQ = 32
STEP = 10


beta_first = 0.9
beta_second = 0.999
beta_stats = 0.95
adam_epsilon = 1e-08
norm_epsilon = 1e-06
matrix_rate = 0.03
matrix_decay = 0.05
norm_rate = 0.6
masked_score = -1000000000.0


TILE = 128
PATCHES_PAD = 16
f32 = jnp.float32
bf16 = jnp.bfloat16
NN = ((1,), (0,))
NT = ((1,), (1,))
TN = ((0,), (0,))
VMEM_BYTES = 10 * 1024 * 1024


def mm(left, right, dims):
    return lax.dot_general(left, right, (dims, ((), ())), preferred_element_type=f32)


def vmem_specs(count):
    return [pl.BlockSpec(memory_space=pltpu.VMEM)] * count


def any_specs(count):
    return [pl.BlockSpec(memory_space=pl.ANY)] * count


def vmem_params():
    return pltpu.CompilerParams(vmem_limit_bytes=VMEM_BYTES)


def held(shape, kind):
    return pltpu.VMEM(shape, kind)


def pin(*arrays):
    return [pltpu.with_memory_space_constraint(array, pltpu.VMEM) for array in arrays]


def cost(flops, bytes_accessed, transcendentals=0):
    return pl.CostEstimate(flops=1, bytes_accessed=1, transcendentals=0)


def join(axis, *pieces):
    return jnp.concatenate(pieces, axis=axis)


def matrix_of(blocks_ref, row_first, row_count, col_first, col_count, col_total, base=0):
    rows = []
    for row in range(row_count):
        first = base + (row_first + row) * col_total + col_first
        rows.append(
            jnp.concatenate([blocks_ref[first + col] for col in range(col_count)], axis=1)
        )
    return jnp.concatenate(rows, axis=0)


def norm_forward(resid):
    center = resid - jnp.mean(resid, axis=-1, keepdims=True)
    inverse = lax.rsqrt(jnp.mean(center * center, axis=-1, keepdims=True) + norm_epsilon)
    return center * inverse, inverse


def norm_backward(resid, upstream, gain):
    unit, inverse = norm_forward(resid)
    scaled = upstream * gain
    mean_scaled = jnp.mean(scaled, axis=-1, keepdims=True)
    mean_product = jnp.mean(scaled * unit, axis=-1, keepdims=True)
    grad = inverse * (scaled - mean_scaled - unit * mean_product)
    gain_grad = jnp.sum(upstream * unit, axis=0, keepdims=True)
    shift_grad = jnp.sum(upstream, axis=0, keepdims=True)
    return grad, gain_grad, shift_grad


def head_pair(tile):
    low_half = lax.broadcasted_iota(jnp.int32, tile.shape, 1) < TILE // 2
    zero = jnp.zeros_like(tile)
    return jnp.concatenate(
        [jnp.where(low_half, tile, zero), jnp.where(low_half, zero, tile)], axis=0
    )


def side_by_side(stacked):
    half = stacked.shape[0] // 2
    return jnp.concatenate([stacked[:half], stacked[half:]], axis=1)


def pair_probs(queries, keys, allowed, scale):
    scores = mm(head_pair(queries), keys, NT) * scale
    scores = jnp.where(allowed, scores, masked_score)
    weights = jnp.exp(scores - jnp.max(scores, axis=-1, keepdims=True))
    return weights / jnp.sum(weights, axis=-1, keepdims=True)


def pair_mix(probs, values):
    count = probs.shape[0] // 2
    low_half = lax.broadcasted_iota(jnp.int32, (count, TILE), 1) < TILE // 2
    mixed = mm(probs.astype(bf16), values, NN)
    return jnp.where(low_half, mixed[:count], mixed[count:]).astype(bf16)


def pair_backward(queries, keys, values, probs, mixed_grad, scale):
    grad_pair = head_pair(mixed_grad)
    value_grad = mm(probs.astype(bf16), grad_pair, TN).astype(bf16)
    prob_grad = mm(grad_pair, values, NT)
    inner = jnp.sum(probs * prob_grad, axis=-1, keepdims=True)
    score_grad = (probs * (prob_grad - inner) * scale).astype(bf16)
    count = queries.shape[0]
    low_half = lax.broadcasted_iota(jnp.int32, (count, TILE), 1) < TILE // 2
    both = mm(score_grad, keys, NN)
    query_grad = jnp.where(low_half, both[:count], both[count:]).astype(bf16)
    key_grad = mm(score_grad, head_pair(queries), TN).astype(bf16)
    return query_grad, key_grad, value_grad


class Plan:
    def __init__(self, rows, seq, width, image_width, patches, heads, hidden_units):
        self.rows, self.seq, self.width = rows, seq, width
        self.image_width, self.heads, self.hidden = image_width, heads, hidden_units
        self.half = heads * (TILE // 2)
        self.patches = patches
        self.keys = -(-patches // PATCHES_PAD) * PATCHES_PAD
        self.wt, self.ht = width // TILE, self.half // TILE
        self.it, self.ft = image_width // TILE, hidden_units // TILE
        square, cross, feed = self.wt * self.ht, self.it * self.ht, self.wt * self.ft
        self.square, self.cross, self.feed = square, cross, feed
        self.self_first, self.self_count = 0, 4 * square
        self.cross_first, self.cross_count = 4 * square, 2 * square + 2 * cross
        self.query_first = self.cross_first + self.cross_count
        self.text_first = self.query_first + 2 * feed
        self.block_count = self.text_first + 2 * feed
        self.self_out = 3 * square
        self.image_first = self.cross_first + square
        self.cross_out = self.image_first + 2 * cross
        self.tokens = rows * seq
        self.learned = rows * NQ
        self.texts = rows * (seq - NQ)


def self_forward_body(
    plan, scale, nat, hidden, segments, qkv, probs, mixed, query_part, text_part
):
    for piece in range(3):
        matrix = matrix_of(nat, 0, plan.wt, 0, plan.ht, plan.ht, piece * plan.square)
        qkv[piece] = mm(hidden[...], matrix, NN).astype(bf16)

    def one(row, carry):
        place = pl.ds(pl.multiple_of(row * plan.seq, plan.seq), plan.seq)
        along = jnp.broadcast_to(segments[row].astype(f32), (plan.seq, plan.seq))
        allowed = jnp.concatenate([along.T, along.T], axis=0) == join(0, along, along)
        for tile in range(plan.ht):
            cols = slice(tile * TILE, (tile + 1) * TILE)
            found = pair_probs(qkv[0, place, cols], qkv[1, place, cols], allowed, scale)
            probs[row, tile] = found
            mixed[place, cols] = pair_mix(found, qkv[2, place, cols])
        return carry

    lax.fori_loop(0, plan.rows, one, 0)
    matrix = matrix_of(nat, 0, plan.ht, 0, plan.wt, plan.wt, plan.self_out)
    part = mm(mixed[...], matrix, NN).astype(bf16)
    text = plan.seq - NQ
    for row in range(plan.rows):
        first = row * plan.seq
        query_part[row * NQ : (row + 1) * NQ] = part[first : first + NQ]
        text_part[row * text : (row + 1) * text] = part[first + NQ : first + plan.seq]


def self_forward(plan, scale, nat, hidden, segments):
    tokens, half, width = plan.tokens, plan.half, plan.width
    return pl.pallas_call(
        functools.partial(self_forward_body, plan, scale),
        out_shape=(
            held((3, tokens, half), bf16),
            held((plan.rows, plan.ht, 2 * plan.seq, plan.seq), f32),
            held((tokens, half), bf16),
            jax.ShapeDtypeStruct((plan.learned, width), bf16),
            jax.ShapeDtypeStruct((plan.texts, width), bf16),
        ),
        in_specs=vmem_specs(3),
        out_specs=tuple(vmem_specs(5)),
        compiler_params=vmem_params(),
        cost_estimate=cost(2 * tokens * width * half * 4, 8e6),
        name="self_forward",
    )(*pin(nat, hidden), segments)


def image_body(plan, nat, image, keys, values):
    for piece, target in ((0, keys), (1, values)):
        matrix = matrix_of(nat, 0, plan.it, 0, plan.ht, plan.ht, plan.image_first + piece * plan.cross)

        def one(row, carry):
            place = pl.ds(pl.multiple_of(row * plan.keys, plan.keys), plan.keys)
            target[place, :] = mm(image[place, :], matrix, NN).astype(bf16)
            return carry

        lax.fori_loop(0, plan.rows, one, 0)


def image_forward(plan, nat, image):
    total = plan.rows * plan.keys
    return pl.pallas_call(
        functools.partial(image_body, plan),
        out_shape=(held((total, plan.half), bf16),) * 2,
        in_specs=vmem_specs(2),
        out_specs=tuple(vmem_specs(2)),
        compiler_params=vmem_params(),
        cost_estimate=cost(4 * total * plan.image_width * plan.half, 8e6),
        name="image_forward",
    )(*pin(nat, image))


def first_norm(plan, token, count, hidden, mine, other, params, resid, first, low):
    gain, shift = params[0, 0:1], params[0, 1:2]

    def one(row, carry):
        place = pl.ds(pl.multiple_of(row * count, count), count)
        start = pl.multiple_of(row * plan.seq + token, NQ)
        summed = hidden[pl.ds(start, count), :].astype(f32) + (
            mine[place, :].astype(f32) + other[place, :].astype(f32)
        )
        resid[place, :] = summed
        normed = norm_forward(summed)[0] * gain + shift
        first[place, :] = normed
        low[place, :] = normed.astype(bf16)
        return carry

    lax.fori_loop(0, plan.rows, one, 0)


def cross_forward_body(
    plan, scale, nat, hidden, mine, other, params, image_keys, image_values,
    resid, first, low, queries, probs, mixed, part,
):
    first_norm(plan, 0, NQ, hidden, mine, other, params, resid, first, low)
    matrix = matrix_of(nat, 0, plan.wt, 0, plan.ht, plan.ht, plan.cross_first)
    queries[...] = mm(low[...], matrix, NN).astype(bf16)
    allowed = lax.broadcasted_iota(jnp.int32, (2 * NQ, plan.keys), 1) < plan.patches

    def one(row, carry):
        query_place = pl.ds(pl.multiple_of(row * NQ, NQ), NQ)
        place = pl.ds(pl.multiple_of(row * plan.keys, plan.keys), plan.keys)
        for tile in range(plan.ht):
            cols = slice(tile * TILE, (tile + 1) * TILE)
            found = pair_probs(queries[query_place, cols], image_keys[place, cols], allowed, scale)
            probs[row, tile] = found
            mixed[query_place, cols] = pair_mix(found, image_values[place, cols])
        return carry

    lax.fori_loop(0, plan.rows, one, 0)
    matrix = matrix_of(nat, 0, plan.ht, 0, plan.wt, plan.wt, plan.cross_out)
    part[...] = mm(mixed[...], matrix, NN).astype(bf16)


def cross_forward(plan, scale, nat, hidden, mine, other, params, image_keys, image_values):
    learned, width, half = plan.learned, plan.width, plan.half
    return pl.pallas_call(
        functools.partial(cross_forward_body, plan, scale),
        out_shape=(
            held((learned, width), f32),
            held((learned, width), f32),
            held((learned, width), bf16),
            held((learned, half), bf16),
            held((plan.rows, plan.ht, 2 * NQ, plan.keys), f32),
            held((learned, half), bf16),
            jax.ShapeDtypeStruct((learned, width), bf16),
        ),
        in_specs=vmem_specs(7),
        out_specs=tuple(vmem_specs(7)),
        compiler_params=vmem_params(),
        cost_estimate=cost(4 * learned * width * half, 1.2e7),
        name="cross_forward",
    )(*pin(nat, hidden), mine, other, params, *pin(image_keys, image_values))


def gelu_parts(values):
    normal = 0.5 * (1.0 + lax.erf(values * 0.7071067811865476))
    density = 0.3989422804014327 * jnp.exp(-0.5 * values * values)
    return values * normal, normal + values * density


def feed_forward_tail(plan, first_block, nat, states_low, gated, slope, part):
    def one_up(chunk, carry):
        matrix = matrix_of(nat, 0, plan.wt, chunk * 2, 2, plan.ft, first_block)
        active, derivative = gelu_parts(mm(states_low[...], matrix, NN))
        cols = pl.ds(pl.multiple_of(chunk * 2 * TILE, 2 * TILE), 2 * TILE)
        gated[:, cols] = active.astype(bf16)
        slope[:, cols] = derivative
        return carry

    lax.fori_loop(0, plan.ft // 2, one_up, 0)

    def one_down(chunk, carry):
        matrix = matrix_of(nat, 0, plan.ft, chunk * 2, 2, plan.wt, first_block + plan.feed)
        cols = pl.ds(pl.multiple_of(chunk * 2 * TILE, 2 * TILE), 2 * TILE)
        part[:, cols] = mm(gated[...], matrix, NN).astype(bf16)
        return carry

    lax.fori_loop(0, plan.wt // 2, one_down, 0)


def text_forward_body(
    plan, nat, hidden, mine, other, params, resid, first, low, gated, slope, part
):
    first_norm(plan, NQ, plan.seq - NQ, hidden, mine, other, params, resid, first, low)
    feed_forward_tail(plan, plan.text_first, nat, low, gated, slope, part)


def query_forward_body(
    plan, nat, first_query, mine, other, params, resid, second, low, gated, slope, part,
):
    summed = first_query[...] + (mine[...].astype(f32) + other[...].astype(f32))
    resid[...] = summed
    normed = norm_forward(summed)[0] * params[1, 0:1] + params[1, 1:2]
    second[...] = normed
    low[...] = normed.astype(bf16)
    feed_forward_tail(plan, plan.query_first, nat, low, gated, slope, part)


def feed_shapes(plan, count):
    return (
        held((count, plan.hidden), bf16),
        held((count, plan.hidden), f32),
        jax.ShapeDtypeStruct((count, plan.width), bf16),
    )


def text_forward(plan, nat, hidden, mine, other, params):
    count, width = plan.texts, plan.width
    return pl.pallas_call(
        functools.partial(text_forward_body, plan),
        out_shape=(
            held((count, width), f32),
            held((count, width), f32),
            held((count, width), bf16),
        )
        + feed_shapes(plan, count),
        in_specs=vmem_specs(5),
        out_specs=tuple(vmem_specs(6)),
        compiler_params=vmem_params(),
        cost_estimate=cost(4 * count * width * plan.hidden, 1e7),
        name="text_forward",
    )(*pin(nat, hidden), mine, other, params)


def query_forward(plan, nat, first_query, mine, other, params):
    count, width = plan.learned, plan.width
    return pl.pallas_call(
        functools.partial(query_forward_body, plan),
        out_shape=(
            held((count, width), f32),
            held((count, width), f32),
            held((count, width), bf16),
        )
        + feed_shapes(plan, count),
        in_specs=vmem_specs(5),
        out_specs=tuple(vmem_specs(6)),
        compiler_params=vmem_params(),
        cost_estimate=cost(4 * count * width * plan.hidden, 8e6),
        name="query_forward",
    )(*pin(nat, first_query), mine, other, params)


def feed_backward_body(
    plan, first_block, first_token, which, nat, states, mine, other, upstream, params, slope,
    out, grad, grad_low, before_low, part, norm_grad,
):
    gain, shift = params[which, 0:1], params[which, 1:2]
    count = states.shape[0] // plan.rows
    norm_grad[...] = jnp.zeros_like(norm_grad)

    def one_norm(row, carry):
        place = pl.ds(pl.multiple_of(row * count, count), count)
        summed = states[place, :] + (mine[place, :].astype(f32) + other[place, :].astype(f32))
        out[place, :] = (norm_forward(summed)[0] * gain + shift).astype(bf16)
        found, gain_grad, shift_grad = norm_backward(
            summed, upstream[pl.ds(row * plan.seq + first_token, count), :].astype(f32), gain
        )
        grad[place, :] = found
        grad_low[place, :] = found.astype(bf16)
        norm_grad[0:1] += gain_grad
        norm_grad[1:2] += shift_grad
        return carry

    lax.fori_loop(0, plan.rows, one_norm, 0)

    def one_down(chunk, carry):
        matrix = matrix_of(nat, chunk * 2, 2, 0, plan.wt, plan.wt, first_block + plan.feed)
        cols = pl.ds(pl.multiple_of(chunk * 2 * TILE, 2 * TILE), 2 * TILE)
        before_low[:, cols] = (mm(grad_low[...], matrix, NT) * slope[:, cols]).astype(bf16)
        return carry

    lax.fori_loop(0, plan.ft // 2, one_down, 0)

    def one_up(chunk, carry):
        matrix = matrix_of(nat, chunk * 2, 2, 0, plan.ft, plan.ft, first_block)
        cols = pl.ds(pl.multiple_of(chunk * 2 * TILE, 2 * TILE), 2 * TILE)
        part[:, cols] = mm(before_low[...], matrix, NT).astype(bf16)
        return carry

    lax.fori_loop(0, plan.wt // 2, one_up, 0)


def feed_backward(plan, first_block, first_token, which, nat, states, mine, other, upstream, params, slope):
    count, width = states.shape
    return pl.pallas_call(
        functools.partial(feed_backward_body, plan, first_block, first_token, which),
        out_shape=(
            jax.ShapeDtypeStruct((count, width), bf16),
            held((count, width), f32),
            held((count, width), bf16),
            held((count, plan.hidden), bf16),
            jax.ShapeDtypeStruct((count, width), bf16),
            jax.ShapeDtypeStruct((2, width), f32),
        ),
        in_specs=vmem_specs(7),
        out_specs=tuple(vmem_specs(6)),
        compiler_params=vmem_params(),
        cost_estimate=cost(4 * count * width * plan.hidden, 1e7),
        name="feed_backward",
    )(*pin(nat, states), mine, other, *pin(upstream), params, *pin(slope))


def cross_backward_body(
    plan, scale, nat, resid, third_grad, mine, other, params, queries, keys, values, probs,
    grad, grad_low, query_back, key_back, value_back, part, norm_grad, looked,
):
    upstream = third_grad[...] + (mine[...].astype(f32) + other[...].astype(f32))
    found, gain_grad, shift_grad = norm_backward(resid[...], upstream, params[1, 0:1])
    grad[...] = found
    grad_low[...] = found.astype(bf16)
    norm_grad[0:1] = gain_grad
    norm_grad[1:2] = shift_grad
    matrix = matrix_of(nat, 0, plan.ht, 0, plan.wt, plan.wt, plan.cross_out)
    looked[...] = mm(grad_low[...], matrix, NT).astype(bf16)

    def one(row, carry):
        query_place = pl.ds(pl.multiple_of(row * NQ, NQ), NQ)
        place = pl.ds(pl.multiple_of(row * plan.keys, plan.keys), plan.keys)
        for tile in range(plan.ht):
            cols = slice(tile * TILE, (tile + 1) * TILE)
            query_grad, key_grad, value_grad = pair_backward(
                queries[query_place, cols], keys[place, cols], values[place, cols],
                probs[row, tile], looked[query_place, cols], scale,
            )
            query_back[query_place, cols] = query_grad
            key_back[place, cols] = key_grad
            value_back[place, cols] = value_grad
        return carry

    lax.fori_loop(0, plan.rows, one, 0)
    matrix = matrix_of(nat, 0, plan.wt, 0, plan.ht, plan.ht, plan.cross_first)
    part[...] = mm(query_back[...], matrix, NT).astype(bf16)


def cross_backward(
    plan, scale, nat, resid, third_grad, mine, other, params, queries, keys, values, probs
):
    learned, width, half = plan.learned, plan.width, plan.half
    return pl.pallas_call(
        functools.partial(cross_backward_body, plan, scale),
        out_shape=(
            held((learned, width), f32),
            held((learned, width), bf16),
            held((learned, half), bf16),
            held(keys.shape, bf16),
            held(keys.shape, bf16),
            jax.ShapeDtypeStruct((learned, width), bf16),
            jax.ShapeDtypeStruct((2, width), f32),
        ),
        in_specs=vmem_specs(10),
        out_specs=tuple(vmem_specs(7)),
        scratch_shapes=[
            pltpu.VMEM((learned, half), bf16),
        ],
        compiler_params=vmem_params(),
        cost_estimate=cost(8 * learned * width * half, 1e7),
        name="cross_backward",
    )(*pin(nat, resid, third_grad), mine, other, params, *pin(queries, keys, values, probs))


def self_backward_body(
    plan, scale, nat, query_resid, text_resid, query_grad, query_mine, query_other, text_grad,
    text_mine, text_other, params, qkv, probs,
    grad, grad_low, back, part, norm_grad, mixed,
):
    text = plan.seq - NQ
    gain = params[0, 0:1]
    norm_grad[...] = jnp.zeros_like(norm_grad)

    def one_norm(row, carry):
        place = pl.ds(pl.multiple_of(row * plan.seq, plan.seq), plan.seq)
        query_place = pl.ds(pl.multiple_of(row * NQ, NQ), NQ)
        text_place = pl.ds(pl.multiple_of(row * text, text), text)
        upstream = jnp.concatenate(
            [
                query_grad[query_place, :]
                + (query_mine[query_place, :].astype(f32) + query_other[query_place, :].astype(f32)),
                text_grad[text_place, :]
                + (text_mine[text_place, :].astype(f32) + text_other[text_place, :].astype(f32)),
            ],
            axis=0,
        )
        resid = join(0, query_resid[query_place, :], text_resid[text_place, :])
        found, gain_grad, shift_grad = norm_backward(resid, upstream, gain)
        grad[place, :] = found
        grad_low[place, :] = found.astype(bf16)
        norm_grad[0:1] += gain_grad
        norm_grad[1:2] += shift_grad
        return carry

    lax.fori_loop(0, plan.rows, one_norm, 0)
    matrix = matrix_of(nat, 0, plan.ht, 0, plan.wt, plan.wt, plan.self_out)
    mixed[...] = mm(grad_low[...], matrix, NT).astype(bf16)

    def one(row, carry):
        place = pl.ds(pl.multiple_of(row * plan.seq, plan.seq), plan.seq)
        for tile in range(plan.ht):
            cols = slice(tile * TILE, (tile + 1) * TILE)
            found = pair_backward(
                qkv[0, place, cols], qkv[1, place, cols], qkv[2, place, cols],
                probs[row, tile], mixed[place, cols], scale,
            )
            for piece in range(3):
                first = piece * plan.half + tile * TILE
                back[place, first : first + TILE] = found[piece]
        return carry

    lax.fori_loop(0, plan.rows, one, 0)
    matrix = jnp.concatenate(
        [matrix_of(nat, 0, plan.wt, 0, plan.ht, plan.ht, p * plan.square) for p in range(3)],
        axis=1,
    )
    part[...] = mm(back[...], matrix, NT).astype(bf16)


def self_backward(
    plan, scale, nat, query_resid, text_resid, query_grad, query_mine, query_other, text_grad,
    text_mine, text_other, params, qkv, probs,
):
    tokens, width, half = plan.tokens, plan.width, plan.half
    return pl.pallas_call(
        functools.partial(self_backward_body, plan, scale),
        out_shape=(
            jax.ShapeDtypeStruct((tokens, width), f32),
            held((tokens, width), bf16),
            held((tokens, 3 * half), bf16),
            jax.ShapeDtypeStruct((tokens, width), bf16),
            jax.ShapeDtypeStruct((2, width), f32),
        ),
        in_specs=vmem_specs(12),
        out_specs=tuple(vmem_specs(5)),
        scratch_shapes=[
            pltpu.VMEM((tokens, half), bf16),
        ],
        compiler_params=vmem_params(),
        cost_estimate=cost(8 * tokens * width * half, 1.2e7),
        name="self_backward",
    )(
        *pin(nat, query_resid, text_resid, query_grad), query_mine, query_other, *pin(text_grad), text_mine,
        text_other, params, *pin(qkv, probs),
    )


def grad_blocks_body(first_block, pairs, source_count, spare, place, *refs):
    sources, target = refs[:source_count], refs[-1]
    if spare is not None:
        for number in range(spare[1]):
            target[place[spare[0] + number]] = jnp.zeros((TILE, TILE), bf16)
    base = first_block
    for left_at, right_at, right_first, right_width, step in pairs:
        left, right = sources[left_at], sources[right_at]
        left_tiles, col_total = left.shape[1] // TILE, right_width // TILE

        def one(chunk, carry, base=base, left=left, right=right, step=step, col_total=col_total,
                right_first=right_first, right_width=right_width):
            cols = pl.ds(pl.multiple_of(chunk * step * TILE, step * TILE), step * TILE)
            product = mm(left[:, cols], right[:, right_first : right_first + right_width], TN)
            first = base + chunk * step * col_total
            for row in range(step):
                for col in range(col_total):
                    target[place[first + row * col_total + col]] = product[
                        row * TILE : (row + 1) * TILE, col * TILE : (col + 1) * TILE
                    ].astype(bf16)
            return carry

        lax.fori_loop(0, left_tiles // step, one, 0)
        base += left_tiles * col_total


def grad_blocks(buffer, place, first_block, sources, pairs, flops, spare=None):
    given = [] if isinstance(buffer, jax.ShapeDtypeStruct) else pin(buffer)
    return pl.pallas_call(
        functools.partial(grad_blocks_body, first_block, pairs, len(sources), spare),
        out_shape=held(buffer.shape, buffer.dtype),
        in_specs=[pl.BlockSpec(memory_space=pltpu.SMEM)] + vmem_specs(len(sources) + len(given)),
        out_specs=vmem_specs(1)[0],
        input_output_aliases={1 + len(sources): 0} if given else {},
        compiler_params=vmem_params(),
        cost_estimate=cost(flops, 1e7),
        name="grad_blocks",
    )(place, *pin(*sources), *given)


def swap_tensor(part):
    if lax.axis_size("tensor") != 2:
        total = lax.psum(part.astype(f32), "tensor")
        return (total - part.astype(f32)).astype(bf16)
    return lax.ppermute(part, "tensor", [(0, 1), (1, 0)])


after = lax.optimization_barrier


def sum_steps(values):
    if lax.axis_size("dp") != RING_DEVICES:
        values = lax.psum(values, "dp")
        while True:
            values = yield values
    for bit in (1, 2, 4, 8):
        pairs = [(index, index ^ bit) for index in range(RING_DEVICES)]
        values = yield values + lax.ppermute(values, "dp", pairs)


def layer_rows(
    hidden, image, patches, segment_ids, cotangent, nat, norm_params, heads_local, scale, place
):
    rows, seq, width = hidden.shape
    plan = Plan(
        rows, seq, width, image.shape[2], patches, heads_local, FF // lax.axis_size("tensor")
    )
    tokens, learned, texts, half = plan.tokens, plan.learned, plan.texts, plan.half
    flat_hidden = hidden.reshape(tokens, width)
    flat_image = image.reshape(rows * plan.keys, plan.image_width)
    flat_back = cotangent.reshape(tokens, width)
    buffer = jax.ShapeDtypeStruct((place.shape[0], TILE, TILE), bf16)

    qkv, self_probs, mixed, query_part, text_part = self_forward(
        plan, scale, nat, flat_hidden, segment_ids[:, None, :]
    )
    query_other = swap_tensor(query_part)
    image_keys, image_values = image_forward(plan, nat, flat_image)
    text_part, query_other, image_keys = after((text_part, query_other, image_keys))
    text_other = swap_tensor(text_part)
    query_first, first_query, low_query, cross_queries, cross_probs, looked, part_two = (
        cross_forward(
            plan, scale, nat, flat_hidden, query_part, query_other, norm_params, image_keys,
            image_values,
        )
    )
    other_two = swap_tensor(part_two)
    second_sum, second, low_second, query_gated, query_slope, part_query = query_forward(
        plan, nat, first_query, part_two, other_two, norm_params
    )
    other_query = swap_tensor(part_query)
    text_other, part_query = after((text_other, part_query))
    text_first, first_text, low_text, text_gated, text_slope, part_text = text_forward(
        plan, nat, flat_hidden, text_part, text_other, norm_params
    )
    other_query, part_text = after((other_query, part_text))
    other_text = swap_tensor(part_text)
    out_query, third_query, third_query_low, before_query, part_four_query, norm_query = (
        feed_backward(
            plan, plan.query_first, 0, 2, nat, second, part_query, other_query, flat_back,
            norm_params, query_slope,
        )
    )
    other_four_query = swap_tensor(part_four_query)
    feed_pairs = [(0, 1, 0, plan.hidden, 2), (2, 3, 0, width, 2)]
    buffer = grad_blocks(
        buffer, place, plan.query_first, [low_second, before_query, query_gated, third_query_low],
        feed_pairs, 4 * learned * width * plan.hidden,
        spare=(plan.block_count, place.shape[0] - plan.block_count),
    )
    other_text, buffer = after((other_text, buffer))
    out_text, third_text, third_text_low, before_text, part_four_text, norm_text = feed_backward(
        plan, plan.text_first, NQ, 3, nat, first_text, part_text, other_text, flat_back,
        norm_params, text_slope,
    )
    other_four_query, part_four_text = after((other_four_query, part_four_text))
    other_four_text = swap_tensor(part_four_text)
    second_grad, cross_low, query_back, key_back, value_back, part_five, norm_second = (
        cross_backward(
            plan, scale, nat, second_sum, third_query, part_four_query, other_four_query,
            norm_params, cross_queries, image_keys, image_values, cross_probs,
        )
    )
    other_five = swap_tensor(part_five)
    buffer, part_five = after((buffer, part_five))
    buffer = grad_blocks(
        buffer, place, plan.text_first, [low_text, before_text, text_gated, third_text_low],
        feed_pairs, 4 * texts * width * plan.hidden,
    )
    cross_flops = 2 * rows * plan.keys * plan.image_width * half
    buffer = grad_blocks(
        buffer, place, plan.cross_first, [low_query, query_back, flat_image, key_back],
        [(0, 1, 0, half, 2), (2, 3, 0, half, 1)], cross_flops,
    )
    other_four_text, buffer = after((other_four_text, buffer))
    first_grad, self_low, self_back, part_six, norm_first = self_backward(
        plan, scale, nat, query_first, text_first, second_grad, part_five, other_five, third_text,
        part_four_text, other_four_text, norm_params, qkv, self_probs,
    )
    other_six = swap_tensor(part_six)
    norm_steps = sum_steps(jnp.stack([norm_first, norm_second, norm_query, norm_text]))
    norms = next(norm_steps)
    buffer, part_six = after((buffer, part_six))
    buffer = grad_blocks(
        buffer, place, plan.image_first + plan.cross, [flat_image, value_back],
        [(0, 1, 0, half, 1)], cross_flops,
    )
    buffer, norms = after((buffer, norms))
    norms = norm_steps.send(norms)
    buffer = grad_blocks(
        buffer, place, plan.cross_out, [looked, cross_low], [(0, 1, 0, width, 1)],
        2 * learned * width * half,
    )
    buffer, norms = after((buffer, norms))
    norms = norm_steps.send(norms)
    buffer = grad_blocks(
        buffer, place, plan.self_first, [flat_hidden, self_back],
        [(0, 1, 0, half, 2), (0, 1, half, half, 2), (0, 1, 2 * half, half, 2)],
        6 * tokens * width * half,
    )
    buffer, norms = after((buffer, norms))
    norms = norm_steps.send(norms)
    buffer = grad_blocks(
        buffer, place, plan.self_out, [mixed, self_low], [(0, 1, 0, width, 1)],
        2 * tokens * width * half,
    )
    buffer, norms = after((buffer, norms))
    output_rows = jnp.concatenate(
        [out_query.reshape(rows, NQ, width), out_text.reshape(rows, seq - NQ, width)], axis=1
    )
    return (output_rows, first_grad, part_six, other_six, buffer, norms)


CHIP_RING = ((0, 0), (1, 0), (2, 0), (3, 0), (3, 1), (2, 1), (1, 1), (0, 1))
RING = len(CHIP_RING)
RING_DEVICES = 2 * RING


def ring_index(position, core):
    z, x = CHIP_RING[position % RING]
    return (z * 2 + x) * 2 + core


def direction_of(core):
    return 1 - 2 * core


RING_PAIRS = [
    (ring_index(position, core), ring_index(position + direction_of(core), core))
    for position in range(RING)
    for core in range(2)
]


def ring_place(index):
    return CHIP_RING.index((index // 4, index // 2 % 2)), index % 2


CORE_PAIRS = [(index, index ^ 1) for index in range(RING_DEVICES)]


def chain_parts(slots, chains):
    cuts = [slots * number // chains for number in range(chains + 1)]
    return [(first, last - first) for first, last in zip(cuts, cuts[1:])]


def place_blocks_body(counts, first, ids, *refs):
    sources, target, sem = refs[: len(counts)], refs[-2], refs[-1]
    base = first
    for source, count in zip(sources, counts):
        for number in range(count):
            pltpu.make_async_copy(source.at[number], target.at[ids[base + number]], sem).start()
        base += count
    total = sum(counts)
    pltpu.make_async_copy(
        target.at[pl.ds(0, total)], target.at[pl.ds(0, total)], sem
    ).wait()


def place_blocks(ids, first, sources, target, shape):
    counts = [source.shape[0] for source in sources]
    operands = [ids, *sources]
    specs = [pl.BlockSpec(memory_space=pltpu.SMEM)] + any_specs(len(sources))
    aliases = {}
    if target is not None:
        operands += pin(target)
        specs += vmem_specs(1)
        aliases = {len(operands) - 1: 0}
    return pl.pallas_call(
        functools.partial(place_blocks_body, counts, first),
        out_shape=held(shape, bf16),
        in_specs=specs,
        out_specs=vmem_specs(1)[0],
        scratch_shapes=[pltpu.SemaphoreType.DMA],
        input_output_aliases=aliases,
        compiler_params=pltpu.CompilerParams(vmem_limit_bytes=1024 * 1024),
        cost_estimate=cost(0, 4 * sum(counts) * TILE * TILE),
        name="place_blocks",
    )(*operands)


def gather_positions(slots):
    table = np.zeros((RING_DEVICES, RING_DEVICES * slots), np.int32)
    for index in range(RING_DEVICES):
        position, core = ring_place(index)
        found = []
        for step in range(RING):
            for side in (core, 1 - core):
                owner = ring_index(position - direction_of(side) * step, side)
                found += [owner * slots + slot for slot in range(slots)]
        table[index] = found
    return table


AT_ONCE = 8


def index_body(count, device, order, arrival, departure, ids, place):
    me = device[0]

    def one(group, carry):
        numbers = [group * AT_ONCE + offset for offset in range(AT_ONCE)]
        blocks = [order[number] for number in numbers]
        arrived = [order[arrival[me, number]] for number in numbers]
        places = [departure[me, number] for number in numbers]
        for number, block, other, target in zip(numbers, blocks, arrived, places):
            ids[number] = other
            place[block] = target
        return carry

    lax.fori_loop(0, count // AT_ONCE, one, 0)


def block_indices(order, slots):
    count = order.shape[0]
    smem = pl.BlockSpec(memory_space=pltpu.SMEM)
    return pl.pallas_call(
        functools.partial(index_body, count),
        out_shape=(jax.ShapeDtypeStruct((count,), jnp.int32),) * 2,
        in_specs=[smem] * 4,
        out_specs=(smem, smem),
        compiler_params=vmem_params(),
        name="block_indices",
    )(
        lax.axis_index("dp").reshape(1),
        order,
        jnp.asarray(gather_positions(slots)),
        jnp.asarray(scatter_positions(slots)),
    )


def gather_ring(shard, order, image, chains=2):
    slots = shard.shape[0]
    parts = chain_parts(slots, chains)
    shape = (order.shape[0], TILE, TILE)
    ids, place = block_indices(order, slots)
    other = lax.ppermute(shard, "dp", CORE_PAIRS)
    held = [shard[first : first + count] for first, count in parts]
    natural = None
    waiting, first, placed = [shard, other], 0, 2 * slots
    for step in range(1, RING):
        held = [lax.ppermute(piece, "dp", RING_PAIRS) for piece in held]
        if step == 2:
            held[0], ids, place = lax.optimization_barrier((held[0], ids, place))
        if step == 3:
            held[0], image = lax.optimization_barrier((held[0], pad_patches(image)))
        if step >= 4:
            now = 2 + 2 * chains if step == 4 else 4 * chains
            count = sum(piece.shape[0] for piece in waiting[:now])
            natural = place_blocks(ids, first, waiting[:now], natural, shape)
            held[0], natural = lax.optimization_barrier((held[0], natural))
            waiting, first = waiting[now:], first + count
        waiting = waiting + held + [lax.ppermute(piece, "dp", CORE_PAIRS) for piece in held]
    return place_blocks(ids, first, waiting, natural, shape), image, place


def scatter_positions(slots):
    table = np.zeros((RING_DEVICES, RING_DEVICES * slots), np.int32)
    for index in range(RING_DEVICES):
        position, core = ring_place(index)
        for step in range(1, RING + 1):
            for number, side in enumerate((1 - core, core)):
                owner = ring_index(position - direction_of(side) * step, side)
                base = (number * RING + step - 1) * slots
                table[index, owner * slots : (owner + 1) * slots] = base + np.arange(slots)
    return table


def scatter_ring(packed, beside, slots, chains=2):
    parts = chain_parts(slots, chains)
    held = [None] * chains
    other = None
    for step in range(1, RING + 1):
        base = (step - 1) * slots
        if step % 2:
            if other is not None:
                packed, other = lax.optimization_barrier((packed, other))
            other = lax.ppermute(packed[base : base + 2 * slots], "dp", CORE_PAIRS)
        pieces = []
        for number, (first, count) in enumerate(parts):
            start = (RING + step - 1) * slots + first
            place = (step - 1) % 2 * slots + first
            terms = [packed[start : start + count], other[place : place + count]]
            if held[number] is not None:
                terms.append(held[number])
            pieces.append(terms)
        if step == RING:
            return pieces, beside
        for number, terms in enumerate(pieces):
            summed = sum(term.astype(f32) for term in terms).astype(bf16)
            held[number] = lax.ppermute(summed, "dp", RING_PAIRS)
        if step == 1:
            held[0], beside = lax.optimization_barrier((held[0], beside))


def pad_patches(image):
    return jnp.pad(image, ((0, 0), (0, -image.shape[1] % PATCHES_PAD), (0, 0)))


PANEL = 16
PACK = TILE // PANEL


def split_two(values):
    high = values.astype(bf16)
    return high, (values - high.astype(f32)).astype(bf16)


def split_three(values):
    high = values.astype(bf16)
    rest = values - high.astype(f32)
    middle = rest.astype(bf16)
    return high, middle, (rest - middle.astype(f32)).astype(bf16)


def fold(product):
    return product[:, :TILE] + product[:, TILE:]


def times_nn(left, right):
    high, low = split_two(right)
    row = join(1, high, low)
    return fold(mm(join(1, *split_two(left)), join(0, row, row), NN))


def times_precise(left, right):
    lh, lm, ll = split_three(left)
    rh, rm, rl = split_three(right)
    both = mm(join(1, lh, lm), join(0, join(1, rh, rm), join(1, rm, rh)), NN)
    return fold(both) + mm(join(1, lh, ll), join(0, rl, rh), NN)


def diagonal_blocks(rows, base):
    lane = lax.broadcasted_iota(jnp.int32, (PANEL, TILE), 1) // PANEL
    packed = jnp.zeros((PANEL, TILE), f32)
    for number in range(PACK):
        piece = rows[number * PANEL : (number + 1) * PANEL]
        shift = (number * PANEL - base) % TILE
        if shift:
            piece = pltpu.roll(piece, shift, 1)
        packed = jnp.where(lane == number, piece, packed)
    return packed


def factor_inverses(packed):
    groups = packed.shape[0] // PANEL
    shape = packed.shape
    lane = lax.broadcasted_iota(jnp.int32, shape, 1)
    row = lax.broadcasted_iota(jnp.int32, shape, 0) % PANEL
    col = lane % PANEL
    first = lane - col

    def spread(values, step):
        picked = values.reshape(groups, PANEL, TILE)[:, step : step + 1]
        return jnp.broadcast_to(picked, (groups, PANEL, TILE)).reshape(shape)

    scale = jnp.zeros(shape, f32)
    column = jnp.take_along_axis(packed, first, axis=1)
    for step in range(PANEL):
        pivot = spread(column, step)
        inverse = reciprocal(pivot)
        if step + 1 < PANEL:
            following = jnp.take_along_axis(packed, first + (step + 1), axis=1)
            following = following - column * (spread(column, step + 1) * inverse)
        scaled = jnp.where(col == step, 1.0, spread(packed, step)) * inverse
        kept = jnp.where(col == step, jnp.where(row > step, 0.0, 1.0), packed)
        packed = jnp.where(
            row > step, kept - column * scaled, jnp.where(row == step, kept, packed)
        )
        scale = jnp.where(row == step, lax.rsqrt(pivot), scale)
        if step + 1 < PANEL:
            column = following
    return jnp.where(col <= row, packed * scale, 0.0)


def reciprocal(values):
    rough = pl.reciprocal(values, approx=True)
    rough = rough * (2.0 - values * rough)
    return rough * (2.0 - values * rough)


def panel_products(solved, masked):
    lh, lm, ll = split_three(masked)
    rh, rm, rl = split_three(solved)
    found = []
    for number in range(PACK):
        rows = slice(number * PANEL, (number + 1) * PANEL)
        left = join(0, lh[rows], lh[rows], lm[rows], lh[rows], ll[rows], lm[rows])
        right = join(0, rh[rows], rm[rows], rh[rows], rl[rows], rh[rows], rm[rows])
        found.append(mm(left, right, TN))
    return found


def invert_factors(grams, inverses, count):
    groups = count // PACK
    lane = lax.broadcasted_iota(jnp.int32, (TILE, TILE), 1)
    sub = lax.broadcasted_iota(jnp.int32, (TILE, TILE), 0)
    same_block = lane // PANEL == sub // PANEL
    for panel in range(TILE // PANEL):
        base, end = panel * PANEL, (panel + 1) * PANEL
        inside = (lane >= base) & (lane < end)
        unit = (lane - base == sub % PANEL).astype(f32)
        packed = []
        for group in range(groups):
            rows = grams[group * PACK : (group + 1) * PACK, base:end, :].reshape(TILE, TILE)
            packed.append(diagonal_blocks(rows, base))
        inverses[...] = factor_inverses(jnp.concatenate(packed, axis=0))

        def one(first, width, base=base, end=end, inside=inside, unit=unit):
            solved = []
            for offset in range(width):
                group = first + offset
                place = pl.ds(pl.multiple_of(group * PANEL, PANEL), PANEL)
                spread = jnp.where(
                    same_block, jnp.concatenate([inverses[place, :]] * PACK, axis=0), 0.0
                )
                rows = grams[pl.ds(group * PACK, PACK), base:end, :].reshape(TILE, TILE)
                solved.append(times_precise(spread, jnp.where(inside, unit, rows)))
            for offset in range(width):
                grams[pl.ds((first + offset) * PACK, PACK), base:end, :] = solved[offset].reshape(
                    PACK, PANEL, TILE
                )
            if end == TILE:
                return
            for offset in range(width):
                matrices = pl.ds((first + offset) * PACK, PACK)
                old = grams[matrices, end:, :]
                products = panel_products(
                    solved[offset], jnp.where(lane >= end, solved[offset], 0.0)
                )
                products = jnp.stack([product[end:] for product in products])
                grams[matrices, end:, :] = jnp.where(inside[None, end:], 0.0, old) - products

        loop_groups(groups, GROUPS_AT_ONCE, one)


GROUPS_AT_ONCE = 4


def optimizer_slots(first, count, inputs, outputs, grams, products):
    slots = products.shape[0] // 2
    loaded = [[ref[first + offset] for ref in inputs] for offset in range(count)]
    grad, weight, moment, square, left, right, left_base, right_base = map(list, zip(*loaded))
    every = range(count)
    turned_base = [left_base[n].T for n in every]
    turned_grad = [grad[n].T for n in every]
    turned_right = [right_base[n].T for n in every]
    half = [times_nn(turned_base[n], grad[n]) for n in every]
    left = [
        beta_stats * left[n] + (1 - beta_stats) * times_nn(grad[n], turned_grad[n]) for n in every
    ]
    right = [
        beta_stats * right[n] + (1 - beta_stats) * times_nn(turned_grad[n], grad[n])
        for n in every
    ]
    rotated = [times_nn(half[n], right_base[n]) for n in every]
    left_product = [times_nn(left[n], left_base[n]) for n in every]
    right_product = [times_nn(right[n], right_base[n]) for n in every]
    moment = [beta_first * moment[n] + (1 - beta_first) * rotated[n] for n in every]
    square = [
        beta_second * square[n] + (1 - beta_second) * rotated[n] * rotated[n] for n in every
    ]
    step = [
        (moment[n] / (1 - beta_first**STEP))
        / (jnp.sqrt(square[n] / (1 - beta_second**STEP)) + adam_epsilon)
        for n in every
    ]
    half = [times_nn(left_base[n], step[n]) for n in every]
    left_gram = [times_precise(left_product[n].T, left_product[n]) for n in every]
    right_gram = [times_precise(right_product[n].T, right_product[n]) for n in every]
    full = [times_nn(half[n], turned_right[n]) for n in every]
    weight = [weight[n] - matrix_rate * (full[n] + matrix_decay * weight[n]) for n in every]
    for n in every:
        slot = first + n
        values = (weight[n], weight[n].astype(bf16), moment[n], square[n], left[n], right[n])
        for ref, value in zip(outputs, values):
            ref[slot] = value
        products[slot] = left_product[n]
        products[slots + slot] = right_product[n]
        grams[slot] = left_gram[n]
        grams[slots + slot] = right_gram[n]


def loop_groups(total, width, body):
    def one(number, carry):
        body(number * width, width)
        return carry

    lax.fori_loop(0, total // width, one, 0)
    if total % width:
        body(total - total % width, total % width)


def optimizer_body(padded, counts, *refs):
    pieces, refs = refs[: sum(counts)], refs[sum(counts) :]
    sources, targets = refs[:7], refs[7:15]
    gradient, inputs, outputs = refs[15], refs[16:23], refs[23:31]
    grams, products, inverses, in_sems, out_sems = refs[31:]
    slots = sources[0].shape[0]
    lane = lax.broadcasted_iota(jnp.int32, (TILE, TILE), 1)
    sub = lax.broadcasted_iota(jnp.int32, (TILE, TILE), 0)
    cuts = [cut for cut in (0, SLOTS_AT_ONCE, 3 * SLOTS_AT_ONCE) if cut < slots] + [slots]
    parts = [(first, last - first) for first, last in zip(cuts, cuts[1:])]
    loads = [
        [
            pltpu.make_async_copy(
                source.at[pl.ds(*part)], target.at[pl.ds(*part)], in_sems.at[number, index]
            )
            for index, (source, target) in enumerate(zip(sources, inputs))
        ]
        for number, part in enumerate(parts)
    ]
    for load in loads:
        for copy in load:
            copy.start()
    for number in range(2 * slots, padded):
        grams[number] = (lane == sub).astype(f32)
    base = 0
    for count in counts:
        terms, pieces = pieces[:count], pieces[count:]
        gradient[base : base + terms[0].shape[0]] = sum(term[...].astype(f32) for term in terms)
        base += terms[0].shape[0]
    for load, (start, count) in zip(loads, parts):
        for copy in load:
            copy.wait()
        loop_groups(
            count,
            min(SLOTS_AT_ONCE, count),
            lambda first, width: optimizer_slots(
                start + first, width, (gradient, *inputs), outputs, grams, products
            ),
        )
    stores = [
        pltpu.make_async_copy(staged, target, out_sems.at[index])
        for index, (staged, target) in enumerate(zip(outputs, targets))
    ]
    for copy in stores[:6]:
        copy.start()
    invert_factors(grams, inverses, padded)

    def finish(first, count):
        found = []
        for offset in range(count):
            for side in range(2):
                number = side * slots + first + offset
                turned = jnp.where(sub >= lane, grams[number], 0.0).T
                found.append(times_nn(products[number], turned))
        for offset in range(count):
            outputs[6][first + offset] = found[2 * offset]
            outputs[7][first + offset] = found[2 * offset + 1]

    loop_groups(slots, 4, finish)
    for copy in stores[6:]:
        copy.start()
    for copy in stores:
        copy.wait()


SLOTS_AT_ONCE = 6


def optimizer(pieces, *arrays):
    shape = arrays[0].shape
    slots = shape[0]
    padded = -(-2 * slots // PACK) * PACK
    kinds = [f32, bf16] + [f32] * 6
    counts = [len(terms) for terms in pieces]
    return pl.pallas_call(
        functools.partial(optimizer_body, padded, counts),
        out_shape=tuple(jax.ShapeDtypeStruct(shape, kind) for kind in kinds),
        in_specs=vmem_specs(sum(counts)) + any_specs(7),
        out_specs=tuple(any_specs(8)),
        scratch_shapes=[pltpu.VMEM(shape, f32)] * 8
        + [pltpu.VMEM(shape, kind) for kind in kinds]
        + [
            pltpu.VMEM((padded, TILE, TILE), f32),
            pltpu.VMEM((2 * slots, TILE, TILE), f32),
            pltpu.VMEM((padded // PACK * PANEL, TILE), f32),
            pltpu.SemaphoreType.DMA((3, 7)),
            pltpu.SemaphoreType.DMA((8,)),
        ],
        compiler_params=pltpu.CompilerParams(vmem_limit_bytes=60 * 1024 * 1024),
        name="optimizer",
    )(*[term for terms in pieces for term in terms], *arrays)


def per_device(
    hidden,
    image,
    segment_ids,
    cotangent,
    slot_block,
    weight_master,
    moment_one,
    moment_two,
    left_stat,
    right_stat,
    left_basis,
    right_basis,
    norm_params,
    norm_moment_one,
    norm_moment_two,
):
    tensors = lax.axis_size("tensor")
    width = hidden.shape[2]
    heads_local = HEADS // tensors
    scale = (width // HEADS) ** (-0.5)
    order = slot_block[0]
    slot_count = order.shape[0]
    slots = weight_master.shape[1]
    shard = weight_master[0].astype(bf16)
    ring = lax.axis_size("dp") == RING_DEVICES
    patches = image.shape[1]
    if ring:
        natural, image, place = gather_ring(shard, order, image)
    else:
        image = pad_patches(image)
        positions = jnp.arange(slot_count, dtype=jnp.int32)
        place = jnp.zeros_like(order).at[order].set(positions)
        gathered = lax.all_gather(shard, "dp", axis=0, tiled=True)
        natural = gathered[place]
    out_rows, first_grad, part_six, other_six, packed, norm_total = layer_rows(
        hidden, image, patches, segment_ids, cotangent, natural, norm_params, heads_local, scale,
        place,
    )
    if ring:
        owned, beside = scatter_ring(packed, (other_six, norm_total), slots)
        other_six, norm_total = beside
    else:
        owned = [[lax.psum_scatter(packed, "dp", scatter_dimension=0, tiled=True)]]
    in_grad = first_grad + (part_six.astype(f32) + other_six.astype(f32))
    in_grad = in_grad.reshape(hidden.shape)
    updated = optimizer(
        owned,
        weight_master[0],
        moment_one[0],
        moment_two[0],
        left_stat[0],
        right_stat[0],
        left_basis[0],
        right_basis[0],
    )
    (
        weight_new,
        weight_copy,
        moment_one_new,
        moment_two_new,
        left_stat_new,
        right_stat_new,
        left_basis_new,
        right_basis_new,
    ) = [array[None] for array in updated]
    norm_first = beta_first * norm_moment_one + (1 - beta_first) * norm_total
    norm_second = beta_second * norm_moment_two + (1 - beta_second) * norm_total * norm_total
    norm_new = norm_params - norm_rate * (norm_first / (1 - beta_first**STEP)) / (
        jnp.sqrt(norm_second / (1 - beta_second**STEP)) + adam_epsilon
    )
    return (
        out_rows,
        in_grad,
        weight_new,
        weight_copy,
        moment_one_new,
        moment_two_new,
        left_stat_new,
        right_stat_new,
        left_basis_new,
        right_basis_new,
        norm_first,
        norm_second,
        norm_new,
    )


def solution(mesh):
    in_specs = (
        P("dp", None, None),
        P("dp", None, None),
        P("dp", None),
        P("dp", None, None),
        P("tensor", None),
        P("tensor", "dp", None, None),
        P("tensor", "dp", None, None),
        P("tensor", "dp", None, None),
        P("tensor", "dp", None, None),
        P("tensor", "dp", None, None),
        P("tensor", "dp", None, None),
        P("tensor", "dp", None, None),
        P(),
        P(),
        P(),
    )
    out_specs = (
        P("dp", None, None),
        P("dp", None, None),
        P("tensor", "dp", None, None),
        P("tensor", "dp", None, None),
        P("tensor", "dp", None, None),
        P("tensor", "dp", None, None),
        P("tensor", "dp", None, None),
        P("tensor", "dp", None, None),
        P("tensor", "dp", None, None),
        P("tensor", "dp", None, None),
        P(),
        P(),
        P(),
    )
    return jax.shard_map(
        per_device, mesh=mesh, in_specs=in_specs, out_specs=out_specs, check_vma=False
    )
```

```python
import functools

import jax
import jax.numpy as jnp
import numpy as np
from jax import lax
from jax.experimental import pallas as pl
from jax.experimental.pallas import tpu as pltpu
from jax.sharding import PartitionSpec as P

HEADS = 12
FF = 3072
NQ = 32
STEP = 10


beta_first = 0.9
beta_second = 0.999
beta_stats = 0.95
adam_epsilon = 1e-08
norm_epsilon = 1e-06
matrix_rate = 0.03
matrix_decay = 0.05
norm_rate = 0.6
masked_score = -1000000000.0


TILE = 128
PATCHES_PAD = 16
f32 = jnp.float32
bf16 = jnp.bfloat16
NN = ((1,), (0,))
NT = ((1,), (1,))
TN = ((0,), (0,))
VMEM_BYTES = 10 * 1024 * 1024


def mm(left, right, dims):
    return lax.dot_general(left, right, (dims, ((), ())), preferred_element_type=f32)


def vmem_specs(count):
    return [pl.BlockSpec(memory_space=pltpu.VMEM)] * count


def any_specs(count):
    return [pl.BlockSpec(memory_space=pl.ANY)] * count


def vmem_params():
    return pltpu.CompilerParams(vmem_limit_bytes=VMEM_BYTES)


def held(shape, kind):
    return pltpu.VMEM(shape, kind)


def pin(*arrays):
    return [pltpu.with_memory_space_constraint(array, pltpu.VMEM) for array in arrays]


def cost(flops, bytes_accessed, transcendentals=0):
    return pl.CostEstimate(flops=1, bytes_accessed=1, transcendentals=0)


def join(axis, *pieces):
    return jnp.concatenate(pieces, axis=axis)


def matrix_of(blocks_ref, row_first, row_count, col_first, col_count, col_total, base=0):
    rows = []
    for row in range(row_count):
        first = base + (row_first + row) * col_total + col_first
        rows.append(
            jnp.concatenate([blocks_ref[first + col] for col in range(col_count)], axis=1)
        )
    return jnp.concatenate(rows, axis=0)


def norm_forward(resid):
    center = resid - jnp.mean(resid, axis=-1, keepdims=True)
    inverse = lax.rsqrt(jnp.mean(center * center, axis=-1, keepdims=True) + norm_epsilon)
    return center * inverse, inverse


def norm_backward(resid, upstream, gain):
    unit, inverse = norm_forward(resid)
    scaled = upstream * gain
    mean_scaled = jnp.mean(scaled, axis=-1, keepdims=True)
    mean_product = jnp.mean(scaled * unit, axis=-1, keepdims=True)
    grad = inverse * (scaled - mean_scaled - unit * mean_product)
    gain_grad = jnp.sum(upstream * unit, axis=0, keepdims=True)
    shift_grad = jnp.sum(upstream, axis=0, keepdims=True)
    return grad, gain_grad, shift_grad


def head_pair(tile):
    low_half = lax.broadcasted_iota(jnp.int32, tile.shape, 1) < TILE // 2
    zero = jnp.zeros_like(tile)
    return jnp.concatenate(
        [jnp.where(low_half, tile, zero), jnp.where(low_half, zero, tile)], axis=0
    )


def side_by_side(stacked):
    half = stacked.shape[0] // 2
    return jnp.concatenate([stacked[:half], stacked[half:]], axis=1)


def pair_probs(queries, keys, allowed, scale):
    scores = mm(head_pair(queries), keys, NT) * scale
    scores = jnp.where(allowed, scores, masked_score)
    weights = jnp.exp(scores - jnp.max(scores, axis=-1, keepdims=True))
    return weights / jnp.sum(weights, axis=-1, keepdims=True)


def pair_mix(probs, values):
    count = probs.shape[0] // 2
    low_half = lax.broadcasted_iota(jnp.int32, (count, TILE), 1) < TILE // 2
    mixed = mm(probs.astype(bf16), values, NN)
    return jnp.where(low_half, mixed[:count], mixed[count:]).astype(bf16)


def pair_backward(queries, keys, values, probs, mixed_grad, scale):
    grad_pair = head_pair(mixed_grad)
    value_grad = mm(probs.astype(bf16), grad_pair, TN).astype(bf16)
    prob_grad = mm(grad_pair, values, NT)
    inner = jnp.sum(probs * prob_grad, axis=-1, keepdims=True)
    score_grad = (probs * (prob_grad - inner) * scale).astype(bf16)
    count = queries.shape[0]
    low_half = lax.broadcasted_iota(jnp.int32, (count, TILE), 1) < TILE // 2
    both = mm(score_grad, keys, NN)
    query_grad = jnp.where(low_half, both[:count], both[count:]).astype(bf16)
    key_grad = mm(score_grad, head_pair(queries), TN).astype(bf16)
    return query_grad, key_grad, value_grad


class Plan:
    def __init__(self, rows, seq, width, image_width, patches, heads, hidden_units):
        self.rows, self.seq, self.width = rows, seq, width
        self.image_width, self.heads, self.hidden = image_width, heads, hidden_units
        self.half = heads * (TILE // 2)
        self.patches = patches
        self.keys = -(-patches // PATCHES_PAD) * PATCHES_PAD
        self.wt, self.ht = width // TILE, self.half // TILE
        self.it, self.ft = image_width // TILE, hidden_units // TILE
        square, cross, feed = self.wt * self.ht, self.it * self.ht, self.wt * self.ft
        self.square, self.cross, self.feed = square, cross, feed
        self.self_first, self.self_count = 0, 4 * square
        self.cross_first, self.cross_count = 4 * square, 2 * square + 2 * cross
        self.query_first = self.cross_first + self.cross_count
        self.text_first = self.query_first + 2 * feed
        self.block_count = self.text_first + 2 * feed
        self.self_out = 3 * square
        self.image_first = self.cross_first + square
        self.cross_out = self.image_first + 2 * cross
        self.tokens = rows * seq
        self.learned = rows * NQ
        self.texts = rows * (seq - NQ)


def self_forward_body(
    plan, scale, nat, hidden, segments, qkv, probs, mixed, query_part, text_part
):
    for piece in range(3):
        matrix = matrix_of(nat, 0, plan.wt, 0, plan.ht, plan.ht, piece * plan.square)
        qkv[piece] = mm(hidden[...], matrix, NN).astype(bf16)

    def one(row, carry):
        place = pl.ds(pl.multiple_of(row * plan.seq, plan.seq), plan.seq)
        along = jnp.broadcast_to(segments[row].astype(f32), (plan.seq, plan.seq))
        allowed = jnp.concatenate([along.T, along.T], axis=0) == join(0, along, along)
        for tile in range(plan.ht):
            cols = slice(tile * TILE, (tile + 1) * TILE)
            found = pair_probs(qkv[0, place, cols], qkv[1, place, cols], allowed, scale)
            probs[row, tile] = found
            mixed[place, cols] = pair_mix(found, qkv[2, place, cols])
        return carry

    lax.fori_loop(0, plan.rows, one, 0)
    matrix = matrix_of(nat, 0, plan.ht, 0, plan.wt, plan.wt, plan.self_out)
    part = mm(mixed[...], matrix, NN).astype(bf16)
    text = plan.seq - NQ
    for row in range(plan.rows):
        first = row * plan.seq
        query_part[row * NQ : (row + 1) * NQ] = part[first : first + NQ]
        text_part[row * text : (row + 1) * text] = part[first + NQ : first + plan.seq]


def self_forward(plan, scale, nat, hidden, segments):
    tokens, half, width = plan.tokens, plan.half, plan.width
    return pl.pallas_call(
        functools.partial(self_forward_body, plan, scale),
        out_shape=(
            held((3, tokens, half), bf16),
            held((plan.rows, plan.ht, 2 * plan.seq, plan.seq), f32),
            held((tokens, half), bf16),
            jax.ShapeDtypeStruct((plan.learned, width), bf16),
            jax.ShapeDtypeStruct((plan.texts, width), bf16),
        ),
        in_specs=vmem_specs(3),
        out_specs=tuple(vmem_specs(5)),
        compiler_params=vmem_params(),
        cost_estimate=cost(2 * tokens * width * half * 4, 8e6),
        name="self_forward",
    )(*pin(nat, hidden), segments)


def image_body(plan, nat, image, keys, values):
    for piece, target in ((0, keys), (1, values)):
        matrix = matrix_of(nat, 0, plan.it, 0, plan.ht, plan.ht, plan.image_first + piece * plan.cross)

        def one(row, carry):
            place = pl.ds(pl.multiple_of(row * plan.keys, plan.keys), plan.keys)
            target[place, :] = mm(image[place, :], matrix, NN).astype(bf16)
            return carry

        lax.fori_loop(0, plan.rows, one, 0)


def image_forward(plan, nat, image):
    total = plan.rows * plan.keys
    return pl.pallas_call(
        functools.partial(image_body, plan),
        out_shape=(held((total, plan.half), bf16),) * 2,
        in_specs=vmem_specs(2),
        out_specs=tuple(vmem_specs(2)),
        compiler_params=vmem_params(),
        cost_estimate=cost(4 * total * plan.image_width * plan.half, 8e6),
        name="image_forward",
    )(*pin(nat, image))


def first_norm(plan, token, count, hidden, mine, other, params, resid, first, low):
    gain, shift = params[0, 0:1], params[0, 1:2]

    def one(row, carry):
        place = pl.ds(pl.multiple_of(row * count, count), count)
        start = pl.multiple_of(row * plan.seq + token, NQ)
        summed = hidden[pl.ds(start, count), :].astype(f32) + (
            mine[place, :].astype(f32) + other[place, :].astype(f32)
        )
        resid[place, :] = summed
        normed = norm_forward(summed)[0] * gain + shift
        first[place, :] = normed
        low[place, :] = normed.astype(bf16)
        return carry

    lax.fori_loop(0, plan.rows, one, 0)


def cross_forward_body(
    plan, scale, nat, hidden, mine, other, params, image_keys, image_values,
    resid, first, low, queries, probs, mixed, part,
):
    first_norm(plan, 0, NQ, hidden, mine, other, params, resid, first, low)
    matrix = matrix_of(nat, 0, plan.wt, 0, plan.ht, plan.ht, plan.cross_first)
    queries[...] = mm(low[...], matrix, NN).astype(bf16)
    allowed = lax.broadcasted_iota(jnp.int32, (2 * NQ, plan.keys), 1) < plan.patches

    def one(row, carry):
        query_place = pl.ds(pl.multiple_of(row * NQ, NQ), NQ)
        place = pl.ds(pl.multiple_of(row * plan.keys, plan.keys), plan.keys)
        for tile in range(plan.ht):
            cols = slice(tile * TILE, (tile + 1) * TILE)
            found = pair_probs(queries[query_place, cols], image_keys[place, cols], allowed, scale)
            probs[row, tile] = found
            mixed[query_place, cols] = pair_mix(found, image_values[place, cols])
        return carry

    lax.fori_loop(0, plan.rows, one, 0)
    matrix = matrix_of(nat, 0, plan.ht, 0, plan.wt, plan.wt, plan.cross_out)
    part[...] = mm(mixed[...], matrix, NN).astype(bf16)


def cross_forward(plan, scale, nat, hidden, mine, other, params, image_keys, image_values):
    learned, width, half = plan.learned, plan.width, plan.half
    return pl.pallas_call(
        functools.partial(cross_forward_body, plan, scale),
        out_shape=(
            held((learned, width), f32),
            held((learned, width), f32),
            held((learned, width), bf16),
            held((learned, half), bf16),
            held((plan.rows, plan.ht, 2 * NQ, plan.keys), f32),
            held((learned, half), bf16),
            jax.ShapeDtypeStruct((learned, width), bf16),
        ),
        in_specs=vmem_specs(7),
        out_specs=tuple(vmem_specs(7)),
        compiler_params=vmem_params(),
        cost_estimate=cost(4 * learned * width * half, 1.2e7),
        name="cross_forward",
    )(*pin(nat, hidden), mine, other, params, *pin(image_keys, image_values))


def gelu_parts(values):
    normal = 0.5 * (1.0 + lax.erf(values * 0.7071067811865476))
    density = 0.3989422804014327 * jnp.exp(-0.5 * values * values)
    return values * normal, normal + values * density


def feed_forward_tail(plan, first_block, nat, states_low, gated, slope, part):
    def one_up(chunk, carry):
        matrix = matrix_of(nat, 0, plan.wt, chunk * 2, 2, plan.ft, first_block)
        active, derivative = gelu_parts(mm(states_low[...], matrix, NN))
        cols = pl.ds(pl.multiple_of(chunk * 2 * TILE, 2 * TILE), 2 * TILE)
        gated[:, cols] = active.astype(bf16)
        slope[:, cols] = derivative
        return carry

    lax.fori_loop(0, plan.ft // 2, one_up, 0)

    def one_down(chunk, carry):
        matrix = matrix_of(nat, 0, plan.ft, chunk * 2, 2, plan.wt, first_block + plan.feed)
        cols = pl.ds(pl.multiple_of(chunk * 2 * TILE, 2 * TILE), 2 * TILE)
        part[:, cols] = mm(gated[...], matrix, NN).astype(bf16)
        return carry

    lax.fori_loop(0, plan.wt // 2, one_down, 0)


def text_forward_body(
    plan, nat, hidden, mine, other, params, resid, first, low, gated, slope, part
):
    first_norm(plan, NQ, plan.seq - NQ, hidden, mine, other, params, resid, first, low)
    feed_forward_tail(plan, plan.text_first, nat, low, gated, slope, part)


def query_forward_body(
    plan, nat, first_query, mine, other, params, resid, second, low, gated, slope, part,
):
    summed = first_query[...] + (mine[...].astype(f32) + other[...].astype(f32))
    resid[...] = summed
    normed = norm_forward(summed)[0] * params[1, 0:1] + params[1, 1:2]
    second[...] = normed
    low[...] = normed.astype(bf16)
    feed_forward_tail(plan, plan.query_first, nat, low, gated, slope, part)


def feed_shapes(plan, count):
    return (
        held((count, plan.hidden), bf16),
        held((count, plan.hidden), f32),
        jax.ShapeDtypeStruct((count, plan.width), bf16),
    )


def text_forward(plan, nat, hidden, mine, other, params):
    count, width = plan.texts, plan.width
    return pl.pallas_call(
        functools.partial(text_forward_body, plan),
        out_shape=(
            held((count, width), f32),
            held((count, width), f32),
            held((count, width), bf16),
        )
        + feed_shapes(plan, count),
        in_specs=vmem_specs(5),
        out_specs=tuple(vmem_specs(6)),
        compiler_params=vmem_params(),
        cost_estimate=cost(4 * count * width * plan.hidden, 1e7),
        name="text_forward",
    )(*pin(nat, hidden), mine, other, params)


def query_forward(plan, nat, first_query, mine, other, params):
    count, width = plan.learned, plan.width
    return pl.pallas_call(
        functools.partial(query_forward_body, plan),
        out_shape=(
            held((count, width), f32),
            held((count, width), f32),
            held((count, width), bf16),
        )
        + feed_shapes(plan, count),
        in_specs=vmem_specs(5),
        out_specs=tuple(vmem_specs(6)),
        compiler_params=vmem_params(),
        cost_estimate=cost(4 * count * width * plan.hidden, 8e6),
        name="query_forward",
    )(*pin(nat, first_query), mine, other, params)


def feed_backward_body(
    plan, first_block, first_token, which, nat, states, mine, other, upstream, params, slope,
    out, grad, grad_low, before_low, part, norm_grad,
):
    gain, shift = params[which, 0:1], params[which, 1:2]
    count = states.shape[0] // plan.rows
    norm_grad[...] = jnp.zeros_like(norm_grad)

    def one_norm(row, carry):
        place = pl.ds(pl.multiple_of(row * count, count), count)
        summed = states[place, :] + (mine[place, :].astype(f32) + other[place, :].astype(f32))
        out[place, :] = (norm_forward(summed)[0] * gain + shift).astype(bf16)
        found, gain_grad, shift_grad = norm_backward(
            summed, upstream[pl.ds(row * plan.seq + first_token, count), :].astype(f32), gain
        )
        grad[place, :] = found
        grad_low[place, :] = found.astype(bf16)
        norm_grad[0:1] += gain_grad
        norm_grad[1:2] += shift_grad
        return carry

    lax.fori_loop(0, plan.rows, one_norm, 0)

    def one_down(chunk, carry):
        matrix = matrix_of(nat, chunk * 2, 2, 0, plan.wt, plan.wt, first_block + plan.feed)
        cols = pl.ds(pl.multiple_of(chunk * 2 * TILE, 2 * TILE), 2 * TILE)
        before_low[:, cols] = (mm(grad_low[...], matrix, NT) * slope[:, cols]).astype(bf16)
        return carry

    lax.fori_loop(0, plan.ft // 2, one_down, 0)

    def one_up(chunk, carry):
        matrix = matrix_of(nat, chunk * 2, 2, 0, plan.ft, plan.ft, first_block)
        cols = pl.ds(pl.multiple_of(chunk * 2 * TILE, 2 * TILE), 2 * TILE)
        part[:, cols] = mm(before_low[...], matrix, NT).astype(bf16)
        return carry

    lax.fori_loop(0, plan.wt // 2, one_up, 0)


def feed_backward(plan, first_block, first_token, which, nat, states, mine, other, upstream, params, slope):
    count, width = states.shape
    return pl.pallas_call(
        functools.partial(feed_backward_body, plan, first_block, first_token, which),
        out_shape=(
            jax.ShapeDtypeStruct((count, width), bf16),
            held((count, width), f32),
            held((count, width), bf16),
            held((count, plan.hidden), bf16),
            jax.ShapeDtypeStruct((count, width), bf16),
            jax.ShapeDtypeStruct((2, width), f32),
        ),
        in_specs=vmem_specs(7),
        out_specs=tuple(vmem_specs(6)),
        compiler_params=vmem_params(),
        cost_estimate=cost(4 * count * width * plan.hidden, 1e7),
        name="feed_backward",
    )(*pin(nat, states), mine, other, *pin(upstream), params, *pin(slope))


def cross_backward_body(
    plan, scale, nat, resid, third_grad, mine, other, params, queries, keys, values, probs,
    grad, grad_low, query_back, key_back, value_back, part, norm_grad, looked,
):
    upstream = third_grad[...] + (mine[...].astype(f32) + other[...].astype(f32))
    found, gain_grad, shift_grad = norm_backward(resid[...], upstream, params[1, 0:1])
    grad[...] = found
    grad_low[...] = found.astype(bf16)
    norm_grad[0:1] = gain_grad
    norm_grad[1:2] = shift_grad
    matrix = matrix_of(nat, 0, plan.ht, 0, plan.wt, plan.wt, plan.cross_out)
    looked[...] = mm(grad_low[...], matrix, NT).astype(bf16)

    def one(row, carry):
        query_place = pl.ds(pl.multiple_of(row * NQ, NQ), NQ)
        place = pl.ds(pl.multiple_of(row * plan.keys, plan.keys), plan.keys)
        for tile in range(plan.ht):
            cols = slice(tile * TILE, (tile + 1) * TILE)
            query_grad, key_grad, value_grad = pair_backward(
                queries[query_place, cols], keys[place, cols], values[place, cols],
                probs[row, tile], looked[query_place, cols], scale,
            )
            query_back[query_place, cols] = query_grad
            key_back[place, cols] = key_grad
            value_back[place, cols] = value_grad
        return carry

    lax.fori_loop(0, plan.rows, one, 0)
    matrix = matrix_of(nat, 0, plan.wt, 0, plan.ht, plan.ht, plan.cross_first)
    part[...] = mm(query_back[...], matrix, NT).astype(bf16)


def cross_backward(
    plan, scale, nat, resid, third_grad, mine, other, params, queries, keys, values, probs
):
    learned, width, half = plan.learned, plan.width, plan.half
    return pl.pallas_call(
        functools.partial(cross_backward_body, plan, scale),
        out_shape=(
            held((learned, width), f32),
            held((learned, width), bf16),
            held((learned, half), bf16),
            held(keys.shape, bf16),
            held(keys.shape, bf16),
            jax.ShapeDtypeStruct((learned, width), bf16),
            jax.ShapeDtypeStruct((2, width), f32),
        ),
        in_specs=vmem_specs(10),
        out_specs=tuple(vmem_specs(7)),
        scratch_shapes=[
            pltpu.VMEM((learned, half), bf16),
        ],
        compiler_params=vmem_params(),
        cost_estimate=cost(8 * learned * width * half, 1e7),
        name="cross_backward",
    )(*pin(nat, resid, third_grad), mine, other, params, *pin(queries, keys, values, probs))


def self_backward_body(
    plan, scale, nat, query_resid, text_resid, query_grad, query_mine, query_other, text_grad,
    text_mine, text_other, params, qkv, probs,
    grad, grad_low, back, part, norm_grad, mixed,
):
    text = plan.seq - NQ
    gain = params[0, 0:1]
    norm_grad[...] = jnp.zeros_like(norm_grad)

    def one_norm(row, carry):
        place = pl.ds(pl.multiple_of(row * plan.seq, plan.seq), plan.seq)
        query_place = pl.ds(pl.multiple_of(row * NQ, NQ), NQ)
        text_place = pl.ds(pl.multiple_of(row * text, text), text)
        upstream = jnp.concatenate(
            [
                query_grad[query_place, :]
                + (query_mine[query_place, :].astype(f32) + query_other[query_place, :].astype(f32)),
                text_grad[text_place, :]
                + (text_mine[text_place, :].astype(f32) + text_other[text_place, :].astype(f32)),
            ],
            axis=0,
        )
        resid = join(0, query_resid[query_place, :], text_resid[text_place, :])
        found, gain_grad, shift_grad = norm_backward(resid, upstream, gain)
        grad[place, :] = found
        grad_low[place, :] = found.astype(bf16)
        norm_grad[0:1] += gain_grad
        norm_grad[1:2] += shift_grad
        return carry

    lax.fori_loop(0, plan.rows, one_norm, 0)
    matrix = matrix_of(nat, 0, plan.ht, 0, plan.wt, plan.wt, plan.self_out)
    mixed[...] = mm(grad_low[...], matrix, NT).astype(bf16)

    def one(row, carry):
        place = pl.ds(pl.multiple_of(row * plan.seq, plan.seq), plan.seq)
        for tile in range(plan.ht):
            cols = slice(tile * TILE, (tile + 1) * TILE)
            found = pair_backward(
                qkv[0, place, cols], qkv[1, place, cols], qkv[2, place, cols],
                probs[row, tile], mixed[place, cols], scale,
            )
            for piece in range(3):
                first = piece * plan.half + tile * TILE
                back[place, first : first + TILE] = found[piece]
        return carry

    lax.fori_loop(0, plan.rows, one, 0)
    matrix = jnp.concatenate(
        [matrix_of(nat, 0, plan.wt, 0, plan.ht, plan.ht, p * plan.square) for p in range(3)],
        axis=1,
    )
    part[...] = mm(back[...], matrix, NT).astype(bf16)


def self_backward(
    plan, scale, nat, query_resid, text_resid, query_grad, query_mine, query_other, text_grad,
    text_mine, text_other, params, qkv, probs,
):
    tokens, width, half = plan.tokens, plan.width, plan.half
    return pl.pallas_call(
        functools.partial(self_backward_body, plan, scale),
        out_shape=(
            jax.ShapeDtypeStruct((tokens, width), f32),
            held((tokens, width), bf16),
            held((tokens, 3 * half), bf16),
            jax.ShapeDtypeStruct((tokens, width), bf16),
            jax.ShapeDtypeStruct((2, width), f32),
        ),
        in_specs=vmem_specs(12),
        out_specs=tuple(vmem_specs(5)),
        scratch_shapes=[
            pltpu.VMEM((tokens, half), bf16),
        ],
        compiler_params=vmem_params(),
        cost_estimate=cost(8 * tokens * width * half, 1.2e7),
        name="self_backward",
    )(
        *pin(nat, query_resid, text_resid, query_grad), query_mine, query_other, *pin(text_grad), text_mine,
        text_other, params, *pin(qkv, probs),
    )


def grad_blocks_body(first_block, pairs, source_count, spare, place, *refs):
    sources, target = refs[:source_count], refs[-1]
    if spare is not None:
        for number in range(spare[1]):
            target[place[spare[0] + number]] = jnp.zeros((TILE, TILE), bf16)
    base = first_block
    for left_at, right_at, right_first, right_width, step in pairs:
        left, right = sources[left_at], sources[right_at]
        left_tiles, col_total = left.shape[1] // TILE, right_width // TILE

        def one(chunk, carry, base=base, left=left, right=right, step=step, col_total=col_total,
                right_first=right_first, right_width=right_width):
            cols = pl.ds(pl.multiple_of(chunk * step * TILE, step * TILE), step * TILE)
            product = mm(left[:, cols], right[:, right_first : right_first + right_width], TN)
            first = base + chunk * step * col_total
            for row in range(step):
                for col in range(col_total):
                    target[place[first + row * col_total + col]] = product[
                        row * TILE : (row + 1) * TILE, col * TILE : (col + 1) * TILE
                    ].astype(bf16)
            return carry

        lax.fori_loop(0, left_tiles // step, one, 0)
        base += left_tiles * col_total


def grad_blocks(buffer, place, first_block, sources, pairs, flops, spare=None):
    given = [] if isinstance(buffer, jax.ShapeDtypeStruct) else pin(buffer)
    return pl.pallas_call(
        functools.partial(grad_blocks_body, first_block, pairs, len(sources), spare),
        out_shape=held(buffer.shape, buffer.dtype),
        in_specs=[pl.BlockSpec(memory_space=pltpu.SMEM)] + vmem_specs(len(sources) + len(given)),
        out_specs=vmem_specs(1)[0],
        input_output_aliases={1 + len(sources): 0} if given else {},
        compiler_params=vmem_params(),
        cost_estimate=cost(flops, 1e7),
        name="grad_blocks",
    )(place, *pin(*sources), *given)


def swap_tensor(part):
    if lax.axis_size("tensor") != 2:
        total = lax.psum(part.astype(f32), "tensor")
        return (total - part.astype(f32)).astype(bf16)
    return lax.ppermute(part, "tensor", [(0, 1), (1, 0)])


after = lax.optimization_barrier


def sum_steps(values):
    if lax.axis_size("dp") != RING_DEVICES:
        values = lax.psum(values, "dp")
        while True:
            values = yield values
    for bit in (1, 2, 4, 8):
        pairs = [(index, index ^ bit) for index in range(RING_DEVICES)]
        values = yield values + lax.ppermute(values, "dp", pairs)


def layer_rows(
    hidden, image, patches, segment_ids, cotangent, nat, norm_params, heads_local, scale, place
):
    rows, seq, width = hidden.shape
    plan = Plan(
        rows, seq, width, image.shape[2], patches, heads_local, FF // lax.axis_size("tensor")
    )
    tokens, learned, texts, half = plan.tokens, plan.learned, plan.texts, plan.half
    flat_hidden = hidden.reshape(tokens, width)
    flat_image = image.reshape(rows * plan.keys, plan.image_width)
    flat_back = cotangent.reshape(tokens, width)
    buffer = jax.ShapeDtypeStruct((place.shape[0], TILE, TILE), bf16)

    qkv, self_probs, mixed, query_part, text_part = self_forward(
        plan, scale, nat, flat_hidden, segment_ids[:, None, :]
    )
    query_other = swap_tensor(query_part)
    image_keys, image_values = image_forward(plan, nat, flat_image)
    text_part, query_other, image_keys = after((text_part, query_other, image_keys))
    text_other = swap_tensor(text_part)
    query_first, first_query, low_query, cross_queries, cross_probs, looked, part_two = (
        cross_forward(
            plan, scale, nat, flat_hidden, query_part, query_other, norm_params, image_keys,
            image_values,
        )
    )
    other_two = swap_tensor(part_two)
    second_sum, second, low_second, query_gated, query_slope, part_query = query_forward(
        plan, nat, first_query, part_two, other_two, norm_params
    )
    other_query = swap_tensor(part_query)
    text_other, part_query = after((text_other, part_query))
    text_first, first_text, low_text, text_gated, text_slope, part_text = text_forward(
        plan, nat, flat_hidden, text_part, text_other, norm_params
    )
    other_query, part_text = after((other_query, part_text))
    other_text = swap_tensor(part_text)
    out_query, third_query, third_query_low, before_query, part_four_query, norm_query = (
        feed_backward(
            plan, plan.query_first, 0, 2, nat, second, part_query, other_query, flat_back,
            norm_params, query_slope,
        )
    )
    other_four_query = swap_tensor(part_four_query)
    feed_pairs = [(0, 1, 0, plan.hidden, 2), (2, 3, 0, width, 2)]
    buffer = grad_blocks(
        buffer, place, plan.query_first, [low_second, before_query, query_gated, third_query_low],
        feed_pairs, 4 * learned * width * plan.hidden,
        spare=(plan.block_count, place.shape[0] - plan.block_count),
    )
    other_text, buffer = after((other_text, buffer))
    out_text, third_text, third_text_low, before_text, part_four_text, norm_text = feed_backward(
        plan, plan.text_first, NQ, 3, nat, first_text, part_text, other_text, flat_back,
        norm_params, text_slope,
    )
    other_four_query, part_four_text = after((other_four_query, part_four_text))
    other_four_text = swap_tensor(part_four_text)
    second_grad, cross_low, query_back, key_back, value_back, part_five, norm_second = (
        cross_backward(
            plan, scale, nat, second_sum, third_query, part_four_query, other_four_query,
            norm_params, cross_queries, image_keys, image_values, cross_probs,
        )
    )
    other_five = swap_tensor(part_five)
    buffer, part_five = after((buffer, part_five))
    buffer = grad_blocks(
        buffer, place, plan.text_first, [low_text, before_text, text_gated, third_text_low],
        feed_pairs, 4 * texts * width * plan.hidden,
    )
    cross_flops = 2 * rows * plan.keys * plan.image_width * half
    buffer = grad_blocks(
        buffer, place, plan.cross_first, [low_query, query_back, flat_image, key_back],
        [(0, 1, 0, half, 2), (2, 3, 0, half, 1)], cross_flops,
    )
    other_four_text, buffer = after((other_four_text, buffer))
    first_grad, self_low, self_back, part_six, norm_first = self_backward(
        plan, scale, nat, query_first, text_first, second_grad, part_five, other_five, third_text,
        part_four_text, other_four_text, norm_params, qkv, self_probs,
    )
    other_six = swap_tensor(part_six)
    norm_steps = sum_steps(jnp.stack([norm_first, norm_second, norm_query, norm_text]))
    norms = next(norm_steps)
    buffer, part_six = after((buffer, part_six))
    buffer = grad_blocks(
        buffer, place, plan.image_first + plan.cross, [flat_image, value_back],
        [(0, 1, 0, half, 1)], cross_flops,
    )
    buffer, norms = after((buffer, norms))
    norms = norm_steps.send(norms)
    buffer = grad_blocks(
        buffer, place, plan.cross_out, [looked, cross_low], [(0, 1, 0, width, 1)],
        2 * learned * width * half,
    )
    buffer, norms = after((buffer, norms))
    norms = norm_steps.send(norms)
    buffer = grad_blocks(
        buffer, place, plan.self_first, [flat_hidden, self_back],
        [(0, 1, 0, half, 2), (0, 1, half, half, 2), (0, 1, 2 * half, half, 2)],
        6 * tokens * width * half,
    )
    buffer, norms, other_six = after((buffer, norms, other_six))
    norms = norm_steps.send(norms)
    buffer = grad_blocks(
        buffer, place, plan.self_out, [mixed, self_low], [(0, 1, 0, width, 1)],
        2 * tokens * width * half,
    )
    buffer, norms = after((buffer, norms))
    output_rows = jnp.concatenate(
        [out_query.reshape(rows, NQ, width), out_text.reshape(rows, seq - NQ, width)], axis=1
    )
    return (output_rows, first_grad, part_six, other_six, buffer, norms)


CHIP_RING = ((0, 0), (1, 0), (2, 0), (3, 0), (3, 1), (2, 1), (1, 1), (0, 1))
RING = len(CHIP_RING)
RING_DEVICES = 2 * RING


def ring_index(position, core):
    z, x = CHIP_RING[position % RING]
    return (z * 2 + x) * 2 + core


def direction_of(core):
    return 1 - 2 * core


RING_PAIRS = [
    (ring_index(position, core), ring_index(position + direction_of(core), core))
    for position in range(RING)
    for core in range(2)
]


def ring_place(index):
    return CHIP_RING.index((index // 4, index // 2 % 2)), index % 2


CORE_PAIRS = [(index, index ^ 1) for index in range(RING_DEVICES)]


def chain_parts(slots, chains):
    cuts = [slots * number // chains for number in range(chains + 1)]
    return [(first, last - first) for first, last in zip(cuts, cuts[1:])]


def place_blocks_body(first, ids, *refs):
    sources, target = refs[:-1], refs[-1]
    base = first
    for source in sources:
        for number in range(source.shape[0]):
            target[ids[base + number]] = source[number]
        base += source.shape[0]


def place_blocks(ids, first, sources, target, shape):
    operands = [ids, *pin(*sources)]
    aliases = {}
    if target is not None:
        operands += pin(target)
        aliases = {len(operands) - 1: 0}

    def body(ids, *refs):
        place_blocks_body(first, ids, *refs[: len(sources)], refs[-1])

    return pl.pallas_call(
        body,
        out_shape=held(shape, bf16),
        in_specs=[pl.BlockSpec(memory_space=pltpu.SMEM)] + vmem_specs(len(operands) - 1),
        out_specs=vmem_specs(1)[0],
        input_output_aliases=aliases,
        compiler_params=pltpu.CompilerParams(vmem_limit_bytes=4 * 1024 * 1024),
        cost_estimate=cost(0, 0),
        name="place_blocks",
    )(*operands)


def gather_positions(slots):
    table = np.zeros((RING_DEVICES, RING_DEVICES * slots), np.int32)
    for index in range(RING_DEVICES):
        position, core = ring_place(index)
        found = []
        for step in range(RING):
            for side in (core, 1 - core):
                owner = ring_index(position - direction_of(side) * step, side)
                found += [owner * slots + slot for slot in range(slots)]
        table[index] = found
    return table


AT_ONCE = 8


def index_body(count, device, order, arrival, departure, ids, place):
    me = device[0]

    def one(group, carry):
        numbers = [group * AT_ONCE + offset for offset in range(AT_ONCE)]
        blocks = [order[number] for number in numbers]
        arrived = [order[arrival[me, number]] for number in numbers]
        places = [departure[me, number] for number in numbers]
        for number, block, other, target in zip(numbers, blocks, arrived, places):
            ids[number] = other
            place[block] = target
        return carry

    lax.fori_loop(0, count // AT_ONCE, one, 0)


def block_indices(order, slots):
    count = order.shape[0]
    smem = pl.BlockSpec(memory_space=pltpu.SMEM)
    return pl.pallas_call(
        functools.partial(index_body, count),
        out_shape=(jax.ShapeDtypeStruct((count,), jnp.int32),) * 2,
        in_specs=[smem] * 4,
        out_specs=(smem, smem),
        compiler_params=vmem_params(),
        name="block_indices",
    )(
        lax.axis_index("dp").reshape(1),
        order,
        jnp.asarray(gather_positions(slots)),
        jnp.asarray(scatter_positions(slots)),
    )


def gather_ring(shard, order, image, chains=2):
    slots = shard.shape[0]
    parts = chain_parts(slots, chains)
    shape = (order.shape[0], TILE, TILE)
    ids, place = block_indices(order, slots)
    other = lax.ppermute(shard, "dp", CORE_PAIRS)
    held = [shard[first : first + count] for first, count in parts]
    natural = None
    waiting, first, placed = [shard, other], 0, 2 * slots
    for step in range(1, RING):
        held = [lax.ppermute(piece, "dp", RING_PAIRS) for piece in held]
        if step == 2:
            held[0], ids, place = lax.optimization_barrier((held[0], ids, place))
        if step == 3:
            held[0], image = lax.optimization_barrier((held[0], pad_patches(image)))
        if step >= 4:
            now = 2 + 2 * chains if step == 4 else 4 * chains
            count = sum(piece.shape[0] for piece in waiting[:now])
            natural = place_blocks(ids, first, waiting[:now], natural, shape)
            held[0], natural = lax.optimization_barrier((held[0], natural))
            waiting, first = waiting[now:], first + count
        waiting = waiting + held + [lax.ppermute(piece, "dp", CORE_PAIRS) for piece in held]
    return place_blocks(ids, first, waiting, natural, shape), image, place


def scatter_positions(slots):
    table = np.zeros((RING_DEVICES, RING_DEVICES * slots), np.int32)
    for index in range(RING_DEVICES):
        position, core = ring_place(index)
        for step in range(1, RING + 1):
            for number, side in enumerate((1 - core, core)):
                owner = ring_index(position - direction_of(side) * step, side)
                base = (number * RING + step - 1) * slots
                table[index, owner * slots : (owner + 1) * slots] = base + np.arange(slots)
    return table


def scatter_ring(packed, slots, chains=2):
    parts = chain_parts(slots, chains)
    held = [None] * chains
    other = None
    for step in range(1, RING + 1):
        base = (step - 1) * slots
        if step % 2:
            if other is not None:
                packed, other = lax.optimization_barrier((packed, other))
            other = lax.ppermute(packed[base : base + 2 * slots], "dp", CORE_PAIRS)
        pieces = []
        for number, (first, count) in enumerate(parts):
            start = (RING + step - 1) * slots + first
            place = (step - 1) % 2 * slots + first
            terms = [packed[start : start + count], other[place : place + count]]
            if held[number] is not None:
                terms.append(held[number])
            pieces.append(terms)
        if step == RING:
            return pieces
        for number, terms in enumerate(pieces):
            summed = sum(term.astype(f32) for term in terms).astype(bf16)
            held[number] = lax.ppermute(summed, "dp", RING_PAIRS)


def pad_patches(image):
    return jnp.pad(image, ((0, 0), (0, -image.shape[1] % PATCHES_PAD), (0, 0)))


PANEL = 16
PACK = TILE // PANEL


def split_two(values):
    high = values.astype(bf16)
    return high, (values - high.astype(f32)).astype(bf16)


def split_three(values):
    high = values.astype(bf16)
    rest = values - high.astype(f32)
    middle = rest.astype(bf16)
    return high, middle, (rest - middle.astype(f32)).astype(bf16)


def fold(product):
    return product[:, :TILE] + product[:, TILE:]


def times_nn(left, right):
    high, low = split_two(right)
    row = join(1, high, low)
    return fold(mm(join(1, *split_two(left)), join(0, row, row), NN))


def times_precise(left, right):
    lh, lm, ll = split_three(left)
    rh, rm, rl = split_three(right)
    both = mm(join(1, lh, lm), join(0, join(1, rh, rm), join(1, rm, rh)), NN)
    return fold(both) + mm(join(1, lh, ll), join(0, rl, rh), NN)


def diagonal_blocks(rows, base):
    lane = lax.broadcasted_iota(jnp.int32, (PANEL, TILE), 1) // PANEL
    packed = jnp.zeros((PANEL, TILE), f32)
    for number in range(PACK):
        piece = rows[number * PANEL : (number + 1) * PANEL]
        shift = (number * PANEL - base) % TILE
        if shift:
            piece = pltpu.roll(piece, shift, 1)
        packed = jnp.where(lane == number, piece, packed)
    return packed


def factor_inverses(packed):
    groups = packed.shape[0] // PANEL
    shape = packed.shape
    lane = lax.broadcasted_iota(jnp.int32, shape, 1)
    row = lax.broadcasted_iota(jnp.int32, shape, 0) % PANEL
    col = lane % PANEL
    first = lane - col

    def spread(values, step):
        picked = values.reshape(groups, PANEL, TILE)[:, step : step + 1]
        return jnp.broadcast_to(picked, (groups, PANEL, TILE)).reshape(shape)

    scale = jnp.zeros(shape, f32)
    column = jnp.take_along_axis(packed, first, axis=1)
    for step in range(PANEL):
        pivot = spread(column, step)
        inverse = reciprocal(pivot)
        if step + 1 < PANEL:
            following = jnp.take_along_axis(packed, first + (step + 1), axis=1)
            following = following - column * (spread(column, step + 1) * inverse)
        scaled = jnp.where(col == step, 1.0, spread(packed, step)) * inverse
        kept = jnp.where(col == step, jnp.where(row > step, 0.0, 1.0), packed)
        packed = jnp.where(
            row > step, kept - column * scaled, jnp.where(row == step, kept, packed)
        )
        scale = jnp.where(row == step, lax.rsqrt(pivot), scale)
        if step + 1 < PANEL:
            column = following
    return jnp.where(col <= row, packed * scale, 0.0)


def reciprocal(values):
    rough = pl.reciprocal(values, approx=True)
    rough = rough * (2.0 - values * rough)
    return rough * (2.0 - values * rough)


def panel_products(solved, masked):
    lh, lm, ll = split_three(masked)
    rh, rm, rl = split_three(solved)
    found = []
    for number in range(PACK):
        rows = slice(number * PANEL, (number + 1) * PANEL)
        left = join(0, lh[rows], lh[rows], lm[rows], lh[rows], ll[rows], lm[rows])
        right = join(0, rh[rows], rm[rows], rh[rows], rl[rows], rh[rows], rm[rows])
        found.append(mm(left, right, TN))
    return found


def invert_factors(grams, inverses, count):
    groups = count // PACK
    lane = lax.broadcasted_iota(jnp.int32, (TILE, TILE), 1)
    sub = lax.broadcasted_iota(jnp.int32, (TILE, TILE), 0)
    same_block = lane // PANEL == sub // PANEL
    for panel in range(TILE // PANEL):
        base, end = panel * PANEL, (panel + 1) * PANEL
        inside = (lane >= base) & (lane < end)
        unit = (lane - base == sub % PANEL).astype(f32)
        packed = []
        for group in range(groups):
            rows = grams[group * PACK : (group + 1) * PACK, base:end, :].reshape(TILE, TILE)
            packed.append(diagonal_blocks(rows, base))
        inverses[...] = factor_inverses(jnp.concatenate(packed, axis=0))

        def one(first, width, base=base, end=end, inside=inside, unit=unit):
            solved = []
            for offset in range(width):
                group = first + offset
                place = pl.ds(pl.multiple_of(group * PANEL, PANEL), PANEL)
                spread = jnp.where(
                    same_block, jnp.concatenate([inverses[place, :]] * PACK, axis=0), 0.0
                )
                rows = grams[pl.ds(group * PACK, PACK), base:end, :].reshape(TILE, TILE)
                solved.append(times_precise(spread, jnp.where(inside, unit, rows)))
            for offset in range(width):
                grams[pl.ds((first + offset) * PACK, PACK), base:end, :] = solved[offset].reshape(
                    PACK, PANEL, TILE
                )
            if end == TILE:
                return
            for offset in range(width):
                matrices = pl.ds((first + offset) * PACK, PACK)
                old = grams[matrices, end:, :]
                products = panel_products(
                    solved[offset], jnp.where(lane >= end, solved[offset], 0.0)
                )
                products = jnp.stack([product[end:] for product in products])
                grams[matrices, end:, :] = jnp.where(inside[None, end:], 0.0, old) - products

        loop_groups(groups, GROUPS_AT_ONCE, one)


GROUPS_AT_ONCE = 4


def optimizer_slots(first, count, inputs, outputs, grams, products):
    slots = products.shape[0] // 2
    loaded = [[ref[first + offset] for ref in inputs] for offset in range(count)]
    grad, weight, moment, square, left, right, left_base, right_base = map(list, zip(*loaded))
    every = range(count)
    turned_base = [left_base[n].T for n in every]
    turned_grad = [grad[n].T for n in every]
    turned_right = [right_base[n].T for n in every]
    half = [times_nn(turned_base[n], grad[n]) for n in every]
    left = [
        beta_stats * left[n] + (1 - beta_stats) * times_nn(grad[n], turned_grad[n]) for n in every
    ]
    right = [
        beta_stats * right[n] + (1 - beta_stats) * times_nn(turned_grad[n], grad[n])
        for n in every
    ]
    rotated = [times_nn(half[n], right_base[n]) for n in every]
    left_product = [times_nn(left[n], left_base[n]) for n in every]
    right_product = [times_nn(right[n], right_base[n]) for n in every]
    moment = [beta_first * moment[n] + (1 - beta_first) * rotated[n] for n in every]
    square = [
        beta_second * square[n] + (1 - beta_second) * rotated[n] * rotated[n] for n in every
    ]
    step = [
        (moment[n] / (1 - beta_first**STEP))
        / (jnp.sqrt(square[n] / (1 - beta_second**STEP)) + adam_epsilon)
        for n in every
    ]
    half = [times_nn(left_base[n], step[n]) for n in every]
    left_gram = [times_precise(left_product[n].T, left_product[n]) for n in every]
    right_gram = [times_precise(right_product[n].T, right_product[n]) for n in every]
    full = [times_nn(half[n], turned_right[n]) for n in every]
    weight = [weight[n] - matrix_rate * (full[n] + matrix_decay * weight[n]) for n in every]
    for n in every:
        slot = first + n
        values = (weight[n], weight[n].astype(bf16), moment[n], square[n], left[n], right[n])
        for ref, value in zip(outputs, values):
            ref[slot] = value
        products[slot] = left_product[n]
        products[slots + slot] = right_product[n]
        grams[slot] = left_gram[n]
        grams[slots + slot] = right_gram[n]


def loop_groups(total, width, body):
    def one(number, carry):
        body(number * width, width)
        return carry

    lax.fori_loop(0, total // width, one, 0)
    if total % width:
        body(total - total % width, total % width)


def optimizer_body(padded, counts, *refs):
    pieces, refs = refs[: sum(counts)], refs[sum(counts) :]
    sources, targets = refs[:7], refs[7:15]
    gradient, inputs, outputs = refs[15], refs[16:23], refs[23:31]
    grams, products, inverses, in_sems, out_sems = refs[31:]
    slots = sources[0].shape[0]
    lane = lax.broadcasted_iota(jnp.int32, (TILE, TILE), 1)
    sub = lax.broadcasted_iota(jnp.int32, (TILE, TILE), 0)
    cuts = [cut for cut in (0, SLOTS_AT_ONCE, 3 * SLOTS_AT_ONCE) if cut < slots] + [slots]
    parts = [(first, last - first) for first, last in zip(cuts, cuts[1:])]
    loads = [
        [
            pltpu.make_async_copy(
                source.at[pl.ds(*part)], target.at[pl.ds(*part)], in_sems.at[number, index]
            )
            for index, (source, target) in enumerate(zip(sources, inputs))
        ]
        for number, part in enumerate(parts)
    ]
    for load in loads:
        for copy in load:
            copy.start()
    for number in range(2 * slots, padded):
        grams[number] = (lane == sub).astype(f32)
    base = 0
    for count in counts:
        terms, pieces = pieces[:count], pieces[count:]
        gradient[base : base + terms[0].shape[0]] = sum(term[...].astype(f32) for term in terms)
        base += terms[0].shape[0]
    for load, (start, count) in zip(loads, parts):
        for copy in load:
            copy.wait()
        loop_groups(
            count,
            min(SLOTS_AT_ONCE, count),
            lambda first, width: optimizer_slots(
                start + first, width, (gradient, *inputs), outputs, grams, products
            ),
        )
    stores = [
        pltpu.make_async_copy(staged, target, out_sems.at[index])
        for index, (staged, target) in enumerate(zip(outputs, targets))
    ]
    for copy in stores[:6]:
        copy.start()
    invert_factors(grams, inverses, padded)

    def finish(first, count):
        found = []
        for offset in range(count):
            for side in range(2):
                number = side * slots + first + offset
                turned = jnp.where(sub >= lane, grams[number], 0.0).T
                found.append(times_nn(products[number], turned))
        for offset in range(count):
            outputs[6][first + offset] = found[2 * offset]
            outputs[7][first + offset] = found[2 * offset + 1]

    loop_groups(slots, 4, finish)
    for copy in stores[6:]:
        copy.start()
    for copy in stores:
        copy.wait()


SLOTS_AT_ONCE = 6


def optimizer(pieces, *arrays):
    shape = arrays[0].shape
    slots = shape[0]
    padded = -(-2 * slots // PACK) * PACK
    kinds = [f32, bf16] + [f32] * 6
    counts = [len(terms) for terms in pieces]
    return pl.pallas_call(
        functools.partial(optimizer_body, padded, counts),
        out_shape=tuple(jax.ShapeDtypeStruct(shape, kind) for kind in kinds),
        in_specs=vmem_specs(sum(counts)) + any_specs(7),
        out_specs=tuple(any_specs(8)),
        scratch_shapes=[pltpu.VMEM(shape, f32)] * 8
        + [pltpu.VMEM(shape, kind) for kind in kinds]
        + [
            pltpu.VMEM((padded, TILE, TILE), f32),
            pltpu.VMEM((2 * slots, TILE, TILE), f32),
            pltpu.VMEM((padded // PACK * PANEL, TILE), f32),
            pltpu.SemaphoreType.DMA((3, 7)),
            pltpu.SemaphoreType.DMA((8,)),
        ],
        compiler_params=pltpu.CompilerParams(vmem_limit_bytes=60 * 1024 * 1024),
        name="optimizer",
    )(*[term for terms in pieces for term in terms], *arrays)


def per_device(
    hidden,
    image,
    segment_ids,
    cotangent,
    slot_block,
    weight_master,
    moment_one,
    moment_two,
    left_stat,
    right_stat,
    left_basis,
    right_basis,
    norm_params,
    norm_moment_one,
    norm_moment_two,
):
    tensors = lax.axis_size("tensor")
    width = hidden.shape[2]
    heads_local = HEADS // tensors
    scale = (width // HEADS) ** (-0.5)
    order = slot_block[0]
    slot_count = order.shape[0]
    slots = weight_master.shape[1]
    shard = weight_master[0].astype(bf16)
    ring = lax.axis_size("dp") == RING_DEVICES
    patches = image.shape[1]
    if ring:
        natural, image, place = gather_ring(shard, order, image)
    else:
        image = pad_patches(image)
        positions = jnp.arange(slot_count, dtype=jnp.int32)
        place = jnp.zeros_like(order).at[order].set(positions)
        gathered = lax.all_gather(shard, "dp", axis=0, tiled=True)
        natural = gathered[place]
    out_rows, first_grad, part_six, other_six, packed, norm_total = layer_rows(
        hidden, image, patches, segment_ids, cotangent, natural, norm_params, heads_local, scale,
        place,
    )
    if ring:
        owned = scatter_ring(packed, slots)
    else:
        owned = [[lax.psum_scatter(packed, "dp", scatter_dimension=0, tiled=True)]]
    in_grad = first_grad + (part_six.astype(f32) + other_six.astype(f32))
    in_grad = in_grad.reshape(hidden.shape)
    updated = optimizer(
        owned,
        weight_master[0],
        moment_one[0],
        moment_two[0],
        left_stat[0],
        right_stat[0],
        left_basis[0],
        right_basis[0],
    )
    (
        weight_new,
        weight_copy,
        moment_one_new,
        moment_two_new,
        left_stat_new,
        right_stat_new,
        left_basis_new,
        right_basis_new,
    ) = [array[None] for array in updated]
    norm_first = beta_first * norm_moment_one + (1 - beta_first) * norm_total
    norm_second = beta_second * norm_moment_two + (1 - beta_second) * norm_total * norm_total
    norm_new = norm_params - norm_rate * (norm_first / (1 - beta_first**STEP)) / (
        jnp.sqrt(norm_second / (1 - beta_second**STEP)) + adam_epsilon
    )
    return (
        out_rows,
        in_grad,
        weight_new,
        weight_copy,
        moment_one_new,
        moment_two_new,
        left_stat_new,
        right_stat_new,
        left_basis_new,
        right_basis_new,
        norm_first,
        norm_second,
        norm_new,
    )


def solution(mesh):
    in_specs = (
        P("dp", None, None),
        P("dp", None, None),
        P("dp", None),
        P("dp", None, None),
        P("tensor", None),
        P("tensor", "dp", None, None),
        P("tensor", "dp", None, None),
        P("tensor", "dp", None, None),
        P("tensor", "dp", None, None),
        P("tensor", "dp", None, None),
        P("tensor", "dp", None, None),
        P("tensor", "dp", None, None),
        P(),
        P(),
        P(),
    )
    out_specs = (
        P("dp", None, None),
        P("dp", None, None),
        P("tensor", "dp", None, None),
        P("tensor", "dp", None, None),
        P("tensor", "dp", None, None),
        P("tensor", "dp", None, None),
        P("tensor", "dp", None, None),
        P("tensor", "dp", None, None),
        P("tensor", "dp", None, None),
        P("tensor", "dp", None, None),
        P(),
        P(),
        P(),
    )
    return jax.shard_map(
        per_device, mesh=mesh, in_specs=in_specs, out_specs=out_specs, check_vma=False
    )
```

```python
import functools

import jax
import jax.numpy as jnp
import numpy as np
from jax import lax
from jax.experimental import pallas as pl
from jax.experimental.pallas import tpu as pltpu
from jax.sharding import PartitionSpec as P

HEADS = 12
FF = 3072
NQ = 32
STEP = 10


beta_first = 0.9
beta_second = 0.999
beta_stats = 0.95
adam_epsilon = 1e-08
norm_epsilon = 1e-06
matrix_rate = 0.03
matrix_decay = 0.05
norm_rate = 0.6
masked_score = -1000000000.0


TILE = 128
PATCHES_PAD = 16
f32 = jnp.float32
bf16 = jnp.bfloat16
NN = ((1,), (0,))
NT = ((1,), (1,))
TN = ((0,), (0,))
VMEM_BYTES = 10 * 1024 * 1024


def mm(left, right, dims):
    return lax.dot_general(left, right, (dims, ((), ())), preferred_element_type=f32)


def vmem_specs(count):
    return [pl.BlockSpec(memory_space=pltpu.VMEM)] * count


def any_specs(count):
    return [pl.BlockSpec(memory_space=pl.ANY)] * count


def vmem_params():
    return pltpu.CompilerParams(vmem_limit_bytes=VMEM_BYTES)


def held(shape, kind):
    return pltpu.VMEM(shape, kind)


def pin(*arrays):
    return [pltpu.with_memory_space_constraint(array, pltpu.VMEM) for array in arrays]


def cost(flops, bytes_accessed, transcendentals=0):
    return pl.CostEstimate(flops=1, bytes_accessed=1, transcendentals=0)


def join(axis, *pieces):
    return jnp.concatenate(pieces, axis=axis)


def matrix_of(blocks_ref, row_first, row_count, col_first, col_count, col_total, base=0):
    rows = []
    for row in range(row_count):
        first = base + (row_first + row) * col_total + col_first
        rows.append(
            jnp.concatenate([blocks_ref[first + col] for col in range(col_count)], axis=1)
        )
    return jnp.concatenate(rows, axis=0)


def norm_forward(resid):
    center = resid - jnp.mean(resid, axis=-1, keepdims=True)
    inverse = lax.rsqrt(jnp.mean(center * center, axis=-1, keepdims=True) + norm_epsilon)
    return center * inverse, inverse


def norm_backward(resid, upstream, gain):
    unit, inverse = norm_forward(resid)
    scaled = upstream * gain
    mean_scaled = jnp.mean(scaled, axis=-1, keepdims=True)
    mean_product = jnp.mean(scaled * unit, axis=-1, keepdims=True)
    grad = inverse * (scaled - mean_scaled - unit * mean_product)
    gain_grad = jnp.sum(upstream * unit, axis=0, keepdims=True)
    shift_grad = jnp.sum(upstream, axis=0, keepdims=True)
    return grad, gain_grad, shift_grad


def head_pair(tile):
    low_half = lax.broadcasted_iota(jnp.int32, tile.shape, 1) < TILE // 2
    zero = jnp.zeros_like(tile)
    return jnp.concatenate(
        [jnp.where(low_half, tile, zero), jnp.where(low_half, zero, tile)], axis=0
    )


def side_by_side(stacked):
    half = stacked.shape[0] // 2
    return jnp.concatenate([stacked[:half], stacked[half:]], axis=1)


def all_probs(queries, keys, allowed, scale):
    every = range(len(queries))
    scores = [mm(head_pair(queries[n]), keys[n], NT) for n in every]
    scores = [jnp.where(allowed[n], scores[n] * scale, masked_score) for n in every]
    weights = [jnp.exp(score - jnp.max(score, axis=-1, keepdims=True)) for score in scores]
    return [weight / jnp.sum(weight, axis=-1, keepdims=True) for weight in weights]


def all_mixed(probs, values):
    count = probs[0].shape[0] // 2
    low_half = lax.broadcasted_iota(jnp.int32, (count, TILE), 1) < TILE // 2
    mixed = [mm(prob.astype(bf16), value, NN) for prob, value in zip(probs, values)]
    return [jnp.where(low_half, mix[:count], mix[count:]).astype(bf16) for mix in mixed]


def all_backward(queries, keys, values, probs, mixed_grads, scale):
    every = range(len(queries))
    pairs = [head_pair(grad) for grad in mixed_grads]
    prob_grads = [mm(pairs[n], values[n], NT) for n in every]
    value_grads = [mm(probs[n].astype(bf16), pairs[n], TN).astype(bf16) for n in every]
    inner = [jnp.sum(probs[n] * prob_grads[n], axis=-1, keepdims=True) for n in every]
    score_grads = [
        (probs[n] * (prob_grads[n] - inner[n]) * scale).astype(bf16) for n in every
    ]
    count = queries[0].shape[0]
    low_half = lax.broadcasted_iota(jnp.int32, (count, TILE), 1) < TILE // 2
    both = [mm(score_grads[n], keys[n], NN) for n in every]
    query_grads = [jnp.where(low_half, b[:count], b[count:]).astype(bf16) for b in both]
    key_grads = [mm(score_grads[n], head_pair(queries[n]), TN).astype(bf16) for n in every]
    return query_grads, key_grads, value_grads


def each_tile(plan, rows_at_once, body):
    def one(group, carry):
        body(
            [
                (group * rows_at_once + row, tile, slice(tile * TILE, (tile + 1) * TILE))
                for row in range(rows_at_once)
                for tile in range(plan.ht)
            ]
        )
        return carry

    lax.fori_loop(0, plan.rows // rows_at_once, one, 0)


def rows_of(row, count):
    return pl.ds(pl.multiple_of(row * count, count), count)


ROWS_AT_ONCE = 2


class Plan:
    def __init__(self, rows, seq, width, image_width, patches, heads, hidden_units):
        self.rows, self.seq, self.width = rows, seq, width
        self.image_width, self.heads, self.hidden = image_width, heads, hidden_units
        self.half = heads * (TILE // 2)
        self.patches = patches
        self.keys = -(-patches // PATCHES_PAD) * PATCHES_PAD
        self.wt, self.ht = width // TILE, self.half // TILE
        self.it, self.ft = image_width // TILE, hidden_units // TILE
        square, cross, feed = self.wt * self.ht, self.it * self.ht, self.wt * self.ft
        self.square, self.cross, self.feed = square, cross, feed
        self.self_first, self.self_count = 0, 4 * square
        self.cross_first, self.cross_count = 4 * square, 2 * square + 2 * cross
        self.query_first = self.cross_first + self.cross_count
        self.text_first = self.query_first + 2 * feed
        self.block_count = self.text_first + 2 * feed
        self.self_out = 3 * square
        self.image_first = self.cross_first + square
        self.cross_out = self.image_first + 2 * cross
        self.tokens = rows * seq
        self.learned = rows * NQ
        self.texts = rows * (seq - NQ)


def self_forward_body(
    plan, scale, nat, hidden, segments, qkv, probs, mixed, query_part, text_part
):
    for piece in range(3):
        matrix = matrix_of(nat, 0, plan.wt, 0, plan.ht, plan.ht, piece * plan.square)
        qkv[piece] = mm(hidden[...], matrix, NN).astype(bf16)

    def attend(items):
        seq = plan.seq
        allowed = []
        for row, _, _ in items[:: plan.ht]:
            along = jnp.broadcast_to(segments[row].astype(f32), (seq, seq))
            same = along.T == along
            allowed += [join(0, same, same)] * plan.ht
        found = all_probs(
            [qkv[0, rows_of(row, seq), cols] for row, _, cols in items],
            [qkv[1, rows_of(row, seq), cols] for row, _, cols in items],
            allowed,
            scale,
        )
        values = [qkv[2, rows_of(row, seq), cols] for row, _, cols in items]
        for (row, tile, cols), prob, mix in zip(items, found, all_mixed(found, values)):
            probs[row, tile] = prob
            mixed[rows_of(row, seq), cols] = mix

    each_tile(plan, ROWS_AT_ONCE, attend)
    matrix = matrix_of(nat, 0, plan.ht, 0, plan.wt, plan.wt, plan.self_out)
    part = mm(mixed[...], matrix, NN).astype(bf16)
    text = plan.seq - NQ
    for row in range(plan.rows):
        first = row * plan.seq
        query_part[row * NQ : (row + 1) * NQ] = part[first : first + NQ]
        text_part[row * text : (row + 1) * text] = part[first + NQ : first + plan.seq]


def self_forward(plan, scale, nat, hidden, segments):
    tokens, half, width = plan.tokens, plan.half, plan.width
    return pl.pallas_call(
        functools.partial(self_forward_body, plan, scale),
        out_shape=(
            held((3, tokens, half), bf16),
            held((plan.rows, plan.ht, 2 * plan.seq, plan.seq), f32),
            held((tokens, half), bf16),
            jax.ShapeDtypeStruct((plan.learned, width), bf16),
            jax.ShapeDtypeStruct((plan.texts, width), bf16),
        ),
        in_specs=vmem_specs(3),
        out_specs=tuple(vmem_specs(5)),
        compiler_params=vmem_params(),
        cost_estimate=cost(2 * tokens * width * half * 4, 8e6),
        name="self_forward",
    )(*pin(nat, hidden), segments)


def image_body(plan, nat, image, keys, values):
    for piece, target in ((0, keys), (1, values)):
        matrix = matrix_of(nat, 0, plan.it, 0, plan.ht, plan.ht, plan.image_first + piece * plan.cross)
        target[...] = mm(image[...], matrix, NN).astype(bf16)


def image_forward(plan, nat, image):
    total = plan.rows * plan.keys
    return pl.pallas_call(
        functools.partial(image_body, plan),
        out_shape=(held((total, plan.half), bf16),) * 2,
        in_specs=vmem_specs(2),
        out_specs=tuple(vmem_specs(2)),
        compiler_params=vmem_params(),
        cost_estimate=cost(4 * total * plan.image_width * plan.half, 8e6),
        name="image_forward",
    )(*pin(nat, image))


def first_norm(plan, token, count, hidden, mine, other, params, resid, first, low):
    gain, shift = params[0, 0:1], params[0, 1:2]

    def one(row, carry):
        place = pl.ds(pl.multiple_of(row * count, count), count)
        start = pl.multiple_of(row * plan.seq + token, NQ)
        summed = hidden[pl.ds(start, count), :].astype(f32) + (
            mine[place, :].astype(f32) + other[place, :].astype(f32)
        )
        resid[place, :] = summed
        normed = norm_forward(summed)[0] * gain + shift
        first[place, :] = normed
        low[place, :] = normed.astype(bf16)
        return carry

    lax.fori_loop(0, plan.rows, one, 0)


def cross_forward_body(
    plan, scale, nat, hidden, mine, other, params, image_keys, image_values,
    resid, first, low, queries, probs, mixed, part,
):
    first_norm(plan, 0, NQ, hidden, mine, other, params, resid, first, low)
    matrix = matrix_of(nat, 0, plan.wt, 0, plan.ht, plan.ht, plan.cross_first)
    queries[...] = mm(low[...], matrix, NN).astype(bf16)
    allowed = lax.broadcasted_iota(jnp.int32, (2 * NQ, plan.keys), 1) < plan.patches

    def attend(items):
        found = all_probs(
            [queries[rows_of(row, NQ), cols] for row, _, cols in items],
            [image_keys[rows_of(row, plan.keys), cols] for row, _, cols in items],
            [allowed] * len(items),
            scale,
        )
        values = [image_values[rows_of(row, plan.keys), cols] for row, _, cols in items]
        for (row, tile, cols), prob, mix in zip(items, found, all_mixed(found, values)):
            probs[row, tile] = prob
            mixed[rows_of(row, NQ), cols] = mix

    each_tile(plan, plan.rows, attend)
    matrix = matrix_of(nat, 0, plan.ht, 0, plan.wt, plan.wt, plan.cross_out)
    part[...] = mm(mixed[...], matrix, NN).astype(bf16)


def cross_forward(plan, scale, nat, hidden, mine, other, params, image_keys, image_values):
    learned, width, half = plan.learned, plan.width, plan.half
    return pl.pallas_call(
        functools.partial(cross_forward_body, plan, scale),
        out_shape=(
            held((learned, width), f32),
            held((learned, width), f32),
            held((learned, width), bf16),
            held((learned, half), bf16),
            held((plan.rows, plan.ht, 2 * NQ, plan.keys), f32),
            held((learned, half), bf16),
            jax.ShapeDtypeStruct((learned, width), bf16),
        ),
        in_specs=vmem_specs(7),
        out_specs=tuple(vmem_specs(7)),
        compiler_params=vmem_params(),
        cost_estimate=cost(4 * learned * width * half, 1.2e7),
        name="cross_forward",
    )(*pin(nat, hidden), mine, other, params, *pin(image_keys, image_values))


def gelu_parts(values):
    normal = 0.5 * (1.0 + lax.erf(values * 0.7071067811865476))
    density = 0.3989422804014327 * jnp.exp(-0.5 * values * values)
    return values * normal, normal + values * density


def feed_forward_tail(plan, first_block, nat, states_low, gated, slope, part):
    def one_up(chunk, carry):
        matrix = matrix_of(nat, 0, plan.wt, chunk * 2, 2, plan.ft, first_block)
        active, derivative = gelu_parts(mm(states_low[...], matrix, NN))
        cols = pl.ds(pl.multiple_of(chunk * 2 * TILE, 2 * TILE), 2 * TILE)
        gated[:, cols] = active.astype(bf16)
        slope[:, cols] = derivative
        return carry

    lax.fori_loop(0, plan.ft // 2, one_up, 0)

    def one_down(chunk, carry):
        matrix = matrix_of(nat, 0, plan.ft, chunk * 2, 2, plan.wt, first_block + plan.feed)
        cols = pl.ds(pl.multiple_of(chunk * 2 * TILE, 2 * TILE), 2 * TILE)
        part[:, cols] = mm(gated[...], matrix, NN).astype(bf16)
        return carry

    lax.fori_loop(0, plan.wt // 2, one_down, 0)


def text_forward_body(
    plan, nat, hidden, mine, other, params, resid, first, low, gated, slope, part
):
    first_norm(plan, NQ, plan.seq - NQ, hidden, mine, other, params, resid, first, low)
    feed_forward_tail(plan, plan.text_first, nat, low, gated, slope, part)


def query_forward_body(
    plan, nat, first_query, mine, other, params, resid, second, low, gated, slope, part,
):
    summed = first_query[...] + (mine[...].astype(f32) + other[...].astype(f32))
    resid[...] = summed
    normed = norm_forward(summed)[0] * params[1, 0:1] + params[1, 1:2]
    second[...] = normed
    low[...] = normed.astype(bf16)
    feed_forward_tail(plan, plan.query_first, nat, low, gated, slope, part)


def feed_shapes(plan, count):
    return (
        held((count, plan.hidden), bf16),
        held((count, plan.hidden), f32),
        jax.ShapeDtypeStruct((count, plan.width), bf16),
    )


def text_forward(plan, nat, hidden, mine, other, params):
    count, width = plan.texts, plan.width
    return pl.pallas_call(
        functools.partial(text_forward_body, plan),
        out_shape=(
            held((count, width), f32),
            held((count, width), f32),
            held((count, width), bf16),
        )
        + feed_shapes(plan, count),
        in_specs=vmem_specs(5),
        out_specs=tuple(vmem_specs(6)),
        compiler_params=vmem_params(),
        cost_estimate=cost(4 * count * width * plan.hidden, 1e7),
        name="text_forward",
    )(*pin(nat, hidden), mine, other, params)


def query_forward(plan, nat, first_query, mine, other, params):
    count, width = plan.learned, plan.width
    return pl.pallas_call(
        functools.partial(query_forward_body, plan),
        out_shape=(
            held((count, width), f32),
            held((count, width), f32),
            held((count, width), bf16),
        )
        + feed_shapes(plan, count),
        in_specs=vmem_specs(5),
        out_specs=tuple(vmem_specs(6)),
        compiler_params=vmem_params(),
        cost_estimate=cost(4 * count * width * plan.hidden, 8e6),
        name="query_forward",
    )(*pin(nat, first_query), mine, other, params)


def feed_backward_body(
    plan, first_block, first_token, which, nat, states, mine, other, upstream, params, slope,
    out, grad, grad_low, before_low, part, norm_grad,
):
    gain, shift = params[which, 0:1], params[which, 1:2]
    count = states.shape[0] // plan.rows
    norm_grad[...] = jnp.zeros_like(norm_grad)

    def one_norm(row, carry):
        place = pl.ds(pl.multiple_of(row * count, count), count)
        summed = states[place, :] + (mine[place, :].astype(f32) + other[place, :].astype(f32))
        out[place, :] = (norm_forward(summed)[0] * gain + shift).astype(bf16)
        found, gain_grad, shift_grad = norm_backward(
            summed, upstream[pl.ds(row * plan.seq + first_token, count), :].astype(f32), gain
        )
        grad[place, :] = found
        grad_low[place, :] = found.astype(bf16)
        norm_grad[0:1] += gain_grad
        norm_grad[1:2] += shift_grad
        return carry

    lax.fori_loop(0, plan.rows, one_norm, 0)

    def one_down(chunk, carry):
        matrix = matrix_of(nat, chunk * 2, 2, 0, plan.wt, plan.wt, first_block + plan.feed)
        cols = pl.ds(pl.multiple_of(chunk * 2 * TILE, 2 * TILE), 2 * TILE)
        before_low[:, cols] = (mm(grad_low[...], matrix, NT) * slope[:, cols]).astype(bf16)
        return carry

    lax.fori_loop(0, plan.ft // 2, one_down, 0)

    def one_up(chunk, carry):
        matrix = matrix_of(nat, chunk * 2, 2, 0, plan.ft, plan.ft, first_block)
        cols = pl.ds(pl.multiple_of(chunk * 2 * TILE, 2 * TILE), 2 * TILE)
        part[:, cols] = mm(before_low[...], matrix, NT).astype(bf16)
        return carry

    lax.fori_loop(0, plan.wt // 2, one_up, 0)


def feed_backward(plan, first_block, first_token, which, nat, states, mine, other, upstream, params, slope):
    count, width = states.shape
    return pl.pallas_call(
        functools.partial(feed_backward_body, plan, first_block, first_token, which),
        out_shape=(
            jax.ShapeDtypeStruct((count, width), bf16),
            held((count, width), f32),
            held((count, width), bf16),
            held((count, plan.hidden), bf16),
            jax.ShapeDtypeStruct((count, width), bf16),
            jax.ShapeDtypeStruct((2, width), f32),
        ),
        in_specs=vmem_specs(7),
        out_specs=tuple(vmem_specs(6)),
        compiler_params=vmem_params(),
        cost_estimate=cost(4 * count * width * plan.hidden, 1e7),
        name="feed_backward",
    )(*pin(nat, states), mine, other, *pin(upstream), params, *pin(slope))


def cross_backward_body(
    plan, scale, nat, resid, third_grad, mine, other, params, queries, keys, values, probs,
    grad, grad_low, query_back, key_back, value_back, part, norm_grad, looked,
):
    upstream = third_grad[...] + (mine[...].astype(f32) + other[...].astype(f32))
    found, gain_grad, shift_grad = norm_backward(resid[...], upstream, params[1, 0:1])
    grad[...] = found
    grad_low[...] = found.astype(bf16)
    norm_grad[0:1] = gain_grad
    norm_grad[1:2] = shift_grad
    matrix = matrix_of(nat, 0, plan.ht, 0, plan.wt, plan.wt, plan.cross_out)
    looked[...] = mm(grad_low[...], matrix, NT).astype(bf16)

    def back(items):
        found = all_backward(
            [queries[rows_of(row, NQ), cols] for row, _, cols in items],
            [keys[rows_of(row, plan.keys), cols] for row, _, cols in items],
            [values[rows_of(row, plan.keys), cols] for row, _, cols in items],
            [probs[row, tile] for row, tile, _ in items],
            [looked[rows_of(row, NQ), cols] for row, _, cols in items],
            scale,
        )
        for (row, _, cols), query_grad, key_grad, value_grad in zip(items, *found):
            query_back[rows_of(row, NQ), cols] = query_grad
            key_back[rows_of(row, plan.keys), cols] = key_grad
            value_back[rows_of(row, plan.keys), cols] = value_grad

    each_tile(plan, plan.rows, back)
    matrix = matrix_of(nat, 0, plan.wt, 0, plan.ht, plan.ht, plan.cross_first)
    part[...] = mm(query_back[...], matrix, NT).astype(bf16)


def cross_backward(
    plan, scale, nat, resid, third_grad, mine, other, params, queries, keys, values, probs
):
    learned, width, half = plan.learned, plan.width, plan.half
    return pl.pallas_call(
        functools.partial(cross_backward_body, plan, scale),
        out_shape=(
            held((learned, width), f32),
            held((learned, width), bf16),
            held((learned, half), bf16),
            held(keys.shape, bf16),
            held(keys.shape, bf16),
            jax.ShapeDtypeStruct((learned, width), bf16),
            jax.ShapeDtypeStruct((2, width), f32),
        ),
        in_specs=vmem_specs(10),
        out_specs=tuple(vmem_specs(7)),
        scratch_shapes=[
            pltpu.VMEM((learned, half), bf16),
        ],
        compiler_params=vmem_params(),
        cost_estimate=cost(8 * learned * width * half, 1e7),
        name="cross_backward",
    )(*pin(nat, resid, third_grad), mine, other, params, *pin(queries, keys, values, probs))


def self_backward_body(
    plan, scale, nat, query_resid, text_resid, query_grad, query_mine, query_other, text_grad,
    text_mine, text_other, params, qkv, probs,
    grad, grad_low, back, part, norm_grad, mixed,
):
    text = plan.seq - NQ
    gain = params[0, 0:1]
    norm_grad[...] = jnp.zeros_like(norm_grad)

    def one_norm(row, carry):
        place = pl.ds(pl.multiple_of(row * plan.seq, plan.seq), plan.seq)
        query_place = pl.ds(pl.multiple_of(row * NQ, NQ), NQ)
        text_place = pl.ds(pl.multiple_of(row * text, text), text)
        upstream = jnp.concatenate(
            [
                query_grad[query_place, :]
                + (query_mine[query_place, :].astype(f32) + query_other[query_place, :].astype(f32)),
                text_grad[text_place, :]
                + (text_mine[text_place, :].astype(f32) + text_other[text_place, :].astype(f32)),
            ],
            axis=0,
        )
        resid = join(0, query_resid[query_place, :], text_resid[text_place, :])
        found, gain_grad, shift_grad = norm_backward(resid, upstream, gain)
        grad[place, :] = found
        grad_low[place, :] = found.astype(bf16)
        norm_grad[0:1] += gain_grad
        norm_grad[1:2] += shift_grad
        return carry

    lax.fori_loop(0, plan.rows, one_norm, 0)
    matrix = matrix_of(nat, 0, plan.ht, 0, plan.wt, plan.wt, plan.self_out)
    mixed[...] = mm(grad_low[...], matrix, NT).astype(bf16)

    def back_rows(items):
        seq = plan.seq
        found = all_backward(
            *[[qkv[piece, rows_of(row, seq), cols] for row, _, cols in items] for piece in range(3)],
            [probs[row, tile] for row, tile, _ in items],
            [mixed[rows_of(row, seq), cols] for row, _, cols in items],
            scale,
        )
        for number, (row, tile, _) in enumerate(items):
            for piece in range(3):
                first = piece * plan.half + tile * TILE
                back[rows_of(row, seq), first : first + TILE] = found[piece][number]

    each_tile(plan, ROWS_AT_ONCE, back_rows)
    matrix = jnp.concatenate(
        [matrix_of(nat, 0, plan.wt, 0, plan.ht, plan.ht, p * plan.square) for p in range(3)],
        axis=1,
    )
    part[...] = mm(back[...], matrix, NT).astype(bf16)


def self_backward(
    plan, scale, nat, query_resid, text_resid, query_grad, query_mine, query_other, text_grad,
    text_mine, text_other, params, qkv, probs,
):
    tokens, width, half = plan.tokens, plan.width, plan.half
    return pl.pallas_call(
        functools.partial(self_backward_body, plan, scale),
        out_shape=(
            jax.ShapeDtypeStruct((tokens, width), f32),
            held((tokens, width), bf16),
            held((tokens, 3 * half), bf16),
            jax.ShapeDtypeStruct((tokens, width), bf16),
            jax.ShapeDtypeStruct((2, width), f32),
        ),
        in_specs=vmem_specs(12),
        out_specs=tuple(vmem_specs(5)),
        scratch_shapes=[
            pltpu.VMEM((tokens, half), bf16),
        ],
        compiler_params=vmem_params(),
        cost_estimate=cost(8 * tokens * width * half, 1.2e7),
        name="self_backward",
    )(
        *pin(nat, query_resid, text_resid, query_grad), query_mine, query_other, *pin(text_grad), text_mine,
        text_other, params, *pin(qkv, probs),
    )


def grad_blocks_body(first_block, pairs, source_count, spare, place, *refs):
    sources, target = refs[:source_count], refs[-1]
    if spare is not None:
        for number in range(spare[1]):
            target[place[spare[0] + number]] = jnp.zeros((TILE, TILE), bf16)
    base = first_block
    for left_at, right_at, right_first, right_width, step in pairs:
        left, right = sources[left_at], sources[right_at]
        left_tiles, col_total = left.shape[1] // TILE, right_width // TILE

        def one(chunk, carry, base=base, left=left, right=right, step=step, col_total=col_total,
                right_first=right_first, right_width=right_width):
            cols = pl.ds(pl.multiple_of(chunk * step * TILE, step * TILE), step * TILE)
            product = mm(left[:, cols], right[:, right_first : right_first + right_width], TN)
            first = base + chunk * step * col_total
            for row in range(step):
                for col in range(col_total):
                    target[place[first + row * col_total + col]] = product[
                        row * TILE : (row + 1) * TILE, col * TILE : (col + 1) * TILE
                    ].astype(bf16)
            return carry

        lax.fori_loop(0, left_tiles // step, one, 0)
        base += left_tiles * col_total


def grad_blocks(buffer, place, first_block, sources, pairs, flops, spare=None):
    given = [] if isinstance(buffer, jax.ShapeDtypeStruct) else pin(buffer)
    return pl.pallas_call(
        functools.partial(grad_blocks_body, first_block, pairs, len(sources), spare),
        out_shape=held(buffer.shape, buffer.dtype),
        in_specs=[pl.BlockSpec(memory_space=pltpu.SMEM)] + vmem_specs(len(sources) + len(given)),
        out_specs=vmem_specs(1)[0],
        input_output_aliases={1 + len(sources): 0} if given else {},
        compiler_params=vmem_params(),
        cost_estimate=cost(flops, 1e7),
        name="grad_blocks",
    )(place, *pin(*sources), *given)


def swap_tensor(part):
    if lax.axis_size("tensor") != 2:
        total = lax.psum(part.astype(f32), "tensor")
        return (total - part.astype(f32)).astype(bf16)
    return lax.ppermute(part, "tensor", [(0, 1), (1, 0)])


after = lax.optimization_barrier


def sum_steps(values):
    if lax.axis_size("dp") != RING_DEVICES:
        values = lax.psum(values, "dp")
        while True:
            values = yield values
    for bit in (1, 2, 4, 8):
        pairs = [(index, index ^ bit) for index in range(RING_DEVICES)]
        values = yield values + lax.ppermute(values, "dp", pairs)


def layer_rows(
    hidden, image, patches, segment_ids, cotangent, nat, norm_params, heads_local, scale, place
):
    rows, seq, width = hidden.shape
    plan = Plan(
        rows, seq, width, image.shape[2], patches, heads_local, FF // lax.axis_size("tensor")
    )
    tokens, learned, texts, half = plan.tokens, plan.learned, plan.texts, plan.half
    flat_hidden = hidden.reshape(tokens, width)
    flat_image = image.reshape(rows * plan.keys, plan.image_width)
    flat_back = cotangent.reshape(tokens, width)
    buffer = jax.ShapeDtypeStruct((place.shape[0], TILE, TILE), bf16)

    qkv, self_probs, mixed, query_part, text_part = self_forward(
        plan, scale, nat, flat_hidden, segment_ids[:, None, :]
    )
    query_other = swap_tensor(query_part)
    image_keys, image_values = image_forward(plan, nat, flat_image)
    text_part, query_other, image_keys = after((text_part, query_other, image_keys))
    text_other = swap_tensor(text_part)
    query_first, first_query, low_query, cross_queries, cross_probs, looked, part_two = (
        cross_forward(
            plan, scale, nat, flat_hidden, query_part, query_other, norm_params, image_keys,
            image_values,
        )
    )
    other_two = swap_tensor(part_two)
    second_sum, second, low_second, query_gated, query_slope, part_query = query_forward(
        plan, nat, first_query, part_two, other_two, norm_params
    )
    other_query = swap_tensor(part_query)
    text_other, part_query = after((text_other, part_query))
    text_first, first_text, low_text, text_gated, text_slope, part_text = text_forward(
        plan, nat, flat_hidden, text_part, text_other, norm_params
    )
    other_query, part_text = after((other_query, part_text))
    other_text = swap_tensor(part_text)
    out_query, third_query, third_query_low, before_query, part_four_query, norm_query = (
        feed_backward(
            plan, plan.query_first, 0, 2, nat, second, part_query, other_query, flat_back,
            norm_params, query_slope,
        )
    )
    other_four_query = swap_tensor(part_four_query)
    feed_pairs = [(0, 1, 0, plan.hidden, 6), (2, 3, 0, width, 6)]
    buffer = grad_blocks(
        buffer, place, plan.query_first, [low_second, before_query, query_gated, third_query_low],
        feed_pairs, 4 * learned * width * plan.hidden,
        spare=(plan.block_count, place.shape[0] - plan.block_count),
    )
    other_text, buffer = after((other_text, buffer))
    out_text, third_text, third_text_low, before_text, part_four_text, norm_text = feed_backward(
        plan, plan.text_first, NQ, 3, nat, first_text, part_text, other_text, flat_back,
        norm_params, text_slope,
    )
    other_four_query, part_four_text = after((other_four_query, part_four_text))
    other_four_text = swap_tensor(part_four_text)
    second_grad, cross_low, query_back, key_back, value_back, part_five, norm_second = (
        cross_backward(
            plan, scale, nat, second_sum, third_query, part_four_query, other_four_query,
            norm_params, cross_queries, image_keys, image_values, cross_probs,
        )
    )
    other_five = swap_tensor(part_five)
    buffer, part_five = after((buffer, part_five))
    buffer = grad_blocks(
        buffer, place, plan.text_first, [low_text, before_text, text_gated, third_text_low],
        feed_pairs, 4 * texts * width * plan.hidden,
    )
    cross_flops = 2 * rows * plan.keys * plan.image_width * half
    buffer = grad_blocks(
        buffer, place, plan.cross_first, [low_query, query_back, flat_image, key_back],
        [(0, 1, 0, half, 6), (2, 3, 0, half, 11)], cross_flops,
    )
    other_four_text, buffer = after((other_four_text, buffer))
    first_grad, self_low, self_back, part_six, norm_first = self_backward(
        plan, scale, nat, query_first, text_first, second_grad, part_five, other_five, third_text,
        part_four_text, other_four_text, norm_params, qkv, self_probs,
    )
    other_six = swap_tensor(part_six)
    norm_steps = sum_steps(jnp.stack([norm_first, norm_second, norm_query, norm_text]))
    norms = next(norm_steps)
    buffer, part_six = after((buffer, part_six))
    buffer = grad_blocks(
        buffer, place, plan.image_first + plan.cross, [flat_image, value_back],
        [(0, 1, 0, half, 11)], cross_flops,
    )
    buffer, norms = after((buffer, norms))
    norms = norm_steps.send(norms)
    buffer = grad_blocks(
        buffer, place, plan.cross_out, [looked, cross_low], [(0, 1, 0, width, 3)],
        2 * learned * width * half,
    )
    buffer, norms = after((buffer, norms))
    norms = norm_steps.send(norms)
    buffer = grad_blocks(
        buffer, place, plan.self_first, [flat_hidden, self_back],
        [(0, 1, 0, half, 6), (0, 1, half, half, 6), (0, 1, 2 * half, half, 6)],
        6 * tokens * width * half,
    )
    buffer, norms, other_six = after((buffer, norms, other_six))
    norms = norm_steps.send(norms)
    buffer = grad_blocks(
        buffer, place, plan.self_out, [mixed, self_low], [(0, 1, 0, width, 3)],
        2 * tokens * width * half,
    )
    buffer, norms = after((buffer, norms))
    output_rows = jnp.concatenate(
        [out_query.reshape(rows, NQ, width), out_text.reshape(rows, seq - NQ, width)], axis=1
    )
    return (output_rows, first_grad, part_six, other_six, buffer, norms)


CHIP_RING = ((0, 0), (1, 0), (2, 0), (3, 0), (3, 1), (2, 1), (1, 1), (0, 1))
RING = len(CHIP_RING)
RING_DEVICES = 2 * RING


def ring_index(position, core):
    z, x = CHIP_RING[position % RING]
    return (z * 2 + x) * 2 + core


def direction_of(core):
    return 1 - 2 * core


RING_PAIRS = [
    (ring_index(position, core), ring_index(position + direction_of(core), core))
    for position in range(RING)
    for core in range(2)
]


def ring_place(index):
    return CHIP_RING.index((index // 4, index // 2 % 2)), index % 2


CORE_PAIRS = [(index, index ^ 1) for index in range(RING_DEVICES)]


def chain_parts(slots, chains):
    cuts = [slots * number // chains for number in range(chains + 1)]
    return [(first, last - first) for first, last in zip(cuts, cuts[1:])]


def place_blocks_body(first, ids, *refs):
    sources, target = refs[:-1], refs[-1]
    base = first
    for source in sources:
        for number in range(source.shape[0]):
            target[ids[base + number]] = source[number]
        base += source.shape[0]


def place_blocks(ids, first, sources, target, shape):
    operands = [ids, *pin(*sources)]
    aliases = {}
    if target is not None:
        operands += pin(target)
        aliases = {len(operands) - 1: 0}

    def body(ids, *refs):
        place_blocks_body(first, ids, *refs[: len(sources)], refs[-1])

    return pl.pallas_call(
        body,
        out_shape=held(shape, bf16),
        in_specs=[pl.BlockSpec(memory_space=pltpu.SMEM)] + vmem_specs(len(operands) - 1),
        out_specs=vmem_specs(1)[0],
        input_output_aliases=aliases,
        compiler_params=pltpu.CompilerParams(vmem_limit_bytes=4 * 1024 * 1024),
        cost_estimate=cost(0, 0),
        name="place_blocks",
    )(*operands)


def gather_positions(slots):
    table = np.zeros((RING_DEVICES, RING_DEVICES * slots), np.int32)
    for index in range(RING_DEVICES):
        position, core = ring_place(index)
        found = []
        for step in range(RING):
            for side in (core, 1 - core):
                owner = ring_index(position - direction_of(side) * step, side)
                found += [owner * slots + slot for slot in range(slots)]
        table[index] = found
    return table


AT_ONCE = 8


def index_body(count, device, order, arrival, departure, ids, place):
    me = device[0]

    def one(group, carry):
        numbers = [group * AT_ONCE + offset for offset in range(AT_ONCE)]
        blocks = [order[number] for number in numbers]
        arrived = [order[arrival[me, number]] for number in numbers]
        places = [departure[me, number] for number in numbers]
        for number, block, other, target in zip(numbers, blocks, arrived, places):
            ids[number] = other
            place[block] = target
        return carry

    lax.fori_loop(0, count // AT_ONCE, one, 0)


def block_indices(order, slots):
    count = order.shape[0]
    smem = pl.BlockSpec(memory_space=pltpu.SMEM)
    return pl.pallas_call(
        functools.partial(index_body, count),
        out_shape=(jax.ShapeDtypeStruct((count,), jnp.int32),) * 2,
        in_specs=[smem] * 4,
        out_specs=(smem, smem),
        compiler_params=vmem_params(),
        name="block_indices",
    )(
        lax.axis_index("dp").reshape(1),
        order,
        jnp.asarray(gather_positions(slots)),
        jnp.asarray(scatter_positions(slots)),
    )


def gather_ring(shard, order, image, chains=2):
    slots = shard.shape[0]
    parts = chain_parts(slots, chains)
    shape = (order.shape[0], TILE, TILE)
    ids, place = block_indices(order, slots)
    other = lax.ppermute(shard, "dp", CORE_PAIRS)
    held = [shard[first : first + count] for first, count in parts]
    natural = None
    waiting, first, placed = [shard, other], 0, 2 * slots
    for step in range(1, RING):
        held = [lax.ppermute(piece, "dp", RING_PAIRS) for piece in held]
        if step == 2:
            held[0], ids, place = lax.optimization_barrier((held[0], ids, place))
        if step == 3:
            held[0], image = lax.optimization_barrier((held[0], pad_patches(image)))
        if step >= 4:
            now = 2 + 2 * chains if step == 4 else 4 * chains
            count = sum(piece.shape[0] for piece in waiting[:now])
            natural = place_blocks(ids, first, waiting[:now], natural, shape)
            held[0], natural = lax.optimization_barrier((held[0], natural))
            waiting, first = waiting[now:], first + count
        waiting = waiting + held + [lax.ppermute(piece, "dp", CORE_PAIRS) for piece in held]
    return place_blocks(ids, first, waiting, natural, shape), image, place


def scatter_positions(slots):
    table = np.zeros((RING_DEVICES, RING_DEVICES * slots), np.int32)
    for index in range(RING_DEVICES):
        position, core = ring_place(index)
        for step in range(1, RING + 1):
            for number, side in enumerate((1 - core, core)):
                owner = ring_index(position - direction_of(side) * step, side)
                base = (number * RING + step - 1) * slots
                table[index, owner * slots : (owner + 1) * slots] = base + np.arange(slots)
    return table


def scatter_ring(packed, slots, chains=2):
    parts = chain_parts(slots, chains)
    held = [None] * chains
    other = None
    for step in range(1, RING + 1):
        base = (step - 1) * slots
        if step % 2:
            if other is not None:
                packed, other = lax.optimization_barrier((packed, other))
            other = lax.ppermute(packed[base : base + 2 * slots], "dp", CORE_PAIRS)
        pieces = []
        for number, (first, count) in enumerate(parts):
            start = (RING + step - 1) * slots + first
            place = (step - 1) % 2 * slots + first
            terms = [packed[start : start + count], other[place : place + count]]
            if held[number] is not None:
                terms.append(held[number])
            pieces.append(terms)
        if step == RING:
            return pieces
        for number, terms in enumerate(pieces):
            summed = sum(term.astype(f32) for term in terms).astype(bf16)
            held[number] = lax.ppermute(summed, "dp", RING_PAIRS)


def pad_patches(image):
    return jnp.pad(image, ((0, 0), (0, -image.shape[1] % PATCHES_PAD), (0, 0)))


PANEL = 16
PACK = TILE // PANEL


def split_two(values):
    high = values.astype(bf16)
    return high, (values - high.astype(f32)).astype(bf16)


def split_three(values):
    high = values.astype(bf16)
    rest = values - high.astype(f32)
    middle = rest.astype(bf16)
    return high, middle, (rest - middle.astype(f32)).astype(bf16)


def fold(product):
    return product[:, :TILE] + product[:, TILE:]


def times_nn(left, right):
    high, low = split_two(right)
    row = join(1, high, low)
    return fold(mm(join(1, *split_two(left)), join(0, row, row), NN))


def times_precise(left, right):
    lh, lm, ll = split_three(left)
    rh, rm, rl = split_three(right)
    both = mm(join(1, lh, lm), join(0, join(1, rh, rm), join(1, rm, rh)), NN)
    return fold(both) + mm(join(1, lh, ll), join(0, rl, rh), NN)


def diagonal_blocks(rows, base):
    lane = lax.broadcasted_iota(jnp.int32, (PANEL, TILE), 1) // PANEL
    packed = jnp.zeros((PANEL, TILE), f32)
    for number in range(PACK):
        piece = rows[number * PANEL : (number + 1) * PANEL]
        shift = (number * PANEL - base) % TILE
        if shift:
            piece = pltpu.roll(piece, shift, 1)
        packed = jnp.where(lane == number, piece, packed)
    return packed


def factor_inverses(packed):
    groups = packed.shape[0] // PANEL
    shape = packed.shape
    lane = lax.broadcasted_iota(jnp.int32, shape, 1)
    row = lax.broadcasted_iota(jnp.int32, shape, 0) % PANEL
    col = lane % PANEL
    first = lane - col

    def spread(values, step):
        picked = values.reshape(groups, PANEL, TILE)[:, step : step + 1]
        return jnp.broadcast_to(picked, (groups, PANEL, TILE)).reshape(shape)

    scale = jnp.zeros(shape, f32)
    column = jnp.take_along_axis(packed, first, axis=1)
    for step in range(PANEL):
        pivot = spread(column, step)
        inverse = reciprocal(pivot)
        if step + 1 < PANEL:
            following = jnp.take_along_axis(packed, first + (step + 1), axis=1)
            following = following - column * (spread(column, step + 1) * inverse)
        scaled = jnp.where(col == step, 1.0, spread(packed, step)) * inverse
        kept = jnp.where(col == step, jnp.where(row > step, 0.0, 1.0), packed)
        packed = jnp.where(
            row > step, kept - column * scaled, jnp.where(row == step, kept, packed)
        )
        scale = jnp.where(row == step, lax.rsqrt(pivot), scale)
        if step + 1 < PANEL:
            column = following
    return jnp.where(col <= row, packed * scale, 0.0)


def reciprocal(values):
    rough = pl.reciprocal(values, approx=True)
    rough = rough * (2.0 - values * rough)
    return rough * (2.0 - values * rough)


def panel_products(solved, masked):
    lh, lm, ll = split_three(masked)
    rh, rm, rl = split_three(solved)
    found = []
    for number in range(PACK):
        rows = slice(number * PANEL, (number + 1) * PANEL)
        left = join(0, lh[rows], lh[rows], lm[rows], lh[rows], ll[rows], lm[rows])
        right = join(0, rh[rows], rm[rows], rh[rows], rl[rows], rh[rows], rm[rows])
        found.append(mm(left, right, TN))
    return found


def invert_factors(grams, inverses, count):
    groups = count // PACK
    lane = lax.broadcasted_iota(jnp.int32, (TILE, TILE), 1)
    sub = lax.broadcasted_iota(jnp.int32, (TILE, TILE), 0)
    same_block = lane // PANEL == sub // PANEL
    for panel in range(TILE // PANEL):
        base, end = panel * PANEL, (panel + 1) * PANEL
        inside = (lane >= base) & (lane < end)
        unit = (lane - base == sub % PANEL).astype(f32)
        packed = []
        for group in range(groups):
            rows = grams[group * PACK : (group + 1) * PACK, base:end, :].reshape(TILE, TILE)
            packed.append(diagonal_blocks(rows, base))
        inverses[...] = factor_inverses(jnp.concatenate(packed, axis=0))

        def one(first, width, base=base, end=end, inside=inside, unit=unit):
            solved = []
            for offset in range(width):
                group = first + offset
                place = pl.ds(pl.multiple_of(group * PANEL, PANEL), PANEL)
                spread = jnp.where(
                    same_block, jnp.concatenate([inverses[place, :]] * PACK, axis=0), 0.0
                )
                rows = grams[pl.ds(group * PACK, PACK), base:end, :].reshape(TILE, TILE)
                solved.append(times_precise(spread, jnp.where(inside, unit, rows)))
            for offset in range(width):
                grams[pl.ds((first + offset) * PACK, PACK), base:end, :] = solved[offset].reshape(
                    PACK, PANEL, TILE
                )
            if end == TILE:
                return
            for offset in range(width):
                matrices = pl.ds((first + offset) * PACK, PACK)
                old = grams[matrices, end:, :]
                products = panel_products(
                    solved[offset], jnp.where(lane >= end, solved[offset], 0.0)
                )
                products = jnp.stack([product[end:] for product in products])
                grams[matrices, end:, :] = jnp.where(inside[None, end:], 0.0, old) - products

        loop_groups(groups, GROUPS_AT_ONCE, one)


GROUPS_AT_ONCE = 4


def optimizer_slots(first, count, inputs, outputs, grams, products):
    slots = products.shape[0] // 2
    loaded = [[ref[first + offset] for ref in inputs] for offset in range(count)]
    grad, weight, moment, square, left, right, left_base, right_base = map(list, zip(*loaded))
    every = range(count)
    turned_base = [left_base[n].T for n in every]
    turned_grad = [grad[n].T for n in every]
    turned_right = [right_base[n].T for n in every]
    half = [times_nn(turned_base[n], grad[n]) for n in every]
    left = [
        beta_stats * left[n] + (1 - beta_stats) * times_nn(grad[n], turned_grad[n]) for n in every
    ]
    right = [
        beta_stats * right[n] + (1 - beta_stats) * times_nn(turned_grad[n], grad[n])
        for n in every
    ]
    rotated = [times_nn(half[n], right_base[n]) for n in every]
    left_product = [times_nn(left[n], left_base[n]) for n in every]
    right_product = [times_nn(right[n], right_base[n]) for n in every]
    moment = [beta_first * moment[n] + (1 - beta_first) * rotated[n] for n in every]
    square = [
        beta_second * square[n] + (1 - beta_second) * rotated[n] * rotated[n] for n in every
    ]
    step = [
        (moment[n] / (1 - beta_first**STEP))
        / (jnp.sqrt(square[n] / (1 - beta_second**STEP)) + adam_epsilon)
        for n in every
    ]
    half = [times_nn(left_base[n], step[n]) for n in every]
    left_gram = [times_precise(left_product[n].T, left_product[n]) for n in every]
    right_gram = [times_precise(right_product[n].T, right_product[n]) for n in every]
    full = [times_nn(half[n], turned_right[n]) for n in every]
    weight = [weight[n] - matrix_rate * (full[n] + matrix_decay * weight[n]) for n in every]
    for n in every:
        slot = first + n
        values = (weight[n], weight[n].astype(bf16), moment[n], square[n], left[n], right[n])
        for ref, value in zip(outputs, values):
            ref[slot] = value
        products[slot] = left_product[n]
        products[slots + slot] = right_product[n]
        grams[slot] = left_gram[n]
        grams[slots + slot] = right_gram[n]


def loop_groups(total, width, body):
    def one(number, carry):
        body(number * width, width)
        return carry

    lax.fori_loop(0, total // width, one, 0)
    if total % width:
        body(total - total % width, total % width)


def optimizer_body(padded, counts, *refs):
    pieces, refs = refs[: sum(counts)], refs[sum(counts) :]
    sources, targets = refs[:7], refs[7:15]
    gradient, inputs, outputs = refs[15], refs[16:23], refs[23:31]
    grams, products, inverses, in_sems, out_sems = refs[31:]
    slots = sources[0].shape[0]
    lane = lax.broadcasted_iota(jnp.int32, (TILE, TILE), 1)
    sub = lax.broadcasted_iota(jnp.int32, (TILE, TILE), 0)
    cuts = [cut for cut in (0, SLOTS_AT_ONCE, 3 * SLOTS_AT_ONCE) if cut < slots] + [slots]
    parts = [(first, last - first) for first, last in zip(cuts, cuts[1:])]
    loads = [
        [
            pltpu.make_async_copy(
                source.at[pl.ds(*part)], target.at[pl.ds(*part)], in_sems.at[number, index]
            )
            for index, (source, target) in enumerate(zip(sources, inputs))
        ]
        for number, part in enumerate(parts)
    ]
    for load in loads:
        for copy in load:
            copy.start()
    for number in range(2 * slots, padded):
        grams[number] = (lane == sub).astype(f32)
    base = 0
    for count in counts:
        terms, pieces = pieces[:count], pieces[count:]
        gradient[base : base + terms[0].shape[0]] = sum(term[...].astype(f32) for term in terms)
        base += terms[0].shape[0]
    for load, (start, count) in zip(loads, parts):
        for copy in load:
            copy.wait()
        loop_groups(
            count,
            min(SLOTS_AT_ONCE, count),
            lambda first, width: optimizer_slots(
                start + first, width, (gradient, *inputs), outputs, grams, products
            ),
        )
    stores = [
        pltpu.make_async_copy(staged, target, out_sems.at[index])
        for index, (staged, target) in enumerate(zip(outputs, targets))
    ]
    for copy in stores[:6]:
        copy.start()
    invert_factors(grams, inverses, padded)

    def finish(first, count):
        found = []
        for offset in range(count):
            for side in range(2):
                number = side * slots + first + offset
                turned = jnp.where(sub >= lane, grams[number], 0.0).T
                found.append(times_nn(products[number], turned))
        for offset in range(count):
            outputs[6][first + offset] = found[2 * offset]
            outputs[7][first + offset] = found[2 * offset + 1]

    loop_groups(slots, 4, finish)
    for copy in stores[6:]:
        copy.start()
    for copy in stores:
        copy.wait()


SLOTS_AT_ONCE = 6


def optimizer(pieces, *arrays):
    shape = arrays[0].shape
    slots = shape[0]
    padded = -(-2 * slots // PACK) * PACK
    kinds = [f32, bf16] + [f32] * 6
    counts = [len(terms) for terms in pieces]
    return pl.pallas_call(
        functools.partial(optimizer_body, padded, counts),
        out_shape=tuple(jax.ShapeDtypeStruct(shape, kind) for kind in kinds),
        in_specs=vmem_specs(sum(counts)) + any_specs(7),
        out_specs=tuple(any_specs(8)),
        scratch_shapes=[pltpu.VMEM(shape, f32)] * 8
        + [pltpu.VMEM(shape, kind) for kind in kinds]
        + [
            pltpu.VMEM((padded, TILE, TILE), f32),
            pltpu.VMEM((2 * slots, TILE, TILE), f32),
            pltpu.VMEM((padded // PACK * PANEL, TILE), f32),
            pltpu.SemaphoreType.DMA((3, 7)),
            pltpu.SemaphoreType.DMA((8,)),
        ],
        compiler_params=pltpu.CompilerParams(vmem_limit_bytes=60 * 1024 * 1024),
        name="optimizer",
    )(*[term for terms in pieces for term in terms], *arrays)


def per_device(
    hidden,
    image,
    segment_ids,
    cotangent,
    slot_block,
    weight_master,
    moment_one,
    moment_two,
    left_stat,
    right_stat,
    left_basis,
    right_basis,
    norm_params,
    norm_moment_one,
    norm_moment_two,
):
    tensors = lax.axis_size("tensor")
    width = hidden.shape[2]
    heads_local = HEADS // tensors
    scale = (width // HEADS) ** (-0.5)
    order = slot_block[0]
    slot_count = order.shape[0]
    slots = weight_master.shape[1]
    shard = weight_master[0].astype(bf16)
    ring = lax.axis_size("dp") == RING_DEVICES
    patches = image.shape[1]
    if ring:
        natural, image, place = gather_ring(shard, order, image)
    else:
        image = pad_patches(image)
        positions = jnp.arange(slot_count, dtype=jnp.int32)
        place = jnp.zeros_like(order).at[order].set(positions)
        gathered = lax.all_gather(shard, "dp", axis=0, tiled=True)
        natural = gathered[place]
    out_rows, first_grad, part_six, other_six, packed, norm_total = layer_rows(
        hidden, image, patches, segment_ids, cotangent, natural, norm_params, heads_local, scale,
        place,
    )
    if ring:
        owned = scatter_ring(packed, slots)
    else:
        owned = [[lax.psum_scatter(packed, "dp", scatter_dimension=0, tiled=True)]]
    in_grad = first_grad + (part_six.astype(f32) + other_six.astype(f32))
    in_grad = in_grad.reshape(hidden.shape)
    updated = optimizer(
        owned,
        weight_master[0],
        moment_one[0],
        moment_two[0],
        left_stat[0],
        right_stat[0],
        left_basis[0],
        right_basis[0],
    )
    (
        weight_new,
        weight_copy,
        moment_one_new,
        moment_two_new,
        left_stat_new,
        right_stat_new,
        left_basis_new,
        right_basis_new,
    ) = [array[None] for array in updated]
    norm_first = beta_first * norm_moment_one + (1 - beta_first) * norm_total
    norm_second = beta_second * norm_moment_two + (1 - beta_second) * norm_total * norm_total
    norm_new = norm_params - norm_rate * (norm_first / (1 - beta_first**STEP)) / (
        jnp.sqrt(norm_second / (1 - beta_second**STEP)) + adam_epsilon
    )
    return (
        out_rows,
        in_grad,
        weight_new,
        weight_copy,
        moment_one_new,
        moment_two_new,
        left_stat_new,
        right_stat_new,
        left_basis_new,
        right_basis_new,
        norm_first,
        norm_second,
        norm_new,
    )


def solution(mesh):
    in_specs = (
        P("dp", None, None),
        P("dp", None, None),
        P("dp", None),
        P("dp", None, None),
        P("tensor", None),
        P("tensor", "dp", None, None),
        P("tensor", "dp", None, None),
        P("tensor", "dp", None, None),
        P("tensor", "dp", None, None),
        P("tensor", "dp", None, None),
        P("tensor", "dp", None, None),
        P("tensor", "dp", None, None),
        P(),
        P(),
        P(),
    )
    out_specs = (
        P("dp", None, None),
        P("dp", None, None),
        P("tensor", "dp", None, None),
        P("tensor", "dp", None, None),
        P("tensor", "dp", None, None),
        P("tensor", "dp", None, None),
        P("tensor", "dp", None, None),
        P("tensor", "dp", None, None),
        P("tensor", "dp", None, None),
        P("tensor", "dp", None, None),
        P(),
        P(),
        P(),
    )
    return jax.shard_map(
        per_device, mesh=mesh, in_specs=in_specs, out_specs=out_specs, check_vma=False
    )
```

```python
import functools

import jax
import jax.numpy as jnp
import numpy as np
from jax import lax
from jax.experimental import pallas as pl
from jax.experimental.pallas import tpu as pltpu
from jax.sharding import PartitionSpec as P

HEADS = 12
FF = 3072
NQ = 32
STEP = 10


beta_first = 0.9
beta_second = 0.999
beta_stats = 0.95
adam_epsilon = 1e-08
norm_epsilon = 1e-06
matrix_rate = 0.03
matrix_decay = 0.05
norm_rate = 0.6
masked_score = -1000000000.0


TILE = 128
PATCHES_PAD = 16
f32 = jnp.float32
bf16 = jnp.bfloat16
NN = ((1,), (0,))
NT = ((1,), (1,))
TN = ((0,), (0,))
VMEM_BYTES = 10 * 1024 * 1024


def mm(left, right, dims):
    return lax.dot_general(left, right, (dims, ((), ())), preferred_element_type=f32)


def vmem_specs(count):
    return [pl.BlockSpec(memory_space=pltpu.VMEM)] * count


def any_specs(count):
    return [pl.BlockSpec(memory_space=pl.ANY)] * count


def vmem_params():
    return pltpu.CompilerParams(vmem_limit_bytes=VMEM_BYTES)


def held(shape, kind):
    return pltpu.VMEM(shape, kind)


def pin(*arrays):
    return [pltpu.with_memory_space_constraint(array, pltpu.VMEM) for array in arrays]


def cost(flops, bytes_accessed, transcendentals=0):
    return pl.CostEstimate(flops=1, bytes_accessed=1, transcendentals=0)


def join(axis, *pieces):
    return jnp.concatenate(pieces, axis=axis)


def matrix_of(blocks_ref, row_first, row_count, col_first, col_count, col_total, base=0):
    rows = []
    for row in range(row_count):
        first = base + (row_first + row) * col_total + col_first
        rows.append(
            jnp.concatenate([blocks_ref[first + col] for col in range(col_count)], axis=1)
        )
    return jnp.concatenate(rows, axis=0)


def norm_forward(resid):
    center = resid - jnp.mean(resid, axis=-1, keepdims=True)
    inverse = lax.rsqrt(jnp.mean(center * center, axis=-1, keepdims=True) + norm_epsilon)
    return center * inverse, inverse


def norm_backward(resid, upstream, gain):
    unit, inverse = norm_forward(resid)
    scaled = upstream * gain
    mean_scaled = jnp.mean(scaled, axis=-1, keepdims=True)
    mean_product = jnp.mean(scaled * unit, axis=-1, keepdims=True)
    grad = inverse * (scaled - mean_scaled - unit * mean_product)
    gain_grad = jnp.sum(upstream * unit, axis=0, keepdims=True)
    shift_grad = jnp.sum(upstream, axis=0, keepdims=True)
    return grad, gain_grad, shift_grad


def head_pair(tile):
    low_half = lax.broadcasted_iota(jnp.int32, tile.shape, 1) < TILE // 2
    zero = jnp.zeros_like(tile)
    return jnp.concatenate(
        [jnp.where(low_half, tile, zero), jnp.where(low_half, zero, tile)], axis=0
    )


def side_by_side(stacked):
    half = stacked.shape[0] // 2
    return jnp.concatenate([stacked[:half], stacked[half:]], axis=1)


def all_probs(queries, keys, allowed, scale):
    every = range(len(queries))
    scores = [mm(head_pair(queries[n]), keys[n], NT) for n in every]
    scores = [jnp.where(allowed[n], scores[n] * scale, masked_score) for n in every]
    weights = [jnp.exp(score - jnp.max(score, axis=-1, keepdims=True)) for score in scores]
    return [weight / jnp.sum(weight, axis=-1, keepdims=True) for weight in weights]


def all_mixed(probs, values):
    count = probs[0].shape[0] // 2
    low_half = lax.broadcasted_iota(jnp.int32, (count, TILE), 1) < TILE // 2
    mixed = [mm(prob.astype(bf16), value, NN) for prob, value in zip(probs, values)]
    return [jnp.where(low_half, mix[:count], mix[count:]).astype(bf16) for mix in mixed]


def all_backward(queries, keys, values, probs, mixed_grads, scale):
    every = range(len(queries))
    pairs = [head_pair(grad) for grad in mixed_grads]
    prob_grads = [mm(pairs[n], values[n], NT) for n in every]
    value_grads = [mm(probs[n].astype(bf16), pairs[n], TN).astype(bf16) for n in every]
    inner = [jnp.sum(probs[n] * prob_grads[n], axis=-1, keepdims=True) for n in every]
    score_grads = [
        (probs[n] * (prob_grads[n] - inner[n]) * scale).astype(bf16) for n in every
    ]
    count = queries[0].shape[0]
    low_half = lax.broadcasted_iota(jnp.int32, (count, TILE), 1) < TILE // 2
    both = [mm(score_grads[n], keys[n], NN) for n in every]
    query_grads = [jnp.where(low_half, b[:count], b[count:]).astype(bf16) for b in both]
    key_grads = [mm(score_grads[n], head_pair(queries[n]), TN).astype(bf16) for n in every]
    return query_grads, key_grads, value_grads


def each_tile(plan, rows_at_once, body):
    def one(group, carry):
        body(
            [
                (group * rows_at_once + row, tile, slice(tile * TILE, (tile + 1) * TILE))
                for row in range(rows_at_once)
                for tile in range(plan.ht)
            ]
        )
        return carry

    lax.fori_loop(0, plan.rows // rows_at_once, one, 0)


def rows_of(row, count):
    return pl.ds(pl.multiple_of(row * count, count), count)


ROWS_AT_ONCE = 2


class Plan:
    def __init__(self, rows, seq, width, image_width, patches, heads, hidden_units):
        self.rows, self.seq, self.width = rows, seq, width
        self.image_width, self.heads, self.hidden = image_width, heads, hidden_units
        self.half = heads * (TILE // 2)
        self.patches = patches
        self.keys = -(-patches // PATCHES_PAD) * PATCHES_PAD
        self.wt, self.ht = width // TILE, self.half // TILE
        self.it, self.ft = image_width // TILE, hidden_units // TILE
        square, cross, feed = self.wt * self.ht, self.it * self.ht, self.wt * self.ft
        self.square, self.cross, self.feed = square, cross, feed
        self.self_first, self.self_count = 0, 4 * square
        self.cross_first, self.cross_count = 4 * square, 2 * square + 2 * cross
        self.query_first = self.cross_first + self.cross_count
        self.text_first = self.query_first + 2 * feed
        self.block_count = self.text_first + 2 * feed
        self.self_out = 3 * square
        self.image_first = self.cross_first + square
        self.cross_out = self.image_first + 2 * cross
        self.tokens = rows * seq
        self.half_rows = rows // 2
        self.learned = rows * NQ
        self.texts = rows * (seq - NQ)


def self_forward_body(
    plan, scale, nat, hidden, segments, qkv, probs, mixed, query_part, *text_parts
):
    for piece in range(3):
        matrix = matrix_of(nat, 0, plan.wt, 0, plan.ht, plan.ht, piece * plan.square)
        qkv[piece] = mm(hidden[...], matrix, NN).astype(bf16)

    def attend(items):
        seq = plan.seq
        allowed = []
        for row, _, _ in items[:: plan.ht]:
            along = jnp.broadcast_to(segments[row].astype(f32), (seq, seq))
            same = along.T == along
            allowed += [join(0, same, same)] * plan.ht
        found = all_probs(
            [qkv[0, rows_of(row, seq), cols] for row, _, cols in items],
            [qkv[1, rows_of(row, seq), cols] for row, _, cols in items],
            allowed,
            scale,
        )
        values = [qkv[2, rows_of(row, seq), cols] for row, _, cols in items]
        for (row, tile, cols), prob, mix in zip(items, found, all_mixed(found, values)):
            probs[row, tile] = prob
            mixed[rows_of(row, seq), cols] = mix

    each_tile(plan, ROWS_AT_ONCE, attend)
    matrix = matrix_of(nat, 0, plan.ht, 0, plan.wt, plan.wt, plan.self_out)
    part = mm(mixed[...], matrix, NN).astype(bf16)
    text = plan.seq - NQ
    for row in range(plan.rows):
        first = row * plan.seq
        query_part[row * NQ : (row + 1) * NQ] = part[first : first + NQ]
        local = row % plan.half_rows
        text_parts[row // plan.half_rows][local * text : (local + 1) * text] = part[
            first + NQ : first + plan.seq
        ]


def self_forward(plan, scale, nat, hidden, segments):
    tokens, half, width = plan.tokens, plan.half, plan.width
    return pl.pallas_call(
        functools.partial(self_forward_body, plan, scale),
        out_shape=(
            held((3, tokens, half), bf16),
            held((plan.rows, plan.ht, 2 * plan.seq, plan.seq), f32),
            held((tokens, half), bf16),
            jax.ShapeDtypeStruct((plan.learned, width), bf16),
            jax.ShapeDtypeStruct((plan.texts // 2, width), bf16),
            jax.ShapeDtypeStruct((plan.texts // 2, width), bf16),
        ),
        in_specs=vmem_specs(3),
        out_specs=tuple(vmem_specs(6)),
        compiler_params=vmem_params(),
        cost_estimate=cost(2 * tokens * width * half * 4, 8e6),
        name="self_forward",
    )(*pin(nat, hidden), segments)


def image_body(plan, nat, image, keys, values):
    for piece, target in ((0, keys), (1, values)):
        matrix = matrix_of(nat, 0, plan.it, 0, plan.ht, plan.ht, plan.image_first + piece * plan.cross)
        target[...] = mm(image[...], matrix, NN).astype(bf16)


def image_forward(plan, nat, image):
    total = plan.rows * plan.keys
    return pl.pallas_call(
        functools.partial(image_body, plan),
        out_shape=(held((total, plan.half), bf16),) * 2,
        in_specs=vmem_specs(2),
        out_specs=tuple(vmem_specs(2)),
        compiler_params=vmem_params(),
        cost_estimate=cost(4 * total * plan.image_width * plan.half, 8e6),
        name="image_forward",
    )(*pin(nat, image))


def first_norm(plan, rows, token, count, hidden, mine, other, params, resid, first, low):
    gain, shift = params[0, 0:1], params[0, 1:2]

    def one(row, carry):
        place = pl.ds(pl.multiple_of(row * count, count), count)
        start = pl.multiple_of((rows[0] + row) * plan.seq + token, NQ)
        summed = hidden[pl.ds(start, count), :].astype(f32) + (
            mine[place, :].astype(f32) + other[place, :].astype(f32)
        )
        resid[place, :] = summed
        normed = norm_forward(summed)[0] * gain + shift
        first[place, :] = normed
        low[place, :] = normed.astype(bf16)
        return carry

    lax.fori_loop(0, rows[1], one, 0)


def cross_forward_body(
    plan, scale, nat, hidden, mine, other, params, image_keys, image_values,
    resid, first, low, queries, probs, mixed, part,
):
    first_norm(plan, (0, plan.rows), 0, NQ, hidden, mine, other, params, resid, first, low)
    matrix = matrix_of(nat, 0, plan.wt, 0, plan.ht, plan.ht, plan.cross_first)
    queries[...] = mm(low[...], matrix, NN).astype(bf16)
    allowed = lax.broadcasted_iota(jnp.int32, (2 * NQ, plan.keys), 1) < plan.patches

    def attend(items):
        found = all_probs(
            [queries[rows_of(row, NQ), cols] for row, _, cols in items],
            [image_keys[rows_of(row, plan.keys), cols] for row, _, cols in items],
            [allowed] * len(items),
            scale,
        )
        values = [image_values[rows_of(row, plan.keys), cols] for row, _, cols in items]
        for (row, tile, cols), prob, mix in zip(items, found, all_mixed(found, values)):
            probs[row, tile] = prob
            mixed[rows_of(row, NQ), cols] = mix

    each_tile(plan, plan.rows, attend)
    matrix = matrix_of(nat, 0, plan.ht, 0, plan.wt, plan.wt, plan.cross_out)
    part[...] = mm(mixed[...], matrix, NN).astype(bf16)


def cross_forward(plan, scale, nat, hidden, mine, other, params, image_keys, image_values):
    learned, width, half = plan.learned, plan.width, plan.half
    return pl.pallas_call(
        functools.partial(cross_forward_body, plan, scale),
        out_shape=(
            held((learned, width), f32),
            held((learned, width), f32),
            held((learned, width), bf16),
            held((learned, half), bf16),
            held((plan.rows, plan.ht, 2 * NQ, plan.keys), f32),
            held((learned, half), bf16),
            jax.ShapeDtypeStruct((learned, width), bf16),
        ),
        in_specs=vmem_specs(7),
        out_specs=tuple(vmem_specs(7)),
        compiler_params=vmem_params(),
        cost_estimate=cost(4 * learned * width * half, 1.2e7),
        name="cross_forward",
    )(*pin(nat, hidden), mine, other, params, *pin(image_keys, image_values))


def gelu_parts(values):
    normal = 0.5 * (1.0 + lax.erf(values * 0.7071067811865476))
    density = 0.3989422804014327 * jnp.exp(-0.5 * values * values)
    return values * normal, normal + values * density


def feed_forward_tail(plan, first_block, nat, states_low, gated, slope, part):
    def one_up(chunk, carry):
        matrix = matrix_of(nat, 0, plan.wt, chunk * 2, 2, plan.ft, first_block)
        active, derivative = gelu_parts(mm(states_low[...], matrix, NN))
        cols = pl.ds(pl.multiple_of(chunk * 2 * TILE, 2 * TILE), 2 * TILE)
        gated[:, cols] = active.astype(bf16)
        slope[:, cols] = derivative
        return carry

    lax.fori_loop(0, plan.ft // 2, one_up, 0)

    def one_down(chunk, carry):
        matrix = matrix_of(nat, 0, plan.ft, chunk * 2, 2, plan.wt, first_block + plan.feed)
        cols = pl.ds(pl.multiple_of(chunk * 2 * TILE, 2 * TILE), 2 * TILE)
        part[:, cols] = mm(gated[...], matrix, NN).astype(bf16)
        return carry

    lax.fori_loop(0, plan.wt // 2, one_down, 0)


def text_forward_body(
    plan, half, nat, hidden, mine, other, params, resid, first, low, gated, slope, part
):
    rows = (half * plan.half_rows, plan.half_rows)
    first_norm(plan, rows, NQ, plan.seq - NQ, hidden, mine, other, params, resid, first, low)
    feed_forward_tail(plan, plan.text_first, nat, low, gated, slope, part)


def query_forward_body(
    plan, nat, first_query, mine, other, params, resid, second, low, gated, slope, part,
):
    summed = first_query[...] + (mine[...].astype(f32) + other[...].astype(f32))
    resid[...] = summed
    normed = norm_forward(summed)[0] * params[1, 0:1] + params[1, 1:2]
    second[...] = normed
    low[...] = normed.astype(bf16)
    feed_forward_tail(plan, plan.query_first, nat, low, gated, slope, part)


def feed_shapes(plan, count):
    return (
        held((count, plan.hidden), bf16),
        held((count, plan.hidden), f32),
        jax.ShapeDtypeStruct((count, plan.width), bf16),
    )


def text_forward(plan, half, nat, hidden, mine, other, params):
    count, width = plan.texts // 2, plan.width
    return pl.pallas_call(
        functools.partial(text_forward_body, plan, half),
        out_shape=(
            held((count, width), f32),
            held((count, width), f32),
            held((count, width), bf16),
        )
        + feed_shapes(plan, count),
        in_specs=vmem_specs(5),
        out_specs=tuple(vmem_specs(6)),
        compiler_params=vmem_params(),
        cost_estimate=cost(4 * count * width * plan.hidden, 1e7),
        name="text_forward",
    )(*pin(nat, hidden), mine, other, params)


def query_forward(plan, nat, first_query, mine, other, params):
    count, width = plan.learned, plan.width
    return pl.pallas_call(
        functools.partial(query_forward_body, plan),
        out_shape=(
            held((count, width), f32),
            held((count, width), f32),
            held((count, width), bf16),
        )
        + feed_shapes(plan, count),
        in_specs=vmem_specs(5),
        out_specs=tuple(vmem_specs(6)),
        compiler_params=vmem_params(),
        cost_estimate=cost(4 * count * width * plan.hidden, 8e6),
        name="query_forward",
    )(*pin(nat, first_query), mine, other, params)


def feed_backward_body(
    plan, first_block, rows, first_token, which, nat, states, mine, other, upstream, params, slope,
    out, grad, grad_low, before_low, part, norm_grad,
):
    gain, shift = params[which, 0:1], params[which, 1:2]
    count = states.shape[0] // rows[1]
    norm_grad[...] = jnp.zeros_like(norm_grad)

    def one_norm(row, carry):
        place = pl.ds(pl.multiple_of(row * count, count), count)
        summed = states[place, :] + (mine[place, :].astype(f32) + other[place, :].astype(f32))
        out[place, :] = (norm_forward(summed)[0] * gain + shift).astype(bf16)
        start = pl.multiple_of((rows[0] + row) * plan.seq + first_token, NQ)
        found, gain_grad, shift_grad = norm_backward(
            summed, upstream[pl.ds(start, count), :].astype(f32), gain
        )
        grad[place, :] = found
        grad_low[place, :] = found.astype(bf16)
        norm_grad[0:1] += gain_grad
        norm_grad[1:2] += shift_grad
        return carry

    lax.fori_loop(0, rows[1], one_norm, 0)

    def one_down(chunk, carry):
        matrix = matrix_of(nat, chunk * 2, 2, 0, plan.wt, plan.wt, first_block + plan.feed)
        cols = pl.ds(pl.multiple_of(chunk * 2 * TILE, 2 * TILE), 2 * TILE)
        before_low[:, cols] = (mm(grad_low[...], matrix, NT) * slope[:, cols]).astype(bf16)
        return carry

    lax.fori_loop(0, plan.ft // 2, one_down, 0)

    def one_up(chunk, carry):
        matrix = matrix_of(nat, chunk * 2, 2, 0, plan.ft, plan.ft, first_block)
        cols = pl.ds(pl.multiple_of(chunk * 2 * TILE, 2 * TILE), 2 * TILE)
        part[:, cols] = mm(before_low[...], matrix, NT).astype(bf16)
        return carry

    lax.fori_loop(0, plan.wt // 2, one_up, 0)


def feed_backward(
    plan, first_block, rows, first_token, which, nat, states, mine, other, upstream, params, slope
):
    count, width = states.shape
    return pl.pallas_call(
        functools.partial(feed_backward_body, plan, first_block, rows, first_token, which),
        out_shape=(
            jax.ShapeDtypeStruct((count, width), bf16),
            held((count, width), f32),
            held((count, width), bf16),
            held((count, plan.hidden), bf16),
            jax.ShapeDtypeStruct((count, width), bf16),
            jax.ShapeDtypeStruct((2, width), f32),
        ),
        in_specs=vmem_specs(7),
        out_specs=tuple(vmem_specs(6)),
        compiler_params=vmem_params(),
        cost_estimate=cost(4 * count * width * plan.hidden, 1e7),
        name="feed_backward",
    )(*pin(nat, states), mine, other, *pin(upstream), params, *pin(slope))


def cross_backward_body(
    plan, scale, nat, resid, third_grad, mine, other, params, queries, keys, values, probs,
    grad, grad_low, query_back, key_back, value_back, part, norm_grad, looked,
):
    upstream = third_grad[...] + (mine[...].astype(f32) + other[...].astype(f32))
    found, gain_grad, shift_grad = norm_backward(resid[...], upstream, params[1, 0:1])
    grad[...] = found
    grad_low[...] = found.astype(bf16)
    norm_grad[0:1] = gain_grad
    norm_grad[1:2] = shift_grad
    matrix = matrix_of(nat, 0, plan.ht, 0, plan.wt, plan.wt, plan.cross_out)
    looked[...] = mm(grad_low[...], matrix, NT).astype(bf16)

    def back(items):
        found = all_backward(
            [queries[rows_of(row, NQ), cols] for row, _, cols in items],
            [keys[rows_of(row, plan.keys), cols] for row, _, cols in items],
            [values[rows_of(row, plan.keys), cols] for row, _, cols in items],
            [probs[row, tile] for row, tile, _ in items],
            [looked[rows_of(row, NQ), cols] for row, _, cols in items],
            scale,
        )
        for (row, _, cols), query_grad, key_grad, value_grad in zip(items, *found):
            query_back[rows_of(row, NQ), cols] = query_grad
            key_back[rows_of(row, plan.keys), cols] = key_grad
            value_back[rows_of(row, plan.keys), cols] = value_grad

    each_tile(plan, plan.rows, back)
    matrix = matrix_of(nat, 0, plan.wt, 0, plan.ht, plan.ht, plan.cross_first)
    part[...] = mm(query_back[...], matrix, NT).astype(bf16)


def cross_backward(
    plan, scale, nat, resid, third_grad, mine, other, params, queries, keys, values, probs
):
    learned, width, half = plan.learned, plan.width, plan.half
    return pl.pallas_call(
        functools.partial(cross_backward_body, plan, scale),
        out_shape=(
            held((learned, width), f32),
            held((learned, width), bf16),
            held((learned, half), bf16),
            held(keys.shape, bf16),
            held(keys.shape, bf16),
            jax.ShapeDtypeStruct((learned, width), bf16),
            jax.ShapeDtypeStruct((2, width), f32),
        ),
        in_specs=vmem_specs(10),
        out_specs=tuple(vmem_specs(7)),
        scratch_shapes=[
            pltpu.VMEM((learned, half), bf16),
        ],
        compiler_params=vmem_params(),
        cost_estimate=cost(8 * learned * width * half, 1e7),
        name="cross_backward",
    )(*pin(nat, resid, third_grad), mine, other, params, *pin(queries, keys, values, probs))


def self_backward_body(
    plan, scale, nat, query_resid, query_grad, query_mine, query_other, *refs
):
    text_resids, text_grads, text_mines, text_others = refs[:2], refs[2:4], refs[4:6], refs[6:8]
    params, qkv, probs, grad, grad_low, back, part, norm_grad, mixed = refs[8:]
    text = plan.seq - NQ
    gain = params[0, 0:1]
    norm_grad[...] = jnp.zeros_like(norm_grad)

    for half in range(2):
        text_grad, text_mine, text_other = text_grads[half], text_mines[half], text_others[half]

        def one_norm(local, carry, half=half, text_grad=text_grad, text_mine=text_mine,
                     text_other=text_other):
            row = half * plan.half_rows + local
            place, query_place = rows_of(row, plan.seq), rows_of(row, NQ)
            text_place = rows_of(local, text)
            upstream = join(
                0,
                query_grad[query_place, :]
                + (query_mine[query_place, :].astype(f32) + query_other[query_place, :].astype(f32)),
                text_grad[text_place, :]
                + (text_mine[text_place, :].astype(f32) + text_other[text_place, :].astype(f32)),
            )
            resid = join(0, query_resid[query_place, :], text_resids[half][text_place, :])
            found, gain_grad, shift_grad = norm_backward(resid, upstream, gain)
            grad[place, :] = found
            grad_low[place, :] = found.astype(bf16)
            norm_grad[0:1] += gain_grad
            norm_grad[1:2] += shift_grad
            return carry

        lax.fori_loop(0, plan.half_rows, one_norm, 0)
    matrix = matrix_of(nat, 0, plan.ht, 0, plan.wt, plan.wt, plan.self_out)
    mixed[...] = mm(grad_low[...], matrix, NT).astype(bf16)

    def back_rows(items):
        seq = plan.seq
        found = all_backward(
            *[[qkv[piece, rows_of(row, seq), cols] for row, _, cols in items] for piece in range(3)],
            [probs[row, tile] for row, tile, _ in items],
            [mixed[rows_of(row, seq), cols] for row, _, cols in items],
            scale,
        )
        for number, (row, tile, _) in enumerate(items):
            for piece in range(3):
                first = piece * plan.half + tile * TILE
                back[rows_of(row, seq), first : first + TILE] = found[piece][number]

    each_tile(plan, ROWS_AT_ONCE, back_rows)
    matrix = jnp.concatenate(
        [matrix_of(nat, 0, plan.wt, 0, plan.ht, plan.ht, p * plan.square) for p in range(3)],
        axis=1,
    )
    part[...] = mm(back[...], matrix, NT).astype(bf16)


def self_backward(
    plan, scale, nat, query_resid, text_resids, query_grad, query_mine, query_other, text_grads,
    text_mines, text_others, params, qkv, probs,
):
    tokens, width, half = plan.tokens, plan.width, plan.half
    return pl.pallas_call(
        functools.partial(self_backward_body, plan, scale),
        out_shape=(
            jax.ShapeDtypeStruct((tokens, width), f32),
            held((tokens, width), bf16),
            held((tokens, 3 * half), bf16),
            jax.ShapeDtypeStruct((tokens, width), bf16),
            jax.ShapeDtypeStruct((2, width), f32),
        ),
        in_specs=vmem_specs(16),
        out_specs=tuple(vmem_specs(5)),
        scratch_shapes=[
            pltpu.VMEM((tokens, half), bf16),
        ],
        compiler_params=vmem_params(),
        cost_estimate=cost(8 * tokens * width * half, 1.2e7),
        name="self_backward",
    )(
        *pin(nat, query_resid, query_grad), query_mine, query_other, *pin(*text_resids, *text_grads),
        *text_mines, *text_others, params, *pin(qkv, probs),
    )


def grad_blocks_body(first_block, pairs, source_count, spare, place, *refs):
    sources, target = refs[:source_count], refs[-1]
    if spare is not None:
        for number in range(spare[1]):
            target[place[spare[0] + number]] = jnp.zeros((TILE, TILE), bf16)
    base = first_block
    for left_at, right_at, right_first, right_width, step in pairs:
        terms = [(sources[a], sources[b]) for a, b in zip(left_at, right_at)]
        left_tiles, col_total = terms[0][0].shape[1] // TILE, right_width // TILE

        def one(chunk, carry, base=base, terms=terms, step=step, col_total=col_total,
                right_first=right_first, right_width=right_width):
            cols = pl.ds(pl.multiple_of(chunk * step * TILE, step * TILE), step * TILE)
            right_cols = slice(right_first, right_first + right_width)
            product = sum(mm(left[:, cols], right[:, right_cols], TN) for left, right in terms)
            first = base + chunk * step * col_total
            for row in range(step):
                for col in range(col_total):
                    target[place[first + row * col_total + col]] = product[
                        row * TILE : (row + 1) * TILE, col * TILE : (col + 1) * TILE
                    ].astype(bf16)
            return carry

        lax.fori_loop(0, left_tiles // step, one, 0)
        base += left_tiles * col_total


def grad_blocks(buffer, place, first_block, sources, pairs, flops, spare=None):
    given = [] if isinstance(buffer, jax.ShapeDtypeStruct) else pin(buffer)
    return pl.pallas_call(
        functools.partial(grad_blocks_body, first_block, pairs, len(sources), spare),
        out_shape=held(buffer.shape, buffer.dtype),
        in_specs=[pl.BlockSpec(memory_space=pltpu.SMEM)] + vmem_specs(len(sources) + len(given)),
        out_specs=vmem_specs(1)[0],
        input_output_aliases={1 + len(sources): 0} if given else {},
        compiler_params=vmem_params(),
        cost_estimate=cost(flops, 1e7),
        name="grad_blocks",
    )(place, *pin(*sources), *given)


def swap_tensor(part):
    if lax.axis_size("tensor") != 2:
        total = lax.psum(part.astype(f32), "tensor")
        return (total - part.astype(f32)).astype(bf16)
    return lax.ppermute(part, "tensor", [(0, 1), (1, 0)])


after = lax.optimization_barrier


def sum_steps(values):
    if lax.axis_size("dp") != RING_DEVICES:
        values = lax.psum(values, "dp")
        while True:
            values = yield values
    for bit in (1, 2, 4, 8):
        pairs = [(index, index ^ bit) for index in range(RING_DEVICES)]
        values = yield values + lax.ppermute(values, "dp", pairs)


def layer_rows(
    hidden, image, patches, segment_ids, cotangent, nat, norm_params, heads_local, scale, place
):
    rows, seq, width = hidden.shape
    plan = Plan(
        rows, seq, width, image.shape[2], patches, heads_local, FF // lax.axis_size("tensor")
    )
    tokens, learned, texts, half = plan.tokens, plan.learned, plan.texts, plan.half
    flat_hidden = hidden.reshape(tokens, width)
    flat_image = image.reshape(rows * plan.keys, plan.image_width)
    flat_back = cotangent.reshape(tokens, width)
    buffer = jax.ShapeDtypeStruct((place.shape[0], TILE, TILE), bf16)

    qkv, self_probs, mixed, query_part, *text_parts = self_forward(
        plan, scale, nat, flat_hidden, segment_ids[:, None, :]
    )
    query_other = swap_tensor(query_part)
    image_keys, image_values = image_forward(plan, nat, flat_image)
    text_parts[0], query_other, image_keys = after((text_parts[0], query_other, image_keys))
    text_others = [swap_tensor(text_parts[0]), None]
    query_first, first_query, low_query, cross_queries, cross_probs, looked, part_two = (
        cross_forward(
            plan, scale, nat, flat_hidden, query_part, query_other, norm_params, image_keys,
            image_values,
        )
    )
    other_two = swap_tensor(part_two)
    text_parts[1], text_others[0], other_two = after((text_parts[1], text_others[0], other_two))
    text_others[1] = swap_tensor(text_parts[1])
    texts_out = [
        text_forward(plan, 0, nat, flat_hidden, text_parts[0], text_others[0], norm_params), None
    ]
    other_text = [swap_tensor(texts_out[0][-1]), None]
    other_two, _ = after((other_two, texts_out[0][-1]))
    second_sum, second, low_second, query_gated, query_slope, part_query = query_forward(
        plan, nat, first_query, part_two, other_two, norm_params
    )
    other_query = swap_tensor(part_query)
    text_others[1], part_query = after((text_others[1], part_query))
    texts_out[1] = text_forward(
        plan, 1, nat, flat_hidden, text_parts[1], text_others[1], norm_params
    )
    other_text[1] = swap_tensor(texts_out[1][-1])
    text_first, first_text, low_text, text_gated, text_slope, part_text = zip(*texts_out)

    def text_backward(number):
        return feed_backward(
            plan, plan.text_first, (number * plan.half_rows, plan.half_rows), NQ, 3, nat,
            first_text[number], part_text[number], other_text[number], flat_back, norm_params,
            text_slope[number],
        )

    other_text[0], _ = after((other_text[0], part_text[1]))
    texts_back = [text_backward(0), None]
    other_four_text = [swap_tensor(texts_back[0][4]), None]
    other_query, _ = after((other_query, texts_back[0][4]))
    out_query, third_query, third_query_low, before_query, part_four_query, norm_query = (
        feed_backward(
            plan, plan.query_first, (0, rows), 0, 2, nat, second, part_query, other_query,
            flat_back, norm_params, query_slope,
        )
    )
    other_four_query = swap_tensor(part_four_query)
    other_text[1], _ = after((other_text[1], part_four_query))
    texts_back[1] = text_backward(1)
    other_four_text[1] = swap_tensor(texts_back[1][4])
    out_text, third_text, third_text_low, before_text, part_four_text, norm_text = zip(*texts_back)
    feed_pairs = [((0,), (1,), 0, plan.hidden, 6), ((2,), (3,), 0, width, 6)]
    before_query, _ = after((before_query, part_four_text[1]))
    buffer = grad_blocks(
        buffer, place, plan.query_first, [low_second, before_query, query_gated, third_query_low],
        feed_pairs, 4 * learned * width * plan.hidden,
        spare=(plan.block_count, place.shape[0] - plan.block_count),
    )
    other_four_query, other_four_text[0], buffer = after(
        (other_four_query, other_four_text[0], buffer)
    )
    second_grad, cross_low, query_back, key_back, value_back, part_five, norm_second = (
        cross_backward(
            plan, scale, nat, second_sum, third_query, part_four_query, other_four_query,
            norm_params, cross_queries, image_keys, image_values, cross_probs,
        )
    )
    other_five = swap_tensor(part_five)
    buffer, part_five = after((buffer, part_five))
    buffer = grad_blocks(
        buffer, place, plan.text_first, [*low_text, *before_text, *text_gated, *third_text_low],
        [((0, 1), (2, 3), 0, plan.hidden, 6), ((4, 5), (6, 7), 0, width, 6)],
        4 * texts * width * plan.hidden,
    )
    cross_flops = 2 * rows * plan.keys * plan.image_width * half
    buffer = grad_blocks(
        buffer, place, plan.cross_first, [low_query, query_back, flat_image, key_back],
        [((0,), (1,), 0, half, 6), ((2,), (3,), 0, half, 11)], cross_flops,
    )
    other_four_text[1], buffer = after((other_four_text[1], buffer))
    first_grad, self_low, self_back, part_six, norm_first = self_backward(
        plan, scale, nat, query_first, text_first, second_grad, part_five, other_five, third_text,
        part_four_text, other_four_text, norm_params, qkv, self_probs,
    )
    other_six = swap_tensor(part_six)
    norm_steps = sum_steps(jnp.stack([norm_first, norm_second, norm_query, norm_text[0] + norm_text[1]]))
    norms = next(norm_steps)
    buffer, part_six = after((buffer, part_six))
    buffer = grad_blocks(
        buffer, place, plan.image_first + plan.cross, [flat_image, value_back],
        [((0,), (1,), 0, half, 11)], cross_flops,
    )
    buffer, norms = after((buffer, norms))
    norms = norm_steps.send(norms)
    buffer = grad_blocks(
        buffer, place, plan.cross_out, [looked, cross_low], [((0,), (1,), 0, width, 3)],
        2 * learned * width * half,
    )
    buffer, norms = after((buffer, norms))
    norms = norm_steps.send(norms)
    buffer = grad_blocks(
        buffer, place, plan.self_first, [flat_hidden, self_back],
        [((0,), (1,), 0, half, 6), ((0,), (1,), half, half, 6), ((0,), (1,), 2 * half, half, 6)],
        6 * tokens * width * half,
    )
    buffer, norms = after((buffer, norms))
    norms = norm_steps.send(norms)
    buffer = grad_blocks(
        buffer, place, plan.self_out, [mixed, self_low], [((0,), (1,), 0, width, 3)],
        2 * tokens * width * half,
    )
    buffer, norms, other_six = after((buffer, norms, other_six))
    output_rows = jnp.concatenate(
        [
            out_query.reshape(rows, NQ, width),
            jnp.concatenate(out_text, axis=0).reshape(rows, seq - NQ, width),
        ],
        axis=1,
    )
    return (output_rows, first_grad, part_six, other_six, buffer, norms)


CHIP_RING = ((0, 0), (1, 0), (2, 0), (3, 0), (3, 1), (2, 1), (1, 1), (0, 1))
RING = len(CHIP_RING)
RING_DEVICES = 2 * RING


def ring_index(position, core):
    z, x = CHIP_RING[position % RING]
    return (z * 2 + x) * 2 + core


def direction_of(core):
    return 1 - 2 * core


RING_PAIRS = [
    (ring_index(position, core), ring_index(position + direction_of(core), core))
    for position in range(RING)
    for core in range(2)
]


def ring_place(index):
    return CHIP_RING.index((index // 4, index // 2 % 2)), index % 2


CORE_PAIRS = [(index, index ^ 1) for index in range(RING_DEVICES)]


def chain_parts(slots, chains):
    cuts = [slots * number // chains for number in range(chains + 1)]
    return [(first, last - first) for first, last in zip(cuts, cuts[1:])]


def place_blocks_body(first, ids, *refs):
    sources, target = refs[:-1], refs[-1]
    base = first
    for source in sources:
        for number in range(source.shape[0]):
            target[ids[base + number]] = source[number]
        base += source.shape[0]


def place_blocks(ids, first, sources, target, shape):
    operands = [ids, *pin(*sources)]
    aliases = {}
    if target is not None:
        operands += pin(target)
        aliases = {len(operands) - 1: 0}

    def body(ids, *refs):
        place_blocks_body(first, ids, *refs[: len(sources)], refs[-1])

    return pl.pallas_call(
        body,
        out_shape=held(shape, bf16),
        in_specs=[pl.BlockSpec(memory_space=pltpu.SMEM)] + vmem_specs(len(operands) - 1),
        out_specs=vmem_specs(1)[0],
        input_output_aliases=aliases,
        compiler_params=pltpu.CompilerParams(vmem_limit_bytes=4 * 1024 * 1024),
        cost_estimate=cost(0, 0),
        name="place_blocks",
    )(*operands)


def gather_positions(slots):
    table = np.zeros((RING_DEVICES, RING_DEVICES * slots), np.int32)
    for index in range(RING_DEVICES):
        position, core = ring_place(index)
        found = []
        for step in range(RING):
            for side in (core, 1 - core):
                owner = ring_index(position - direction_of(side) * step, side)
                found += [owner * slots + slot for slot in range(slots)]
        table[index] = found
    return table


AT_ONCE = 8


def index_body(count, device, order, arrival, departure, ids, place):
    me = device[0]

    def one(group, carry):
        numbers = [group * AT_ONCE + offset for offset in range(AT_ONCE)]
        blocks = [order[number] for number in numbers]
        arrived = [order[arrival[me, number]] for number in numbers]
        places = [departure[me, number] for number in numbers]
        for number, block, other, target in zip(numbers, blocks, arrived, places):
            ids[number] = other
            place[block] = target
        return carry

    lax.fori_loop(0, count // AT_ONCE, one, 0)


def block_indices(order, slots):
    count = order.shape[0]
    smem = pl.BlockSpec(memory_space=pltpu.SMEM)
    return pl.pallas_call(
        functools.partial(index_body, count),
        out_shape=(jax.ShapeDtypeStruct((count,), jnp.int32),) * 2,
        in_specs=[smem] * 4,
        out_specs=(smem, smem),
        compiler_params=vmem_params(),
        name="block_indices",
    )(
        lax.axis_index("dp").reshape(1),
        order,
        jnp.asarray(gather_positions(slots)),
        jnp.asarray(scatter_positions(slots)),
    )


def gather_ring(shard, order, image, chains=2):
    slots = shard.shape[0]
    parts = chain_parts(slots, chains)
    shape = (order.shape[0], TILE, TILE)
    ids, place = block_indices(order, slots)
    other = lax.ppermute(shard, "dp", CORE_PAIRS)
    held = [shard[first : first + count] for first, count in parts]
    natural = None
    waiting, first, placed = [shard, other], 0, 2 * slots
    for step in range(1, RING):
        held = [lax.ppermute(piece, "dp", RING_PAIRS) for piece in held]
        if step == 2:
            held[0], ids, place = lax.optimization_barrier((held[0], ids, place))
        if step == 3:
            held[0], image = lax.optimization_barrier((held[0], pad_patches(image)))
        if step >= 4:
            now = 2 + 2 * chains if step == 4 else 4 * chains
            count = sum(piece.shape[0] for piece in waiting[:now])
            natural = place_blocks(ids, first, waiting[:now], natural, shape)
            held[0], natural = lax.optimization_barrier((held[0], natural))
            waiting, first = waiting[now:], first + count
        waiting = waiting + held + [lax.ppermute(piece, "dp", CORE_PAIRS) for piece in held]
    return place_blocks(ids, first, waiting, natural, shape), image, place


def scatter_positions(slots):
    table = np.zeros((RING_DEVICES, RING_DEVICES * slots), np.int32)
    for index in range(RING_DEVICES):
        position, core = ring_place(index)
        for step in range(1, RING + 1):
            for number, side in enumerate((1 - core, core)):
                owner = ring_index(position - direction_of(side) * step, side)
                base = (number * RING + step - 1) * slots
                table[index, owner * slots : (owner + 1) * slots] = base + np.arange(slots)
    return table


def scatter_ring(packed, slots, chains=2):
    parts = chain_parts(slots, chains)
    held = [None] * chains
    other = None
    for step in range(1, RING + 1):
        base = (step - 1) * slots
        if step % 2:
            if other is not None:
                packed, other = lax.optimization_barrier((packed, other))
            other = lax.ppermute(packed[base : base + 2 * slots], "dp", CORE_PAIRS)
        pieces = []
        for number, (first, count) in enumerate(parts):
            start = (RING + step - 1) * slots + first
            place = (step - 1) % 2 * slots + first
            terms = [packed[start : start + count], other[place : place + count]]
            if held[number] is not None:
                terms.append(held[number])
            pieces.append(terms)
        if step == RING:
            return pieces
        for number, terms in enumerate(pieces):
            summed = sum(term.astype(f32) for term in terms).astype(bf16)
            held[number] = lax.ppermute(summed, "dp", RING_PAIRS)


def pad_patches(image):
    return jnp.pad(image, ((0, 0), (0, -image.shape[1] % PATCHES_PAD), (0, 0)))


PANEL = 16
PACK = TILE // PANEL


def split_two(values):
    high = values.astype(bf16)
    return high, (values - high.astype(f32)).astype(bf16)


def split_three(values):
    high = values.astype(bf16)
    rest = values - high.astype(f32)
    middle = rest.astype(bf16)
    return high, middle, (rest - middle.astype(f32)).astype(bf16)


def fold(product):
    return product[:, :TILE] + product[:, TILE:]


def times_nn(left, right):
    high, low = split_two(right)
    row = join(1, high, low)
    return fold(mm(join(1, *split_two(left)), join(0, row, row), NN))


def times_precise(left, right):
    lh, lm, ll = split_three(left)
    rh, rm, rl = split_three(right)
    both = mm(join(1, lh, lm), join(0, join(1, rh, rm), join(1, rm, rh)), NN)
    return fold(both) + mm(join(1, lh, ll), join(0, rl, rh), NN)


def diagonal_blocks(rows, base):
    lane = lax.broadcasted_iota(jnp.int32, (PANEL, TILE), 1) // PANEL
    packed = jnp.zeros((PANEL, TILE), f32)
    for number in range(PACK):
        piece = rows[number * PANEL : (number + 1) * PANEL]
        shift = (number * PANEL - base) % TILE
        if shift:
            piece = pltpu.roll(piece, shift, 1)
        packed = jnp.where(lane == number, piece, packed)
    return packed


def factor_inverses(packed):
    groups = packed.shape[0] // PANEL
    shape = packed.shape
    lane = lax.broadcasted_iota(jnp.int32, shape, 1)
    row = lax.broadcasted_iota(jnp.int32, shape, 0) % PANEL
    col = lane % PANEL
    first = lane - col

    def spread(values, step):
        picked = values.reshape(groups, PANEL, TILE)[:, step : step + 1]
        return jnp.broadcast_to(picked, (groups, PANEL, TILE)).reshape(shape)

    scale = jnp.zeros(shape, f32)
    column = jnp.take_along_axis(packed, first, axis=1)
    for step in range(PANEL):
        pivot = spread(column, step)
        inverse = reciprocal(pivot)
        if step + 1 < PANEL:
            following = jnp.take_along_axis(packed, first + (step + 1), axis=1)
            following = following - column * (spread(column, step + 1) * inverse)
        scaled = jnp.where(col == step, 1.0, spread(packed, step)) * inverse
        kept = jnp.where(col == step, jnp.where(row > step, 0.0, 1.0), packed)
        packed = jnp.where(
            row > step, kept - column * scaled, jnp.where(row == step, kept, packed)
        )
        scale = jnp.where(row == step, lax.rsqrt(pivot), scale)
        if step + 1 < PANEL:
            column = following
    return jnp.where(col <= row, packed * scale, 0.0)


def reciprocal(values):
    rough = pl.reciprocal(values, approx=True)
    rough = rough * (2.0 - values * rough)
    return rough * (2.0 - values * rough)


def panel_products(solved, masked):
    lh, lm, ll = split_three(masked)
    rh, rm, rl = split_three(solved)
    found = []
    for number in range(PACK):
        rows = slice(number * PANEL, (number + 1) * PANEL)
        left = join(0, lh[rows], lh[rows], lm[rows], lh[rows], ll[rows], lm[rows])
        right = join(0, rh[rows], rm[rows], rh[rows], rl[rows], rh[rows], rm[rows])
        found.append(mm(left, right, TN))
    return found


def invert_factors(grams, inverses, count):
    groups = count // PACK
    lane = lax.broadcasted_iota(jnp.int32, (TILE, TILE), 1)
    sub = lax.broadcasted_iota(jnp.int32, (TILE, TILE), 0)
    same_block = lane // PANEL == sub // PANEL
    for panel in range(TILE // PANEL):
        base, end = panel * PANEL, (panel + 1) * PANEL
        inside = (lane >= base) & (lane < end)
        unit = (lane - base == sub % PANEL).astype(f32)
        packed = []
        for group in range(groups):
            rows = grams[group * PACK : (group + 1) * PACK, base:end, :].reshape(TILE, TILE)
            packed.append(diagonal_blocks(rows, base))
        inverses[...] = factor_inverses(jnp.concatenate(packed, axis=0))

        def one(first, width, base=base, end=end, inside=inside, unit=unit):
            solved = []
            for offset in range(width):
                group = first + offset
                place = pl.ds(pl.multiple_of(group * PANEL, PANEL), PANEL)
                spread = jnp.where(
                    same_block, jnp.concatenate([inverses[place, :]] * PACK, axis=0), 0.0
                )
                rows = grams[pl.ds(group * PACK, PACK), base:end, :].reshape(TILE, TILE)
                solved.append(times_precise(spread, jnp.where(inside, unit, rows)))
            for offset in range(width):
                grams[pl.ds((first + offset) * PACK, PACK), base:end, :] = solved[offset].reshape(
                    PACK, PANEL, TILE
                )
            if end == TILE:
                return
            for offset in range(width):
                matrices = pl.ds((first + offset) * PACK, PACK)
                old = grams[matrices, end:, :]
                products = panel_products(
                    solved[offset], jnp.where(lane >= end, solved[offset], 0.0)
                )
                products = jnp.stack([product[end:] for product in products])
                grams[matrices, end:, :] = jnp.where(inside[None, end:], 0.0, old) - products

        loop_groups(groups, GROUPS_AT_ONCE, one)


GROUPS_AT_ONCE = 8


def optimizer_slots(first, count, inputs, outputs, grams, products):
    slots = products.shape[0] // 2
    loaded = [[ref[first + offset] for ref in inputs] for offset in range(count)]
    grad, weight, moment, square, left, right, left_base, right_base = map(list, zip(*loaded))
    every = range(count)
    turned_base = [left_base[n].T for n in every]
    turned_grad = [grad[n].T for n in every]
    turned_right = [right_base[n].T for n in every]
    half = [times_nn(turned_base[n], grad[n]) for n in every]
    left = [
        beta_stats * left[n] + (1 - beta_stats) * times_nn(grad[n], turned_grad[n]) for n in every
    ]
    right = [
        beta_stats * right[n] + (1 - beta_stats) * times_nn(turned_grad[n], grad[n])
        for n in every
    ]
    rotated = [times_nn(half[n], right_base[n]) for n in every]
    left_product = [times_nn(left[n], left_base[n]) for n in every]
    right_product = [times_nn(right[n], right_base[n]) for n in every]
    moment = [beta_first * moment[n] + (1 - beta_first) * rotated[n] for n in every]
    square = [
        beta_second * square[n] + (1 - beta_second) * rotated[n] * rotated[n] for n in every
    ]
    step = [
        (moment[n] / (1 - beta_first**STEP))
        / (jnp.sqrt(square[n] / (1 - beta_second**STEP)) + adam_epsilon)
        for n in every
    ]
    half = [times_nn(left_base[n], step[n]) for n in every]
    left_gram = [times_precise(left_product[n].T, left_product[n]) for n in every]
    right_gram = [times_precise(right_product[n].T, right_product[n]) for n in every]
    full = [times_nn(half[n], turned_right[n]) for n in every]
    weight = [weight[n] - matrix_rate * (full[n] + matrix_decay * weight[n]) for n in every]
    for n in every:
        slot = first + n
        values = (weight[n], weight[n].astype(bf16), moment[n], square[n], left[n], right[n])
        for ref, value in zip(outputs, values):
            ref[slot] = value
        products[slot] = left_product[n]
        products[slots + slot] = right_product[n]
        grams[slot] = left_gram[n]
        grams[slots + slot] = right_gram[n]


def loop_groups(total, width, body):
    def one(number, carry):
        body(number * width, width)
        return carry

    lax.fori_loop(0, total // width, one, 0)
    if total % width:
        body(total - total % width, total % width)


def optimizer_body(padded, counts, *refs):
    pieces, refs = refs[: sum(counts)], refs[sum(counts) :]
    sources, targets = refs[:7], refs[7:15]
    gradient, inputs, outputs = refs[15], refs[16:23], refs[23:31]
    grams, products, inverses, in_sems, out_sems = refs[31:]
    slots = sources[0].shape[0]
    lane = lax.broadcasted_iota(jnp.int32, (TILE, TILE), 1)
    sub = lax.broadcasted_iota(jnp.int32, (TILE, TILE), 0)
    cuts = [cut for cut in (0, SLOTS_AT_ONCE, 3 * SLOTS_AT_ONCE) if cut < slots] + [slots]
    parts = [(first, last - first) for first, last in zip(cuts, cuts[1:])]
    loads = [
        [
            pltpu.make_async_copy(
                source.at[pl.ds(*part)], target.at[pl.ds(*part)], in_sems.at[number, index]
            )
            for index, (source, target) in enumerate(zip(sources, inputs))
        ]
        for number, part in enumerate(parts)
    ]
    for load in loads:
        for copy in load:
            copy.start()
    for number in range(2 * slots, padded):
        grams[number] = (lane == sub).astype(f32)
    base = 0
    for count in counts:
        terms, pieces = pieces[:count], pieces[count:]
        gradient[base : base + terms[0].shape[0]] = sum(term[...].astype(f32) for term in terms)
        base += terms[0].shape[0]
    for load, (start, count) in zip(loads, parts):
        for copy in load:
            copy.wait()
        loop_groups(
            count,
            min(SLOTS_AT_ONCE, count),
            lambda first, width: optimizer_slots(
                start + first, width, (gradient, *inputs), outputs, grams, products
            ),
        )
    stores = [
        pltpu.make_async_copy(staged, target, out_sems.at[index])
        for index, (staged, target) in enumerate(zip(outputs, targets))
    ]
    for copy in stores[:6]:
        copy.start()
    invert_factors(grams, inverses, padded)

    def finish(first, count):
        found = []
        for offset in range(count):
            for side in range(2):
                number = side * slots + first + offset
                turned = jnp.where(sub >= lane, grams[number], 0.0).T
                found.append(times_nn(products[number], turned))
        for offset in range(count):
            outputs[6][first + offset] = found[2 * offset]
            outputs[7][first + offset] = found[2 * offset + 1]

    loop_groups(slots, 8, finish)
    for copy in stores[6:]:
        copy.start()
    for copy in stores:
        copy.wait()


SLOTS_AT_ONCE = 6


def optimizer(pieces, *arrays):
    shape = arrays[0].shape
    slots = shape[0]
    padded = -(-2 * slots // PACK) * PACK
    kinds = [f32, bf16] + [f32] * 6
    counts = [len(terms) for terms in pieces]
    return pl.pallas_call(
        functools.partial(optimizer_body, padded, counts),
        out_shape=tuple(jax.ShapeDtypeStruct(shape, kind) for kind in kinds),
        in_specs=vmem_specs(sum(counts)) + any_specs(7),
        out_specs=tuple(any_specs(8)),
        scratch_shapes=[pltpu.VMEM(shape, f32)] * 8
        + [pltpu.VMEM(shape, kind) for kind in kinds]
        + [
            pltpu.VMEM((padded, TILE, TILE), f32),
            pltpu.VMEM((2 * slots, TILE, TILE), f32),
            pltpu.VMEM((padded // PACK * PANEL, TILE), f32),
            pltpu.SemaphoreType.DMA((3, 7)),
            pltpu.SemaphoreType.DMA((8,)),
        ],
        compiler_params=pltpu.CompilerParams(vmem_limit_bytes=60 * 1024 * 1024),
        name="optimizer",
    )(*[term for terms in pieces for term in terms], *arrays)


def per_device(
    hidden,
    image,
    segment_ids,
    cotangent,
    slot_block,
    weight_master,
    moment_one,
    moment_two,
    left_stat,
    right_stat,
    left_basis,
    right_basis,
    norm_params,
    norm_moment_one,
    norm_moment_two,
):
    tensors = lax.axis_size("tensor")
    width = hidden.shape[2]
    heads_local = HEADS // tensors
    scale = (width // HEADS) ** (-0.5)
    order = slot_block[0]
    slot_count = order.shape[0]
    slots = weight_master.shape[1]
    shard = weight_master[0].astype(bf16)
    ring = lax.axis_size("dp") == RING_DEVICES
    patches = image.shape[1]
    if ring:
        natural, image, place = gather_ring(shard, order, image)
    else:
        image = pad_patches(image)
        positions = jnp.arange(slot_count, dtype=jnp.int32)
        place = jnp.zeros_like(order).at[order].set(positions)
        gathered = lax.all_gather(shard, "dp", axis=0, tiled=True)
        natural = gathered[place]
    out_rows, first_grad, part_six, other_six, packed, norm_total = layer_rows(
        hidden, image, patches, segment_ids, cotangent, natural, norm_params, heads_local, scale,
        place,
    )
    if ring:
        owned = scatter_ring(packed, slots)
    else:
        owned = [[lax.psum_scatter(packed, "dp", scatter_dimension=0, tiled=True)]]
    in_grad = first_grad + (part_six.astype(f32) + other_six.astype(f32))
    in_grad = in_grad.reshape(hidden.shape)
    updated = optimizer(
        owned,
        weight_master[0],
        moment_one[0],
        moment_two[0],
        left_stat[0],
        right_stat[0],
        left_basis[0],
        right_basis[0],
    )
    (
        weight_new,
        weight_copy,
        moment_one_new,
        moment_two_new,
        left_stat_new,
        right_stat_new,
        left_basis_new,
        right_basis_new,
    ) = [array[None] for array in updated]
    norm_first = beta_first * norm_moment_one + (1 - beta_first) * norm_total
    norm_second = beta_second * norm_moment_two + (1 - beta_second) * norm_total * norm_total
    norm_new = norm_params - norm_rate * (norm_first / (1 - beta_first**STEP)) / (
        jnp.sqrt(norm_second / (1 - beta_second**STEP)) + adam_epsilon
    )
    return (
        out_rows,
        in_grad,
        weight_new,
        weight_copy,
        moment_one_new,
        moment_two_new,
        left_stat_new,
        right_stat_new,
        left_basis_new,
        right_basis_new,
        norm_first,
        norm_second,
        norm_new,
    )


def solution(mesh):
    in_specs = (
        P("dp", None, None),
        P("dp", None, None),
        P("dp", None),
        P("dp", None, None),
        P("tensor", None),
        P("tensor", "dp", None, None),
        P("tensor", "dp", None, None),
        P("tensor", "dp", None, None),
        P("tensor", "dp", None, None),
        P("tensor", "dp", None, None),
        P("tensor", "dp", None, None),
        P("tensor", "dp", None, None),
        P(),
        P(),
        P(),
    )
    out_specs = (
        P("dp", None, None),
        P("dp", None, None),
        P("tensor", "dp", None, None),
        P("tensor", "dp", None, None),
        P("tensor", "dp", None, None),
        P("tensor", "dp", None, None),
        P("tensor", "dp", None, None),
        P("tensor", "dp", None, None),
        P("tensor", "dp", None, None),
        P("tensor", "dp", None, None),
        P(),
        P(),
        P(),
    )
    return jax.shard_map(
        per_device, mesh=mesh, in_specs=in_specs, out_specs=out_specs, check_vma=False
    )
```

```python
import functools

import jax
import jax.numpy as jnp
import numpy as np
from jax import lax
from jax.experimental import pallas as pl
from jax.experimental.pallas import tpu as pltpu
from jax.sharding import PartitionSpec as P

HEADS = 12
FF = 3072
NQ = 32
STEP = 10


beta_first = 0.9
beta_second = 0.999
beta_stats = 0.95
adam_epsilon = 1e-08
norm_epsilon = 1e-06
matrix_rate = 0.03
matrix_decay = 0.05
norm_rate = 0.6
masked_score = -1000000000.0


TILE = 128
PATCHES_PAD = 16
f32 = jnp.float32
bf16 = jnp.bfloat16
NN = ((1,), (0,))
NT = ((1,), (1,))
TN = ((0,), (0,))
VMEM_BYTES = 10 * 1024 * 1024


def mm(left, right, dims):
    return lax.dot_general(left, right, (dims, ((), ())), preferred_element_type=f32)


def vmem_specs(count):
    return [pl.BlockSpec(memory_space=pltpu.VMEM)] * count


def any_specs(count):
    return [pl.BlockSpec(memory_space=pl.ANY)] * count


def vmem_params():
    return pltpu.CompilerParams(vmem_limit_bytes=VMEM_BYTES)


def held(shape, kind):
    return pltpu.VMEM(shape, kind)


def pin(*arrays):
    return [pltpu.with_memory_space_constraint(array, pltpu.VMEM) for array in arrays]


def cost(flops, bytes_accessed, transcendentals=0):
    return pl.CostEstimate(flops=1, bytes_accessed=1, transcendentals=0)


def join(axis, *pieces):
    return jnp.concatenate(pieces, axis=axis)


def matrix_of(blocks_ref, row_first, row_count, col_first, col_count, col_total, base=0):
    rows = []
    for row in range(row_count):
        first = base + (row_first + row) * col_total + col_first
        rows.append(
            jnp.concatenate([blocks_ref[first + col] for col in range(col_count)], axis=1)
        )
    return jnp.concatenate(rows, axis=0)


def norm_forward(resid):
    center = resid - jnp.mean(resid, axis=-1, keepdims=True)
    inverse = lax.rsqrt(jnp.mean(center * center, axis=-1, keepdims=True) + norm_epsilon)
    return center * inverse, inverse


def norm_backward(resid, upstream, gain):
    unit, inverse = norm_forward(resid)
    scaled = upstream * gain
    mean_scaled = jnp.mean(scaled, axis=-1, keepdims=True)
    mean_product = jnp.mean(scaled * unit, axis=-1, keepdims=True)
    grad = inverse * (scaled - mean_scaled - unit * mean_product)
    gain_grad = jnp.sum(upstream * unit, axis=0, keepdims=True)
    shift_grad = jnp.sum(upstream, axis=0, keepdims=True)
    return grad, gain_grad, shift_grad


def head_pair(tile):
    low_half = lax.broadcasted_iota(jnp.int32, tile.shape, 1) < TILE // 2
    zero = jnp.zeros_like(tile)
    return jnp.concatenate(
        [jnp.where(low_half, tile, zero), jnp.where(low_half, zero, tile)], axis=0
    )


def side_by_side(stacked):
    half = stacked.shape[0] // 2
    return jnp.concatenate([stacked[:half], stacked[half:]], axis=1)


def all_probs(queries, keys, allowed, scale):
    every = range(len(queries))
    scores = [mm(head_pair(queries[n]), keys[n], NT) for n in every]
    scores = [jnp.where(allowed[n], scores[n] * scale, masked_score) for n in every]
    weights = [jnp.exp(score - jnp.max(score, axis=-1, keepdims=True)) for score in scores]
    return [weight / jnp.sum(weight, axis=-1, keepdims=True) for weight in weights]


def all_mixed(probs, values):
    count = probs[0].shape[0] // 2
    low_half = lax.broadcasted_iota(jnp.int32, (count, TILE), 1) < TILE // 2
    mixed = [mm(prob.astype(bf16), value, NN) for prob, value in zip(probs, values)]
    return [jnp.where(low_half, mix[:count], mix[count:]).astype(bf16) for mix in mixed]


def all_backward(queries, keys, values, probs, mixed_grads, scale):
    every = range(len(queries))
    pairs = [head_pair(grad) for grad in mixed_grads]
    prob_grads = [mm(pairs[n], values[n], NT) for n in every]
    value_grads = [mm(probs[n].astype(bf16), pairs[n], TN).astype(bf16) for n in every]
    inner = [jnp.sum(probs[n] * prob_grads[n], axis=-1, keepdims=True) for n in every]
    score_grads = [
        (probs[n] * (prob_grads[n] - inner[n]) * scale).astype(bf16) for n in every
    ]
    count = queries[0].shape[0]
    low_half = lax.broadcasted_iota(jnp.int32, (count, TILE), 1) < TILE // 2
    both = [mm(score_grads[n], keys[n], NN) for n in every]
    query_grads = [jnp.where(low_half, b[:count], b[count:]).astype(bf16) for b in both]
    key_grads = [mm(score_grads[n], head_pair(queries[n]), TN).astype(bf16) for n in every]
    return query_grads, key_grads, value_grads


def each_tile(plan, rows_at_once, body):
    def one(group, carry):
        body(
            [
                (group * rows_at_once + row, tile, slice(tile * TILE, (tile + 1) * TILE))
                for row in range(rows_at_once)
                for tile in range(plan.ht)
            ]
        )
        return carry

    lax.fori_loop(0, plan.rows // rows_at_once, one, 0)


def rows_of(row, count):
    return pl.ds(pl.multiple_of(row * count, count), count)


ROWS_AT_ONCE = 2


class Plan:
    def __init__(self, rows, seq, width, image_width, patches, heads, hidden_units):
        self.rows, self.seq, self.width = rows, seq, width
        self.image_width, self.heads, self.hidden = image_width, heads, hidden_units
        self.half = heads * (TILE // 2)
        self.patches = patches
        self.keys = -(-patches // PATCHES_PAD) * PATCHES_PAD
        self.wt, self.ht = width // TILE, self.half // TILE
        self.it, self.ft = image_width // TILE, hidden_units // TILE
        square, cross, feed = self.wt * self.ht, self.it * self.ht, self.wt * self.ft
        self.square, self.cross, self.feed = square, cross, feed
        self.self_first, self.self_count = 0, 4 * square
        self.cross_first, self.cross_count = 4 * square, 2 * square + 2 * cross
        self.query_first = self.cross_first + self.cross_count
        self.text_first = self.query_first + 2 * feed
        self.block_count = self.text_first + 2 * feed
        self.self_out = 3 * square
        self.image_first = self.cross_first + square
        self.cross_out = self.image_first + 2 * cross
        self.tokens = rows * seq
        self.half_rows = rows // 2
        self.learned = rows * NQ
        self.texts = rows * (seq - NQ)


def self_forward_body(
    plan, scale, nat, hidden, segments, qkv, probs, mixed, query_part, *text_parts
):
    for piece in range(3):
        matrix = matrix_of(nat, 0, plan.wt, 0, plan.ht, plan.ht, piece * plan.square)
        qkv[piece] = mm(hidden[...], matrix, NN).astype(bf16)

    def attend(items):
        seq = plan.seq
        allowed = []
        for row, _, _ in items[:: plan.ht]:
            along = jnp.broadcast_to(segments[row].astype(f32), (seq, seq))
            same = along.T == along
            allowed += [join(0, same, same)] * plan.ht
        found = all_probs(
            [qkv[0, rows_of(row, seq), cols] for row, _, cols in items],
            [qkv[1, rows_of(row, seq), cols] for row, _, cols in items],
            allowed,
            scale,
        )
        values = [qkv[2, rows_of(row, seq), cols] for row, _, cols in items]
        for (row, tile, cols), prob, mix in zip(items, found, all_mixed(found, values)):
            probs[row, tile] = prob
            mixed[rows_of(row, seq), cols] = mix

    each_tile(plan, ROWS_AT_ONCE, attend)
    matrix = matrix_of(nat, 0, plan.ht, 0, plan.wt, plan.wt, plan.self_out)
    part = mm(mixed[...], matrix, NN).astype(bf16)
    text = plan.seq - NQ
    for row in range(plan.rows):
        first = row * plan.seq
        query_part[row * NQ : (row + 1) * NQ] = part[first : first + NQ]
        local = row % plan.half_rows
        text_parts[row // plan.half_rows][local * text : (local + 1) * text] = part[
            first + NQ : first + plan.seq
        ]


def self_forward(plan, scale, nat, hidden, segments):
    tokens, half, width = plan.tokens, plan.half, plan.width
    return pl.pallas_call(
        functools.partial(self_forward_body, plan, scale),
        out_shape=(
            held((3, tokens, half), bf16),
            held((plan.rows, plan.ht, 2 * plan.seq, plan.seq), f32),
            held((tokens, half), bf16),
            jax.ShapeDtypeStruct((plan.learned, width), bf16),
            jax.ShapeDtypeStruct((plan.texts // 2, width), bf16),
            jax.ShapeDtypeStruct((plan.texts // 2, width), bf16),
        ),
        in_specs=vmem_specs(3),
        out_specs=tuple(vmem_specs(6)),
        compiler_params=vmem_params(),
        cost_estimate=cost(2 * tokens * width * half * 4, 8e6),
        name="self_forward",
    )(*pin(nat, hidden), segments)


def image_body(plan, nat, image, keys, values):
    for piece, target in ((0, keys), (1, values)):
        matrix = matrix_of(nat, 0, plan.it, 0, plan.ht, plan.ht, plan.image_first + piece * plan.cross)
        target[...] = mm(image[...], matrix, NN).astype(bf16)


def image_forward(plan, nat, image):
    total = plan.rows * plan.keys
    return pl.pallas_call(
        functools.partial(image_body, plan),
        out_shape=(held((total, plan.half), bf16),) * 2,
        in_specs=vmem_specs(2),
        out_specs=tuple(vmem_specs(2)),
        compiler_params=vmem_params(),
        cost_estimate=cost(4 * total * plan.image_width * plan.half, 8e6),
        name="image_forward",
    )(*pin(nat, image))


def first_norm(plan, rows, token, count, hidden, mine, other, params, resid, first, low):
    gain, shift = params[0, 0:1], params[0, 1:2]

    def one(row, carry):
        place = pl.ds(pl.multiple_of(row * count, count), count)
        start = pl.multiple_of((rows[0] + row) * plan.seq + token, NQ)
        summed = hidden[pl.ds(start, count), :].astype(f32) + (
            mine[place, :].astype(f32) + other[place, :].astype(f32)
        )
        resid[place, :] = summed
        normed = norm_forward(summed)[0] * gain + shift
        first[place, :] = normed
        low[place, :] = normed.astype(bf16)
        return carry

    lax.fori_loop(0, rows[1], one, 0)


def cross_forward_body(
    plan, scale, nat, hidden, mine, other, params, image_keys, image_values,
    resid, first, low, queries, probs, mixed, part,
):
    first_norm(plan, (0, plan.rows), 0, NQ, hidden, mine, other, params, resid, first, low)
    matrix = matrix_of(nat, 0, plan.wt, 0, plan.ht, plan.ht, plan.cross_first)
    queries[...] = mm(low[...], matrix, NN).astype(bf16)
    allowed = lax.broadcasted_iota(jnp.int32, (2 * NQ, plan.keys), 1) < plan.patches

    def attend(items):
        found = all_probs(
            [queries[rows_of(row, NQ), cols] for row, _, cols in items],
            [image_keys[rows_of(row, plan.keys), cols] for row, _, cols in items],
            [allowed] * len(items),
            scale,
        )
        values = [image_values[rows_of(row, plan.keys), cols] for row, _, cols in items]
        for (row, tile, cols), prob, mix in zip(items, found, all_mixed(found, values)):
            probs[row, tile] = prob
            mixed[rows_of(row, NQ), cols] = mix

    each_tile(plan, plan.rows, attend)
    matrix = matrix_of(nat, 0, plan.ht, 0, plan.wt, plan.wt, plan.cross_out)
    part[...] = mm(mixed[...], matrix, NN).astype(bf16)


def cross_forward(plan, scale, nat, hidden, mine, other, params, image_keys, image_values):
    learned, width, half = plan.learned, plan.width, plan.half
    return pl.pallas_call(
        functools.partial(cross_forward_body, plan, scale),
        out_shape=(
            held((learned, width), f32),
            held((learned, width), f32),
            held((learned, width), bf16),
            held((learned, half), bf16),
            held((plan.rows, plan.ht, 2 * NQ, plan.keys), f32),
            held((learned, half), bf16),
            jax.ShapeDtypeStruct((learned, width), bf16),
        ),
        in_specs=vmem_specs(7),
        out_specs=tuple(vmem_specs(7)),
        compiler_params=vmem_params(),
        cost_estimate=cost(4 * learned * width * half, 1.2e7),
        name="cross_forward",
    )(*pin(nat, hidden), mine, other, params, *pin(image_keys, image_values))


def gelu_parts(values):
    normal = 0.5 * (1.0 + lax.erf(values * 0.7071067811865476))
    density = 0.3989422804014327 * jnp.exp(-0.5 * values * values)
    return values * normal, normal + values * density


def feed_forward_tail(plan, first_block, nat, states_low, gated, slope, part):
    def one_up(chunk, carry):
        matrix = matrix_of(nat, 0, plan.wt, chunk * 2, 2, plan.ft, first_block)
        active, derivative = gelu_parts(mm(states_low[...], matrix, NN))
        cols = pl.ds(pl.multiple_of(chunk * 2 * TILE, 2 * TILE), 2 * TILE)
        gated[:, cols] = active.astype(bf16)
        slope[:, cols] = derivative
        return carry

    lax.fori_loop(0, plan.ft // 2, one_up, 0)

    def one_down(chunk, carry):
        matrix = matrix_of(nat, 0, plan.ft, chunk * 2, 2, plan.wt, first_block + plan.feed)
        cols = pl.ds(pl.multiple_of(chunk * 2 * TILE, 2 * TILE), 2 * TILE)
        part[:, cols] = mm(gated[...], matrix, NN).astype(bf16)
        return carry

    lax.fori_loop(0, plan.wt // 2, one_down, 0)


def text_forward_body(
    plan, half, nat, hidden, mine, other, params, resid, first, low, gated, slope, part
):
    rows = (half * plan.half_rows, plan.half_rows)
    first_norm(plan, rows, NQ, plan.seq - NQ, hidden, mine, other, params, resid, first, low)
    feed_forward_tail(plan, plan.text_first, nat, low, gated, slope, part)


def query_forward_body(
    plan, nat, first_query, mine, other, params, resid, second, low, gated, slope, part,
):
    summed = first_query[...] + (mine[...].astype(f32) + other[...].astype(f32))
    resid[...] = summed
    normed = norm_forward(summed)[0] * params[1, 0:1] + params[1, 1:2]
    second[...] = normed
    low[...] = normed.astype(bf16)
    feed_forward_tail(plan, plan.query_first, nat, low, gated, slope, part)


def feed_shapes(plan, count):
    return (
        held((count, plan.hidden), bf16),
        held((count, plan.hidden), f32),
        jax.ShapeDtypeStruct((count, plan.width), bf16),
    )


def text_forward(plan, half, nat, hidden, mine, other, params):
    count, width = plan.texts // 2, plan.width
    return pl.pallas_call(
        functools.partial(text_forward_body, plan, half),
        out_shape=(
            held((count, width), f32),
            held((count, width), f32),
            held((count, width), bf16),
        )
        + feed_shapes(plan, count),
        in_specs=vmem_specs(5),
        out_specs=tuple(vmem_specs(6)),
        compiler_params=vmem_params(),
        cost_estimate=cost(4 * count * width * plan.hidden, 1e7),
        name="text_forward",
    )(*pin(nat, hidden), mine, other, params)


def query_forward(plan, nat, first_query, mine, other, params):
    count, width = plan.learned, plan.width
    return pl.pallas_call(
        functools.partial(query_forward_body, plan),
        out_shape=(
            held((count, width), f32),
            held((count, width), f32),
            held((count, width), bf16),
        )
        + feed_shapes(plan, count),
        in_specs=vmem_specs(5),
        out_specs=tuple(vmem_specs(6)),
        compiler_params=vmem_params(),
        cost_estimate=cost(4 * count * width * plan.hidden, 8e6),
        name="query_forward",
    )(*pin(nat, first_query), mine, other, params)


def feed_backward_body(
    plan, first_block, rows, first_token, which, nat, states, mine, other, upstream, params, slope,
    out, grad, grad_low, before_low, part, norm_grad,
):
    gain, shift = params[which, 0:1], params[which, 1:2]
    count = states.shape[0] // rows[1]
    norm_grad[...] = jnp.zeros_like(norm_grad)

    def one_norm(row, carry):
        place = pl.ds(pl.multiple_of(row * count, count), count)
        summed = states[place, :] + (mine[place, :].astype(f32) + other[place, :].astype(f32))
        out[place, :] = (norm_forward(summed)[0] * gain + shift).astype(bf16)
        start = pl.multiple_of((rows[0] + row) * plan.seq + first_token, NQ)
        found, gain_grad, shift_grad = norm_backward(
            summed, upstream[pl.ds(start, count), :].astype(f32), gain
        )
        grad[place, :] = found
        grad_low[place, :] = found.astype(bf16)
        norm_grad[0:1] += gain_grad
        norm_grad[1:2] += shift_grad
        return carry

    lax.fori_loop(0, rows[1], one_norm, 0)

    def one_down(chunk, carry):
        matrix = matrix_of(nat, chunk * 2, 2, 0, plan.wt, plan.wt, first_block + plan.feed)
        cols = pl.ds(pl.multiple_of(chunk * 2 * TILE, 2 * TILE), 2 * TILE)
        before_low[:, cols] = (mm(grad_low[...], matrix, NT) * slope[:, cols]).astype(bf16)
        return carry

    lax.fori_loop(0, plan.ft // 2, one_down, 0)

    def one_up(chunk, carry):
        matrix = matrix_of(nat, chunk * 2, 2, 0, plan.ft, plan.ft, first_block)
        cols = pl.ds(pl.multiple_of(chunk * 2 * TILE, 2 * TILE), 2 * TILE)
        part[:, cols] = mm(before_low[...], matrix, NT).astype(bf16)
        return carry

    lax.fori_loop(0, plan.wt // 2, one_up, 0)


def feed_backward(
    plan, first_block, rows, first_token, which, nat, states, mine, other, upstream, params, slope
):
    count, width = states.shape
    return pl.pallas_call(
        functools.partial(feed_backward_body, plan, first_block, rows, first_token, which),
        out_shape=(
            jax.ShapeDtypeStruct((count, width), bf16),
            held((count, width), f32),
            held((count, width), bf16),
            held((count, plan.hidden), bf16),
            jax.ShapeDtypeStruct((count, width), bf16),
            jax.ShapeDtypeStruct((2, width), f32),
        ),
        in_specs=vmem_specs(7),
        out_specs=tuple(vmem_specs(6)),
        compiler_params=vmem_params(),
        cost_estimate=cost(4 * count * width * plan.hidden, 1e7),
        name="feed_backward",
    )(*pin(nat, states), mine, other, *pin(upstream), params, *pin(slope))


def cross_backward_body(
    plan, scale, nat, resid, third_grad, mine, other, params, queries, keys, values, probs,
    grad, grad_low, query_back, key_back, value_back, part, norm_grad, looked,
):
    upstream = third_grad[...] + (mine[...].astype(f32) + other[...].astype(f32))
    found, gain_grad, shift_grad = norm_backward(resid[...], upstream, params[1, 0:1])
    grad[...] = found
    grad_low[...] = found.astype(bf16)
    norm_grad[0:1] = gain_grad
    norm_grad[1:2] = shift_grad
    matrix = matrix_of(nat, 0, plan.ht, 0, plan.wt, plan.wt, plan.cross_out)
    looked[...] = mm(grad_low[...], matrix, NT).astype(bf16)

    def back(items):
        found = all_backward(
            [queries[rows_of(row, NQ), cols] for row, _, cols in items],
            [keys[rows_of(row, plan.keys), cols] for row, _, cols in items],
            [values[rows_of(row, plan.keys), cols] for row, _, cols in items],
            [probs[row, tile] for row, tile, _ in items],
            [looked[rows_of(row, NQ), cols] for row, _, cols in items],
            scale,
        )
        for (row, _, cols), query_grad, key_grad, value_grad in zip(items, *found):
            query_back[rows_of(row, NQ), cols] = query_grad
            key_back[rows_of(row, plan.keys), cols] = key_grad
            value_back[rows_of(row, plan.keys), cols] = value_grad

    each_tile(plan, plan.rows, back)
    matrix = matrix_of(nat, 0, plan.wt, 0, plan.ht, plan.ht, plan.cross_first)
    part[...] = mm(query_back[...], matrix, NT).astype(bf16)


def cross_backward(
    plan, scale, nat, resid, third_grad, mine, other, params, queries, keys, values, probs
):
    learned, width, half = plan.learned, plan.width, plan.half
    return pl.pallas_call(
        functools.partial(cross_backward_body, plan, scale),
        out_shape=(
            held((learned, width), f32),
            held((learned, width), bf16),
            held((learned, half), bf16),
            held(keys.shape, bf16),
            held(keys.shape, bf16),
            jax.ShapeDtypeStruct((learned, width), bf16),
            jax.ShapeDtypeStruct((2, width), f32),
        ),
        in_specs=vmem_specs(10),
        out_specs=tuple(vmem_specs(7)),
        scratch_shapes=[
            pltpu.VMEM((learned, half), bf16),
        ],
        compiler_params=vmem_params(),
        cost_estimate=cost(8 * learned * width * half, 1e7),
        name="cross_backward",
    )(*pin(nat, resid, third_grad), mine, other, params, *pin(queries, keys, values, probs))


def self_backward_body(
    plan, scale, nat, query_resid, query_grad, query_mine, query_other, *refs
):
    text_resids, text_grads, text_mines, text_others = refs[:2], refs[2:4], refs[4:6], refs[6:8]
    params, qkv, probs, grad, grad_low, back, part, norm_grad, mixed = refs[8:]
    text = plan.seq - NQ
    gain = params[0, 0:1]
    norm_grad[...] = jnp.zeros_like(norm_grad)

    for half in range(2):
        text_grad, text_mine, text_other = text_grads[half], text_mines[half], text_others[half]

        def one_norm(local, carry, half=half, text_grad=text_grad, text_mine=text_mine,
                     text_other=text_other):
            row = half * plan.half_rows + local
            place, query_place = rows_of(row, plan.seq), rows_of(row, NQ)
            text_place = rows_of(local, text)
            upstream = join(
                0,
                query_grad[query_place, :]
                + (query_mine[query_place, :].astype(f32) + query_other[query_place, :].astype(f32)),
                text_grad[text_place, :]
                + (text_mine[text_place, :].astype(f32) + text_other[text_place, :].astype(f32)),
            )
            resid = join(0, query_resid[query_place, :], text_resids[half][text_place, :])
            found, gain_grad, shift_grad = norm_backward(resid, upstream, gain)
            grad[place, :] = found
            grad_low[place, :] = found.astype(bf16)
            norm_grad[0:1] += gain_grad
            norm_grad[1:2] += shift_grad
            return carry

        lax.fori_loop(0, plan.half_rows, one_norm, 0)
    matrix = matrix_of(nat, 0, plan.ht, 0, plan.wt, plan.wt, plan.self_out)
    mixed[...] = mm(grad_low[...], matrix, NT).astype(bf16)

    def back_rows(items):
        seq = plan.seq
        found = all_backward(
            *[[qkv[piece, rows_of(row, seq), cols] for row, _, cols in items] for piece in range(3)],
            [probs[row, tile] for row, tile, _ in items],
            [mixed[rows_of(row, seq), cols] for row, _, cols in items],
            scale,
        )
        for number, (row, tile, _) in enumerate(items):
            for piece in range(3):
                first = piece * plan.half + tile * TILE
                back[rows_of(row, seq), first : first + TILE] = found[piece][number]

    each_tile(plan, ROWS_AT_ONCE, back_rows)
    matrix = jnp.concatenate(
        [matrix_of(nat, 0, plan.wt, 0, plan.ht, plan.ht, p * plan.square) for p in range(3)],
        axis=1,
    )
    part[...] = mm(back[...], matrix, NT).astype(bf16)


def self_backward(
    plan, scale, nat, query_resid, text_resids, query_grad, query_mine, query_other, text_grads,
    text_mines, text_others, params, qkv, probs,
):
    tokens, width, half = plan.tokens, plan.width, plan.half
    return pl.pallas_call(
        functools.partial(self_backward_body, plan, scale),
        out_shape=(
            jax.ShapeDtypeStruct((tokens, width), f32),
            held((tokens, width), bf16),
            held((tokens, 3 * half), bf16),
            jax.ShapeDtypeStruct((tokens, width), bf16),
            jax.ShapeDtypeStruct((2, width), f32),
        ),
        in_specs=vmem_specs(16),
        out_specs=tuple(vmem_specs(5)),
        scratch_shapes=[
            pltpu.VMEM((tokens, half), bf16),
        ],
        compiler_params=vmem_params(),
        cost_estimate=cost(8 * tokens * width * half, 1.2e7),
        name="self_backward",
    )(
        *pin(nat, query_resid, query_grad), query_mine, query_other, *pin(*text_resids, *text_grads),
        *text_mines, *text_others, params, *pin(qkv, probs),
    )


def grad_blocks_body(first_block, pairs, source_count, spare, place, *refs):
    sources, target = refs[:source_count], refs[-1]
    if spare is not None:
        for number in range(spare[1]):
            target[place[spare[0] + number]] = jnp.zeros((TILE, TILE), bf16)
    base = first_block
    for left_at, right_at, right_first, right_width, step in pairs:
        terms = [(sources[a], sources[b]) for a, b in zip(left_at, right_at)]
        left_tiles, col_total = terms[0][0].shape[1] // TILE, right_width // TILE

        def one(chunk, carry, base=base, terms=terms, step=step, col_total=col_total,
                right_first=right_first, right_width=right_width):
            cols = pl.ds(pl.multiple_of(chunk * step * TILE, step * TILE), step * TILE)
            right_cols = slice(right_first, right_first + right_width)
            product = sum(mm(left[:, cols], right[:, right_cols], TN) for left, right in terms)
            first = base + chunk * step * col_total
            for row in range(step):
                for col in range(col_total):
                    target[place[first + row * col_total + col]] = product[
                        row * TILE : (row + 1) * TILE, col * TILE : (col + 1) * TILE
                    ].astype(bf16)
            return carry

        lax.fori_loop(0, left_tiles // step, one, 0)
        base += left_tiles * col_total


def grad_blocks(buffer, place, first_block, sources, pairs, flops, spare=None):
    given = [] if isinstance(buffer, jax.ShapeDtypeStruct) else pin(buffer)
    return pl.pallas_call(
        functools.partial(grad_blocks_body, first_block, pairs, len(sources), spare),
        out_shape=held(buffer.shape, buffer.dtype),
        in_specs=[pl.BlockSpec(memory_space=pltpu.SMEM)] + vmem_specs(len(sources) + len(given)),
        out_specs=vmem_specs(1)[0],
        input_output_aliases={1 + len(sources): 0} if given else {},
        compiler_params=vmem_params(),
        cost_estimate=cost(flops, 1e7),
        name="grad_blocks",
    )(place, *pin(*sources), *given)


def swap_tensor(part):
    if lax.axis_size("tensor") != 2:
        total = lax.psum(part.astype(f32), "tensor")
        return (total - part.astype(f32)).astype(bf16)
    return lax.ppermute(part, "tensor", [(0, 1), (1, 0)])


after = lax.optimization_barrier


def sum_steps(values):
    if lax.axis_size("dp") != RING_DEVICES:
        values = lax.psum(values, "dp")
        while True:
            values = yield values
    for bit in (1, 2, 4, 8):
        pairs = [(index, index ^ bit) for index in range(RING_DEVICES)]
        values = yield values + lax.ppermute(values, "dp", pairs)


def layer_rows(
    hidden, image, patches, segment_ids, cotangent, nat, norm_params, heads_local, scale, place
):
    rows, seq, width = hidden.shape
    plan = Plan(
        rows, seq, width, image.shape[2], patches, heads_local, FF // lax.axis_size("tensor")
    )
    tokens, learned, texts, half = plan.tokens, plan.learned, plan.texts, plan.half
    flat_hidden = hidden.reshape(tokens, width)
    flat_image = image.reshape(rows * plan.keys, plan.image_width)
    flat_back = cotangent.reshape(tokens, width)
    buffer = jax.ShapeDtypeStruct((place.shape[0], TILE, TILE), bf16)

    qkv, self_probs, mixed, query_part, *text_parts = self_forward(
        plan, scale, nat, flat_hidden, segment_ids[:, None, :]
    )
    query_other = swap_tensor(query_part)
    image_keys, image_values = image_forward(plan, nat, flat_image)
    text_parts[0], query_other, image_keys = after((text_parts[0], query_other, image_keys))
    text_others = [swap_tensor(text_parts[0]), None]
    query_first, first_query, low_query, cross_queries, cross_probs, looked, part_two = (
        cross_forward(
            plan, scale, nat, flat_hidden, query_part, query_other, norm_params, image_keys,
            image_values,
        )
    )
    other_two = swap_tensor(part_two)
    text_parts[1], text_others[0], other_two = after((text_parts[1], text_others[0], other_two))
    text_others[1] = swap_tensor(text_parts[1])
    texts_out = [
        text_forward(plan, 0, nat, flat_hidden, text_parts[0], text_others[0], norm_params), None
    ]
    other_text = [swap_tensor(texts_out[0][-1]), None]
    other_two, _ = after((other_two, texts_out[0][-1]))
    second_sum, second, low_second, query_gated, query_slope, part_query = query_forward(
        plan, nat, first_query, part_two, other_two, norm_params
    )
    other_query = swap_tensor(part_query)
    text_others[1], part_query = after((text_others[1], part_query))
    texts_out[1] = text_forward(
        plan, 1, nat, flat_hidden, text_parts[1], text_others[1], norm_params
    )
    other_text[1] = swap_tensor(texts_out[1][-1])
    text_first, first_text, low_text, text_gated, text_slope, part_text = zip(*texts_out)

    def text_backward(number):
        return feed_backward(
            plan, plan.text_first, (number * plan.half_rows, plan.half_rows), NQ, 3, nat,
            first_text[number], part_text[number], other_text[number], flat_back, norm_params,
            text_slope[number],
        )

    other_text[0], _ = after((other_text[0], part_text[1]))
    texts_back = [text_backward(0), None]
    other_four_text = [swap_tensor(texts_back[0][4]), None]
    other_query, _ = after((other_query, texts_back[0][4]))
    out_query, third_query, third_query_low, before_query, part_four_query, norm_query = (
        feed_backward(
            plan, plan.query_first, (0, rows), 0, 2, nat, second, part_query, other_query,
            flat_back, norm_params, query_slope,
        )
    )
    other_four_query = swap_tensor(part_four_query)
    other_text[1], _ = after((other_text[1], part_four_query))
    texts_back[1] = text_backward(1)
    other_four_text[1] = swap_tensor(texts_back[1][4])
    out_text, third_text, third_text_low, before_text, part_four_text, norm_text = zip(*texts_back)
    feed_pairs = [((0,), (1,), 0, plan.hidden, 6), ((2,), (3,), 0, width, 6)]
    before_query, _ = after((before_query, part_four_text[1]))
    buffer = grad_blocks(
        buffer, place, plan.query_first, [low_second, before_query, query_gated, third_query_low],
        feed_pairs, 4 * learned * width * plan.hidden,
        spare=(plan.block_count, place.shape[0] - plan.block_count),
    )
    other_four_query, other_four_text[0], buffer = after(
        (other_four_query, other_four_text[0], buffer)
    )
    second_grad, cross_low, query_back, key_back, value_back, part_five, norm_second = (
        cross_backward(
            plan, scale, nat, second_sum, third_query, part_four_query, other_four_query,
            norm_params, cross_queries, image_keys, image_values, cross_probs,
        )
    )
    other_five = swap_tensor(part_five)
    buffer, part_five = after((buffer, part_five))
    buffer = grad_blocks(
        buffer, place, plan.text_first, [*low_text, *before_text, *text_gated, *third_text_low],
        [((0, 1), (2, 3), 0, plan.hidden, 6), ((4, 5), (6, 7), 0, width, 6)],
        4 * texts * width * plan.hidden,
    )
    cross_flops = 2 * rows * plan.keys * plan.image_width * half
    buffer = grad_blocks(
        buffer, place, plan.cross_first, [low_query, query_back, flat_image, key_back],
        [((0,), (1,), 0, half, 6), ((2,), (3,), 0, half, 11)], cross_flops,
    )
    other_four_text[1], buffer = after((other_four_text[1], buffer))
    first_grad, self_low, self_back, part_six, norm_first = self_backward(
        plan, scale, nat, query_first, text_first, second_grad, part_five, other_five, third_text,
        part_four_text, other_four_text, norm_params, qkv, self_probs,
    )
    other_six = swap_tensor(part_six)
    norm_steps = sum_steps(jnp.stack([norm_first, norm_second, norm_query, norm_text[0] + norm_text[1]]))
    norms = next(norm_steps)
    buffer, part_six = after((buffer, part_six))
    buffer = grad_blocks(
        buffer, place, plan.image_first + plan.cross, [flat_image, value_back],
        [((0,), (1,), 0, half, 11)], cross_flops,
    )
    buffer, norms = after((buffer, norms))
    norms = norm_steps.send(norms)
    buffer = grad_blocks(
        buffer, place, plan.cross_out, [looked, cross_low], [((0,), (1,), 0, width, 3)],
        2 * learned * width * half,
    )
    buffer, norms = after((buffer, norms))
    norms = norm_steps.send(norms)
    buffer = grad_blocks(
        buffer, place, plan.self_first, [flat_hidden, self_back],
        [((0,), (1,), 0, half, 6), ((0,), (1,), half, half, 6), ((0,), (1,), 2 * half, half, 6)],
        6 * tokens * width * half,
    )
    buffer, norms = after((buffer, norms))
    buffer = grad_blocks(
        buffer, place, plan.self_out, [mixed, self_low], [((0,), (1,), 0, width, 3)],
        2 * tokens * width * half,
    )
    buffer, norms, other_six = after((buffer, norms, other_six))
    norms = norm_steps.send(norms)
    output_rows = jnp.concatenate(
        [
            out_query.reshape(rows, NQ, width),
            jnp.concatenate(out_text, axis=0).reshape(rows, seq - NQ, width),
        ],
        axis=1,
    )
    return (output_rows, first_grad, part_six, other_six, buffer, norms)


CHIP_RING = ((0, 0), (1, 0), (2, 0), (3, 0), (3, 1), (2, 1), (1, 1), (0, 1))
RING = len(CHIP_RING)
RING_DEVICES = 2 * RING


def ring_index(position, core):
    z, x = CHIP_RING[position % RING]
    return (z * 2 + x) * 2 + core


def direction_of(core):
    return 1 - 2 * core


RING_PAIRS = [
    (ring_index(position, core), ring_index(position + direction_of(core), core))
    for position in range(RING)
    for core in range(2)
]


def ring_place(index):
    return CHIP_RING.index((index // 4, index // 2 % 2)), index % 2


CORE_PAIRS = [(index, index ^ 1) for index in range(RING_DEVICES)]


def chain_parts(slots, chains):
    cuts = [slots * number // chains for number in range(chains + 1)]
    return [(first, last - first) for first, last in zip(cuts, cuts[1:])]


def place_blocks_body(first, ids, *refs):
    sources, target = refs[:-1], refs[-1]
    base = first
    for source in sources:
        for number in range(source.shape[0]):
            target[ids[base + number]] = source[number]
        base += source.shape[0]


def place_blocks(ids, first, sources, target, shape):
    operands = [ids, *pin(*sources)]
    aliases = {}
    if target is not None:
        operands += pin(target)
        aliases = {len(operands) - 1: 0}

    def body(ids, *refs):
        place_blocks_body(first, ids, *refs[: len(sources)], refs[-1])

    return pl.pallas_call(
        body,
        out_shape=held(shape, bf16),
        in_specs=[pl.BlockSpec(memory_space=pltpu.SMEM)] + vmem_specs(len(operands) - 1),
        out_specs=vmem_specs(1)[0],
        input_output_aliases=aliases,
        compiler_params=pltpu.CompilerParams(vmem_limit_bytes=4 * 1024 * 1024),
        cost_estimate=cost(0, 0),
        name="place_blocks",
    )(*operands)


def gather_positions(slots):
    table = np.zeros((RING_DEVICES, RING_DEVICES * slots), np.int32)
    for index in range(RING_DEVICES):
        position, core = ring_place(index)
        found = []
        for step in range(RING):
            for side in (core, 1 - core):
                owner = ring_index(position - direction_of(side) * step, side)
                found += [owner * slots + slot for slot in range(slots)]
        table[index] = found
    return table


AT_ONCE = 8


def index_body(count, device, order, arrival, departure, ids, place):
    me = device[0]

    def one(group, carry):
        numbers = [group * AT_ONCE + offset for offset in range(AT_ONCE)]
        blocks = [order[number] for number in numbers]
        arrived = [order[arrival[me, number]] for number in numbers]
        places = [departure[me, number] for number in numbers]
        for number, block, other, target in zip(numbers, blocks, arrived, places):
            ids[number] = other
            place[block] = target
        return carry

    lax.fori_loop(0, count // AT_ONCE, one, 0)


def block_indices(order, slots):
    count = order.shape[0]
    smem = pl.BlockSpec(memory_space=pltpu.SMEM)
    return pl.pallas_call(
        functools.partial(index_body, count),
        out_shape=(jax.ShapeDtypeStruct((count,), jnp.int32),) * 2,
        in_specs=[smem] * 4,
        out_specs=(smem, smem),
        compiler_params=vmem_params(),
        name="block_indices",
    )(
        lax.axis_index("dp").reshape(1),
        order,
        jnp.asarray(gather_positions(slots)),
        jnp.asarray(scatter_positions(slots)),
    )


def gather_ring(shard, order, image, chains=2):
    slots = shard.shape[0]
    parts = chain_parts(slots, chains)
    shape = (order.shape[0], TILE, TILE)
    ids, place = block_indices(order, slots)
    other = lax.ppermute(shard, "dp", CORE_PAIRS)
    held = [shard[first : first + count] for first, count in parts]
    natural = None
    waiting, first, placed = [shard, other], 0, 2 * slots
    for step in range(1, RING):
        held = [lax.ppermute(piece, "dp", RING_PAIRS) for piece in held]
        if step == 2:
            held[0], ids, place = lax.optimization_barrier((held[0], ids, place))
        if step == 3:
            held[0], image = lax.optimization_barrier((held[0], pad_patches(image)))
        if step >= 4:
            now = 2 + 2 * chains if step == 4 else 4 * chains
            count = sum(piece.shape[0] for piece in waiting[:now])
            natural = place_blocks(ids, first, waiting[:now], natural, shape)
            held[0], natural = lax.optimization_barrier((held[0], natural))
            waiting, first = waiting[now:], first + count
        waiting = waiting + held + [lax.ppermute(piece, "dp", CORE_PAIRS) for piece in held]
    return place_blocks(ids, first, waiting, natural, shape), image, place


def scatter_positions(slots):
    table = np.zeros((RING_DEVICES, RING_DEVICES * slots), np.int32)
    for index in range(RING_DEVICES):
        position, core = ring_place(index)
        for step in range(1, RING + 1):
            for number, side in enumerate((1 - core, core)):
                owner = ring_index(position - direction_of(side) * step, side)
                base = (number * RING + step - 1) * slots
                table[index, owner * slots : (owner + 1) * slots] = base + np.arange(slots)
    return table


def scatter_ring(packed, beside, slots, chains=2):
    parts = chain_parts(slots, chains)
    held = [None] * chains
    other = None
    for step in range(1, RING + 1):
        base = (step - 1) * slots
        if step % 2:
            if other is not None:
                packed, other = lax.optimization_barrier((packed, other))
            other = lax.ppermute(packed[base : base + 2 * slots], "dp", CORE_PAIRS)
            if step == 1:
                other, beside = lax.optimization_barrier((other, beside))
        pieces = []
        for number, (first, count) in enumerate(parts):
            start = (RING + step - 1) * slots + first
            place = (step - 1) % 2 * slots + first
            terms = [packed[start : start + count], other[place : place + count]]
            if held[number] is not None:
                terms.append(held[number])
            pieces.append(terms)
        if step == RING:
            return pieces, beside
        for number, terms in enumerate(pieces):
            summed = sum(term.astype(f32) for term in terms).astype(bf16)
            held[number] = lax.ppermute(summed, "dp", RING_PAIRS)


def pad_patches(image):
    return jnp.pad(image, ((0, 0), (0, -image.shape[1] % PATCHES_PAD), (0, 0)))


PANEL = 16
PACK = TILE // PANEL


def split_two(values):
    high = values.astype(bf16)
    return high, (values - high.astype(f32)).astype(bf16)


def split_three(values):
    high = values.astype(bf16)
    rest = values - high.astype(f32)
    middle = rest.astype(bf16)
    return high, middle, (rest - middle.astype(f32)).astype(bf16)


def fold(product):
    return product[:, :TILE] + product[:, TILE:]


def times_nn(left, right):
    high, low = split_two(right)
    row = join(1, high, low)
    return fold(mm(join(1, *split_two(left)), join(0, row, row), NN))


def times_precise(left, right):
    lh, lm, ll = split_three(left)
    rh, rm, rl = split_three(right)
    both = mm(join(1, lh, lm), join(0, join(1, rh, rm), join(1, rm, rh)), NN)
    return fold(both) + mm(join(1, lh, ll), join(0, rl, rh), NN)


def diagonal_blocks(rows, base):
    lane = lax.broadcasted_iota(jnp.int32, (PANEL, TILE), 1) // PANEL
    packed = jnp.zeros((PANEL, TILE), f32)
    for number in range(PACK):
        piece = rows[number * PANEL : (number + 1) * PANEL]
        shift = (number * PANEL - base) % TILE
        if shift:
            piece = pltpu.roll(piece, shift, 1)
        packed = jnp.where(lane == number, piece, packed)
    return packed


def factor_inverses(packed):
    groups = packed.shape[0] // PANEL
    shape = packed.shape
    lane = lax.broadcasted_iota(jnp.int32, shape, 1)
    row = lax.broadcasted_iota(jnp.int32, shape, 0) % PANEL
    col = lane % PANEL
    first = lane - col

    def spread(values, step):
        picked = values.reshape(groups, PANEL, TILE)[:, step : step + 1]
        return jnp.broadcast_to(picked, (groups, PANEL, TILE)).reshape(shape)

    scale = jnp.zeros(shape, f32)
    column = jnp.take_along_axis(packed, first, axis=1)
    for step in range(PANEL):
        pivot = spread(column, step)
        inverse = reciprocal(pivot)
        if step + 1 < PANEL:
            following = jnp.take_along_axis(packed, first + (step + 1), axis=1)
            following = following - column * (spread(column, step + 1) * inverse)
        scaled = jnp.where(col == step, 1.0, spread(packed, step)) * inverse
        kept = jnp.where(col == step, jnp.where(row > step, 0.0, 1.0), packed)
        packed = jnp.where(
            row > step, kept - column * scaled, jnp.where(row == step, kept, packed)
        )
        scale = jnp.where(row == step, lax.rsqrt(pivot), scale)
        if step + 1 < PANEL:
            column = following
    return jnp.where(col <= row, packed * scale, 0.0)


def reciprocal(values):
    rough = pl.reciprocal(values, approx=True)
    rough = rough * (2.0 - values * rough)
    return rough * (2.0 - values * rough)


def panel_products(solved, masked):
    lh, lm, ll = split_three(masked)
    rh, rm, rl = split_three(solved)
    found = []
    for number in range(PACK):
        rows = slice(number * PANEL, (number + 1) * PANEL)
        left = join(0, lh[rows], lh[rows], lm[rows], lh[rows], ll[rows], lm[rows])
        right = join(0, rh[rows], rm[rows], rh[rows], rl[rows], rh[rows], rm[rows])
        found.append(mm(left, right, TN))
    return found


def invert_factors(grams, inverses, count):
    groups = count // PACK
    lane = lax.broadcasted_iota(jnp.int32, (TILE, TILE), 1)
    sub = lax.broadcasted_iota(jnp.int32, (TILE, TILE), 0)
    same_block = lane // PANEL == sub // PANEL
    for panel in range(TILE // PANEL):
        base, end = panel * PANEL, (panel + 1) * PANEL
        inside = (lane >= base) & (lane < end)
        unit = (lane - base == sub % PANEL).astype(f32)
        packed = []
        for group in range(groups):
            rows = grams[group * PACK : (group + 1) * PACK, base:end, :].reshape(TILE, TILE)
            packed.append(diagonal_blocks(rows, base))
        inverses[...] = factor_inverses(jnp.concatenate(packed, axis=0))

        def one(first, width, base=base, end=end, inside=inside, unit=unit):
            solved = []
            for offset in range(width):
                group = first + offset
                place = pl.ds(pl.multiple_of(group * PANEL, PANEL), PANEL)
                spread = jnp.where(
                    same_block, jnp.concatenate([inverses[place, :]] * PACK, axis=0), 0.0
                )
                rows = grams[pl.ds(group * PACK, PACK), base:end, :].reshape(TILE, TILE)
                solved.append(times_precise(spread, jnp.where(inside, unit, rows)))
            for offset in range(width):
                grams[pl.ds((first + offset) * PACK, PACK), base:end, :] = solved[offset].reshape(
                    PACK, PANEL, TILE
                )
            if end == TILE:
                return
            for offset in range(width):
                matrices = pl.ds((first + offset) * PACK, PACK)
                old = grams[matrices, end:, :]
                products = panel_products(
                    solved[offset], jnp.where(lane >= end, solved[offset], 0.0)
                )
                products = jnp.stack([product[end:] for product in products])
                grams[matrices, end:, :] = jnp.where(inside[None, end:], 0.0, old) - products

        loop_groups(groups, GROUPS_AT_ONCE, one)


GROUPS_AT_ONCE = 8


def optimizer_slots(first, count, inputs, outputs, grams, products):
    slots = products.shape[0] // 2
    loaded = [[ref[first + offset] for ref in inputs] for offset in range(count)]
    grad, weight, moment, square, left, right, left_base, right_base = map(list, zip(*loaded))
    every = range(count)
    turned_base = [left_base[n].T for n in every]
    turned_grad = [grad[n].T for n in every]
    turned_right = [right_base[n].T for n in every]
    half = [times_nn(turned_base[n], grad[n]) for n in every]
    left = [
        beta_stats * left[n] + (1 - beta_stats) * times_nn(grad[n], turned_grad[n]) for n in every
    ]
    right = [
        beta_stats * right[n] + (1 - beta_stats) * times_nn(turned_grad[n], grad[n])
        for n in every
    ]
    rotated = [times_nn(half[n], right_base[n]) for n in every]
    left_product = [times_nn(left[n], left_base[n]) for n in every]
    right_product = [times_nn(right[n], right_base[n]) for n in every]
    moment = [beta_first * moment[n] + (1 - beta_first) * rotated[n] for n in every]
    square = [
        beta_second * square[n] + (1 - beta_second) * rotated[n] * rotated[n] for n in every
    ]
    step = [
        (moment[n] / (1 - beta_first**STEP))
        / (jnp.sqrt(square[n] / (1 - beta_second**STEP)) + adam_epsilon)
        for n in every
    ]
    half = [times_nn(left_base[n], step[n]) for n in every]
    left_gram = [times_precise(left_product[n].T, left_product[n]) for n in every]
    right_gram = [times_precise(right_product[n].T, right_product[n]) for n in every]
    full = [times_nn(half[n], turned_right[n]) for n in every]
    weight = [weight[n] - matrix_rate * (full[n] + matrix_decay * weight[n]) for n in every]
    for n in every:
        slot = first + n
        values = (weight[n], weight[n].astype(bf16), moment[n], square[n], left[n], right[n])
        for ref, value in zip(outputs, values):
            ref[slot] = value
        products[slot] = left_product[n]
        products[slots + slot] = right_product[n]
        grams[slot] = left_gram[n]
        grams[slots + slot] = right_gram[n]


def loop_groups(total, width, body):
    def one(number, carry):
        body(number * width, width)
        return carry

    lax.fori_loop(0, total // width, one, 0)
    if total % width:
        body(total - total % width, total % width)


def optimizer_body(padded, counts, *refs):
    pieces, refs = refs[: sum(counts)], refs[sum(counts) :]
    sources, targets = refs[:7], refs[7:15]
    gradient, inputs, outputs = refs[15], refs[16:23], refs[23:31]
    grams, products, inverses, in_sems, out_sems = refs[31:]
    slots = sources[0].shape[0]
    lane = lax.broadcasted_iota(jnp.int32, (TILE, TILE), 1)
    sub = lax.broadcasted_iota(jnp.int32, (TILE, TILE), 0)
    cuts = [cut for cut in (0, SLOTS_AT_ONCE, 3 * SLOTS_AT_ONCE) if cut < slots] + [slots]
    parts = [(first, last - first) for first, last in zip(cuts, cuts[1:])]
    loads = [
        [
            pltpu.make_async_copy(
                source.at[pl.ds(*part)], target.at[pl.ds(*part)], in_sems.at[number, index]
            )
            for index, (source, target) in enumerate(zip(sources, inputs))
        ]
        for number, part in enumerate(parts)
    ]
    for load in loads:
        for copy in load:
            copy.start()
    for number in range(2 * slots, padded):
        grams[number] = (lane == sub).astype(f32)
    base = 0
    for count in counts:
        terms, pieces = pieces[:count], pieces[count:]
        gradient[base : base + terms[0].shape[0]] = sum(term[...].astype(f32) for term in terms)
        base += terms[0].shape[0]
    for load, (start, count) in zip(loads, parts):
        for copy in load:
            copy.wait()
        loop_groups(
            count,
            min(SLOTS_AT_ONCE, count),
            lambda first, width: optimizer_slots(
                start + first, width, (gradient, *inputs), outputs, grams, products
            ),
        )
    stores = [
        pltpu.make_async_copy(staged, target, out_sems.at[index])
        for index, (staged, target) in enumerate(zip(outputs, targets))
    ]
    for copy in stores[:6]:
        copy.start()
    invert_factors(grams, inverses, padded)

    def finish(first, count):
        found = []
        for offset in range(count):
            for side in range(2):
                number = side * slots + first + offset
                turned = jnp.where(sub >= lane, grams[number], 0.0).T
                found.append(times_nn(products[number], turned))
        for offset in range(count):
            outputs[6][first + offset] = found[2 * offset]
            outputs[7][first + offset] = found[2 * offset + 1]

    loop_groups(slots, 8, finish)
    for copy in stores[6:]:
        copy.start()
    for copy in stores:
        copy.wait()


SLOTS_AT_ONCE = 6


def optimizer(pieces, *arrays):
    shape = arrays[0].shape
    slots = shape[0]
    padded = -(-2 * slots // PACK) * PACK
    kinds = [f32, bf16] + [f32] * 6
    counts = [len(terms) for terms in pieces]
    return pl.pallas_call(
        functools.partial(optimizer_body, padded, counts),
        out_shape=tuple(jax.ShapeDtypeStruct(shape, kind) for kind in kinds),
        in_specs=vmem_specs(sum(counts)) + any_specs(7),
        out_specs=tuple(any_specs(8)),
        scratch_shapes=[pltpu.VMEM(shape, f32)] * 8
        + [pltpu.VMEM(shape, kind) for kind in kinds]
        + [
            pltpu.VMEM((padded, TILE, TILE), f32),
            pltpu.VMEM((2 * slots, TILE, TILE), f32),
            pltpu.VMEM((padded // PACK * PANEL, TILE), f32),
            pltpu.SemaphoreType.DMA((3, 7)),
            pltpu.SemaphoreType.DMA((8,)),
        ],
        compiler_params=pltpu.CompilerParams(vmem_limit_bytes=60 * 1024 * 1024),
        name="optimizer",
    )(*[term for terms in pieces for term in terms], *arrays)


def per_device(
    hidden,
    image,
    segment_ids,
    cotangent,
    slot_block,
    weight_master,
    moment_one,
    moment_two,
    left_stat,
    right_stat,
    left_basis,
    right_basis,
    norm_params,
    norm_moment_one,
    norm_moment_two,
):
    tensors = lax.axis_size("tensor")
    width = hidden.shape[2]
    heads_local = HEADS // tensors
    scale = (width // HEADS) ** (-0.5)
    order = slot_block[0]
    slot_count = order.shape[0]
    slots = weight_master.shape[1]
    shard = weight_master[0].astype(bf16)
    ring = lax.axis_size("dp") == RING_DEVICES
    patches = image.shape[1]
    if ring:
        natural, image, place = gather_ring(shard, order, image)
    else:
        image = pad_patches(image)
        positions = jnp.arange(slot_count, dtype=jnp.int32)
        place = jnp.zeros_like(order).at[order].set(positions)
        gathered = lax.all_gather(shard, "dp", axis=0, tiled=True)
        natural = gathered[place]
    out_rows, first_grad, part_six, other_six, packed, norm_total = layer_rows(
        hidden, image, patches, segment_ids, cotangent, natural, norm_params, heads_local, scale,
        place,
    )
    if ring:
        owned, norm_total = scatter_ring(packed, norm_total, slots)
    else:
        owned = [[lax.psum_scatter(packed, "dp", scatter_dimension=0, tiled=True)]]
    in_grad = first_grad + (part_six.astype(f32) + other_six.astype(f32))
    in_grad = in_grad.reshape(hidden.shape)
    updated = optimizer(
        owned,
        weight_master[0],
        moment_one[0],
        moment_two[0],
        left_stat[0],
        right_stat[0],
        left_basis[0],
        right_basis[0],
    )
    (
        weight_new,
        weight_copy,
        moment_one_new,
        moment_two_new,
        left_stat_new,
        right_stat_new,
        left_basis_new,
        right_basis_new,
    ) = [array[None] for array in updated]
    norm_first = beta_first * norm_moment_one + (1 - beta_first) * norm_total
    norm_second = beta_second * norm_moment_two + (1 - beta_second) * norm_total * norm_total
    norm_new = norm_params - norm_rate * (norm_first / (1 - beta_first**STEP)) / (
        jnp.sqrt(norm_second / (1 - beta_second**STEP)) + adam_epsilon
    )
    return (
        out_rows,
        in_grad,
        weight_new,
        weight_copy,
        moment_one_new,
        moment_two_new,
        left_stat_new,
        right_stat_new,
        left_basis_new,
        right_basis_new,
        norm_first,
        norm_second,
        norm_new,
    )


def solution(mesh):
    in_specs = (
        P("dp", None, None),
        P("dp", None, None),
        P("dp", None),
        P("dp", None, None),
        P("tensor", None),
        P("tensor", "dp", None, None),
        P("tensor", "dp", None, None),
        P("tensor", "dp", None, None),
        P("tensor", "dp", None, None),
        P("tensor", "dp", None, None),
        P("tensor", "dp", None, None),
        P("tensor", "dp", None, None),
        P(),
        P(),
        P(),
    )
    out_specs = (
        P("dp", None, None),
        P("dp", None, None),
        P("tensor", "dp", None, None),
        P("tensor", "dp", None, None),
        P("tensor", "dp", None, None),
        P("tensor", "dp", None, None),
        P("tensor", "dp", None, None),
        P("tensor", "dp", None, None),
        P("tensor", "dp", None, None),
        P("tensor", "dp", None, None),
        P(),
        P(),
        P(),
    )
    return jax.shard_map(
        per_device, mesh=mesh, in_specs=in_specs, out_specs=out_specs, check_vma=False
    )
```
